128 devices in a mesh: gx: 8 (over y, core), gy: 16 (over x, z).
Axes of the slice: x: 4, y: 4, z: 4, core: 2. Of those that a mesh axis runs over, the one named last changes fastest.
Arguments:
- source: float32 [16, 256, 2048], P(None, 'gx', 'gy'), may hold values from -6 to 6
- absorption: float32 [16, 256, 2048], P(None, 'gx', 'gy'), may hold values from 0.05 to 2
- basis: bfloat16 [32, 16, 256, 2048], P(None, None, 'gx', 'gy'), may hold values from -0.0234375 to 0.0234375
- coarse_inverse: float32 [4096, 4096], P(('gx', 'gy')), as said below
- margin_width: int32 [8, 16], P('gx', 'gy'), may hold values from 1 to 8, as said below
- coarse_slot: int32 [8, 16, 32], P('gx', 'gy'), may hold values from 0 to 4095, as said below
Outputs:
- concentration: float32 [16, 256, 2048], P(None, 'gx', 'gy')
- residual: float32 [16, 256, 2048], P(None, 'gx', 'gy')
The draws below stay inside these ranges and needn't reach their ends.
Inputs may be any that keep to these rules, and one draw needn't show every extreme that they name: `margin_width`: some subdomain has margin width exactly 8. `coarse_slot`: each number of 0 to 4095 appears exactly once. `coarse_inverse`: symmetric and positive definite.
All inputs are finite; a program needn't handle non-finite values.
Results may differ from the reference program's by a relative error of at most 0.01.
Values sent between devices are 32-bit elements; how exact they have to be, the bound alone decides.
No kernel may reach another device: no remote copies, remote signals or barrier semaphores. Data moves between devices by JAX's collectives and lax.ppermute only.
A program may use at most 64 MiB of HBM per device.

```python
import math
import jax
import jax.numpy as jnp
from jax import lax

CX = 32
CY = 128
NZ = 16
NDEF = 32
WMAX = 8
KCHEB = 9
ITERS = 2
SUBX = 8
SUBY = 16
NX = 256
NY = 2048
COARSE = 4096


def draw_coarse_inverse(key, part):
    key = jax.random.fold_in(key, 37)
    first_key, second_key = jax.random.split(key)
    spread = jax.random.normal(first_key, (COARSE, COARSE), jnp.float32)
    diagonal = jnp.exp(jax.random.uniform(second_key, (COARSE,), jnp.float32, math.log(4.0), math.log(12.0)))
    symmetric = (spread + spread.T) * (2.0 * 0.70710678 / math.sqrt(COARSE))
    return (symmetric + jnp.diag(diagonal)).astype(jnp.float32)


def draw_margin_width(key, part):
    key = jax.random.fold_in(key, 11)
    first_key, second_key = jax.random.split(key)
    widths = jax.random.randint(first_key, (SUBX * SUBY,), 1, WMAX + 1)
    chosen = jax.random.randint(second_key, (), 0, SUBX * SUBY)
    widths = jnp.where(jnp.arange(SUBX * SUBY) == chosen, WMAX, widths)
    return widths.reshape(SUBX, SUBY).astype(jnp.int32)


def draw_coarse_slot(key, part):
    key = jax.random.fold_in(key, 23)
    return jax.random.permutation(key, COARSE).astype(jnp.int32).reshape(SUBX, SUBY, NDEF)


def steps_of(own_key, shape, shards, least, high):
    loudness, own = 1.0, jax.random.fold_in(own_key, 6)
    for position, shards_of in shards:
        draws = jnp.exp(jax.random.uniform(jax.random.fold_in(own, position), (shards_of,), jnp.float32, least / len(shards), high / len(shards)))
        loudness = loudness * jnp.repeat(draws, shape[position] // shards_of).reshape([-1 if axis == position else 1 for axis in range(len(shape))])
    return loudness


def gaussian(stream_key, dims, scale, most, cuts=(), held_as=jnp.bfloat16):
    values = scale * jax.random.normal(stream_key, dims, jnp.float32)
    if cuts:
        values = values * steps_of(stream_key, dims, cuts, -0.22, 0.18)
    return jnp.clip(values, -most, most).astype(held_as)


def setup_inputs(seed: int = 0) -> dict:
    seeds = jax.random.split(jax.random.key(seed), 7)
    source = gaussian(seeds[0], (NZ, NX, NY), 1.0, 6.0, ((1, 8), (2, 16)), jnp.float32)
    absorption = jnp.clip(jnp.exp(math.log(2.0) - 3.6888794 * jax.random.uniform(seeds[1], (NZ, NX, NY), jnp.float32) ** steps_of(seeds[1], (NZ, NX, NY), ((1, 8), (2, 16)), -0.2, 0.2)), 0.05, 2.0)
    basis = gaussian(seeds[2], (NDEF, NZ, NX, NY), (NZ * CX * CY) ** -0.5, 0.0234375, ((2, 8), (3, 16)))
    coarse_inverse = draw_coarse_inverse(jax.random.fold_in(seeds[6], 71), 0)
    margin_width = draw_margin_width(jax.random.fold_in(seeds[6], 71), 0)
    coarse_slot = draw_coarse_slot(jax.random.fold_in(seeds[6], 71), 0)
    return dict(source=source, absorption=absorption, basis=basis, coarse_inverse=coarse_inverse, margin_width=margin_width, coarse_slot=coarse_slot)


lowest_rate = 0.05
highest_rate = 18.5
vertical = 2.0


def apply_stencil(padded, coefficient):
    center = padded[:, 1:-1, 1:-1]
    stacked = jnp.pad(center, ((1, 1), (0, 0), (0, 0)))
    beside = padded[:, 2:, 1:-1] + padded[:, :-2, 1:-1] + padded[:, 1:-1, 2:] + padded[:, 1:-1, :-2]
    above = stacked[2:] + stacked[:-2]
    return (coefficient + (4.0 + 2.0 * vertical)) * center - beside - vertical * above


def pad_sides(field, width):
    return jnp.pad(field, ((0, 0), (width, width), (width, width)))


def window_of(row_start, col_start, margin, block_x, block_y, total_x, total_y, reach):
    row_local = jnp.arange(block_x + 2 * reach, dtype=jnp.int32)
    col_local = jnp.arange(block_y + 2 * reach, dtype=jnp.int32)
    row_global = row_start + row_local - reach
    col_global = col_start + col_local - reach
    row_inside = (row_global >= 0) & (row_global < total_x) & (row_local >= reach - margin) & (row_local < block_x + reach + margin)
    col_inside = (col_global >= 0) & (col_global < total_y) & (col_local >= reach - margin) & (col_local < block_y + reach + margin)
    return (row_inside[:, None] & col_inside[None, :]).astype(jnp.float32)[None]


def local_solve(source_window, coefficient, window, steps_count):
    theta = 0.5 * (highest_rate + lowest_rate)
    delta = 0.5 * (highest_rate - lowest_rate)
    ratio = theta / delta
    guess = source_window / theta
    update = guess
    rho_old = 1.0 / ratio
    for sweep in range(steps_count - 1):
        applied = window * apply_stencil(pad_sides(guess, 1), coefficient)
        defect = source_window - applied
        rho_new = 1.0 / (2.0 * ratio - rho_old)
        update = (rho_new * rho_old) * update + (2.0 * rho_new / delta) * defect
        guess = guess + update
        rho_old = rho_new
    return guess


def precondition(resid, coef_pad, basis, coarse_inverse, margin_width, coarse_slot):
    reach = WMAX
    ext_x = CX + 2 * reach
    ext_y = CY + 2 * reach
    resid_pad = pad_sides(resid, reach)
    zero_index = jnp.int32(0)

    def visit(index, summed):
        index = jnp.asarray(index).astype(jnp.int32)
        block_i = (index // SUBY).astype(jnp.int32)
        block_j = (index % SUBY).astype(jnp.int32)
        row_start = (block_i * CX).astype(jnp.int32)
        col_start = (block_j * CY).astype(jnp.int32)
        local_resid = lax.dynamic_slice(resid_pad, (zero_index, row_start, col_start), (NZ, ext_x, ext_y))
        local_coef = lax.dynamic_slice(coef_pad, (zero_index, row_start, col_start), (NZ, ext_x, ext_y))
        window = window_of(row_start, col_start, margin_width[block_i, block_j], CX, CY, NX, NY, reach)
        result = local_solve(window * local_resid, local_coef, window, KCHEB)
        current = lax.dynamic_slice(summed, (zero_index, row_start, col_start), (NZ, ext_x, ext_y))
        return lax.dynamic_update_slice(summed, current + result, (zero_index, row_start, col_start))

    summed = lax.fori_loop(0, SUBX * SUBY, visit, jnp.zeros((NZ, NX + 2 * reach, NY + 2 * reach), jnp.float32))
    smoothed = summed[:, reach:reach + NX, reach:reach + NY]
    resid_b = resid.astype(jnp.bfloat16)

    def basis_block(index):
        block_i = (index // SUBY).astype(jnp.int32)
        block_j = (index % SUBY).astype(jnp.int32)
        start = (zero_index, zero_index, (block_i * CX).astype(jnp.int32), (block_j * CY).astype(jnp.int32))
        return lax.dynamic_slice(basis, start, (NDEF, NZ, CX, CY)).reshape(NDEF, NZ * CX * CY)

    def resid_block(index):
        block_i = (index // SUBY).astype(jnp.int32)
        block_j = (index % SUBY).astype(jnp.int32)
        start = (zero_index, (block_i * CX).astype(jnp.int32), (block_j * CY).astype(jnp.int32))
        return lax.dynamic_slice(resid_b, start, (NZ, CX, CY)).reshape(NZ * CX * CY)

    def project(index):
        return jnp.dot(basis_block(index), resid_block(index), preferred_element_type=jnp.float32)

    indices = jnp.arange(SUBX * SUBY, dtype=jnp.int32)
    projected = lax.map(project, indices)
    slots = coarse_slot.reshape(SUBX * SUBY * NDEF).astype(jnp.int32)
    projection = jnp.zeros((COARSE,), jnp.float32).at[slots].set(projected.reshape(-1))
    coarse = jnp.dot(coarse_inverse, projection, precision=lax.Precision.HIGHEST)
    coefficient = coarse[slots].reshape(SUBX * SUBY, NDEF).astype(jnp.bfloat16)

    def correct(index):
        row = lax.dynamic_slice_in_dim(coefficient, index, 1, 0)
        return jnp.dot(row, basis_block(index), preferred_element_type=jnp.float32).reshape(NZ, CX, CY)

    pieces = lax.map(correct, indices)
    correction = pieces.reshape(SUBX, SUBY, NZ, CX, CY).transpose(2, 0, 3, 1, 4).reshape(NZ, NX, NY)
    preconditioned = smoothed + correction
    weight = jnp.sum(resid * smoothed) + jnp.dot(projection, coarse, precision=lax.Precision.HIGHEST)
    return preconditioned, weight


def reference(source, absorption, basis, coarse_inverse, margin_width, coarse_slot):
    coef_pad = pad_sides(absorption, WMAX)
    concentration = jnp.zeros_like(source)
    residual = source
    preconditioned, rz_value = precondition(residual, coef_pad, basis, coarse_inverse, margin_width, coarse_slot)
    direction = preconditioned
    for iteration in range(ITERS):
        image = apply_stencil(pad_sides(direction, 1), absorption)
        step_size = rz_value / jnp.sum(direction * image)
        concentration = concentration + step_size * direction
        residual = residual - step_size * image
        if iteration + 1 < ITERS:
            preconditioned, weight = precondition(residual, coef_pad, basis, coarse_inverse, margin_width, coarse_slot)
            direction = preconditioned + (weight / rz_value) * direction
            rz_value = weight
    return concentration, residual
```

```python
import jax
import jax.numpy as jnp
from jax import lax
from jax.sharding import PartitionSpec as P

WMAX = 8
KCHEB = 9
AXES = ("gx", "gy")

lowest_rate = 0.05
highest_rate = 18.5
vertical = 2.0


def extended(block, width):
    for axis, dim in (("gx", 1), ("gy", 2)):
        count = lax.axis_size(axis)
        forward = [(i, i + 1) for i in range(count - 1)]
        backward = [(target, source) for source, target in forward]
        low = lax.ppermute(
            lax.slice_in_dim(block, block.shape[dim] - width, None, axis=dim), axis, forward
        )
        high = lax.ppermute(lax.slice_in_dim(block, 0, width, axis=dim), axis, backward)
        block = jnp.concatenate([low, block, high], axis=dim)
    return block


def ringed(block):
    for_axis = []
    for axis, dim in (("gx", 1), ("gy", 2)):
        count = lax.axis_size(axis)
        forward = [(i, i + 1) for i in range(count - 1)]
        backward = [(target, source) for source, target in forward]
        low = lax.ppermute(
            lax.slice_in_dim(block, block.shape[dim] - 1, None, axis=dim), axis, forward
        )
        high = lax.ppermute(lax.slice_in_dim(block, 0, 1, axis=dim), axis, backward)
        for_axis.append((low, high))
    (up, down), (left, right) = for_axis
    left = jnp.pad(left, ((0, 0), (1, 1), (0, 0)))
    right = jnp.pad(right, ((0, 0), (1, 1), (0, 0)))
    return jnp.concatenate([left, jnp.concatenate([up, block, down], axis=1), right], axis=2)


def everyone(row):
    count = lax.axis_size("gx") * lax.axis_size("gy")
    return lax.all_to_all(
        jnp.broadcast_to(row[None], (count, row.shape[0])), AXES, 0, 0, tiled=True
    )


def apply_stencil(padded, coefficient):
    center = padded[:, 1:-1, 1:-1]
    stacked = jnp.pad(center, ((1, 1), (0, 0), (0, 0)))
    beside = padded[:, 2:, 1:-1] + padded[:, :-2, 1:-1] + padded[:, 1:-1, 2:] + padded[:, 1:-1, :-2]
    above = stacked[2:] + stacked[:-2]
    return (coefficient + (4.0 + 2.0 * vertical)) * center - beside - vertical * above


def window_of(row_start, col_start, margin, block_x, block_y, total_x, total_y, reach):
    row_local = jnp.arange(block_x + 2 * reach, dtype=jnp.int32)
    col_local = jnp.arange(block_y + 2 * reach, dtype=jnp.int32)
    row_global = row_start + row_local - reach
    col_global = col_start + col_local - reach
    row_inside = (
        (row_global >= 0)
        & (row_global < total_x)
        & (row_local >= reach - margin)
        & (row_local < block_x + reach + margin)
    )
    col_inside = (
        (col_global >= 0)
        & (col_global < total_y)
        & (col_local >= reach - margin)
        & (col_local < block_y + reach + margin)
    )
    return (row_inside[:, None] & col_inside[None, :]).astype(jnp.float32)[None]


def local_solve(source_window, coefficient, window):
    theta = 0.5 * (highest_rate + lowest_rate)
    delta = 0.5 * (highest_rate - lowest_rate)
    ratio = theta / delta
    guess = source_window / theta
    update = guess
    rho_old = 1.0 / ratio
    for sweep in range(KCHEB - 1):
        padded = jnp.pad(guess, ((0, 0), (1, 1), (1, 1)))
        defect = source_window - window * apply_stencil(padded, coefficient)
        rho_new = 1.0 / (2.0 * ratio - rho_old)
        update = rho_new * rho_old * update + 2.0 * rho_new / delta * defect
        guess = guess + update
        rho_old = rho_new
    return guess


def fold_window(extended, reach, block_x, block_y):
    def beside(rims, axis, dim):
        count = lax.axis_size(axis)
        forward = [(i, i + 1) for i in range(count - 1)]
        backward = [(target, source) for source, target in forward]
        low = lax.slice_in_dim(rims, 0, reach, axis=dim)
        high = lax.slice_in_dim(rims, rims.shape[dim] - reach, None, axis=dim)
        return lax.ppermute(high, axis, forward), lax.ppermute(low, axis, backward)

    from_low, from_high = beside(extended, "gx", 1)
    middle = extended[:, reach : block_x + reach]
    middle = middle.at[:, :reach].add(from_low)
    middle = middle.at[:, block_x - reach :].add(from_high)
    from_low, from_high = beside(middle, "gy", 2)
    inner = middle[:, :, reach : block_y + reach]
    inner = inner.at[:, :, :reach].add(from_low)
    return inner.at[:, :, block_y - reach :].add(from_high)


def place(values, slots):
    flat = slots.reshape(-1)
    values = values.reshape(-1)
    high = jnp.where((flat // 128)[None, :] == jnp.arange(32)[:, None], values[None, :], 0.0)
    low = ((flat % 128)[:, None] == jnp.arange(128)[None, :]).astype(jnp.float32)
    return jnp.dot(high, low, precision=lax.Precision.HIGHEST)


def shards(source, absorption, basis, coarse_inverse, margin_width, coarse_slot):
    levels, block_x, block_y = source.shape
    reach = WMAX
    slots = coarse_slot.reshape(-1)
    basis_flat = basis.reshape(basis.shape[0], -1)
    window = window_of(
        lax.axis_index("gx") * block_x,
        lax.axis_index("gy") * block_y,
        margin_width[0, 0],
        block_x,
        block_y,
        block_x * lax.axis_size("gx"),
        block_y * lax.axis_size("gy"),
        reach,
    )

    def project(field):
        high = field.astype(jnp.bfloat16)
        low = (field - high.astype(jnp.float32)).astype(jnp.bfloat16)
        both = jnp.stack([high, low]).reshape(2, -1)
        return lax.dot_general(
            basis_flat, both, (((1,), (1,)), ((), ())), preferred_element_type=jnp.float32
        ).sum(1)

    def coarse_solve(projections, all_slots):
        placed = place(projections, all_slots)
        rows = jnp.dot(coarse_inverse, placed.reshape(-1), precision=lax.Precision.HIGHEST)
        solved = everyone(rows)
        pick = (slots[:, None] // 32 == jnp.arange(128)[None, :]).astype(jnp.float32)
        found = jnp.dot(pick, solved, precision=lax.Precision.HIGHEST)
        return jnp.sum(jnp.where(slots[:, None] % 32 == jnp.arange(32)[None, :], found, 0.0), 1)

    def correct(coarse):
        return jnp.dot(
            coarse.astype(jnp.bfloat16)[None, :], basis_flat, preferred_element_type=jnp.float32
        ).reshape(levels, block_x, block_y)

    projected0 = project(source)
    both = extended(jnp.concatenate([source, absorption]), reach)
    coef_ext = both[levels:]
    told = everyone(jnp.concatenate([projected0, slots.astype(jnp.float32)]))
    all_slots = told[:, 32:64].astype(jnp.int32)
    smooth0 = fold_window(local_solve(window * both[:levels], coef_ext, window), reach, block_x, block_y)
    coarse0 = coarse_solve(told[:, :32], all_slots)
    direction = smooth0 + correct(coarse0)
    image_ext = apply_stencil(extended(direction, reach + 1), coef_ext)
    image = image_ext[:, reach:-reach, reach:-reach]
    weight_part = jnp.sum(source * smooth0) + jnp.sum(projected0 * coarse0)
    curve_part = jnp.sum(direction * image)
    projected1 = project(image)
    told = everyone(jnp.concatenate([projected1, jnp.stack([weight_part, curve_part])]))
    weight0 = jnp.sum(told[:, 32])
    curve0 = jnp.sum(told[:, 33])
    smooth1 = fold_window(local_solve(window * image_ext, coef_ext, window), reach, block_x, block_y)
    coarse1 = coarse_solve(told[:, :32], all_slots)
    step0 = weight0 / curve0
    moved = smooth1 + correct(coarse1)
    moved_image = apply_stencil(ringed(moved), absorption)
    residual = source - step0 * image
    precond = direction - step0 * moved
    precond_image = image - step0 * moved_image
    weight_part = jnp.sum(residual * (smooth0 - step0 * smooth1)) + jnp.sum(
        (projected0 - step0 * projected1) * (coarse0 - step0 * coarse1)
    )
    own_part = jnp.sum(precond * precond_image)
    cross_part = jnp.sum(precond * image + direction * precond_image)
    weight1, own, cross = jnp.sum(everyone(jnp.stack([weight_part, own_part, cross_part])), 0)
    ratio = weight1 / weight0
    step1 = weight1 / (own + ratio * (cross + ratio * curve0))
    concentration = step0 * direction + step1 * (precond + ratio * direction)
    residual = residual - step1 * (precond_image + ratio * image)
    return (concentration, residual)


def solution(mesh):
    return jax.shard_map(
        shards,
        mesh=mesh,
        in_specs=(
            P(None, "gx", "gy"),
            P(None, "gx", "gy"),
            P(None, None, "gx", "gy"),
            P(("gx", "gy"), None),
            P("gx", "gy"),
            P("gx", "gy", None),
        ),
        out_specs=(P(None, "gx", "gy"), P(None, "gx", "gy")),
        check_vma=False,
    )
```

```python
import functools

import jax
import jax.numpy as jnp
from jax import lax
from jax.experimental import pallas as pl
from jax.experimental.pallas import tpu as pltpu
from jax.sharding import PartitionSpec as P

KCHEB = 9
AXES = ("gx", "gy")
LEVELS = 16
ROWS = 32
COLS = 128
VECTORS = 32
EDGE = 16
TALL = ROWS + 2 * EDGE
HIGHEST = lax.Precision.HIGHEST

lowest_rate = 0.05
highest_rate = 18.5
vertical = 2.0
theta = 0.5 * (highest_rate + lowest_rate)
delta = 0.5 * (highest_rate - lowest_rate)
VMEM_LIMIT = 44 * 1024 * 1024


def chebyshev_table():
    ratio = theta / delta
    rho_old = 1.0 / ratio
    table = []
    for _ in range(KCHEB - 1):
        rho_new = 1.0 / (2.0 * ratio - rho_old)
        table.append((rho_new * rho_old, 2.0 * rho_new / delta))
        rho_old = rho_new
    return table


def iota(shape, dim):
    return lax.broadcasted_iota(jnp.int32, shape, dim)


def roll(value, shift):
    return pltpu.roll(value, shift % COLS, 1)


def exchange(forward_value, backward_value, axis):
    count = lax.axis_size(axis)
    forward = [(i, i + 1) for i in range(count - 1)]
    backward = [(target, source) for source, target in forward]
    return lax.ppermute(forward_value, axis, forward), lax.ppermute(backward_value, axis, backward)


def everyone(rows):
    return lax.all_to_all(rows, AXES, 0, 0, tiled=True)


def row_of_sums(sums):
    padded = jnp.concatenate([sums, jnp.zeros((COLS - VECTORS, COLS), jnp.float32)], 0)
    ones = jnp.ones((COLS, COLS), jnp.float32)
    return lax.dot_general(
        ones, padded, (((1,), (1,)), ((), ())), precision=HIGHEST, preferred_element_type=jnp.float32
    )


def first_kernel(field_ref, basis_ref, told_ref, out_ref, up_ref, down_ref, left_ref, right_ref, sums_ref):
    step = pl.program_id(0)
    group = basis_ref.shape[0]
    lane = iota((ROWS, COLS), 1)

    @pl.when(step == 0)
    def _():
        left_ref[...] = jnp.zeros_like(left_ref)
        right_ref[...] = jnp.zeros_like(right_ref)

    def level(z, sums):
        field = field_ref[z]
        low = left_ref[z]
        high = right_ref[z]
        new = []
        for j in range(group):
            values = basis_ref[j, z].astype(jnp.float32)
            product = values * field
            new.append(
                sums[j] + product[0:8] + product[8:16] + product[16:24] + product[24:32]
            )
            up_ref[j, pl.ds(z, 1), :] = values[0:1]
            down_ref[j, pl.ds(z, 1), :] = values[ROWS - 1 : ROWS]
            k = step * group + j
            turned = pltpu.roll(values, k, 1)
            low = jnp.where(lane == k, turned, low)
            turned = pltpu.roll(values, k + 1, 1)
            high = jnp.where(lane == k, turned, high)
        left_ref[z] = low
        right_ref[z] = high
        return tuple(new)

    zero = jnp.zeros((8, COLS), jnp.float32)
    sums = lax.fori_loop(0, LEVELS, level, (zero,) * group)
    for j in range(group):
        sums_ref[pl.ds(step * group + j, 1), :] = jnp.sum(sums[j], axis=0, keepdims=True)

    @pl.when(step == pl.num_programs(0) - 1)
    def _():
        out_ref[...] = row_of_sums(sums_ref[...]) + told_ref[...]


def first_projection(field, basis, told_row):
    group = 8
    edge_rows = jax.ShapeDtypeStruct((VECTORS, LEVELS, COLS), jnp.float32)
    edge_cols = jax.ShapeDtypeStruct((LEVELS, ROWS, COLS), jnp.float32)
    rows_spec = pl.BlockSpec((group, LEVELS, COLS), lambda i: (i, 0, 0))
    cols_spec = pl.BlockSpec((LEVELS, ROWS, COLS), lambda i: (0, 0, 0))
    return pl.pallas_call(
        first_kernel,
        grid=(VECTORS // group,),
        in_specs=[
            pl.BlockSpec((LEVELS, ROWS, COLS), lambda i: (0, 0, 0)),
            pl.BlockSpec((group, LEVELS, ROWS, COLS), lambda i: (i, 0, 0, 0)),
            pl.BlockSpec((1, COLS), lambda i: (0, 0)),
        ],
        out_specs=[
            pl.BlockSpec((COLS, COLS), lambda i: (0, 0)),
            rows_spec,
            rows_spec,
            cols_spec,
            cols_spec,
        ],
        out_shape=[jax.ShapeDtypeStruct((COLS, COLS), jnp.float32), edge_rows, edge_rows, edge_cols, edge_cols],
        scratch_shapes=[pltpu.VMEM((VECTORS, COLS), jnp.float32)],
        compiler_params=pltpu.CompilerParams(vmem_limit_bytes=VMEM_LIMIT),
        name="first_projection",
    )(field, basis, told_row)


def coarse_rows(told_ref, slots_ref, inverse_ref, out_ref):
    told = told_ref[...]
    slots = slots_ref[...]
    turned = told.T
    slots_turned = slots.T
    lane = iota((COLS, COLS), 1)
    sub = iota((VECTORS, COLS), 0)
    placed = jnp.zeros((3 * VECTORS, COLS), jnp.float32)
    for k in range(VECTORS):
        slot_column = slots[:, VECTORS + k : VECTORS + k + 1].astype(jnp.int32)
        ones = jnp.where((slot_column & 127) == lane, 1.0, 0.0).astype(jnp.bfloat16)
        slot_row = slots_turned[VECTORS + k : VECTORS + k + 1, :].astype(jnp.int32)
        values = turned[k : k + 1, :]
        spread = jnp.where((slot_row >> 7) == sub, values, 0.0)
        first = spread.astype(jnp.bfloat16)
        rest = spread - first.astype(jnp.float32)
        second = rest.astype(jnp.bfloat16)
        third = (rest - second.astype(jnp.float32)).astype(jnp.bfloat16)
        parts = jnp.concatenate([first, second, third], 0)
        placed = placed + jnp.dot(parts, ones, preferred_element_type=jnp.float32)
    placed = placed[:VECTORS] + placed[VECTORS : 2 * VECTORS] + placed[2 * VECTORS :]
    total = jnp.zeros((VECTORS, COLS), jnp.float32)
    for high in range(VECTORS):
        total = total + inverse_ref[:, high * COLS : (high + 1) * COLS] * placed[high : high + 1]
    out_ref[...] = row_of_sums(total)


def pack_strips(parts, forward_ref, backward_ref, at):
    for group in range(LEVELS // 8):
        row = 0
        for part in parts:
            height = part.shape[1]
            lane = iota((height, COLS), 1)
            ahead = jnp.zeros((height, COLS), jnp.float32)
            behind = ahead
            for j in range(8):
                value = part[group * 8 + j]
                mine = (lane >= EDGE * j) & (lane < EDGE * (j + 1))
                ahead = jnp.where(mine, roll(value, EDGE * j - (COLS - EDGE)), ahead)
                behind = jnp.where(mine, roll(value, EDGE * j), behind)
            forward_ref[at + group, row : row + height, :] = ahead
            backward_ref[at + group, row : row + height, :] = behind
            row += height


def middle_kernel(fields, told_ref, slots_ref, inverse_ref, *refs):
    ins = refs[: 3 * fields]
    out_ref, forward_ref, backward_ref = refs[3 * fields :]
    for f in range(fields):
        pack_strips(ins[3 * f : 3 * f + 3], forward_ref, backward_ref, 2 * f)
    coarse_rows(told_ref, slots_ref, inverse_ref, out_ref)


def middle(told, slots_told, inverse_rows, fields):
    strips = jax.ShapeDtypeStruct((2 * len(fields), TALL, COLS), jnp.float32)
    flat = [part for field in fields for part in field]
    return pl.pallas_call(
        functools.partial(middle_kernel, len(fields)),
        out_shape=[jax.ShapeDtypeStruct((COLS, COLS), jnp.float32), strips, strips],
        compiler_params=pltpu.CompilerParams(vmem_limit_bytes=VMEM_LIMIT),
        name="coarse_rows",
    )(told, slots_told, inverse_rows, *flat)


class Place:
    def __init__(self, place_ref, told_ref):
        self.row = place_ref[0]
        self.col = place_ref[1]
        self.rows = place_ref[2]
        self.cols = place_ref[3]
        self.told_ref = told_ref

    def index(self, down, right):
        row = jnp.clip(self.row + down, 0, self.rows - 1)
        col = jnp.clip(self.col + right, 0, self.cols - 1)
        return row * self.cols + col

    def margin(self, down, right):
        row, col = self.row + down, self.col + right
        real = (row >= 0) & (row < self.rows) & (col >= 0) & (col < self.cols)
        margin = self.told_ref[pl.ds(self.index(down, right), 1), :][:, 64:65]
        return jnp.where(real, margin.astype(jnp.int32), -4096)


def masks(place, own_ref, beside_ref, strip_ref):
    shape = (TALL, COLS)
    row = iota(shape, 0) - EDGE
    lane = iota(shape, 1)
    top, bottom = -ROWS * place.row, ROWS * (place.rows - place.row)
    first, last = -COLS * place.col, COLS * (place.cols - place.col)
    row_real = (row >= top) & (row < bottom)
    m = {(i, j): place.margin(i, j) for i in (-1, 0, 1) for j in (-1, 0, 1)}
    upper, lower = row < 8, row >= ROWS - 8
    for tile in range(2):
        col = lane if tile == 0 else jnp.where(lane < 64, lane + COLS, lane - COLS)
        real = row_real & (col >= first) & (col < last)
        if tile == 1:
            real = real & ((lane < EDGE) | (lane >= COLS - EDGE))

        def across(margin):
            return (col >= -margin) & (col < COLS + margin)

        own = m[0, 0]
        inside = real & (row >= -own) & (row < ROWS + own) & across(own)
        own_ref[tile] = jnp.where(inside, 1.0, 0.0)
        above, below = m[-1, 0], m[1, 0]
        inside = (upper & (row < above) & across(above)) | (lower & (row >= ROWS - below) & across(below))
        beside_ref[tile] = jnp.where(real & inside, 1.0, 0.0)
    group = ((lane + EDGE) & 127) >> 5
    away = ((lane + EDGE) & 31) - EDGE
    inside = row < -4096
    for place_of, side in ((0, -1), (2, 1)):
        col = away if side < 0 else away + COLS
        real = row_real & (col >= first) & (col < last)

        def reached(margin):
            return (away < margin) if side < 0 else (away >= -margin)

        level = m[0, side]
        inside = inside | (
            (group == place_of) & real & (row >= -level) & (row < ROWS + level) & reached(level)
        )
        above, below = m[-1, side], m[1, side]
        corner = (upper & (row < above) & reached(above)) | (
            lower & (row >= ROWS - below) & reached(below)
        )
        inside = inside | ((group == place_of + 1) & real & corner)
    strip_ref[...] = jnp.where(inside, 1.0, 0.0)


def rows_of(parts, z, i):
    low, block, high = parts
    if i < 2:
        return low[z, i * 8 : i * 8 + 8, :]
    if i < 6:
        return block[z, (i - 2) * 8 : (i - 2) * 8 + 8, :]
    return high[z, (i - 6) * 8 : (i - 6) * 8 + 8, :]


def tiles_of(parts, from_left, from_right, at, z, i):
    lane = iota((8, COLS), 1)
    center = rows_of(parts, z, i)
    group, j = divmod(z, 8)
    left = roll(from_left[at + group, i * 8 : i * 8 + 8, :], (COLS - EDGE) - EDGE * j)
    right = roll(from_right[at + group, i * 8 : i * 8 + 8, :], -EDGE * j)
    margin = jnp.where(lane >= COLS - EDGE, left, jnp.where(lane < EDGE, right, 0.0))
    at_left = jnp.where(lane >= 64, margin, center)
    at_right = jnp.where(lane < 64, margin, center)
    near = (lane < EDGE) | (lane >= COLS - EDGE)
    packed = jnp.where(
        near,
        at_left,
        jnp.where(
            lane < 48, roll(at_left, 32), jnp.where(lane < 80, roll(at_right, 64), roll(at_right, 96))
        ),
    )
    return center, margin, packed


def smooth(place, field, coefficient, strips, table_ref, scratch):
    (own_m, beside_m, strip_m, own, beside, strip, diag, strip_diag) = scratch
    masks(place, own_m, beside_m, strip_m)
    own_a, own_b, own_d, own_r = own
    bes_a, bes_b, bes_d, bes_r = beside
    str_a, str_b, str_d, str_r = strip
    left, right, left_c, right_c, at_c = strips
    base = 4.0 + 2.0 * vertical
    zero = jnp.zeros((8, COLS), jnp.float32)
    for i in range(8):
        s = slice(i * 8, i * 8 + 8)
        for z in range(LEVELS):
            tiles = tiles_of(field, left, right, 0, z, i)
            for t in range(2):
                lanes = slice(t * COLS, (t + 1) * COLS)
                value = tiles[t] * own_m[t, s]
                own_r[z, s, lanes] = value
                own_a[z, s, lanes] = value * (1.0 / theta)
                own_d[z, s, lanes] = value * (1.0 / theta)
                value = tiles[t] * beside_m[t, s]
                bes_r[z, s, lanes] = value
                bes_a[z, s, lanes] = value * (1.0 / theta)
                bes_d[z, s, lanes] = value * (1.0 / theta)
                if i in (0, 7):
                    own_b[z, s, lanes] = zero
                if i in (0, 3, 4, 7):
                    bes_b[z, s, lanes] = zero
            value = tiles[2] * strip_m[s]
            str_r[z, s] = value
            str_a[z, s] = value * (1.0 / theta)
            str_d[z, s] = value * (1.0 / theta)
            if i in (0, 7):
                str_b[z, s] = zero
            else:
                tiles = tiles_of(coefficient, left_c, right_c, at_c, z, i)
                diag[z, s, 0:COLS] = tiles[0] + base
                diag[z, s, COLS : 2 * COLS] = tiles[1] + base
                strip_diag[z, s] = tiles[2] + base

    lane = iota((8, COLS), 1)
    at_first, at_last = lane == 0, lane == COLS - 1

    def step(x, y, d, r, a, mask, width, i, keep, scale):
        s = slice(i * 8, i * 8 + 8)
        up, down = slice(i * 8 - 1, i * 8 + 7), slice(i * 8 + 1, i * 8 + 9)
        lanes = [slice(t * COLS, (t + 1) * COLS) for t in range(width)]
        before = [zero] * width
        now = [x[0, s, lanes[t]] for t in range(width)]
        for z in range(LEVELS):
            after = [x[z + 1, s, lanes[t]] for t in range(width)] if z + 1 < LEVELS else [zero] * width
            back = [roll(v, 1) for v in now]
            fore = [roll(v, -1) for v in now]
            if width == 2:
                back = [jnp.where(at_first, back[1], back[0]), jnp.where(at_first, back[0], back[1])]
                fore = [jnp.where(at_last, fore[1], fore[0]), jnp.where(at_last, fore[0], fore[1])]
            for t in range(width):
                high = before[t] + after[t]
                around = (x[z, up, lanes[t]] + x[z, down, lanes[t]]) + (back[t] + fore[t])
                around = around + (high + high)
                defect = r[z, s, lanes[t]] - a[z, s, lanes[t]] * now[t] + around
                move = keep * d[z, s, lanes[t]] + scale * defect
                if mask[t] is not None:
                    move = move * mask[t]
                d[z, s, lanes[t]] = move
                y[z, s, lanes[t]] = now[t] + move
            before, now = now, after

    def sweep(n, x, y, which):
        keep, scale = table_ref[0, n], table_ref[1, n]
        for i in range(1, 7):
            s = slice(i * 8, i * 8 + 8)
            free = 2 <= i < 6
            step(
                own[which], own[1 - which], own_d, own_r, diag,
                [None if free else own_m[0, s], own_m[1, s]], 2, i, keep, scale,
            )
            if i in (1, 2, 5, 6):
                step(
                    beside[which], beside[1 - which], bes_d, bes_r, diag,
                    [beside_m[0, s], beside_m[1, s]], 2, i, keep, scale,
                )
            step(
                strip[which], strip[1 - which], str_d, str_r, strip_diag, [strip_m[s]], 1, i, keep, scale
            )

    def pair(n, carry):
        sweep(2 * n, None, None, 0)
        sweep(2 * n + 1, None, None, 1)
        return carry

    lax.fori_loop(0, (KCHEB - 1) // 2, pair, 0)
    near_first, near_last = lane < EDGE, lane >= COLS - EDGE
    for i in range(1, 7):
        s = slice(i * 8, i * 8 + 8)
        for z in range(LEVELS):
            value = str_a[z, s]
            at_left = value + roll(value, -32)
            at_right = roll(at_left, 64)
            first = jnp.where(near_first, at_left, jnp.where(near_last, at_right, 0.0))
            second = jnp.where(near_last, at_left, jnp.where(near_first, at_right, 0.0))
            first = first + own_a[z, s, 0:COLS]
            second = second + own_a[z, s, COLS : 2 * COLS]
            if i in (1, 2, 5, 6):
                first = first + bes_a[z, s, 0:COLS]
                second = second + bes_a[z, s, COLS : 2 * COLS]
            own_a[z, s, 0:COLS] = first
            own_a[z, s, COLS : 2 * COLS] = second
    return own_a


def coarse_row(place, told_ref, coarse_turned, down, right):
    slots = roll(told_ref[pl.ds(place.index(down, right), 1), :], -VECTORS).astype(jnp.int32)
    lane = iota((1, COLS), 1)
    slots = jnp.where(lane < VECTORS, slots, 0)
    pick = jnp.where(iota((COLS, COLS), 0) == (slots >> 5), 1.0, 0.0)
    found = jnp.dot(coarse_turned, pick, precision=HIGHEST, preferred_element_type=jnp.float32)
    found = jnp.where(iota((VECTORS, COLS), 0) == (slots & 31), found, 0.0)
    return jnp.where(lane < VECTORS, jnp.sum(found, axis=0, keepdims=True), 0.0)


def add_coarse(place, told_ref, coarse_ref, basis_ref, edges, x, column_ref):
    from_up, from_down, from_left, from_right = edges
    turned = coarse_ref[...].T[:VECTORS]
    row_own = coarse_row(place, told_ref, turned, 0, 0)
    lane = iota((8, COLS), 1)

    def columns(row):
        column_ref[...] = jnp.broadcast_to(row, (COLS, COLS)).T[:VECTORS]

    for edge, down, at in ((from_up, -1, EDGE - 1), (from_down, 1, EDGE + ROWS)):
        columns(coarse_row(place, told_ref, turned, down, 0))
        total = jnp.zeros((LEVELS, COLS), jnp.float32)
        for k in range(VECTORS):
            total = total + edge[k] * column_ref[k : k + 1]
        for z in range(LEVELS):
            x[z, at : at + 1, 0:COLS] = x[z, at : at + 1, 0:COLS] + total[z : z + 1]
    row_left = coarse_row(place, told_ref, turned, 0, -1)
    row_right = coarse_row(place, told_ref, turned, 0, 1)
    for z in range(LEVELS):
        for i in range(ROWS // 8):
            s = slice(i * 8, i * 8 + 8)
            t = slice(EDGE + i * 8, EDGE + i * 8 + 8)
            left = jnp.sum(from_left[z, s] * row_left, axis=1, keepdims=True)
            right = jnp.sum(from_right[z, s] * row_right, axis=1, keepdims=True)
            value = x[z, t, COLS : 2 * COLS]
            value = value + jnp.where(lane == COLS - 1, left, jnp.where(lane == 0, right, 0.0))
            x[z, t, COLS : 2 * COLS] = value
    columns(row_own)

    def level(z, carry):
        total = x[z, EDGE : EDGE + ROWS, 0:COLS]
        for k in range(VECTORS):
            total = total + basis_ref[k, z].astype(jnp.float32) * column_ref[k : k + 1]
        x[z, EDGE : EDGE + ROWS, 0:COLS] = total
        return carry

    lax.fori_loop(0, LEVELS, level, 0)
    return row_own


def image_of(x, diag, put):
    lane = iota((8, COLS), 1)
    zero = jnp.zeros((8, COLS), jnp.float32)
    for i in range(2, 6):
        s = slice(i * 8, i * 8 + 8)
        up, down = slice(i * 8 - 1, i * 8 + 7), slice(i * 8 + 1, i * 8 + 9)
        for z in range(LEVELS):
            now = x[z, s, 0:COLS]
            margin = x[z, s, COLS : 2 * COLS]
            back = jnp.where(lane == 0, roll(margin, 1), roll(now, 1))
            fore = jnp.where(lane == COLS - 1, roll(margin, -1), roll(now, -1))
            high = (x[z - 1, s, 0:COLS] if z else zero) + (x[z + 1, s, 0:COLS] if z + 1 < LEVELS else zero)
            around = x[z, up, 0:COLS] + x[z, down, 0:COLS] + back + fore
            put(z, i - 2, now, diag[z, s, 0:COLS] * now - around - vertical * high)


def total_of(value):
    return jnp.sum(jnp.sum(value, axis=0, keepdims=True), axis=1, keepdims=True)


def gather_scratch(refs):
    own_m, beside_m, strip_m = refs[:3]
    own, beside, strip = refs[3:7], refs[7:11], refs[11:15]
    return (own_m, beside_m, strip_m, own, beside, strip, refs[15], refs[16])


def solve_kernel(
    place_ref, table_ref, told_ref, coarse_ref, basis_ref, r_up, r_own, r_down, c_up, c_own, c_down,
    left_ref, right_ref, e_up, e_down, e_left, e_right,
    direction_ref, smooth_ref, image_ref, ahead_ref, behind_ref, out_ref, *refs,
):
    column_ref, sums_ref = refs[:2]
    scratch = gather_scratch(refs[2:])
    place = Place(place_ref, told_ref)
    x = smooth(
        place, (r_up, r_own, r_down), (c_up, c_own, c_down),
        (left_ref, right_ref, left_ref, right_ref, 2), table_ref, scratch,
    )
    smooth_ref[...] = x[:, EDGE : EDGE + ROWS, 0:COLS]
    row = add_coarse(place, told_ref, coarse_ref, basis_ref, (e_up, e_down, e_left, e_right), x, column_ref)
    zero = jnp.zeros((8, COLS), jnp.float32)
    weight = [zero]
    curve = [zero]

    def put(z, i, now, image):
        s = slice(i * 8, i * 8 + 8)
        direction_ref[z, s] = now
        image_ref[z, s] = image
        if i >= 2:
            ahead_ref[z, (i - 2) * 8 : (i - 1) * 8] = image
        else:
            behind_ref[z, s] = image
        weight[0] = weight[0] + r_own[z, s] * smooth_ref[z, s]
        curve[0] = curve[0] + now * image

    image_of(x, scratch[6], put)
    mine = told_ref[pl.ds(place.index(0, 0), 1), :]
    weight_part = total_of(weight[0]) + total_of(row * mine)
    curve_part = total_of(curve[0])
    half = VECTORS // 2
    for part in range(2):

        def level(z, sums):
            image = image_ref[z]
            new = []
            for k in range(half):
                product = basis_ref[part * half + k, z].astype(jnp.float32) * image
                new.append(sums[k] + product[0:8] + product[8:16] + product[16:24] + product[24:32])
            return tuple(new)

        sums = lax.fori_loop(0, LEVELS, level, (zero,) * half)
        for k in range(half):
            sums_ref[part * half + k : part * half + k + 1] = jnp.sum(sums[k], axis=0, keepdims=True)
    lane = iota((1, COLS), 1)
    told = roll(row, VECTORS)
    told = told + jnp.where(lane == 64, weight_part, 0.0) + jnp.where(lane == 65, curve_part, 0.0)
    out_ref[...] = row_of_sums(sums_ref[...]) + told


def scalars(told_ref):
    totals = jnp.sum(told_ref[...], axis=0, keepdims=True)
    return totals[:, 64:65], totals[:, 65:66]


def again_kernel(
    place_ref, table_ref, told_ref, again_ref, coarse_ref, basis_ref, w_up, w_own, w_down, c_up, c_own, c_down,
    left_ref, right_ref, left_c, right_c, e_up, e_down, e_left, e_right, source_ref, direction_ref, smooth_ref,
    residual_ref, precond_ref, image_ref, out_ref, *refs,
):
    column_ref, more_ref = refs[:2]
    scratch = gather_scratch(refs[2:])
    place = Place(place_ref, told_ref)
    x = smooth(
        place, (w_up, w_own, w_down), (c_up, c_own, c_down), (left_ref, right_ref, left_c, right_c, 2),
        table_ref, scratch,
    )
    more_ref[...] = x[:, EDGE : EDGE + ROWS, 0:COLS]
    row = add_coarse(place, told_ref, coarse_ref, basis_ref, (e_up, e_down, e_left, e_right), x, column_ref)
    weight0, curve0 = scalars(again_ref)
    step = weight0 / curve0
    zero = jnp.zeros((8, COLS), jnp.float32)
    sums = [zero, zero, zero]

    def put(z, i, now, image):
        s = slice(i * 8, i * 8 + 8)
        direction, first = direction_ref[z, s], w_own[z, s]
        residual = source_ref[z, s] - step * first
        precond = direction - step * now
        image = first - step * image
        residual_ref[z, s] = residual
        precond_ref[z, s] = precond
        image_ref[z, s] = image
        sums[0] = sums[0] + residual * (smooth_ref[z, s] - step * more_ref[z, s])
        sums[1] = sums[1] + precond * image
        sums[2] = sums[2] + (precond * first + direction * image)

    image_of(x, scratch[6], put)
    mine = pl.ds(place.index(0, 0), 1)
    lane = iota((1, COLS), 1)
    again = again_ref[mine, :]
    projected = told_ref[mine, :] - step * again
    coarse = roll(again, -VECTORS) - step * row
    both = jnp.where(lane < VECTORS, projected * coarse, 0.0)
    told = jnp.where(lane == 0, total_of(sums[0]) + total_of(both), 0.0)
    told = told + jnp.where(lane == 1, total_of(sums[1]), 0.0) + jnp.where(lane == 2, total_of(sums[2]), 0.0)
    out_ref[...] = jnp.broadcast_to(told, (COLS, COLS))


def last_kernel(again_ref, last_ref, direction_ref, first_ref, residual_ref, precond_ref, image_ref, x_ref, r_ref):
    weight0, curve0 = scalars(again_ref)
    step0 = weight0 / curve0
    totals = jnp.sum(last_ref[...], axis=0, keepdims=True)
    weight1, own, cross = totals[:, 0:1], totals[:, 1:2], totals[:, 2:3]
    ratio = weight1 / weight0
    step1 = weight1 / (own + ratio * (cross + ratio * curve0))

    def level(z, carry):
        direction = direction_ref[z]
        x_ref[z] = step0 * direction + step1 * (precond_ref[z] + ratio * direction)
        r_ref[z] = residual_ref[z] - step1 * (image_ref[z] + ratio * first_ref[z])
        return carry

    lax.fori_loop(0, LEVELS, level, 0)


def smoother_scratch():
    wide = pltpu.VMEM((LEVELS, TALL, 2 * COLS), jnp.float32)
    thin = pltpu.VMEM((LEVELS, TALL, COLS), jnp.float32)
    pair = pltpu.VMEM((2, TALL, COLS), jnp.float32)
    return [pair, pair, pltpu.VMEM((TALL, COLS), jnp.float32)] + [wide] * 8 + [thin] * 4 + [wide, thin]


def shards(source, absorption, basis, coarse_inverse, margin_width, coarse_slot):
    block = jax.ShapeDtypeStruct((LEVELS, ROWS, COLS), jnp.float32)
    slab = jax.ShapeDtypeStruct((LEVELS, EDGE, COLS), jnp.float32)
    message = jax.ShapeDtypeStruct((COLS, COLS), jnp.float32)
    params = pltpu.CompilerParams(vmem_limit_bytes=VMEM_LIMIT)
    smem = pl.BlockSpec(memory_space=pltpu.SMEM)
    vmem = pl.BlockSpec(memory_space=pltpu.VMEM)
    place = jnp.stack(
        [lax.axis_index("gx"), lax.axis_index("gy"), lax.axis_size("gx"), lax.axis_size("gy")]
    ).astype(jnp.int32)
    table = jnp.array(list(zip(*chebyshev_table())), jnp.float32)
    told_row = jnp.concatenate(
        [
            jnp.zeros((1, VECTORS), jnp.float32),
            coarse_slot.reshape(1, -1).astype(jnp.float32),
            margin_width.astype(jnp.float32),
            jnp.zeros((1, COLS - 65), jnp.float32),
        ],
        axis=1,
    )
    both = [
        jnp.concatenate([source[:, ROWS - EDGE :], absorption[:, ROWS - EDGE :]]),
        jnp.concatenate([source[:, :EDGE], absorption[:, :EDGE]]),
    ]
    low, high = exchange(both[0], both[1], "gx")
    rows, e_first, e_last, e_left, e_right = first_projection(source, basis, told_row)
    told = everyone(rows)
    r_parts = (low[:LEVELS], source, high[:LEVELS])
    c_parts = (low[LEVELS:], absorption, high[LEVELS:])
    rows, ahead, behind = middle(told, told, coarse_inverse, [r_parts, c_parts])
    left, right = exchange(ahead, behind, "gy")
    coarse = everyone(rows)
    from_up, from_down = exchange(e_last, e_first, "gx")
    from_left, from_right = exchange(e_right, e_left, "gy")
    edges = (from_up, from_down, from_left, from_right)
    direction, smoothed, image, ahead, behind, rows = pl.pallas_call(
        solve_kernel,
        in_specs=[smem] * 2 + [vmem] * 15,
        out_shape=[block, block, block, slab, slab, message],
        scratch_shapes=[pltpu.VMEM((VECTORS, COLS), jnp.float32)] * 2 + smoother_scratch(),
        compiler_params=params,
        name="precondition",
    )(place, table, told, coarse, basis, *r_parts, *c_parts, left, right, *edges)
    low, high = exchange(ahead, behind, "gx")
    again = everyone(rows)
    w_parts = (low, image, high)
    rows, ahead, behind = middle(again, told, coarse_inverse, [w_parts])
    left_w, right_w = exchange(ahead, behind, "gy")
    coarse = everyone(rows)
    residual, precond, precond_image, rows = pl.pallas_call(
        again_kernel,
        in_specs=[smem] * 2 + [vmem] * 21,
        out_shape=[block, block, block, message],
        scratch_shapes=[pltpu.VMEM((VECTORS, COLS), jnp.float32), pltpu.VMEM(block.shape, jnp.float32)]
        + smoother_scratch(),
        compiler_params=params,
        name="precondition_image",
    )(
        place, table, told, again, coarse, basis, *w_parts, *c_parts, left_w, right_w, left, right, *edges,
        source, direction, smoothed,
    )
    last = everyone(rows)
    concentration, residual = pl.pallas_call(
        last_kernel, out_shape=[block, block], compiler_params=params, name="update"
    )(again, last, direction, image, residual, precond, precond_image)
    return (concentration, residual)


def solution(mesh):
    return jax.shard_map(
        shards,
        mesh=mesh,
        in_specs=(
            P(None, "gx", "gy"),
            P(None, "gx", "gy"),
            P(None, None, "gx", "gy"),
            P(("gx", "gy"), None),
            P("gx", "gy"),
            P("gx", "gy", None),
        ),
        out_specs=(P(None, "gx", "gy"), P(None, "gx", "gy")),
        check_vma=False,
    )
```

```python
import functools

import jax
import jax.numpy as jnp
from jax import lax
from jax.experimental import pallas as pl
from jax.experimental.pallas import tpu as pltpu
from jax.sharding import PartitionSpec as P

KCHEB = 9
AXES = ("gx", "gy")
LEVELS = 16
ROWS = 32
COLS = 128
VECTORS = 32
EDGE = 16
TALL = ROWS + 2 * EDGE
HIGHEST = lax.Precision.HIGHEST

lowest_rate = 0.05
highest_rate = 18.5
vertical = 2.0
theta = 0.5 * (highest_rate + lowest_rate)
delta = 0.5 * (highest_rate - lowest_rate)
VMEM_LIMIT = 24 * 1024 * 1024
FIRST_LIMIT = 58 * 1024 * 1024


def chebyshev_table():
    ratio = theta / delta
    rho_old = 1.0 / ratio
    table = []
    for _ in range(KCHEB - 1):
        rho_new = 1.0 / (2.0 * ratio - rho_old)
        table.append((rho_new * rho_old, 2.0 * rho_new / delta))
        rho_old = rho_new
    return table


def iota(shape, dim):
    return lax.broadcasted_iota(jnp.int32, shape, dim)


def roll(value, shift):
    return pltpu.roll(value, shift % COLS, 1)


def exchange(forward_value, backward_value, axis):
    count = lax.axis_size(axis)
    forward = [(i, i + 1) for i in range(count - 1)]
    backward = [(target, source) for source, target in forward]
    return lax.ppermute(forward_value, axis, forward), lax.ppermute(backward_value, axis, backward)


def everyone(rows):
    return lax.all_to_all(rows, AXES, 0, 0, tiled=True)


def row_of_sums(sums):
    padded = jnp.concatenate([sums, jnp.zeros((COLS - VECTORS, COLS), jnp.float32)], 0)
    ones = jnp.ones((COLS, COLS), jnp.float32)
    return lax.dot_general(
        ones, padded, (((1,), (1,)), ((), ())), precision=HIGHEST, preferred_element_type=jnp.float32
    )


def fold_rows(product):
    return (product[0:8] + product[8:16]) + (product[16:24] + product[24:32])


def first_kernel(
    field_ref, coefficient_ref, basis_ref, told_ref, out_ref, ahead_ref, behind_ref, left_ref, right_ref, sums_ref
):
    step = pl.program_id(0)
    group = basis_ref.shape[0]
    lane = iota((ROWS, COLS), 1)

    @pl.when(step == 0)
    def _():
        left_ref[...] = jnp.zeros_like(left_ref)
        right_ref[...] = jnp.zeros_like(right_ref)

        def level(z, carry):
            ahead_ref[z] = field_ref[z, ROWS - EDGE :, :]
            behind_ref[z] = field_ref[z, :EDGE, :]
            ahead_ref[LEVELS + z] = coefficient_ref[z, ROWS - EDGE :, :]
            behind_ref[LEVELS + z] = coefficient_ref[z, :EDGE, :]
            return carry

        lax.fori_loop(0, LEVELS, level, 0)

    def level(z, sums):
        field = field_ref[z]
        low = left_ref[z >> 2]
        high = right_ref[z >> 2]
        new = []
        for j in range(group):
            values = basis_ref[j, z].astype(jnp.float32)
            new.append(sums[j] + fold_rows(values * field))
            at = 2 * LEVELS + step * group + j
            behind_ref[at, pl.ds(z, 1), :] = values[0:1]
            ahead_ref[at, pl.ds(z, 1), :] = values[ROWS - 1 : ROWS]
            k = step * group + j + VECTORS * (z & 3)
            turned = pltpu.roll(values, k, 1)
            low = jnp.where(lane == k, turned, low)
            high = jnp.where(lane == ((k + COLS - 1) & (COLS - 1)), turned, high)
        left_ref[z >> 2] = low
        right_ref[z >> 2] = high
        return tuple(new)

    zero = jnp.zeros((8, COLS), jnp.float32)
    sums = lax.fori_loop(0, LEVELS, level, (zero,) * group)
    for j in range(group):
        sums_ref[pl.ds(step * group + j, 1), :] = jnp.sum(sums[j], axis=0, keepdims=True)

    @pl.when(step == pl.num_programs(0) - 1)
    def _():
        out_ref[...] = row_of_sums(sums_ref[...]) + told_ref[...]


def first_projection(field, coefficient, basis, told_row):
    group = 8
    rows = 2 * LEVELS + VECTORS
    edge_rows = jax.ShapeDtypeStruct((rows, LEVELS, COLS), jnp.float32)
    edge_cols = jax.ShapeDtypeStruct((LEVELS // 4, ROWS, COLS), jnp.float32)
    block_spec = pl.BlockSpec((LEVELS, ROWS, COLS), lambda i: (0, 0, 0))
    rows_spec = pl.BlockSpec(edge_rows.shape, lambda i: (0, 0, 0))
    cols_spec = pl.BlockSpec(edge_cols.shape, lambda i: (0, 0, 0))
    return pl.pallas_call(
        first_kernel,
        grid=(VECTORS // group,),
        in_specs=[
            block_spec,
            block_spec,
            pl.BlockSpec((group, LEVELS, ROWS, COLS), lambda i: (i, 0, 0, 0)),
            pl.BlockSpec((1, COLS), lambda i: (0, 0)),
        ],
        out_specs=[pl.BlockSpec((COLS, COLS), lambda i: (0, 0)), rows_spec, rows_spec, cols_spec, cols_spec],
        out_shape=[jax.ShapeDtypeStruct((COLS, COLS), jnp.float32), edge_rows, edge_rows, edge_cols, edge_cols],
        scratch_shapes=[pltpu.VMEM((VECTORS, COLS), jnp.float32)],
        compiler_params=pltpu.CompilerParams(vmem_limit_bytes=FIRST_LIMIT),
        name="first_projection",
    )(field, coefficient, basis, told_row)


def coarse_rows(told_ref, slots_ref, inverse_ref, out_ref):
    told = told_ref[...]
    slots = slots_ref[...]
    turned = told.T
    slots_turned = slots.T
    lane = iota((COLS, COLS), 1)
    sub = iota((VECTORS, COLS), 0)
    placed = jnp.zeros((3 * VECTORS, COLS), jnp.float32)
    for k in range(VECTORS):
        slot_column = slots[:, VECTORS + k : VECTORS + k + 1].astype(jnp.int32)
        ones = jnp.where((slot_column & 127) == lane, 1.0, 0.0).astype(jnp.bfloat16)
        slot_row = slots_turned[VECTORS + k : VECTORS + k + 1, :].astype(jnp.int32)
        values = turned[k : k + 1, :]
        spread = jnp.where((slot_row >> 7) == sub, values, 0.0)
        first = spread.astype(jnp.bfloat16)
        rest = spread - first.astype(jnp.float32)
        second = rest.astype(jnp.bfloat16)
        third = (rest - second.astype(jnp.float32)).astype(jnp.bfloat16)
        parts = jnp.concatenate([first, second, third], 0)
        placed = placed + jnp.dot(parts, ones, preferred_element_type=jnp.float32)
    placed = placed[:VECTORS] + placed[VECTORS : 2 * VECTORS] + placed[2 * VECTORS :]
    total = jnp.zeros((VECTORS, COLS), jnp.float32)
    for high in range(VECTORS):
        total = total + inverse_ref[:, high * COLS : (high + 1) * COLS] * placed[high : high + 1]
    out_ref[...] = row_of_sums(total)


def pack_strips(parts, forward_ref, backward_ref, at):
    def levels(group, carry):
        row = 0
        for part, start in parts:
            height = EDGE if part.shape[1] == EDGE else ROWS
            lane = iota((height, COLS), 1)
            ahead = jnp.zeros((height, COLS), jnp.float32)
            behind = ahead
            for j in range(8):
                value = part[start + group * 8 + j]
                mine = (lane >= EDGE * j) & (lane < EDGE * (j + 1))
                ahead = jnp.where(mine, roll(value, EDGE * j - (COLS - EDGE)), ahead)
                behind = jnp.where(mine, roll(value, EDGE * j), behind)
            forward_ref[at + group, row : row + height, :] = ahead
            backward_ref[at + group, row : row + height, :] = behind
            row += height
        return carry

    lax.fori_loop(0, LEVELS // 8, levels, 0)


def first_middle_kernel(
    told_ref, inverse_ref, source_ref, absorption_ref, low_ref, high_ref, left_ref, right_ref,
    out_ref, forward_ref, backward_ref,
):
    for f, block in enumerate((source_ref, absorption_ref)):
        pack_strips(((low_ref, LEVELS * f), (block, 0), (high_ref, LEVELS * f)), forward_ref, backward_ref, 2 * f)
    for n in range(LEVELS // 8):
        for half in range(2):
            rows = slice(half * ROWS, (half + 1) * ROWS)
            forward_ref[4 + n, rows, :] = right_ref[2 * n + half]
            backward_ref[4 + n, rows, :] = left_ref[2 * n + half]
    coarse_rows(told_ref, told_ref, inverse_ref, out_ref)


def middle_kernel(told_ref, slots_ref, inverse_ref, block_ref, low_ref, high_ref, out_ref, forward_ref, backward_ref):
    pack_strips(((low_ref, 0), (block_ref, 0), (high_ref, 0)), forward_ref, backward_ref, 0)
    coarse_rows(told_ref, slots_ref, inverse_ref, out_ref)


def middle(kernel, strips, *operands):
    strips = jax.ShapeDtypeStruct((strips, TALL, COLS), jnp.float32)
    return pl.pallas_call(
        kernel,
        out_shape=[jax.ShapeDtypeStruct((COLS, COLS), jnp.float32), strips, strips],
        compiler_params=pltpu.CompilerParams(vmem_limit_bytes=VMEM_LIMIT),
        name="coarse_rows",
    )(*operands)


class Place:
    def __init__(self, place_ref, told_ref):
        self.row = place_ref[0]
        self.col = place_ref[1]
        self.rows = place_ref[2]
        self.cols = place_ref[3]
        self.told_ref = told_ref

    def index(self, down, right):
        row = jnp.clip(self.row + down, 0, self.rows - 1)
        col = jnp.clip(self.col + right, 0, self.cols - 1)
        return row * self.cols + col

    def margin(self, down, right):
        row, col = self.row + down, self.col + right
        real = (row >= 0) & (row < self.rows) & (col >= 0) & (col < self.cols)
        margin = self.told_ref[pl.ds(self.index(down, right), 1), :][:, 64:65]
        return jnp.where(real, margin.astype(jnp.int32), -4096)


def masks(place, own_ref, beside_ref, strip_ref):
    shape = (TALL, COLS)
    row = iota(shape, 0) - EDGE
    lane = iota(shape, 1)
    top, bottom = -ROWS * place.row, ROWS * (place.rows - place.row)
    first, last = -COLS * place.col, COLS * (place.cols - place.col)
    row_real = (row >= top) & (row < bottom)
    m = {(i, j): place.margin(i, j) for i in (-1, 0, 1) for j in (-1, 0, 1)}
    upper, lower = row < 8, row >= ROWS - 8
    for tile in range(2):
        col = lane if tile == 0 else jnp.where(lane < 64, lane + COLS, lane - COLS)
        real = row_real & (col >= first) & (col < last)
        if tile == 1:
            real = real & ((lane < EDGE) | (lane >= COLS - EDGE))

        def across(margin):
            return (col >= -margin) & (col < COLS + margin)

        own = m[0, 0]
        inside = real & (row >= -own) & (row < ROWS + own) & across(own)
        own_ref[tile] = jnp.where(inside, 1.0, 0.0)
        above, below = m[-1, 0], m[1, 0]
        inside = (upper & (row < above) & across(above)) | (lower & (row >= ROWS - below) & across(below))
        beside_ref[tile] = jnp.where(real & inside, 1.0, 0.0)
    group = ((lane + EDGE) & 127) >> 5
    away = ((lane + EDGE) & 31) - EDGE
    inside = row < -4096
    for place_of, side in ((0, -1), (2, 1)):
        col = away if side < 0 else away + COLS
        real = row_real & (col >= first) & (col < last)

        def reached(margin):
            return (away < margin) if side < 0 else (away >= -margin)

        level = m[0, side]
        inside = inside | (
            (group == place_of) & real & (row >= -level) & (row < ROWS + level) & reached(level)
        )
        above, below = m[-1, side], m[1, side]
        corner = (upper & (row < above) & reached(above)) | (
            lower & (row >= ROWS - below) & reached(below)
        )
        inside = inside | ((group == place_of + 1) & real & corner)
    strip_ref[...] = jnp.where(inside, 1.0, 0.0)


def tiles_of(parts, start, strips, at, z, i):
    low, block, high = parts
    from_left, from_right = strips
    lane = iota((8, COLS), 1)
    if i < 2:
        center = low[start + z, i * 8 : i * 8 + 8, :]
    elif i < 6:
        center = block[z, (i - 2) * 8 : (i - 2) * 8 + 8, :]
    else:
        center = high[start + z, (i - 6) * 8 : (i - 6) * 8 + 8, :]
    s = slice(i * 8, i * 8 + 8)
    group, shift = at + (z >> 3), EDGE * (z & 7)
    left = pltpu.roll(from_left[group, s, :], (COLS - EDGE) - shift, 1)
    right = pltpu.roll(from_right[group, s, :], (COLS - shift) & (COLS - 1), 1)
    margin = jnp.where(lane >= COLS - EDGE, left, jnp.where(lane < EDGE, right, 0.0))
    at_left = jnp.where(lane >= 64, margin, center)
    at_right = jnp.where(lane < 64, margin, center)
    near = (lane < EDGE) | (lane >= COLS - EDGE)
    others = jnp.where(lane < 80, roll(at_right, 64), roll(at_right, 96))
    packed = jnp.where(near, at_left, jnp.where(lane < 48, roll(at_left, 32), others))
    return center, margin, packed


PLANES = LEVELS + 2
BESIDE_TILES = (1, 2, 5, 6)


def smooth_kernel(
    starts, place_ref, table_ref, told_ref, block_ref, low_ref, high_ref, left_ref, right_ref,
    absorption_ref, low_c, high_c, left_c, right_c, out_ref,
    own_m, beside_m, strip_m, own, beside, strip, own_d, beside_d, strip_d, own_r, beside_r, strip_r, diag, strip_diag,
):
    field_start, coef_start, coef_at = starts
    masks(Place(place_ref, told_ref), own_m, beside_m, strip_m)
    base = 4.0 + 2.0 * vertical
    zero = jnp.zeros((8, COLS), jnp.float32)
    lane = iota((8, COLS), 1)
    lanes = [slice(0, COLS), slice(COLS, 2 * COLS)]

    def clear(n, carry):
        at = (n & 1) * (PLANES - 1) + (n >> 1) * PLANES
        for i in range(8):
            s = slice(i * 8, i * 8 + 8)
            for t in range(2):
                own[at, s, lanes[t]] = zero
                beside[at, s, lanes[t]] = zero
            strip[at, s] = zero
        return carry

    lax.fori_loop(0, 4, clear, 0)

    def begin(z, carry):
        at = z + 1
        for i in range(8):
            s = slice(i * 8, i * 8 + 8)
            tiles = tiles_of((low_ref, block_ref, high_ref), field_start, (left_ref, right_ref), 0, z, i)
            inner = 1 <= i < 7
            for t in range(2):
                value = tiles[t] * own_m[t, s]
                if inner:
                    own_r[z, s, lanes[t]] = value
                    own_d[z, s, lanes[t]] = value * (1.0 / theta)
                else:
                    own[at + PLANES, s, lanes[t]] = zero
                own[at, s, lanes[t]] = value * (1.0 / theta)
                value = tiles[t] * beside_m[t, s]
                if i in BESIDE_TILES:
                    beside_r[z, s, lanes[t]] = value
                    beside_d[z, s, lanes[t]] = value * (1.0 / theta)
                else:
                    beside[at + PLANES, s, lanes[t]] = zero
                beside[at, s, lanes[t]] = value * (1.0 / theta)
            value = tiles[2] * strip_m[s]
            strip[at, s] = value * (1.0 / theta)
            if inner:
                strip_r[z, s] = value
                strip_d[z, s] = value * (1.0 / theta)
                tiles = tiles_of((low_c, absorption_ref, high_c), coef_start, (left_c, right_c), coef_at, z, i)
                diag[z, s, lanes[0]] = tiles[0] + base
                diag[z, s, lanes[1]] = tiles[1] + base
                strip_diag[z, s] = tiles[2] + base
            else:
                strip[at + PLANES, s] = zero
        return carry

    lax.fori_loop(0, LEVELS, begin, 0)
    at_first, at_last = lane == 0, lane == COLS - 1

    def sweep(n, carry):
        keep, scale = table_ref[0, n], table_ref[1, n]
        source = (n & 1) * PLANES + 1
        target = (PLANES + 2) - source

        def step(z, x, d, r, a, mask, width, i):
            s = slice(i * 8, i * 8 + 8)
            up, down = slice(i * 8 - 1, i * 8 + 7), slice(i * 8 + 1, i * 8 + 9)
            here = source + z
            now = [x[here, s, lanes[t]] for t in range(width)]
            back = [roll(v, 1) for v in now]
            fore = [roll(v, -1) for v in now]
            if width == 2:
                back = [jnp.where(at_first, back[1], back[0]), jnp.where(at_first, back[0], back[1])]
                fore = [jnp.where(at_last, fore[1], fore[0]), jnp.where(at_last, fore[0], fore[1])]
            for t in range(width):
                high = x[here - 1, s, lanes[t]] + x[here + 1, s, lanes[t]]
                around = (x[here, up, lanes[t]] + x[here, down, lanes[t]]) + (back[t] + fore[t])
                around = around + (high + high)
                defect = r[z, s, lanes[t]] - a[z, s, lanes[t]] * now[t] + around
                move = keep * d[z, s, lanes[t]] + scale * defect
                if mask[t] is not None:
                    move = move * mask[t]
                d[z, s, lanes[t]] = move
                x[target + z, s, lanes[t]] = now[t] + move

        def level(z, carry):
            for i in range(1, 7):
                s = slice(i * 8, i * 8 + 8)
                first = None if 2 <= i < 6 else own_m[0, s]
                step(z, own, own_d, own_r, diag, [first, own_m[1, s]], 2, i)
                if i in BESIDE_TILES:
                    step(z, beside, beside_d, beside_r, diag, [beside_m[0, s], beside_m[1, s]], 2, i)
                step(z, strip, strip_d, strip_r, strip_diag, [strip_m[s]], 1, i)
            return carry

        return lax.fori_loop(0, LEVELS, level, carry)

    lax.fori_loop(0, KCHEB - 1, sweep, 0)
    near_first, near_last = lane < EDGE, lane >= COLS - EDGE

    def finish(z, carry):
        at = z + 1
        for i in range(1, 7):
            s = slice(i * 8, i * 8 + 8)
            out = slice(i * 8 - 8, i * 8)
            value = strip[at, s]
            at_left = value + roll(value, -32)
            at_right = roll(at_left, 64)
            first = jnp.where(near_first, at_left, jnp.where(near_last, at_right, 0.0))
            second = jnp.where(near_last, at_left, jnp.where(near_first, at_right, 0.0))
            first = first + own[at, s, lanes[0]]
            second = second + own[at, s, lanes[1]]
            if i in BESIDE_TILES:
                first = first + beside[at, s, lanes[0]]
                second = second + beside[at, s, lanes[1]]
            out_ref[z, out, lanes[0]] = first
            out_ref[z, out, lanes[1]] = second
        return carry

    lax.fori_loop(0, LEVELS, finish, 0)


def smooth(starts, place, table, told, block, low, high, strips, absorption, low_c, high_c, strips_c):
    wide = (TALL, 2 * COLS)
    thin = (TALL, COLS)

    def scratch(*shape):
        return pltpu.VMEM(shape, jnp.float32)

    smem = pl.BlockSpec(memory_space=pltpu.SMEM)
    vmem = pl.BlockSpec(memory_space=pltpu.VMEM)
    return pl.pallas_call(
        functools.partial(smooth_kernel, starts),
        in_specs=[smem] * 2 + [vmem] * 11,
        out_shape=jax.ShapeDtypeStruct((LEVELS, INNER, 2 * COLS), jnp.float32),
        scratch_shapes=[
            scratch(2, *thin), scratch(2, *thin), scratch(*thin),
            scratch(2 * PLANES, *wide), scratch(2 * PLANES, *wide), scratch(2 * PLANES, *thin),
            scratch(LEVELS, *wide), scratch(LEVELS, *wide), scratch(LEVELS, *thin),
            scratch(LEVELS, *wide), scratch(LEVELS, *wide), scratch(LEVELS, *thin),
            scratch(LEVELS, *wide), scratch(LEVELS, *thin),
        ],
        compiler_params=pltpu.CompilerParams(vmem_limit_bytes=VMEM_LIMIT),
        cost_estimate=pl.CostEstimate(flops=60000000, bytes_accessed=4000000, transcendentals=0),
        name="smoother",
    )(place, table, told, block, low, high, *strips, absorption, low_c, high_c, *strips_c)


INNER = ROWS + 16


def slots_of(place, told_ref, moves):
    lane = iota((1, COLS), 1)
    slots = jnp.zeros((1, COLS), jnp.float32)
    for n, (down, right) in enumerate(moves):
        row = roll(told_ref[pl.ds(place.index(down, right), 1), :], VECTORS * (n - 1))
        slots = jnp.where((lane >> 5) == n, row, slots)
    return slots.astype(jnp.int32)


def coarse_at(coarse_turned, slots):
    pick = jnp.where(iota((COLS, COLS), 0) == (slots >> 5), 1.0, 0.0)
    found = jnp.dot(coarse_turned, pick, precision=HIGHEST, preferred_element_type=jnp.float32)
    found = jnp.where(iota((VECTORS, COLS), 0) == (slots & 31), found, 0.0)
    return jnp.sum(found, axis=0, keepdims=True)


def add_coarse(place, told_ref, coarse_ref, basis_ref, low_ref, high_ref, left_ref, right_ref, at, sum_ref, x,
               own_c, edge_c, ring_ref, side_ref):
    turned = coarse_ref[...].T[:VECTORS]
    row = coarse_at(turned, slots_of(place, told_ref, ((0, 0), (-1, 0), (1, 0), (0, -1))))
    other = coarse_at(turned, slots_of(place, told_ref, ((0, 1),)))
    lane = iota((8, COLS), 1)
    lane_row = iota((1, COLS), 1)
    column = jnp.broadcast_to(row, (COLS, COLS)).T
    own_c[...] = column[:VECTORS]
    edge_c[...] = column[VECTORS : 3 * VECTORS]
    for n, edge in ((0, low_ref), (1, high_ref)):

        def vector(k, total):
            return total + edge[2 * LEVELS + k] * edge_c[pl.ds(n * VECTORS + k, 1), :]

        ring_ref[n] = lax.fori_loop(0, VECTORS, vector, jnp.zeros((LEVELS, COLS), jnp.float32))
    for n, (edge, values, shift) in enumerate(((left_ref, roll(row, VECTORS), -1), (right_ref, other, 0))):
        values = jnp.where(lane_row < VECTORS, values, 0.0)
        values = values + roll(values, 32) + roll(values, 64) + roll(values, 96)
        weights = jnp.broadcast_to(roll(values, shift), (COLS, COLS)).T
        which = ((iota((COLS, COLS), 0) - shift) & (COLS - 1)) >> 5
        weights = jnp.where(iota((COLS, COLS), 1) == which, weights, 0.0)
        parts = edge[at : at + 2].reshape(2 * TALL, COLS)
        side_ref[n] = jnp.dot(parts, weights, precision=HIGHEST, preferred_element_type=jnp.float32)

    def level(z, carry):
        total = sum_ref[z, 8 : 8 + ROWS, 0:COLS]
        for k in range(VECTORS):
            total = total + basis_ref[k, z].astype(jnp.float32) * own_c[k : k + 1]
        here = z + 1
        x[here, 8 : 8 + ROWS, 0:COLS] = total
        rows = pl.ds(z, 1)
        x[here, 7:8, 0:COLS] = sum_ref[z, 7:8, 0:COLS] + ring_ref[0, rows, :]
        x[here, 8 + ROWS : 9 + ROWS, 0:COLS] = sum_ref[z, 8 + ROWS : 9 + ROWS, 0:COLS] + ring_ref[1, rows, :]
        q = z & 3
        for i in range(ROWS // 8):
            s = pl.ds(pl.multiple_of((z >> 2) * ROWS + i * 8, 8), 8)
            left = pltpu.roll(side_ref[0, s, :], (COLS - 1) - q, 1)
            right = pltpu.roll(side_ref[1, s, :], (COLS - q) & (COLS - 1), 1)
            t = slice(8 + i * 8, 16 + i * 8)
            value = jnp.where(lane == COLS - 1, left, jnp.where(lane == 0, right, 0.0))
            x[here, t, COLS : 2 * COLS] = sum_ref[z, t, COLS : 2 * COLS] + value
        return carry

    lax.fori_loop(0, LEVELS, level, 0)
    zero = jnp.zeros((ROWS, COLS), jnp.float32)
    x[0, 8 : 8 + ROWS, 0:COLS] = zero
    x[PLANES - 1, 8 : 8 + ROWS, 0:COLS] = zero
    return row


def image_at(x, absorption_ref, z, i):
    lane = iota((8, COLS), 1)
    here = z + 1
    s = slice(8 + i * 8, 16 + i * 8)
    up, down = slice(7 + i * 8, 15 + i * 8), slice(9 + i * 8, 17 + i * 8)
    now = x[here, s, 0:COLS]
    margin = x[here, s, COLS : 2 * COLS]
    back = jnp.where(lane == 0, roll(margin, 1), roll(now, 1))
    fore = jnp.where(lane == COLS - 1, roll(margin, -1), roll(now, -1))
    high = x[here - 1, s, 0:COLS] + x[here + 1, s, 0:COLS]
    around = (x[here, up, 0:COLS] + x[here, down, 0:COLS]) + (back + fore)
    diagonal = absorption_ref[z, i * 8 : i * 8 + 8, :] + (4.0 + 2.0 * vertical)
    return now, diagonal * now - around - vertical * high


def total_of(value):
    return jnp.sum(jnp.sum(value, axis=0, keepdims=True), axis=1, keepdims=True)


def scalars(told_ref):
    totals = jnp.sum(told_ref[...], axis=0, keepdims=True)
    return totals[:, 64:65], totals[:, 65:66]


def first_coarse_kernel(
    place_ref, told_ref, coarse_ref, basis_ref, low_ref, high_ref, left_ref, right_ref, sum_ref, source_ref, absorption_ref,
    direction_ref, image_ref, ahead_ref, behind_ref, out_ref, x, own_c, edge_c, ring_ref, side_ref, sums_ref,
):
    place = Place(place_ref, told_ref)
    row = add_coarse(place, told_ref, coarse_ref, basis_ref, low_ref, high_ref, left_ref, right_ref, 4, sum_ref, x,
                     own_c, edge_c, ring_ref, side_ref)
    zero = jnp.zeros((8, COLS), jnp.float32)

    def images(z, carry):
        weight, curve = carry
        for i in range(ROWS // 8):
            s = slice(i * 8, i * 8 + 8)
            now, image = image_at(x, absorption_ref, z, i)
            direction_ref[z, s] = now
            image_ref[z, s] = image
            if i >= 2:
                ahead_ref[z, (i - 2) * 8 : (i - 1) * 8] = image
            else:
                behind_ref[z, s] = image
            weight = weight + source_ref[z, s] * sum_ref[z, 8 + i * 8 : 16 + i * 8, 0:COLS]
            curve = curve + now * image
        return weight, curve

    weight, curve = lax.fori_loop(0, LEVELS, images, (zero, zero))
    half = VECTORS // 2
    for part in range(2):

        def level(z, sums):
            image = image_ref[z]
            return tuple(
                sums[k] + fold_rows(basis_ref[part * half + k, z].astype(jnp.float32) * image) for k in range(half)
            )

        sums = lax.fori_loop(0, LEVELS, level, (zero,) * half)
        for k in range(half):
            sums_ref[part * half + k : part * half + k + 1] = jnp.sum(sums[k], axis=0, keepdims=True)
    lane = iota((1, COLS), 1)
    row = jnp.where(lane < VECTORS, row, 0.0)
    mine = told_ref[pl.ds(place.index(0, 0), 1), :]
    told = roll(row, VECTORS)
    told = told + jnp.where(lane == 64, total_of(weight) + total_of(row * mine), 0.0)
    told = told + jnp.where(lane == 65, total_of(curve), 0.0)
    out_ref[...] = row_of_sums(sums_ref[...]) + told


def second_coarse_kernel(
    place_ref, told_ref, coarse_ref, basis_ref, low_ref, high_ref, left_ref, right_ref, sum_ref, source_ref, absorption_ref,
    again_ref, first_sum_ref, direction_ref, first_ref,
    residual_ref, precond_ref, image_ref, out_ref, x, own_c, edge_c, ring_ref, side_ref,
):
    place = Place(place_ref, told_ref)
    row = add_coarse(place, told_ref, coarse_ref, basis_ref, low_ref, high_ref, left_ref, right_ref, 4, sum_ref, x,
                     own_c, edge_c, ring_ref, side_ref)
    weight0, curve0 = scalars(again_ref)
    step = weight0 / curve0
    zero = jnp.zeros((8, COLS), jnp.float32)

    def images(z, sums):
        weight, own, cross = sums
        for i in range(ROWS // 8):
            s = slice(i * 8, i * 8 + 8)
            t = slice(8 + i * 8, 16 + i * 8)
            now, image = image_at(x, absorption_ref, z, i)
            direction, first = direction_ref[z, s], first_ref[z, s]
            residual = source_ref[z, s] - step * first
            precond = direction - step * now
            image = first - step * image
            residual_ref[z, s] = residual
            precond_ref[z, s] = precond
            image_ref[z, s] = image
            weight = weight + residual * (first_sum_ref[z, t, 0:COLS] - step * sum_ref[z, t, 0:COLS])
            own = own + precond * image
            cross = cross + (precond * first + direction * image)
        return weight, own, cross

    weight, own, cross = lax.fori_loop(0, LEVELS, images, (zero, zero, zero))
    mine = pl.ds(place.index(0, 0), 1)
    lane = iota((1, COLS), 1)
    again = again_ref[mine, :]
    projected = told_ref[mine, :] - step * again
    coarse = roll(again, -VECTORS) - step * row
    both = jnp.where(lane < VECTORS, projected * coarse, 0.0)
    told = jnp.where(lane == 0, total_of(weight) + total_of(both), 0.0)
    told = told + jnp.where(lane == 1, total_of(own), 0.0) + jnp.where(lane == 2, total_of(cross), 0.0)
    out_ref[...] = jnp.broadcast_to(told, (COLS, COLS))


def last_kernel(again_ref, last_ref, direction_ref, first_ref, residual_ref, precond_ref, image_ref, x_ref, r_ref):
    weight0, curve0 = scalars(again_ref)
    step0 = weight0 / curve0
    totals = jnp.sum(last_ref[...], axis=0, keepdims=True)
    weight1, own, cross = totals[:, 0:1], totals[:, 1:2], totals[:, 2:3]
    ratio = weight1 / weight0
    step1 = weight1 / (own + ratio * (cross + ratio * curve0))

    def level(z, carry):
        direction = direction_ref[z]
        x_ref[z] = step0 * direction + step1 * (precond_ref[z] + ratio * direction)
        r_ref[z] = residual_ref[z] - step1 * (image_ref[z] + ratio * first_ref[z])
        return carry

    lax.fori_loop(0, LEVELS, level, 0)


def shards(source, absorption, basis, coarse_inverse, margin_width, coarse_slot):
    block = jax.ShapeDtypeStruct((LEVELS, ROWS, COLS), jnp.float32)
    slab = jax.ShapeDtypeStruct((LEVELS, EDGE, COLS), jnp.float32)
    message = jax.ShapeDtypeStruct((COLS, COLS), jnp.float32)
    params = pltpu.CompilerParams(vmem_limit_bytes=VMEM_LIMIT)
    smem = pl.BlockSpec(memory_space=pltpu.SMEM)
    vmem = pl.BlockSpec(memory_space=pltpu.VMEM)

    def scratch(*shape):
        return pltpu.VMEM(shape, jnp.float32)

    coarse_scratch = [
        scratch(PLANES, INNER, 2 * COLS), scratch(VECTORS, COLS), scratch(2 * VECTORS, COLS),
        scratch(2, LEVELS, COLS), scratch(2, 2 * TALL, COLS),
    ]
    place = jnp.stack(
        [lax.axis_index("gx"), lax.axis_index("gy"), lax.axis_size("gx"), lax.axis_size("gy")]
    ).astype(jnp.int32)
    table = jnp.array(list(zip(*chebyshev_table())), jnp.float32)
    told_row = jnp.concatenate(
        [
            jnp.zeros((1, VECTORS), jnp.float32),
            coarse_slot.reshape(1, -1).astype(jnp.float32),
            margin_width.astype(jnp.float32),
            jnp.zeros((1, COLS - 65), jnp.float32),
        ],
        axis=1,
    )
    rows, ahead, behind, left_edge, right_edge = first_projection(source, absorption, basis, told_row)
    low, high = exchange(ahead, behind, "gx")
    told = everyone(rows)
    rows, ahead, behind = middle(
        first_middle_kernel, 6, told, coarse_inverse, source, absorption, low, high, left_edge, right_edge
    )
    strips = exchange(ahead, behind, "gy")
    coarse = everyone(rows)
    coef = (absorption, low, high, strips)
    first_sum = smooth((0, LEVELS, 2), place, table, told, source, low, high, strips, *coef)
    edges = (low, high, *strips)
    direction, image, ahead, behind, rows = pl.pallas_call(
        first_coarse_kernel,
        in_specs=[smem] + [vmem] * 10,
        out_shape=[block, block, slab, slab, message],
        scratch_shapes=coarse_scratch + [scratch(VECTORS, COLS)],
        compiler_params=params,
        name="direction_and_image",
    )(place, told, coarse, basis, *edges, first_sum, source, absorption)
    low_w, high_w = exchange(ahead, behind, "gx")
    again = everyone(rows)
    rows, ahead, behind = middle(middle_kernel, 2, again, told, coarse_inverse, image, low_w, high_w)
    strips_w = exchange(ahead, behind, "gy")
    coarse = everyone(rows)
    second_sum = smooth((0, LEVELS, 2), place, table, told, image, low_w, high_w, strips_w, *coef)
    residual, precond, precond_image, rows = pl.pallas_call(
        second_coarse_kernel,
        in_specs=[smem] + [vmem] * 14,
        out_shape=[block, block, block, message],
        scratch_shapes=coarse_scratch,
        compiler_params=params,
        name="second_images",
    )(place, told, coarse, basis, *edges, second_sum, source, absorption, again, first_sum, direction, image)
    last = everyone(rows)
    concentration, residual = pl.pallas_call(
        last_kernel, out_shape=[block, block], compiler_params=params, name="update"
    )(again, last, direction, image, residual, precond, precond_image)
    return (concentration, residual)


def solution(mesh):
    return jax.shard_map(
        shards,
        mesh=mesh,
        in_specs=(
            P(None, "gx", "gy"),
            P(None, "gx", "gy"),
            P(None, None, "gx", "gy"),
            P(("gx", "gy"), None),
            P("gx", "gy"),
            P("gx", "gy", None),
        ),
        out_specs=(P(None, "gx", "gy"), P(None, "gx", "gy")),
        check_vma=False,
    )
```

```python
import functools

import jax
import jax.numpy as jnp
from jax import lax
from jax.experimental import pallas as pl
from jax.experimental.pallas import tpu as pltpu
from jax.sharding import PartitionSpec as P

KCHEB = 9
AXES = ("gx", "gy")
LEVELS = 16
ROWS = 32
COLS = 128
VECTORS = 32
EDGE = 16
TALL = ROWS + 2 * EDGE
HIGHEST = lax.Precision.HIGHEST

lowest_rate = 0.05
highest_rate = 18.5
vertical = 2.0
theta = 0.5 * (highest_rate + lowest_rate)
delta = 0.5 * (highest_rate - lowest_rate)
VMEM_LIMIT = 30 * 1024 * 1024
FIRST_LIMIT = 58 * 1024 * 1024


def chebyshev_table():
    ratio = theta / delta
    rho_old = 1.0 / ratio
    table = []
    for _ in range(KCHEB - 1):
        rho_new = 1.0 / (2.0 * ratio - rho_old)
        table.append((rho_new * rho_old, 2.0 * rho_new / delta))
        rho_old = rho_new
    return table


def iota(shape, dim):
    return lax.broadcasted_iota(jnp.int32, shape, dim)


def roll(value, shift):
    return pltpu.roll(value, shift % COLS, 1)


def exchange(forward_value, backward_value, axis):
    count = lax.axis_size(axis)
    forward = [(i, i + 1) for i in range(count - 1)]
    backward = [(target, source) for source, target in forward]
    return lax.ppermute(forward_value, axis, forward), lax.ppermute(backward_value, axis, backward)


def everyone(rows):
    return lax.all_to_all(rows, AXES, 0, 0, tiled=True)


def row_of_sums(sums):
    padded = jnp.concatenate([sums, jnp.zeros((COLS - VECTORS, COLS), jnp.float32)], 0)
    ones = jnp.ones((COLS, COLS), jnp.float32)
    return lax.dot_general(
        ones, padded, (((1,), (1,)), ((), ())), precision=HIGHEST, preferred_element_type=jnp.float32
    )


def fold_rows(product):
    return (product[0:8] + product[8:16]) + (product[16:24] + product[24:32])


def first_kernel(
    field_ref, coefficient_ref, basis_ref, told_ref, out_ref, ahead_ref, behind_ref, left_ref, right_ref, sums_ref
):
    step = pl.program_id(0)
    group = basis_ref.shape[0]
    lane = iota((ROWS, COLS), 1)

    @pl.when(step == 0)
    def _():
        left_ref[...] = jnp.zeros_like(left_ref)
        right_ref[...] = jnp.zeros_like(right_ref)

        def level(z, carry):
            ahead_ref[z] = field_ref[z, ROWS - EDGE :, :]
            behind_ref[z] = field_ref[z, :EDGE, :]
            ahead_ref[LEVELS + z] = coefficient_ref[z, ROWS - EDGE :, :]
            behind_ref[LEVELS + z] = coefficient_ref[z, :EDGE, :]
            return carry

        lax.fori_loop(0, LEVELS, level, 0)

    def level(z, sums):
        field = field_ref[z]
        low = left_ref[z >> 2]
        high = right_ref[z >> 2]
        new = []
        for j in range(group):
            values = basis_ref[j, z].astype(jnp.float32)
            new.append(sums[j] + fold_rows(values * field))
            at = 2 * LEVELS + step * group + j
            behind_ref[at, pl.ds(z, 1), :] = values[0:1]
            ahead_ref[at, pl.ds(z, 1), :] = values[ROWS - 1 : ROWS]
            k = step * group + j + VECTORS * (z & 3)
            turned = pltpu.roll(values, k, 1)
            low = jnp.where(lane == k, turned, low)
            high = jnp.where(lane == ((k + COLS - 1) & (COLS - 1)), turned, high)
        left_ref[z >> 2] = low
        right_ref[z >> 2] = high
        return tuple(new)

    zero = jnp.zeros((8, COLS), jnp.float32)
    sums = lax.fori_loop(0, LEVELS, level, (zero,) * group)
    for j in range(group):
        sums_ref[pl.ds(step * group + j, 1), :] = jnp.sum(sums[j], axis=0, keepdims=True)

    @pl.when(step == pl.num_programs(0) - 1)
    def _():
        out_ref[...] = row_of_sums(sums_ref[...]) + told_ref[...]


def first_projection(field, coefficient, basis, told_row):
    group = 8
    rows = 2 * LEVELS + VECTORS
    edge_rows = jax.ShapeDtypeStruct((rows, LEVELS, COLS), jnp.float32)
    edge_cols = jax.ShapeDtypeStruct((LEVELS // 4, ROWS, COLS), jnp.float32)
    block_spec = pl.BlockSpec((LEVELS, ROWS, COLS), lambda i: (0, 0, 0))
    rows_spec = pl.BlockSpec(edge_rows.shape, lambda i: (0, 0, 0))
    cols_spec = pl.BlockSpec(edge_cols.shape, lambda i: (0, 0, 0))
    return pl.pallas_call(
        first_kernel,
        grid=(VECTORS // group,),
        in_specs=[
            block_spec,
            block_spec,
            pl.BlockSpec((group, LEVELS, ROWS, COLS), lambda i: (i, 0, 0, 0)),
            pl.BlockSpec((1, COLS), lambda i: (0, 0)),
        ],
        out_specs=[pl.BlockSpec((COLS, COLS), lambda i: (0, 0)), rows_spec, rows_spec, cols_spec, cols_spec],
        out_shape=[jax.ShapeDtypeStruct((COLS, COLS), jnp.float32), edge_rows, edge_rows, edge_cols, edge_cols],
        scratch_shapes=[pltpu.VMEM((VECTORS, COLS), jnp.float32)],
        compiler_params=pltpu.CompilerParams(vmem_limit_bytes=FIRST_LIMIT),
        name="first_projection",
    )(field, coefficient, basis, told_row)


def coarse_rows(told_ref, slots_ref, inverse_ref, out_ref):
    told = told_ref[...]
    slots = slots_ref[...]
    turned = told.T
    slots_turned = slots.T
    lane = iota((COLS, COLS), 1)
    sub = iota((VECTORS, COLS), 0)
    placed = jnp.zeros((3 * VECTORS, COLS), jnp.float32)
    for k in range(VECTORS):
        slot_column = slots[:, VECTORS + k : VECTORS + k + 1].astype(jnp.int32)
        ones = jnp.where((slot_column & 127) == lane, 1.0, 0.0).astype(jnp.bfloat16)
        slot_row = slots_turned[VECTORS + k : VECTORS + k + 1, :].astype(jnp.int32)
        values = turned[k : k + 1, :]
        spread = jnp.where((slot_row >> 7) == sub, values, 0.0)
        first = spread.astype(jnp.bfloat16)
        rest = spread - first.astype(jnp.float32)
        second = rest.astype(jnp.bfloat16)
        third = (rest - second.astype(jnp.float32)).astype(jnp.bfloat16)
        parts = jnp.concatenate([first, second, third], 0)
        placed = placed + jnp.dot(parts, ones, preferred_element_type=jnp.float32)
    placed = placed[:VECTORS] + placed[VECTORS : 2 * VECTORS] + placed[2 * VECTORS :]
    total = jnp.zeros((VECTORS, COLS), jnp.float32)
    for high in range(VECTORS):
        total = total + inverse_ref[:, high * COLS : (high + 1) * COLS] * placed[high : high + 1]
    out_ref[...] = row_of_sums(total)


def pack_strips(parts, forward_ref, backward_ref, at):
    def levels(group, carry):
        row = 0
        for part, start in parts:
            height = EDGE if part.shape[1] == EDGE else ROWS
            lane = iota((height, COLS), 1)
            ahead = jnp.zeros((height, COLS), jnp.float32)
            behind = ahead
            for j in range(8):
                value = part[start + group * 8 + j]
                mine = (lane >= EDGE * j) & (lane < EDGE * (j + 1))
                ahead = jnp.where(mine, roll(value, EDGE * j - (COLS - EDGE)), ahead)
                behind = jnp.where(mine, roll(value, EDGE * j), behind)
            forward_ref[at + group, row : row + height, :] = ahead
            backward_ref[at + group, row : row + height, :] = behind
            row += height
        return carry

    lax.fori_loop(0, LEVELS // 8, levels, 0)


def first_middle_kernel(
    told_ref, inverse_ref, source_ref, absorption_ref, low_ref, high_ref, left_ref, right_ref,
    out_ref, forward_ref, backward_ref,
):
    for f, block in enumerate((source_ref, absorption_ref)):
        pack_strips(((low_ref, LEVELS * f), (block, 0), (high_ref, LEVELS * f)), forward_ref, backward_ref, 2 * f)
    for n in range(LEVELS // 8):
        for half in range(2):
            rows = slice(half * ROWS, (half + 1) * ROWS)
            forward_ref[4 + n, rows, :] = right_ref[2 * n + half]
            backward_ref[4 + n, rows, :] = left_ref[2 * n + half]
    coarse_rows(told_ref, told_ref, inverse_ref, out_ref)


def middle_kernel(told_ref, slots_ref, inverse_ref, block_ref, low_ref, high_ref, out_ref, forward_ref, backward_ref):
    pack_strips(((low_ref, 0), (block_ref, 0), (high_ref, 0)), forward_ref, backward_ref, 0)
    coarse_rows(told_ref, slots_ref, inverse_ref, out_ref)


def middle(kernel, strips, *operands):
    strips = jax.ShapeDtypeStruct((strips, TALL, COLS), jnp.float32)
    return pl.pallas_call(
        kernel,
        out_shape=[jax.ShapeDtypeStruct((COLS, COLS), jnp.float32), strips, strips],
        compiler_params=pltpu.CompilerParams(vmem_limit_bytes=VMEM_LIMIT),
        name="coarse_rows",
    )(*operands)


class Place:
    def __init__(self, place_ref, told_ref):
        self.row = place_ref[0]
        self.col = place_ref[1]
        self.rows = place_ref[2]
        self.cols = place_ref[3]
        self.told_ref = told_ref

    def index(self, down, right):
        row = jnp.clip(self.row + down, 0, self.rows - 1)
        col = jnp.clip(self.col + right, 0, self.cols - 1)
        return row * self.cols + col

    def margin(self, down, right):
        row, col = self.row + down, self.col + right
        real = (row >= 0) & (row < self.rows) & (col >= 0) & (col < self.cols)
        margin = self.told_ref[pl.ds(self.index(down, right), 1), :][:, 64:65]
        return jnp.where(real, margin.astype(jnp.int32), -4096)


def masks(place, own_ref, beside_ref, strip_ref):
    shape = (TALL, COLS)
    row = iota(shape, 0) - EDGE
    lane = iota(shape, 1)
    top, bottom = -ROWS * place.row, ROWS * (place.rows - place.row)
    first, last = -COLS * place.col, COLS * (place.cols - place.col)
    row_real = (row >= top) & (row < bottom)
    m = {(i, j): place.margin(i, j) for i in (-1, 0, 1) for j in (-1, 0, 1)}
    upper, lower = row < 8, row >= ROWS - 8
    for tile in range(2):
        col = lane if tile == 0 else jnp.where(lane < 64, lane + COLS, lane - COLS)
        real = row_real & (col >= first) & (col < last)
        if tile == 1:
            real = real & ((lane < EDGE) | (lane >= COLS - EDGE))

        def across(margin):
            return (col >= -margin) & (col < COLS + margin)

        own = m[0, 0]
        inside = real & (row >= -own) & (row < ROWS + own) & across(own)
        own_ref[tile] = jnp.where(inside, 1.0, 0.0)
        above, below = m[-1, 0], m[1, 0]
        inside = (upper & (row < above) & across(above)) | (lower & (row >= ROWS - below) & across(below))
        beside_ref[tile] = jnp.where(real & inside, 1.0, 0.0)
    group = ((lane + EDGE) & 127) >> 5
    away = ((lane + EDGE) & 31) - EDGE
    inside = row < -4096
    for place_of, side in ((0, -1), (2, 1)):
        col = away if side < 0 else away + COLS
        real = row_real & (col >= first) & (col < last)

        def reached(margin):
            return (away < margin) if side < 0 else (away >= -margin)

        level = m[0, side]
        inside = inside | (
            (group == place_of) & real & (row >= -level) & (row < ROWS + level) & reached(level)
        )
        above, below = m[-1, side], m[1, side]
        corner = (upper & (row < above) & reached(above)) | (
            lower & (row >= ROWS - below) & reached(below)
        )
        inside = inside | ((group == place_of + 1) & real & corner)
    strip_ref[...] = jnp.where(inside, 1.0, 0.0)


def tiles_of(parts, start, strips, at, z, i):
    low, block, high = parts
    from_left, from_right = strips
    lane = iota((8, COLS), 1)
    if i < 2:
        center = low[start + z, i * 8 : i * 8 + 8, :]
    elif i < 6:
        center = block[z, (i - 2) * 8 : (i - 2) * 8 + 8, :]
    else:
        center = high[start + z, (i - 6) * 8 : (i - 6) * 8 + 8, :]
    s = slice(i * 8, i * 8 + 8)
    group, shift = at + (z >> 3), EDGE * (z & 7)
    left = pltpu.roll(from_left[group, s, :], (COLS - EDGE) - shift, 1)
    right = pltpu.roll(from_right[group, s, :], (COLS - shift) & (COLS - 1), 1)
    margin = jnp.where(lane >= COLS - EDGE, left, jnp.where(lane < EDGE, right, 0.0))
    at_left = jnp.where(lane >= 64, margin, center)
    at_right = jnp.where(lane < 64, margin, center)
    near = (lane < EDGE) | (lane >= COLS - EDGE)
    others = jnp.where(lane < 80, roll(at_right, 64), roll(at_right, 96))
    packed = jnp.where(near, at_left, jnp.where(lane < 48, roll(at_left, 32), others))
    return center, margin, packed


UNROLL = 4
PLANES = LEVELS + 2
BESIDE_TILES = (1, 2, 5, 6)


def smooth_kernel(
    starts, place_ref, table_ref, told_ref, block_ref, low_ref, high_ref, left_ref, right_ref,
    absorption_ref, low_c, high_c, left_c, right_c, out_ref,
    own_m, beside_m, strip_m, own, beside, strip, own_y, beside_y, strip_y, own_d, beside_d, strip_d,
    own_e, beside_e, strip_e, own_r, beside_r, strip_r, diag, strip_diag,
):
    field_start, coef_start, coef_at = starts
    masks(Place(place_ref, told_ref), own_m, beside_m, strip_m)
    base = 4.0 + 2.0 * vertical
    zero = jnp.zeros((8, COLS), jnp.float32)
    lane = iota((8, COLS), 1)
    lanes = [slice(0, COLS), slice(COLS, 2 * COLS)]

    def clear(n, carry):
        at = n * (PLANES - 1)
        for i in range(8):
            s = slice(i * 8, i * 8 + 8)
            for t in range(2):
                for x in (own, own_y, beside, beside_y):
                    x[at, s, lanes[t]] = zero
            strip[at, s] = zero
            strip_y[at, s] = zero
        return carry

    lax.fori_loop(0, 2, clear, 0)

    def begin(z, carry):
        at = z + 1
        for i in range(8):
            s = slice(i * 8, i * 8 + 8)
            tiles = tiles_of((low_ref, block_ref, high_ref), field_start, (left_ref, right_ref), 0, z, i)
            inner = 1 <= i < 7
            for t in range(2):
                value = tiles[t] * own_m[t, s]
                if inner:
                    own_r[z, s, lanes[t]] = value
                    own_d[z, s, lanes[t]] = value * (1.0 / theta)
                else:
                    own_y[at, s, lanes[t]] = zero
                own[at, s, lanes[t]] = value * (1.0 / theta)
                value = tiles[t] * beside_m[t, s]
                if i in BESIDE_TILES:
                    beside_r[z, s, lanes[t]] = value
                    beside_d[z, s, lanes[t]] = value * (1.0 / theta)
                else:
                    beside_y[at, s, lanes[t]] = zero
                beside[at, s, lanes[t]] = value * (1.0 / theta)
            value = tiles[2] * strip_m[s]
            strip[at, s] = value * (1.0 / theta)
            if inner:
                strip_r[z, s] = value
                strip_d[z, s] = value * (1.0 / theta)
                tiles = tiles_of((low_c, absorption_ref, high_c), coef_start, (left_c, right_c), coef_at, z, i)
                diag[z, s, lanes[0]] = tiles[0] + base
                diag[z, s, lanes[1]] = tiles[1] + base
                strip_diag[z, s] = tiles[2] + base
            else:
                strip_y[at, s] = zero
        return carry

    lax.fori_loop(0, LEVELS, begin, 0)
    at_first, at_last = lane == 0, lane == COLS - 1

    def step(here, x, y, d, e, r, a, mask, width, i, keep, scale):
        s = slice(i * 8, i * 8 + 8)
        up, down = slice(i * 8 - 1, i * 8 + 7), slice(i * 8 + 1, i * 8 + 9)
        z = here - 1
        now = [x[here, s, lanes[t]] for t in range(width)]
        back = [roll(v, 1) for v in now]
        fore = [roll(v, -1) for v in now]
        if width == 2:
            back = [jnp.where(at_first, back[1], back[0]), jnp.where(at_first, back[0], back[1])]
            fore = [jnp.where(at_last, fore[1], fore[0]), jnp.where(at_last, fore[0], fore[1])]
        for t in range(width):
            high = x[here - 1, s, lanes[t]] + x[here + 1, s, lanes[t]]
            around = (x[here, up, lanes[t]] + x[here, down, lanes[t]]) + (back[t] + fore[t])
            around = around + (high + high)
            defect = r[z, s, lanes[t]] - a[z, s, lanes[t]] * now[t] + around
            move = keep * d[z, s, lanes[t]] + scale * defect
            if mask[t] is not None:
                move = move * mask[t]
            e[z, s, lanes[t]] = move
            y[here, s, lanes[t]] = now[t] + move

    first = ((own, own_y, own_d, own_e), (beside, beside_y, beside_d, beside_e), (strip, strip_y, strip_d, strip_e))
    second = tuple((y, x, e, d) for x, y, d, e in first)

    def sweep(n, arrays):
        keep, scale = table_ref[0, n], table_ref[1, n]
        own, beside, strip = arrays

        def level(z, carry):
            here = z + 1
            for i in range(1, 7):
                s = slice(i * 8, i * 8 + 8)
                free = None if 2 <= i < 6 else own_m[0, s]
                step(here, *own, own_r, diag, [free, own_m[1, s]], 2, i, keep, scale)
                if i in BESIDE_TILES:
                    step(here, *beside, beside_r, diag, [beside_m[0, s], beside_m[1, s]], 2, i, keep, scale)
                step(here, *strip, strip_r, strip_diag, [strip_m[s]], 1, i, keep, scale)
            return carry

        lax.fori_loop(0, LEVELS, level, 0, unroll=UNROLL)

    def pair(n, carry):
        sweep(2 * n, first)
        sweep(2 * n + 1, second)
        return carry

    lax.fori_loop(0, (KCHEB - 1) // 2, pair, 0)
    near_first, near_last = lane < EDGE, lane >= COLS - EDGE

    def finish(z, carry):
        at = z + 1
        for i in range(1, 7):
            s = slice(i * 8, i * 8 + 8)
            out = slice(i * 8 - 8, i * 8)
            value = strip[at, s]
            at_left = value + roll(value, -32)
            at_right = roll(at_left, 64)
            first = jnp.where(near_first, at_left, jnp.where(near_last, at_right, 0.0))
            second = jnp.where(near_last, at_left, jnp.where(near_first, at_right, 0.0))
            first = first + own[at, s, lanes[0]]
            second = second + own[at, s, lanes[1]]
            if i in BESIDE_TILES:
                first = first + beside[at, s, lanes[0]]
                second = second + beside[at, s, lanes[1]]
            out_ref[z, out, lanes[0]] = first
            out_ref[z, out, lanes[1]] = second
        return carry

    lax.fori_loop(0, LEVELS, finish, 0)


def smooth(starts, place, table, told, block, low, high, strips, absorption, low_c, high_c, strips_c):
    wide = (TALL, 2 * COLS)
    thin = (TALL, COLS)

    def scratch(*shape):
        return pltpu.VMEM(shape, jnp.float32)

    smem = pl.BlockSpec(memory_space=pltpu.SMEM)
    vmem = pl.BlockSpec(memory_space=pltpu.VMEM)
    return pl.pallas_call(
        functools.partial(smooth_kernel, starts),
        in_specs=[smem] * 2 + [vmem] * 11,
        out_shape=jax.ShapeDtypeStruct((LEVELS, INNER, 2 * COLS), jnp.float32),
        scratch_shapes=[
            scratch(2, *thin), scratch(2, *thin), scratch(*thin),
            scratch(PLANES, *wide), scratch(PLANES, *wide), scratch(PLANES, *thin),
            scratch(PLANES, *wide), scratch(PLANES, *wide), scratch(PLANES, *thin),
            scratch(LEVELS, *wide), scratch(LEVELS, *wide), scratch(LEVELS, *thin),
            scratch(LEVELS, *wide), scratch(LEVELS, *wide), scratch(LEVELS, *thin),
            scratch(LEVELS, *wide), scratch(LEVELS, *wide), scratch(LEVELS, *thin),
            scratch(LEVELS, *wide), scratch(LEVELS, *thin),
        ],
        compiler_params=pltpu.CompilerParams(vmem_limit_bytes=VMEM_LIMIT),
        cost_estimate=pl.CostEstimate(flops=60000000, bytes_accessed=4000000, transcendentals=0),
        name="smoother",
    )(place, table, told, block, low, high, *strips, absorption, low_c, high_c, *strips_c)


INNER = ROWS + 16


def slots_of(place, told_ref, moves):
    lane = iota((1, COLS), 1)
    slots = jnp.zeros((1, COLS), jnp.float32)
    for n, (down, right) in enumerate(moves):
        row = roll(told_ref[pl.ds(place.index(down, right), 1), :], VECTORS * (n - 1))
        slots = jnp.where((lane >> 5) == n, row, slots)
    return slots.astype(jnp.int32)


def coarse_at(coarse_turned, slots):
    pick = jnp.where(iota((COLS, COLS), 0) == (slots >> 5), 1.0, 0.0)
    found = jnp.dot(coarse_turned, pick, precision=HIGHEST, preferred_element_type=jnp.float32)
    found = jnp.where(iota((VECTORS, COLS), 0) == (slots & 31), found, 0.0)
    return jnp.sum(found, axis=0, keepdims=True)


def add_coarse(place, told_ref, coarse_ref, basis_ref, low_ref, high_ref, left_ref, right_ref, at, sum_ref, x,
               own_c, edge_c, ring_ref, side_ref):
    turned = coarse_ref[...].T[:VECTORS]
    row = coarse_at(turned, slots_of(place, told_ref, ((0, 0), (-1, 0), (1, 0), (0, -1))))
    other = coarse_at(turned, slots_of(place, told_ref, ((0, 1),)))
    lane = iota((8, COLS), 1)
    lane_row = iota((1, COLS), 1)
    column = jnp.broadcast_to(row, (COLS, COLS)).T
    own_c[...] = column[:VECTORS]
    edge_c[...] = column[VECTORS : 3 * VECTORS]
    for n, edge in ((0, low_ref), (1, high_ref)):

        def vector(k, total):
            return total + edge[2 * LEVELS + k] * edge_c[pl.ds(n * VECTORS + k, 1), :]

        ring_ref[n] = lax.fori_loop(0, VECTORS, vector, jnp.zeros((LEVELS, COLS), jnp.float32))
    for n, (edge, values, shift) in enumerate(((left_ref, roll(row, VECTORS), -1), (right_ref, other, 0))):
        values = jnp.where(lane_row < VECTORS, values, 0.0)
        values = values + roll(values, 32) + roll(values, 64) + roll(values, 96)
        weights = jnp.broadcast_to(roll(values, shift), (COLS, COLS)).T
        which = ((iota((COLS, COLS), 0) - shift) & (COLS - 1)) >> 5
        weights = jnp.where(iota((COLS, COLS), 1) == which, weights, 0.0)
        parts = edge[at : at + 2].reshape(2 * TALL, COLS)
        side_ref[n] = jnp.dot(parts, weights, precision=HIGHEST, preferred_element_type=jnp.float32)

    def level(z, carry):
        total = sum_ref[z, 8 : 8 + ROWS, 0:COLS]
        for k in range(VECTORS):
            total = total + basis_ref[k, z].astype(jnp.float32) * own_c[k : k + 1]
        here = z + 1
        x[here, 8 : 8 + ROWS, 0:COLS] = total
        rows = pl.ds(z, 1)
        x[here, 7:8, 0:COLS] = sum_ref[z, 7:8, 0:COLS] + ring_ref[0, rows, :]
        x[here, 8 + ROWS : 9 + ROWS, 0:COLS] = sum_ref[z, 8 + ROWS : 9 + ROWS, 0:COLS] + ring_ref[1, rows, :]
        q = z & 3
        for i in range(ROWS // 8):
            s = pl.ds(pl.multiple_of((z >> 2) * ROWS + i * 8, 8), 8)
            left = pltpu.roll(side_ref[0, s, :], (COLS - 1) - q, 1)
            right = pltpu.roll(side_ref[1, s, :], (COLS - q) & (COLS - 1), 1)
            t = slice(8 + i * 8, 16 + i * 8)
            value = jnp.where(lane == COLS - 1, left, jnp.where(lane == 0, right, 0.0))
            x[here, t, COLS : 2 * COLS] = sum_ref[z, t, COLS : 2 * COLS] + value
        return carry

    lax.fori_loop(0, LEVELS, level, 0)
    zero = jnp.zeros((ROWS, COLS), jnp.float32)
    x[0, 8 : 8 + ROWS, 0:COLS] = zero
    x[PLANES - 1, 8 : 8 + ROWS, 0:COLS] = zero
    return row


def image_at(x, absorption_ref, z, i):
    lane = iota((8, COLS), 1)
    here = z + 1
    s = slice(8 + i * 8, 16 + i * 8)
    up, down = slice(7 + i * 8, 15 + i * 8), slice(9 + i * 8, 17 + i * 8)
    now = x[here, s, 0:COLS]
    margin = x[here, s, COLS : 2 * COLS]
    back = jnp.where(lane == 0, roll(margin, 1), roll(now, 1))
    fore = jnp.where(lane == COLS - 1, roll(margin, -1), roll(now, -1))
    high = x[here - 1, s, 0:COLS] + x[here + 1, s, 0:COLS]
    around = (x[here, up, 0:COLS] + x[here, down, 0:COLS]) + (back + fore)
    diagonal = absorption_ref[z, i * 8 : i * 8 + 8, :] + (4.0 + 2.0 * vertical)
    return now, diagonal * now - around - vertical * high


def total_of(value):
    return jnp.sum(jnp.sum(value, axis=0, keepdims=True), axis=1, keepdims=True)


def scalars(told_ref):
    totals = jnp.sum(told_ref[...], axis=0, keepdims=True)
    return totals[:, 64:65], totals[:, 65:66]


def first_coarse_kernel(
    place_ref, told_ref, coarse_ref, basis_ref, low_ref, high_ref, left_ref, right_ref, sum_ref, source_ref, absorption_ref,
    direction_ref, image_ref, ahead_ref, behind_ref, out_ref, x, own_c, edge_c, ring_ref, side_ref, sums_ref,
):
    place = Place(place_ref, told_ref)
    row = add_coarse(place, told_ref, coarse_ref, basis_ref, low_ref, high_ref, left_ref, right_ref, 4, sum_ref, x,
                     own_c, edge_c, ring_ref, side_ref)
    zero = jnp.zeros((8, COLS), jnp.float32)

    def images(z, carry):
        weight, curve = carry
        for i in range(ROWS // 8):
            s = slice(i * 8, i * 8 + 8)
            now, image = image_at(x, absorption_ref, z, i)
            direction_ref[z, s] = now
            image_ref[z, s] = image
            if i >= 2:
                ahead_ref[z, (i - 2) * 8 : (i - 1) * 8] = image
            else:
                behind_ref[z, s] = image
            weight = weight + source_ref[z, s] * sum_ref[z, 8 + i * 8 : 16 + i * 8, 0:COLS]
            curve = curve + now * image
        return weight, curve

    weight, curve = lax.fori_loop(0, LEVELS, images, (zero, zero))
    half = VECTORS // 2
    for part in range(2):

        def level(z, sums):
            image = image_ref[z]
            return tuple(
                sums[k] + fold_rows(basis_ref[part * half + k, z].astype(jnp.float32) * image) for k in range(half)
            )

        sums = lax.fori_loop(0, LEVELS, level, (zero,) * half)
        for k in range(half):
            sums_ref[part * half + k : part * half + k + 1] = jnp.sum(sums[k], axis=0, keepdims=True)
    lane = iota((1, COLS), 1)
    row = jnp.where(lane < VECTORS, row, 0.0)
    mine = told_ref[pl.ds(place.index(0, 0), 1), :]
    told = roll(row, VECTORS)
    told = told + jnp.where(lane == 64, total_of(weight) + total_of(row * mine), 0.0)
    told = told + jnp.where(lane == 65, total_of(curve), 0.0)
    out_ref[...] = row_of_sums(sums_ref[...]) + told


def second_coarse_kernel(
    place_ref, told_ref, coarse_ref, basis_ref, low_ref, high_ref, left_ref, right_ref, sum_ref, source_ref, absorption_ref,
    again_ref, first_sum_ref, direction_ref, first_ref,
    residual_ref, precond_ref, image_ref, out_ref, x, own_c, edge_c, ring_ref, side_ref,
):
    place = Place(place_ref, told_ref)
    row = add_coarse(place, told_ref, coarse_ref, basis_ref, low_ref, high_ref, left_ref, right_ref, 4, sum_ref, x,
                     own_c, edge_c, ring_ref, side_ref)
    weight0, curve0 = scalars(again_ref)
    step = weight0 / curve0
    zero = jnp.zeros((8, COLS), jnp.float32)

    def images(z, sums):
        weight, own, cross = sums
        for i in range(ROWS // 8):
            s = slice(i * 8, i * 8 + 8)
            t = slice(8 + i * 8, 16 + i * 8)
            now, image = image_at(x, absorption_ref, z, i)
            direction, first = direction_ref[z, s], first_ref[z, s]
            residual = source_ref[z, s] - step * first
            precond = direction - step * now
            image = first - step * image
            residual_ref[z, s] = residual
            precond_ref[z, s] = precond
            image_ref[z, s] = image
            weight = weight + residual * (first_sum_ref[z, t, 0:COLS] - step * sum_ref[z, t, 0:COLS])
            own = own + precond * image
            cross = cross + (precond * first + direction * image)
        return weight, own, cross

    weight, own, cross = lax.fori_loop(0, LEVELS, images, (zero, zero, zero))
    mine = pl.ds(place.index(0, 0), 1)
    lane = iota((1, COLS), 1)
    again = again_ref[mine, :]
    projected = told_ref[mine, :] - step * again
    coarse = roll(again, -VECTORS) - step * row
    both = jnp.where(lane < VECTORS, projected * coarse, 0.0)
    told = jnp.where(lane == 0, total_of(weight) + total_of(both), 0.0)
    told = told + jnp.where(lane == 1, total_of(own), 0.0) + jnp.where(lane == 2, total_of(cross), 0.0)
    out_ref[...] = jnp.broadcast_to(told, (COLS, COLS))


def last_kernel(again_ref, last_ref, direction_ref, first_ref, residual_ref, precond_ref, image_ref, x_ref, r_ref):
    weight0, curve0 = scalars(again_ref)
    step0 = weight0 / curve0
    totals = jnp.sum(last_ref[...], axis=0, keepdims=True)
    weight1, own, cross = totals[:, 0:1], totals[:, 1:2], totals[:, 2:3]
    ratio = weight1 / weight0
    step1 = weight1 / (own + ratio * (cross + ratio * curve0))

    def level(z, carry):
        direction = direction_ref[z]
        x_ref[z] = step0 * direction + step1 * (precond_ref[z] + ratio * direction)
        r_ref[z] = residual_ref[z] - step1 * (image_ref[z] + ratio * first_ref[z])
        return carry

    lax.fori_loop(0, LEVELS, level, 0)


def shards(source, absorption, basis, coarse_inverse, margin_width, coarse_slot):
    block = jax.ShapeDtypeStruct((LEVELS, ROWS, COLS), jnp.float32)
    slab = jax.ShapeDtypeStruct((LEVELS, EDGE, COLS), jnp.float32)
    message = jax.ShapeDtypeStruct((COLS, COLS), jnp.float32)
    params = pltpu.CompilerParams(vmem_limit_bytes=VMEM_LIMIT)
    smem = pl.BlockSpec(memory_space=pltpu.SMEM)
    vmem = pl.BlockSpec(memory_space=pltpu.VMEM)

    def scratch(*shape):
        return pltpu.VMEM(shape, jnp.float32)

    coarse_scratch = [
        scratch(PLANES, INNER, 2 * COLS), scratch(VECTORS, COLS), scratch(2 * VECTORS, COLS),
        scratch(2, LEVELS, COLS), scratch(2, 2 * TALL, COLS),
    ]
    place = jnp.stack(
        [lax.axis_index("gx"), lax.axis_index("gy"), lax.axis_size("gx"), lax.axis_size("gy")]
    ).astype(jnp.int32)
    table = jnp.array(list(zip(*chebyshev_table())), jnp.float32)
    told_row = jnp.concatenate(
        [
            jnp.zeros((1, VECTORS), jnp.float32),
            coarse_slot.reshape(1, -1).astype(jnp.float32),
            margin_width.astype(jnp.float32),
            jnp.zeros((1, COLS - 65), jnp.float32),
        ],
        axis=1,
    )
    rows, ahead, behind, left_edge, right_edge = first_projection(source, absorption, basis, told_row)
    low, high = exchange(ahead, behind, "gx")
    told = everyone(rows)
    rows, ahead, behind = middle(
        first_middle_kernel, 6, told, coarse_inverse, source, absorption, low, high, left_edge, right_edge
    )
    strips = exchange(ahead, behind, "gy")
    coarse = everyone(rows)
    coef = (absorption, low, high, strips)
    first_sum = smooth((0, LEVELS, 2), place, table, told, source, low, high, strips, *coef)
    edges = (low, high, *strips)
    direction, image, ahead, behind, rows = pl.pallas_call(
        first_coarse_kernel,
        in_specs=[smem] + [vmem] * 10,
        out_shape=[block, block, slab, slab, message],
        scratch_shapes=coarse_scratch + [scratch(VECTORS, COLS)],
        compiler_params=params,
        name="direction_and_image",
    )(place, told, coarse, basis, *edges, first_sum, source, absorption)
    low_w, high_w = exchange(ahead, behind, "gx")
    again = everyone(rows)
    rows, ahead, behind = middle(middle_kernel, 2, again, told, coarse_inverse, image, low_w, high_w)
    strips_w = exchange(ahead, behind, "gy")
    coarse = everyone(rows)
    second_sum = smooth((0, LEVELS, 2), place, table, told, image, low_w, high_w, strips_w, *coef)
    residual, precond, precond_image, rows = pl.pallas_call(
        second_coarse_kernel,
        in_specs=[smem] + [vmem] * 14,
        out_shape=[block, block, block, message],
        scratch_shapes=coarse_scratch,
        compiler_params=params,
        name="second_images",
    )(place, told, coarse, basis, *edges, second_sum, source, absorption, again, first_sum, direction, image)
    last = everyone(rows)
    concentration, residual = pl.pallas_call(
        last_kernel, out_shape=[block, block], compiler_params=params, name="update"
    )(again, last, direction, image, residual, precond, precond_image)
    return (concentration, residual)


def solution(mesh):
    return jax.shard_map(
        shards,
        mesh=mesh,
        in_specs=(
            P(None, "gx", "gy"),
            P(None, "gx", "gy"),
            P(None, None, "gx", "gy"),
            P(("gx", "gy"), None),
            P("gx", "gy"),
            P("gx", "gy", None),
        ),
        out_specs=(P(None, "gx", "gy"), P(None, "gx", "gy")),
        check_vma=False,
    )
```

```python
import functools

import jax
import jax.numpy as jnp
from jax import lax
from jax.experimental import pallas as pl
from jax.experimental.pallas import tpu as pltpu
from jax.sharding import PartitionSpec as P

KCHEB = 9
AXES = ("gx", "gy")
LEVELS = 16
ROWS = 32
COLS = 128
VECTORS = 32
EDGE = 16
TALL = ROWS + 2 * EDGE
HIGHEST = lax.Precision.HIGHEST

lowest_rate = 0.05
highest_rate = 18.5
vertical = 2.0
theta = 0.5 * (highest_rate + lowest_rate)
delta = 0.5 * (highest_rate - lowest_rate)
VMEM_LIMIT = 30 * 1024 * 1024
FIRST_LIMIT = 58 * 1024 * 1024


def chebyshev_table():
    ratio = theta / delta
    rho_old = 1.0 / ratio
    table = []
    for _ in range(KCHEB - 1):
        rho_new = 1.0 / (2.0 * ratio - rho_old)
        table.append((rho_new * rho_old, 2.0 * rho_new / delta))
        rho_old = rho_new
    return table


def iota(shape, dim):
    return lax.broadcasted_iota(jnp.int32, shape, dim)


def roll(value, shift):
    return pltpu.roll(value, shift % COLS, 1)


def exchange(forward_value, backward_value, axis):
    count = lax.axis_size(axis)
    forward = [(i, i + 1) for i in range(count - 1)]
    backward = [(target, source) for source, target in forward]
    return lax.ppermute(forward_value, axis, forward), lax.ppermute(backward_value, axis, backward)


def everyone(rows):
    return lax.all_to_all(rows, AXES, 0, 0, tiled=True)


def row_of_sums(sums):
    padded = jnp.concatenate([sums, jnp.zeros((COLS - VECTORS, COLS), jnp.float32)], 0)
    ones = jnp.ones((COLS, COLS), jnp.float32)
    return lax.dot_general(
        ones, padded, (((1,), (1,)), ((), ())), precision=HIGHEST, preferred_element_type=jnp.float32
    )


def fold_rows(product):
    return (product[0:8] + product[8:16]) + (product[16:24] + product[24:32])


def first_kernel(
    field_ref, coefficient_ref, basis_ref, slots_ref, margin_ref,
    out_ref, ahead_ref, behind_ref, left_ref, right_ref, sums_ref, edges_ref,
):
    step = pl.program_id(0)
    group = basis_ref.shape[0]

    @pl.when(step == 0)
    def _():
        edges_ref[...] = jnp.zeros_like(edges_ref)

        def level(z, carry):
            ahead_ref[z] = field_ref[z, ROWS - EDGE :, :]
            behind_ref[z] = field_ref[z, :EDGE, :]
            ahead_ref[LEVELS + z] = coefficient_ref[z, ROWS - EDGE :, :]
            behind_ref[LEVELS + z] = coefficient_ref[z, :EDGE, :]
            return carry

        lax.fori_loop(0, LEVELS, level, 0)

    def level(z, sums):
        field = field_ref[z]
        new = []
        for j in range(group):
            values = basis_ref[j, z].astype(jnp.float32)
            new.append(sums[j] + fold_rows(values * field))
            at = 2 * LEVELS + step * group + j
            behind_ref[at, pl.ds(z, 1), :] = values[0:1]
            ahead_ref[at, pl.ds(z, 1), :] = values[ROWS - 1 : ROWS]
        return tuple(new)

    zero = jnp.zeros((8, COLS), jnp.float32)
    sums = lax.fori_loop(0, LEVELS, level, (zero,) * group, unroll=2)
    for j in range(group):
        sums_ref[pl.ds(step * group + j, 1), :] = jnp.sum(sums[j], axis=0, keepdims=True)
    from_lane, to_lane = iota((COLS, COLS), 0), iota((COLS, COLS), 1)
    picks = []
    for j in range(group):
        k = step * group + j
        pick = ((from_lane == 0) & (to_lane == k)) | ((from_lane == COLS - 1) & (to_lane == VECTORS + k))
        picks.append(jnp.where(pick, 1.0, 0.0).astype(jnp.bfloat16))
    values = jnp.concatenate([basis_ref[j].reshape(LEVELS * ROWS, COLS) for j in range(group)], axis=1)
    edges_ref[...] += jnp.dot(values, jnp.concatenate(picks, 0), preferred_element_type=jnp.float32)

    @pl.when(step == pl.num_programs(0) - 1)
    def _():
        told = jnp.concatenate(
            [
                jnp.zeros((1, VECTORS), jnp.float32),
                slots_ref[0].astype(jnp.float32),
                margin_ref[...].astype(jnp.float32),
                jnp.zeros((1, COLS - 65), jnp.float32),
            ],
            axis=1,
        )
        out_ref[...] = row_of_sums(sums_ref[...]) + told
        place = iota((ROWS, COLS), 1) >> 5
        for n in range(LEVELS // 4):
            left = jnp.zeros((ROWS, COLS), jnp.float32)
            right = left
            for q in range(4):
                z = 4 * n + q
                value = edges_ref[z * ROWS : (z + 1) * ROWS]
                left = jnp.where(place == q, roll(value, VECTORS * q), left)
                right = jnp.where(place == q, roll(value, VECTORS * (q - 1)), right)
            left_ref[n] = left
            right_ref[n] = right


def first_projection(field, coefficient, basis, slots, margin):
    group = 8
    rows = 2 * LEVELS + VECTORS
    edge_rows = jax.ShapeDtypeStruct((rows, LEVELS, COLS), jnp.float32)
    edge_cols = jax.ShapeDtypeStruct((LEVELS // 4, ROWS, COLS), jnp.float32)
    block_spec = pl.BlockSpec((LEVELS, ROWS, COLS), lambda i: (0, 0, 0))
    rows_spec = pl.BlockSpec(edge_rows.shape, lambda i: (0, 0, 0))
    cols_spec = pl.BlockSpec(edge_cols.shape, lambda i: (0, 0, 0))
    return pl.pallas_call(
        first_kernel,
        grid=(VECTORS // group,),
        in_specs=[
            block_spec,
            block_spec,
            pl.BlockSpec((group, LEVELS, ROWS, COLS), lambda i: (i, 0, 0, 0)),
            pl.BlockSpec(slots.shape, lambda i: (0, 0, 0)),
            pl.BlockSpec(margin.shape, lambda i: (0, 0)),
        ],
        out_specs=[pl.BlockSpec((COLS, COLS), lambda i: (0, 0)), rows_spec, rows_spec, cols_spec, cols_spec],
        out_shape=[jax.ShapeDtypeStruct((COLS, COLS), jnp.float32), edge_rows, edge_rows, edge_cols, edge_cols],
        scratch_shapes=[
            pltpu.VMEM((VECTORS, COLS), jnp.float32), pltpu.VMEM((LEVELS * ROWS, COLS), jnp.float32)
        ],
        compiler_params=pltpu.CompilerParams(vmem_limit_bytes=FIRST_LIMIT),
        name="first_projection",
    )(field, coefficient, basis, slots, margin)


def coarse_rows(told_ref, slots_ref, inverse_ref, out_ref):
    told = told_ref[...]
    slots = slots_ref[...]
    turned = told.T
    slots_turned = slots.T
    lane = iota((COLS, COLS), 1)
    sub = iota((VECTORS, COLS), 0)
    placed = jnp.zeros((3 * VECTORS, COLS), jnp.float32)
    for k in range(VECTORS):
        slot_column = slots[:, VECTORS + k : VECTORS + k + 1].astype(jnp.int32)
        ones = jnp.where((slot_column & 127) == lane, 1.0, 0.0).astype(jnp.bfloat16)
        slot_row = slots_turned[VECTORS + k : VECTORS + k + 1, :].astype(jnp.int32)
        values = turned[k : k + 1, :]
        spread = jnp.where((slot_row >> 7) == sub, values, 0.0)
        first = spread.astype(jnp.bfloat16)
        rest = spread - first.astype(jnp.float32)
        second = rest.astype(jnp.bfloat16)
        third = (rest - second.astype(jnp.float32)).astype(jnp.bfloat16)
        parts = jnp.concatenate([first, second, third], 0)
        placed = placed + jnp.dot(parts, ones, preferred_element_type=jnp.float32)
    placed = placed[:VECTORS] + placed[VECTORS : 2 * VECTORS] + placed[2 * VECTORS :]
    total = jnp.zeros((VECTORS, COLS), jnp.float32)
    for high in range(VECTORS):
        total = total + inverse_ref[:, high * COLS : (high + 1) * COLS] * placed[high : high + 1]
    out_ref[...] = row_of_sums(total)


def pack_strips(parts, forward_ref, backward_ref, at):
    def levels(group, carry):
        row = 0
        for part, start in parts:
            height = EDGE if part.shape[1] == EDGE else ROWS
            lane = iota((height, COLS), 1)
            ahead = jnp.zeros((height, COLS), jnp.float32)
            behind = ahead
            for j in range(8):
                value = part[start + group * 8 + j]
                mine = (lane >= EDGE * j) & (lane < EDGE * (j + 1))
                ahead = jnp.where(mine, roll(value, EDGE * j - (COLS - EDGE)), ahead)
                behind = jnp.where(mine, roll(value, EDGE * j), behind)
            forward_ref[at + group, row : row + height, :] = ahead
            backward_ref[at + group, row : row + height, :] = behind
            row += height
        return carry

    lax.fori_loop(0, LEVELS // 8, levels, 0)


def first_pack_kernel(
    source_ref, absorption_ref, low_ref, high_ref, left_ref, right_ref, forward_ref, backward_ref
):
    for f, block in enumerate((source_ref, absorption_ref)):
        pack_strips(((low_ref, LEVELS * f), (block, 0), (high_ref, LEVELS * f)), forward_ref, backward_ref, 2 * f)
    for n in range(LEVELS // 8):
        for half in range(2):
            rows = slice(half * ROWS, (half + 1) * ROWS)
            forward_ref[4 + n, rows, :] = right_ref[2 * n + half]
            backward_ref[4 + n, rows, :] = left_ref[2 * n + half]


def pack_kernel(block_ref, low_ref, high_ref, forward_ref, backward_ref):
    pack_strips(((low_ref, 0), (block_ref, 0), (high_ref, 0)), forward_ref, backward_ref, 0)


FIELDS_SPEC = pl.BlockSpec((2 * LEVELS, EDGE, COLS), lambda i: (0, 0, 0))
VMEM_SPEC = pl.BlockSpec(memory_space=pltpu.VMEM)
SMEM_SPEC = pl.BlockSpec(memory_space=pltpu.SMEM)


def pack(kernel, specs, strips, *operands):
    strips = jax.ShapeDtypeStruct((strips, TALL, COLS), jnp.float32)
    return pl.pallas_call(
        kernel,
        grid=(1,),
        in_specs=specs,
        out_shape=[strips, strips],
        compiler_params=pltpu.CompilerParams(vmem_limit_bytes=VMEM_LIMIT),
        cost_estimate=pl.CostEstimate(flops=2000000, bytes_accessed=2000000, transcendentals=0),
        name="strips",
    )(*operands)


def solve_rows(*operands):
    return pl.pallas_call(
        coarse_rows,
        out_shape=jax.ShapeDtypeStruct((COLS, COLS), jnp.float32),
        compiler_params=pltpu.CompilerParams(vmem_limit_bytes=VMEM_LIMIT),
        name="coarse_rows",
    )(*operands)


class Place:
    def __init__(self, place_ref, told_ref):
        self.row = place_ref[0]
        self.col = place_ref[1]
        self.rows = place_ref[2]
        self.cols = place_ref[3]
        self.told_ref = told_ref

    def index(self, down, right):
        row = jnp.clip(self.row + down, 0, self.rows - 1)
        col = jnp.clip(self.col + right, 0, self.cols - 1)
        return row * self.cols + col

    def margin(self, down, right):
        row, col = self.row + down, self.col + right
        real = (row >= 0) & (row < self.rows) & (col >= 0) & (col < self.cols)
        margin = self.told_ref[pl.ds(self.index(down, right), 1), :][:, 64:65]
        return jnp.where(real, margin.astype(jnp.int32), -4096)


def masks(place, own_ref, beside_ref, strip_ref):
    shape = (TALL, COLS)
    row = iota(shape, 0) - EDGE
    lane = iota(shape, 1)
    top, bottom = -ROWS * place.row, ROWS * (place.rows - place.row)
    first, last = -COLS * place.col, COLS * (place.cols - place.col)
    row_real = (row >= top) & (row < bottom)
    m = {(i, j): place.margin(i, j) for i in (-1, 0, 1) for j in (-1, 0, 1)}
    upper, lower = row < 8, row >= ROWS - 8
    for tile in range(2):
        col = lane if tile == 0 else jnp.where(lane < 64, lane + COLS, lane - COLS)
        real = row_real & (col >= first) & (col < last)
        if tile == 1:
            real = real & ((lane < EDGE) | (lane >= COLS - EDGE))

        def across(margin):
            return (col >= -margin) & (col < COLS + margin)

        own = m[0, 0]
        inside = real & (row >= -own) & (row < ROWS + own) & across(own)
        own_ref[tile] = jnp.where(inside, 1.0, 0.0)
        above, below = m[-1, 0], m[1, 0]
        inside = (upper & (row < above) & across(above)) | (lower & (row >= ROWS - below) & across(below))
        beside_ref[tile] = jnp.where(real & inside, 1.0, 0.0)
    group = ((lane + EDGE) & 127) >> 5
    away = ((lane + EDGE) & 31) - EDGE
    inside = row < -4096
    for place_of, side in ((0, -1), (2, 1)):
        col = away if side < 0 else away + COLS
        real = row_real & (col >= first) & (col < last)

        def reached(margin):
            return (away < margin) if side < 0 else (away >= -margin)

        level = m[0, side]
        inside = inside | (
            (group == place_of) & real & (row >= -level) & (row < ROWS + level) & reached(level)
        )
        above, below = m[-1, side], m[1, side]
        corner = (upper & (row < above) & reached(above)) | (
            lower & (row >= ROWS - below) & reached(below)
        )
        inside = inside | ((group == place_of + 1) & real & corner)
    strip_ref[...] = jnp.where(inside, 1.0, 0.0)


def tiles_of(parts, start, strips, at, z, i):
    low, block, high = parts
    from_left, from_right = strips
    lane = iota((8, COLS), 1)
    if i < 2:
        center = low[start + z, i * 8 : i * 8 + 8, :]
    elif i < 6:
        center = block[z, (i - 2) * 8 : (i - 2) * 8 + 8, :]
    else:
        center = high[start + z, (i - 6) * 8 : (i - 6) * 8 + 8, :]
    s = slice(i * 8, i * 8 + 8)
    group, shift = at + (z >> 3), EDGE * (z & 7)
    left = pltpu.roll(from_left[group, s, :], (COLS - EDGE) - shift, 1)
    right = pltpu.roll(from_right[group, s, :], (COLS - shift) & (COLS - 1), 1)
    margin = jnp.where(lane >= COLS - EDGE, left, jnp.where(lane < EDGE, right, 0.0))
    at_left = jnp.where(lane >= 64, margin, center)
    at_right = jnp.where(lane < 64, margin, center)
    near = (lane < EDGE) | (lane >= COLS - EDGE)
    others = jnp.where(lane < 80, roll(at_right, 64), roll(at_right, 96))
    packed = jnp.where(near, at_left, jnp.where(lane < 48, roll(at_left, 32), others))
    return center, margin, packed


UNROLL = 8
UNROLL_BEGIN = 2
UNROLL_FINISH = 2
PLANES = LEVELS + 2
BESIDE_TILES = (1, 2, 5, 6)


def smooth_kernel(same, place_ref, table_ref, told_ref, block_ref, low_ref, high_ref, left_ref, right_ref, absorption_ref, *refs):
    if same:
        low_c, high_c, left_c, right_c = low_ref, high_ref, left_ref, right_ref
    else:
        low_c, high_c, left_c, right_c = refs[:4]
        refs = refs[4:]
    (
        out_ref, own_m, beside_m, strip_m, own, beside, strip, own_y, beside_y, strip_y,
        wide_r, strip_r, diag, strip_diag,
    ) = refs
    field_start, coef_start, coef_at = 0, LEVELS, 2
    masks(Place(place_ref, told_ref), own_m, beside_m, strip_m)
    base = 4.0 + 2.0 * vertical
    zero = jnp.zeros((8, COLS), jnp.float32)
    lane = iota((8, COLS), 1)
    lanes = [slice(0, COLS), slice(COLS, 2 * COLS)]

    def clear(n, carry):
        at = n * (PLANES - 1)
        for i in range(8):
            s = slice(i * 8, i * 8 + 8)
            for t in range(2):
                for x in (own, own_y, beside, beside_y):
                    x[at, t, s] = zero
            strip[at, 0, s] = zero
            strip_y[at, 0, s] = zero
        return carry

    lax.fori_loop(0, 2, clear, 0)

    def begin(z, carry):
        at = z + 1
        for i in range(8):
            s = slice(i * 8, i * 8 + 8)
            tiles = tiles_of((low_ref, block_ref, high_ref), field_start, (left_ref, right_ref), 0, z, i)
            inner = 1 <= i < 7
            for t in range(2):
                guess = tiles[t] * (1.0 / theta)
                value = guess if t == 0 and 2 <= i < 6 else guess * own_m[t, s]
                own[at, t, s] = value
                own_y[at, t, s] = zero
                if inner:
                    wide_r[z, t, s] = tiles[t]
                beside_y[at, t, s] = zero
                beside[at, t, s] = zero if i in (3, 4) else guess * beside_m[t, s]
            strip[at, 0, s] = tiles[2] * (strip_m[s] * (1.0 / theta))
            strip_y[at, 0, s] = zero
            if inner:
                strip_r[z, 0, s] = tiles[2]
                tiles = tiles_of((low_c, absorption_ref, high_c), coef_start, (left_c, right_c), coef_at, z, i)
                diag[z, 0, s] = tiles[0] + base
                diag[z, 1, s] = tiles[1] + base
                strip_diag[z, 0, s] = tiles[2] + base
        return carry

    lax.fori_loop(0, LEVELS, begin, 0, unroll=UNROLL_BEGIN)
    at_first, at_last = lane == 0, lane == COLS - 1

    def step(here, x, y, r, a, mask, width, i, keep, scale):
        s = slice(i * 8, i * 8 + 8)
        up, down = slice(i * 8 - 1, i * 8 + 7), slice(i * 8 + 1, i * 8 + 9)
        z = here - 1
        now = [x[here, t, s] for t in range(width)]
        back = [roll(v, 1) for v in now]
        fore = [roll(v, -1) for v in now]
        if width == 2:
            back = [jnp.where(at_first, back[1], back[0]), jnp.where(at_first, back[0], back[1])]
            fore = [jnp.where(at_last, fore[1], fore[0]), jnp.where(at_last, fore[0], fore[1])]
        for t in range(width):
            high = x[here - 1, t, s] + x[here + 1, t, s]
            around = (x[here, t, up] + x[here, t, down]) + (back[t] + fore[t])
            around = around + (high + high)
            defect = (r[z, t, s] + around) - a[z, t, s] * now[t]
            move = keep * (now[t] - y[here, t, s]) + scale * defect
            after = now[t] + move
            if mask[t] is not None:
                after = after * mask[t]
            y[here, t, s] = after

    first = ((own, own_y), (beside, beside_y), (strip, strip_y))
    second = tuple((y, x) for x, y in first)

    def sweep(n, arrays):
        keep, scale = table_ref[0, n], table_ref[1, n]
        own, beside, strip = arrays

        def level(z, carry):
            here = z + 1
            for i in range(1, 7):
                s = slice(i * 8, i * 8 + 8)
                free = None if 2 <= i < 6 else own_m[0, s]
                step(here, *own, wide_r, diag, [free, own_m[1, s]], 2, i, keep, scale)
                if i in BESIDE_TILES:
                    step(here, *beside, wide_r, diag, [beside_m[0, s], beside_m[1, s]], 2, i, keep, scale)
                step(here, *strip, strip_r, strip_diag, [strip_m[s]], 1, i, keep, scale)
            return carry

        lax.fori_loop(0, LEVELS, level, 0, unroll=UNROLL)

    def pair(n, carry):
        sweep(2 * n, first)
        sweep(2 * n + 1, second)
        return carry

    lax.fori_loop(0, (KCHEB - 1) // 2, pair, 0)
    near_first, near_last = lane < EDGE, lane >= COLS - EDGE

    def finish(z, carry):
        at = z + 1
        for i in range(1, 7):
            s = slice(i * 8, i * 8 + 8)
            out = slice(i * 8 - 8, i * 8)
            value = strip[at, 0, s]
            at_left = value + roll(value, -32)
            at_right = roll(at_left, 64)
            first = jnp.where(near_first, at_left, jnp.where(near_last, at_right, 0.0))
            second = jnp.where(near_last, at_left, jnp.where(near_first, at_right, 0.0))
            first = first + own[at, 0, s]
            second = second + own[at, 1, s]
            if i in BESIDE_TILES:
                first = first + beside[at, 0, s]
                second = second + beside[at, 1, s]
            out_ref[z, out, lanes[0]] = first
            out_ref[z, out, lanes[1]] = second
        return carry

    lax.fori_loop(0, LEVELS, finish, 0, unroll=UNROLL_FINISH)


def smooth(place, table, told, block, low, high, strips, absorption, coefficient=None):
    wide = (2, TALL, COLS)
    thin = (1, TALL, COLS)

    def scratch(*shape):
        return pltpu.VMEM(shape, jnp.float32)

    more = () if coefficient is None else coefficient
    specs = [SMEM_SPEC] * 2 + [VMEM_SPEC] * 2 + [VMEM_SPEC if more else FIELDS_SPEC] * 2 + [VMEM_SPEC] * 3
    if more:
        specs += [FIELDS_SPEC] * 2 + [VMEM_SPEC] * 2
    return pl.pallas_call(
        functools.partial(smooth_kernel, not more),
        grid=(1,),
        in_specs=specs,
        out_shape=jax.ShapeDtypeStruct((LEVELS, INNER, 2 * COLS), jnp.float32),
        scratch_shapes=[
            scratch(*wide), scratch(*wide), scratch(TALL, COLS),
            scratch(PLANES, *wide), scratch(PLANES, *wide), scratch(PLANES, *thin),
            scratch(PLANES, *wide), scratch(PLANES, *wide), scratch(PLANES, *thin),
            scratch(LEVELS, *wide), scratch(LEVELS, *thin),
            scratch(LEVELS, *wide), scratch(LEVELS, *thin),
        ],
        compiler_params=pltpu.CompilerParams(vmem_limit_bytes=VMEM_LIMIT),
        cost_estimate=pl.CostEstimate(flops=60000000, bytes_accessed=4000000, transcendentals=0),
        name="smoother",
    )(place, table, told, block, low, high, *strips, absorption, *more)


INNER = ROWS + 16


def slots_of(place, told_ref, moves):
    lane = iota((1, COLS), 1)
    slots = jnp.zeros((1, COLS), jnp.float32)
    for n, (down, right) in enumerate(moves):
        row = roll(told_ref[pl.ds(place.index(down, right), 1), :], VECTORS * (n - 1))
        slots = jnp.where((lane >> 5) == n, row, slots)
    return slots.astype(jnp.int32)


def coarse_at(coarse_turned, slots):
    pick = jnp.where(iota((COLS, COLS), 0) == (slots >> 5), 1.0, 0.0)
    found = jnp.dot(coarse_turned, pick, precision=HIGHEST, preferred_element_type=jnp.float32)
    found = jnp.where(iota((VECTORS, COLS), 0) == (slots & 31), found, 0.0)
    return jnp.sum(found, axis=0, keepdims=True)


def add_coarse(place, told_ref, coarse_ref, basis_hbm, basis_ref, sems, low_ref, high_ref, left_ref, right_ref, at, sum_ref, x,
               own_c, edge_c, ring_ref, side_ref):
    def part(q):
        levels = pl.ds(q * 4, 4)
        return pltpu.make_async_copy(basis_hbm.at[:, levels], basis_ref.at[:, levels], sems.at[q])

    for q in range(LEVELS // 4):
        part(q).start()
    turned = coarse_ref[...].T[:VECTORS]
    row = coarse_at(turned, slots_of(place, told_ref, ((0, 0), (-1, 0), (1, 0), (0, -1))))
    other = coarse_at(turned, slots_of(place, told_ref, ((0, 1),)))
    lane = iota((8, COLS), 1)
    lane_row = iota((1, COLS), 1)
    column = jnp.broadcast_to(row, (COLS, COLS)).T
    own_c[...] = column[:VECTORS]
    edge_c[...] = column[VECTORS : 3 * VECTORS]
    for n, edge in ((0, low_ref), (1, high_ref)):

        def vector(k, total):
            return total + edge[2 * LEVELS + k] * edge_c[pl.ds(n * VECTORS + k, 1), :]

        ring_ref[n] = lax.fori_loop(0, VECTORS, vector, jnp.zeros((LEVELS, COLS), jnp.float32))
    which = iota((COLS, COLS), 0) >> 5
    for n, (edge, values) in enumerate(((left_ref, roll(row, VECTORS)), (right_ref, other))):
        values = jnp.where(lane_row < VECTORS, values, 0.0)
        values = values + roll(values, 32) + roll(values, 64) + roll(values, 96)
        weights = jnp.broadcast_to(values, (COLS, COLS)).T
        weights = jnp.where(iota((COLS, COLS), 1) == which, weights, 0.0)
        parts = edge[at : at + 2].reshape(2 * TALL, COLS)
        side_ref[n] = jnp.dot(parts, weights, precision=HIGHEST, preferred_element_type=jnp.float32)

    def level(z, carry):
        total = sum_ref[z, 8 : 8 + ROWS, 0:COLS]
        for k in range(VECTORS):
            total = total + basis_ref[k, z].astype(jnp.float32) * own_c[k : k + 1]
        here = z + 1
        x[here, 8 : 8 + ROWS, 0:COLS] = total
        rows = pl.ds(z, 1)
        x[here, 7:8, 0:COLS] = sum_ref[z, 7:8, 0:COLS] + ring_ref[0, rows, :]
        x[here, 8 + ROWS : 9 + ROWS, 0:COLS] = sum_ref[z, 8 + ROWS : 9 + ROWS, 0:COLS] + ring_ref[1, rows, :]
        q = z & 3
        for i in range(ROWS // 8):
            s = pl.ds(pl.multiple_of((z >> 2) * ROWS + i * 8, 8), 8)
            left = pltpu.roll(side_ref[0, s, :], (COLS - 1) - q, 1)
            right = pltpu.roll(side_ref[1, s, :], (COLS - q) & (COLS - 1), 1)
            t = slice(8 + i * 8, 16 + i * 8)
            value = jnp.where(lane == COLS - 1, left, jnp.where(lane == 0, right, 0.0))
            x[here, t, COLS : 2 * COLS] = sum_ref[z, t, COLS : 2 * COLS] + value
        return carry

    def levels(q, carry):
        part(q).wait()
        return lax.fori_loop(4 * q, 4 * q + 4, level, carry)

    lax.fori_loop(0, LEVELS // 4, levels, 0)
    zero = jnp.zeros((ROWS, COLS), jnp.float32)
    x[0, 8 : 8 + ROWS, 0:COLS] = zero
    x[PLANES - 1, 8 : 8 + ROWS, 0:COLS] = zero
    return row


def image_at(x, absorption_ref, z, i):
    lane = iota((8, COLS), 1)
    here = z + 1
    s = slice(8 + i * 8, 16 + i * 8)
    up, down = slice(7 + i * 8, 15 + i * 8), slice(9 + i * 8, 17 + i * 8)
    now = x[here, s, 0:COLS]
    margin = x[here, s, COLS : 2 * COLS]
    back = jnp.where(lane == 0, roll(margin, 1), roll(now, 1))
    fore = jnp.where(lane == COLS - 1, roll(margin, -1), roll(now, -1))
    high = x[here - 1, s, 0:COLS] + x[here + 1, s, 0:COLS]
    around = (x[here, up, 0:COLS] + x[here, down, 0:COLS]) + (back + fore)
    diagonal = absorption_ref[z, i * 8 : i * 8 + 8, :] + (4.0 + 2.0 * vertical)
    return now, diagonal * now - around - vertical * high


def total_of(value):
    return jnp.sum(jnp.sum(value, axis=0, keepdims=True), axis=1, keepdims=True)


def scalars(told_ref):
    totals = jnp.sum(told_ref[...], axis=0, keepdims=True)
    return totals[:, 64:65], totals[:, 65:66]


def first_coarse_kernel(
    place_ref, told_ref, coarse_ref, basis_hbm, low_ref, high_ref, left_ref, right_ref, sum_ref, source_ref, absorption_ref,
    direction_ref, image_ref, ahead_ref, behind_ref, out_ref, x, own_c, edge_c, ring_ref, side_ref, basis_ref, sems, sums_ref,
):
    place = Place(place_ref, told_ref)
    row = add_coarse(place, told_ref, coarse_ref, basis_hbm, basis_ref, sems, low_ref, high_ref, left_ref, right_ref, 4, sum_ref, x,
                     own_c, edge_c, ring_ref, side_ref)
    zero = jnp.zeros((8, COLS), jnp.float32)

    def images(z, carry):
        weight, curve = carry
        for i in range(ROWS // 8):
            s = slice(i * 8, i * 8 + 8)
            now, image = image_at(x, absorption_ref, z, i)
            direction_ref[z, s] = now
            image_ref[z, s] = image
            if i >= 2:
                ahead_ref[z, (i - 2) * 8 : (i - 1) * 8] = image
            else:
                behind_ref[z, s] = image
            weight = weight + source_ref[z, s] * sum_ref[z, 8 + i * 8 : 16 + i * 8, 0:COLS]
            curve = curve + now * image
        return weight, curve

    weight, curve = lax.fori_loop(0, LEVELS, images, (zero, zero))
    half = VECTORS // 2
    for part in range(2):

        def level(z, sums):
            image = image_ref[z]
            return tuple(
                sums[k] + fold_rows(basis_ref[part * half + k, z].astype(jnp.float32) * image) for k in range(half)
            )

        sums = lax.fori_loop(0, LEVELS, level, (zero,) * half)
        for k in range(half):
            sums_ref[part * half + k : part * half + k + 1] = jnp.sum(sums[k], axis=0, keepdims=True)
    lane = iota((1, COLS), 1)
    row = jnp.where(lane < VECTORS, row, 0.0)
    mine = told_ref[pl.ds(place.index(0, 0), 1), :]
    told = roll(row, VECTORS)
    told = told + jnp.where(lane == 64, total_of(weight) + total_of(row * mine), 0.0)
    told = told + jnp.where(lane == 65, total_of(curve), 0.0)
    out_ref[...] = row_of_sums(sums_ref[...]) + told


def second_coarse_kernel(
    place_ref, told_ref, coarse_ref, basis_hbm, low_ref, high_ref, left_ref, right_ref, sum_ref, source_ref, absorption_ref,
    again_ref, first_sum_ref, direction_ref, first_ref,
    residual_ref, precond_ref, image_ref, out_ref, x, own_c, edge_c, ring_ref, side_ref, basis_ref, sems,
):
    place = Place(place_ref, told_ref)
    row = add_coarse(place, told_ref, coarse_ref, basis_hbm, basis_ref, sems, low_ref, high_ref, left_ref, right_ref, 4, sum_ref, x,
                     own_c, edge_c, ring_ref, side_ref)
    weight0, curve0 = scalars(again_ref)
    step = weight0 / curve0
    zero = jnp.zeros((8, COLS), jnp.float32)

    def images(z, sums):
        weight, own, cross = sums
        for i in range(ROWS // 8):
            s = slice(i * 8, i * 8 + 8)
            t = slice(8 + i * 8, 16 + i * 8)
            now, image = image_at(x, absorption_ref, z, i)
            direction, first = direction_ref[z, s], first_ref[z, s]
            residual = source_ref[z, s] - step * first
            precond = direction - step * now
            image = first - step * image
            residual_ref[z, s] = residual
            precond_ref[z, s] = precond
            image_ref[z, s] = image
            weight = weight + residual * (first_sum_ref[z, t, 0:COLS] - step * sum_ref[z, t, 0:COLS])
            own = own + precond * image
            cross = cross + (precond * first + direction * image)
        return weight, own, cross

    weight, own, cross = lax.fori_loop(0, LEVELS, images, (zero, zero, zero))
    mine = pl.ds(place.index(0, 0), 1)
    lane = iota((1, COLS), 1)
    again = again_ref[mine, :]
    projected = told_ref[mine, :] - step * again
    coarse = roll(again, -VECTORS) - step * row
    both = jnp.where(lane < VECTORS, projected * coarse, 0.0)
    told = jnp.where(lane == 0, total_of(weight) + total_of(both), 0.0)
    told = told + jnp.where(lane == 1, total_of(own), 0.0) + jnp.where(lane == 2, total_of(cross), 0.0)
    out_ref[...] = jnp.broadcast_to(told, (COLS, COLS))


def last_kernel(again_ref, last_ref, direction_ref, first_ref, residual_ref, precond_ref, image_ref, x_ref, r_ref):
    weight0, curve0 = scalars(again_ref)
    step0 = weight0 / curve0
    totals = jnp.sum(last_ref[...], axis=0, keepdims=True)
    weight1, own, cross = totals[:, 0:1], totals[:, 1:2], totals[:, 2:3]
    ratio = weight1 / weight0
    step1 = weight1 / (own + ratio * (cross + ratio * curve0))

    def level(z, carry):
        direction = direction_ref[z]
        x_ref[z] = step0 * direction + step1 * (precond_ref[z] + ratio * direction)
        r_ref[z] = residual_ref[z] - step1 * (image_ref[z] + ratio * first_ref[z])
        return carry

    lax.fori_loop(0, LEVELS, level, 0)


def shards(source, absorption, basis, coarse_inverse, margin_width, coarse_slot):
    block = jax.ShapeDtypeStruct((LEVELS, ROWS, COLS), jnp.float32)
    slab = jax.ShapeDtypeStruct((LEVELS, EDGE, COLS), jnp.float32)
    message = jax.ShapeDtypeStruct((COLS, COLS), jnp.float32)
    params = pltpu.CompilerParams(vmem_limit_bytes=VMEM_LIMIT)
    hbm = pl.BlockSpec(memory_space=pltpu.HBM)

    def scratch(*shape):
        return pltpu.VMEM(shape, jnp.float32)

    coarse_scratch = [
        scratch(PLANES, INNER, 2 * COLS), scratch(VECTORS, COLS), scratch(2 * VECTORS, COLS),
        scratch(2, LEVELS, COLS), scratch(2, 2 * TALL, COLS),
        pltpu.VMEM(basis.shape, basis.dtype), pltpu.SemaphoreType.DMA((LEVELS // 4,)),
    ]
    place = jnp.stack(
        [lax.axis_index("gx"), lax.axis_index("gy"), lax.axis_size("gx"), lax.axis_size("gy")]
    ).astype(jnp.int32)
    table = jnp.array(list(zip(*chebyshev_table())), jnp.float32)
    rows, ahead, behind, left_edge, right_edge = first_projection(
        source, absorption, basis, coarse_slot, margin_width
    )
    low, high = exchange(ahead, behind, "gx")
    told = everyone(rows)
    fields = [VMEM_SPEC] * 2 + [FIELDS_SPEC] * 2 + [VMEM_SPEC] * 2
    strips = exchange(
        *pack(first_pack_kernel, fields, 6, source, absorption, low, high, left_edge, right_edge), "gy"
    )
    coarse = everyone(solve_rows(told, told, coarse_inverse))
    first_sum = smooth(place, table, told, source, low, high, strips, absorption)
    edges = (low, high, *strips)
    direction, image, ahead, behind, rows = pl.pallas_call(
        first_coarse_kernel,
        in_specs=[SMEM_SPEC] + [VMEM_SPEC] * 2 + [hbm] + [VMEM_SPEC] * 7,
        out_shape=[block, block, slab, slab, message],
        scratch_shapes=coarse_scratch + [scratch(VECTORS, COLS)],
        compiler_params=params,
        name="direction_and_image",
    )(place, told, coarse, basis, *edges, first_sum, source, absorption)
    low_w, high_w = exchange(ahead, behind, "gx")
    again = everyone(rows)
    strips_w = exchange(*pack(pack_kernel, [VMEM_SPEC] * 3, 2, image, low_w, high_w), "gy")
    coarse = everyone(solve_rows(again, told, coarse_inverse))
    second_sum = smooth(place, table, told, image, low_w, high_w, strips_w, absorption, edges)
    residual, precond, precond_image, rows = pl.pallas_call(
        second_coarse_kernel,
        in_specs=[SMEM_SPEC] + [VMEM_SPEC] * 2 + [hbm] + [VMEM_SPEC] * 11,
        out_shape=[block, block, block, message],
        scratch_shapes=coarse_scratch,
        compiler_params=params,
        name="second_images",
    )(place, told, coarse, basis, *edges, second_sum, source, absorption, again, first_sum, direction, image)
    last = everyone(rows)
    concentration, residual = pl.pallas_call(
        last_kernel, out_shape=[block, block], compiler_params=params, name="update"
    )(again, last, direction, image, residual, precond, precond_image)
    return (concentration, residual)


def solution(mesh):
    return jax.shard_map(
        shards,
        mesh=mesh,
        in_specs=(
            P(None, "gx", "gy"),
            P(None, "gx", "gy"),
            P(None, None, "gx", "gy"),
            P(("gx", "gy"), None),
            P("gx", "gy"),
            P("gx", "gy", None),
        ),
        out_specs=(P(None, "gx", "gy"), P(None, "gx", "gy")),
        check_vma=False,
    )
```

```python
import functools

import jax
import jax.numpy as jnp
from jax import lax
from jax.experimental import pallas as pl
from jax.experimental.pallas import tpu as pltpu
from jax.sharding import PartitionSpec as P

KCHEB = 9
AXES = ("gx", "gy")
LEVELS = 16
ROWS = 32
COLS = 128
VECTORS = 32
EDGE = 16
TALL = ROWS + 2 * EDGE
HIGHEST = lax.Precision.HIGHEST

lowest_rate = 0.05
highest_rate = 18.5
vertical = 2.0
theta = 0.5 * (highest_rate + lowest_rate)
delta = 0.5 * (highest_rate - lowest_rate)
VMEM_LIMIT = 24 * 1024 * 1024
FIRST_LIMIT = 58 * 1024 * 1024


def chebyshev_table():
    ratio = theta / delta
    rho_old = 1.0 / ratio
    table = []
    for _ in range(KCHEB - 1):
        rho_new = 1.0 / (2.0 * ratio - rho_old)
        table.append((rho_new * rho_old, 2.0 * rho_new / delta))
        rho_old = rho_new
    return table


def iota(shape, dim):
    return lax.broadcasted_iota(jnp.int32, shape, dim)


def roll(value, shift):
    return pltpu.roll(value, shift % COLS, 1)


def exchange(forward_value, backward_value, axis):
    count = lax.axis_size(axis)
    forward = [(i, i + 1) for i in range(count - 1)]
    backward = [(target, source) for source, target in forward]
    return lax.ppermute(forward_value, axis, forward), lax.ppermute(backward_value, axis, backward)


def everyone(rows):
    return lax.all_to_all(rows, AXES, 0, 0, tiled=True)


def row_of_sums(sums):
    padded = jnp.concatenate([sums, jnp.zeros((COLS - VECTORS, COLS), jnp.float32)], 0)
    ones = jnp.ones((COLS, COLS), jnp.float32)
    return lax.dot_general(
        ones, padded, (((1,), (1,)), ((), ())), precision=HIGHEST, preferred_element_type=jnp.float32
    )


def fold_rows(product):
    return (product[0:8] + product[8:16]) + (product[16:24] + product[24:32])


def first_kernel(
    field_ref, coefficient_ref, basis_ref, slots_ref, margin_ref,
    out_ref, ahead_ref, behind_ref, sides_ref, sums_ref, edges_ref,
):
    step = pl.program_id(0)
    group = basis_ref.shape[0]

    @pl.when(step == 0)
    def _():
        edges_ref[...] = jnp.zeros_like(edges_ref)

        def level(z, carry):
            ahead_ref[z] = field_ref[z, ROWS - EDGE :, :]
            behind_ref[z] = field_ref[z, :EDGE, :]
            ahead_ref[LEVELS + z] = coefficient_ref[z, ROWS - EDGE :, :]
            behind_ref[LEVELS + z] = coefficient_ref[z, :EDGE, :]
            return carry

        lax.fori_loop(0, LEVELS, level, 0)

    def level(z, sums):
        field = field_ref[z]
        new = []
        for j in range(group):
            values = basis_ref[j, z].astype(jnp.float32)
            new.append(sums[j] + fold_rows(values * field))
            at = 2 * LEVELS + step * group + j
            behind_ref[at, pl.ds(z, 1), :] = values[0:1]
            ahead_ref[at, pl.ds(z, 1), :] = values[ROWS - 1 : ROWS]
        return tuple(new)

    zero = jnp.zeros((8, COLS), jnp.float32)
    sums = lax.fori_loop(0, LEVELS, level, (zero,) * group, unroll=2)
    for j in range(group):
        sums_ref[pl.ds(step * group + j, 1), :] = jnp.sum(sums[j], axis=0, keepdims=True)
    from_lane, to_lane = iota((COLS, COLS), 0), iota((COLS, COLS), 1)
    picks = []
    for j in range(group):
        k = step * group + j
        pick = ((from_lane == 0) & (to_lane == k)) | ((from_lane == COLS - 1) & (to_lane == VECTORS + k))
        picks.append(jnp.where(pick, 1.0, 0.0).astype(jnp.bfloat16))
    values = jnp.concatenate([basis_ref[j].reshape(LEVELS * ROWS, COLS) for j in range(group)], axis=1)
    edges_ref[...] += jnp.dot(values, jnp.concatenate(picks, 0), preferred_element_type=jnp.float32)

    @pl.when(step == pl.num_programs(0) - 1)
    def _():
        told = jnp.concatenate(
            [
                jnp.zeros((1, VECTORS), jnp.float32),
                slots_ref[0].astype(jnp.float32),
                margin_ref[...].astype(jnp.float32),
                jnp.zeros((1, COLS - 65), jnp.float32),
            ],
            axis=1,
        )
        out_ref[...] = row_of_sums(sums_ref[...]) + told
        place = iota((ROWS, COLS), 1) >> 5
        for n in range(LEVELS // 4):
            left = jnp.zeros((ROWS, COLS), jnp.float32)
            right = left
            for q in range(4):
                z = 4 * n + q
                value = edges_ref[z * ROWS : (z + 1) * ROWS]
                left = jnp.where(place == q, roll(value, VECTORS * q), left)
                right = jnp.where(place == q, roll(value, VECTORS * (q - 1)), right)
            sides_ref[n] = left
            sides_ref[LEVELS // 4 + n] = right


def first_projection(field, coefficient, basis, slots, margin):
    group = 8
    rows = 2 * LEVELS + VECTORS
    edge_rows = jax.ShapeDtypeStruct((rows, LEVELS, COLS), jnp.float32)
    edge_cols = jax.ShapeDtypeStruct((LEVELS // 2, ROWS, COLS), jnp.float32)
    block_spec = pl.BlockSpec((LEVELS, ROWS, COLS), lambda i: (0, 0, 0))
    rows_spec = pl.BlockSpec(edge_rows.shape, lambda i: (0, 0, 0))
    cols_spec = pl.BlockSpec(edge_cols.shape, lambda i: (0, 0, 0))
    return pl.pallas_call(
        first_kernel,
        grid=(VECTORS // group,),
        in_specs=[
            block_spec,
            block_spec,
            pl.BlockSpec((group, LEVELS, ROWS, COLS), lambda i: (i, 0, 0, 0)),
            pl.BlockSpec(slots.shape, lambda i: (0, 0, 0)),
            pl.BlockSpec(margin.shape, lambda i: (0, 0)),
        ],
        out_specs=[pl.BlockSpec((COLS, COLS), lambda i: (0, 0)), rows_spec, rows_spec, cols_spec],
        out_shape=[jax.ShapeDtypeStruct((COLS, COLS), jnp.float32), edge_rows, edge_rows, edge_cols],
        scratch_shapes=[
            pltpu.VMEM((VECTORS, COLS), jnp.float32), pltpu.VMEM((LEVELS * ROWS, COLS), jnp.float32)
        ],
        compiler_params=pltpu.CompilerParams(vmem_limit_bytes=FIRST_LIMIT),
        name="first_projection",
    )(field, coefficient, basis, slots, margin)


def coarse_rows(told_ref, slots_ref, inverse_ref, out_ref):
    told = told_ref[...]
    slots = slots_ref[...]
    turned = told.T
    slots_turned = slots.T
    lane = iota((COLS, COLS), 1)
    sub = iota((VECTORS, COLS), 0)
    placed = jnp.zeros((3 * VECTORS, COLS), jnp.float32)
    for k in range(VECTORS):
        slot_column = slots[:, VECTORS + k : VECTORS + k + 1].astype(jnp.int32)
        ones = jnp.where((slot_column & 127) == lane, 1.0, 0.0).astype(jnp.bfloat16)
        slot_row = slots_turned[VECTORS + k : VECTORS + k + 1, :].astype(jnp.int32)
        values = turned[k : k + 1, :]
        spread = jnp.where((slot_row >> 7) == sub, values, 0.0)
        first = spread.astype(jnp.bfloat16)
        rest = spread - first.astype(jnp.float32)
        second = rest.astype(jnp.bfloat16)
        third = (rest - second.astype(jnp.float32)).astype(jnp.bfloat16)
        parts = jnp.concatenate([first, second, third], 0)
        placed = placed + jnp.dot(parts, ones, preferred_element_type=jnp.float32)
    placed = placed[:VECTORS] + placed[VECTORS : 2 * VECTORS] + placed[2 * VECTORS :]
    total = jnp.zeros((VECTORS, COLS), jnp.float32)
    for high in range(VECTORS):
        total = total + inverse_ref[:, high * COLS : (high + 1) * COLS] * placed[high : high + 1]
    out_ref[...] = row_of_sums(total)


def pack_strips(parts, forward_ref, backward_ref, at):
    def levels(group, carry):
        row = 0
        for part, start in parts:
            height = EDGE if part.shape[1] == EDGE else ROWS
            lane = iota((height, COLS), 1)
            ahead = jnp.zeros((height, COLS), jnp.float32)
            behind = ahead
            for j in range(8):
                value = part[start + group * 8 + j]
                mine = (lane >= EDGE * j) & (lane < EDGE * (j + 1))
                ahead = jnp.where(mine, roll(value, EDGE * j - (COLS - EDGE)), ahead)
                behind = jnp.where(mine, roll(value, EDGE * j), behind)
            forward_ref[at + group, row : row + height, :] = ahead
            backward_ref[at + group, row : row + height, :] = behind
            row += height
        return carry

    lax.fori_loop(0, LEVELS // 8, levels, 0)


def first_pack_kernel(
    told_ref, source_ref, absorption_ref, low_ref, high_ref, sides_ref, forward_ref, backward_ref
):
    for f, block in enumerate((source_ref, absorption_ref)):
        pack_strips(((low_ref, LEVELS * f), (block, 0), (high_ref, LEVELS * f)), forward_ref, backward_ref, 2 * f)
    for n in range(LEVELS // 8):
        for half in range(2):
            rows = slice(half * ROWS, (half + 1) * ROWS)
            forward_ref[4 + n, rows, :] = sides_ref[LEVELS // 4 + 2 * n + half]
            backward_ref[4 + n, rows, :] = sides_ref[2 * n + half]


def pack_kernel(block_ref, low_ref, high_ref, forward_ref, backward_ref):
    pack_strips(((low_ref, 0), (block_ref, 0), (high_ref, 0)), forward_ref, backward_ref, 0)


FIELDS_SPEC = pl.BlockSpec((2 * LEVELS, EDGE, COLS), lambda i: (0, 0, 0))
VMEM_SPEC = pl.BlockSpec(memory_space=pltpu.VMEM)
SMEM_SPEC = pl.BlockSpec(memory_space=pltpu.SMEM)


def pack(kernel, specs, strips, *operands):
    strips = jax.ShapeDtypeStruct((strips, TALL, COLS), jnp.float32)
    return pl.pallas_call(
        kernel,
        grid=(1,),
        in_specs=specs,
        out_shape=[strips, strips],
        compiler_params=pltpu.CompilerParams(vmem_limit_bytes=VMEM_LIMIT),
        cost_estimate=pl.CostEstimate(flops=2000000, bytes_accessed=2000000, transcendentals=0),
        name="strips",
    )(*operands)


def solve_rows(*operands):
    return pl.pallas_call(
        coarse_rows,
        out_shape=jax.ShapeDtypeStruct((COLS, COLS), jnp.float32),
        compiler_params=pltpu.CompilerParams(vmem_limit_bytes=VMEM_LIMIT),
        name="coarse_rows",
    )(*operands)


class Place:
    def __init__(self, place_ref, told_ref):
        self.row = place_ref[0]
        self.col = place_ref[1]
        self.rows = place_ref[2]
        self.cols = place_ref[3]
        self.told_ref = told_ref

    def index(self, down, right):
        row = jnp.clip(self.row + down, 0, self.rows - 1)
        col = jnp.clip(self.col + right, 0, self.cols - 1)
        return row * self.cols + col

    def margin(self, down, right):
        row, col = self.row + down, self.col + right
        real = (row >= 0) & (row < self.rows) & (col >= 0) & (col < self.cols)
        margin = self.told_ref[pl.ds(self.index(down, right), 1), :][:, 64:65]
        return jnp.where(real, margin.astype(jnp.int32), -4096)


def masks(place, own_ref, beside_ref, strip_ref):
    shape = (TALL, COLS)
    row = iota(shape, 0) - EDGE
    lane = iota(shape, 1)
    top, bottom = -ROWS * place.row, ROWS * (place.rows - place.row)
    first, last = -COLS * place.col, COLS * (place.cols - place.col)
    row_real = (row >= top) & (row < bottom)
    m = {(i, j): place.margin(i, j) for i in (-1, 0, 1) for j in (-1, 0, 1)}
    upper, lower = row < 8, row >= ROWS - 8
    for tile in range(2):
        col = lane if tile == 0 else jnp.where(lane < 64, lane + COLS, lane - COLS)
        real = row_real & (col >= first) & (col < last)
        if tile == 1:
            real = real & ((lane < EDGE) | (lane >= COLS - EDGE))

        def across(margin):
            return (col >= -margin) & (col < COLS + margin)

        own = m[0, 0]
        inside = real & (row >= -own) & (row < ROWS + own) & across(own)
        own_ref[tile] = jnp.where(inside, 1.0, 0.0)
        above, below = m[-1, 0], m[1, 0]
        inside = (upper & (row < above) & across(above)) | (lower & (row >= ROWS - below) & across(below))
        beside_ref[tile] = jnp.where(real & inside, 1.0, 0.0)
    group = ((lane + EDGE) & 127) >> 5
    away = ((lane + EDGE) & 31) - EDGE
    inside = row < -4096
    for place_of, side in ((0, -1), (2, 1)):
        col = away if side < 0 else away + COLS
        real = row_real & (col >= first) & (col < last)

        def reached(margin):
            return (away < margin) if side < 0 else (away >= -margin)

        level = m[0, side]
        inside = inside | (
            (group == place_of) & real & (row >= -level) & (row < ROWS + level) & reached(level)
        )
        above, below = m[-1, side], m[1, side]
        corner = (upper & (row < above) & reached(above)) | (
            lower & (row >= ROWS - below) & reached(below)
        )
        inside = inside | ((group == place_of + 1) & real & corner)
    strip_ref[...] = jnp.where(inside, 1.0, 0.0)


def tiles_of(parts, start, strips, at, z, i):
    low, block, high = parts
    from_left, from_right = strips
    lane = iota((8, COLS), 1)
    if i < 2:
        center = low[start + z, i * 8 : i * 8 + 8, :]
    elif i < 6:
        center = block[z, (i - 2) * 8 : (i - 2) * 8 + 8, :]
    else:
        center = high[start + z, (i - 6) * 8 : (i - 6) * 8 + 8, :]
    s = slice(i * 8, i * 8 + 8)
    group, shift = at + (z >> 3), EDGE * (z & 7)
    left = pltpu.roll(from_left[group, s, :], (COLS - EDGE) - shift, 1)
    right = pltpu.roll(from_right[group, s, :], (COLS - shift) & (COLS - 1), 1)
    margin = jnp.where(lane >= COLS - EDGE, left, jnp.where(lane < EDGE, right, 0.0))
    at_left = jnp.where(lane >= 64, margin, center)
    at_right = jnp.where(lane < 64, margin, center)
    near = (lane < EDGE) | (lane >= COLS - EDGE)
    others = jnp.where(lane < 80, roll(at_right, 64), roll(at_right, 96))
    packed = jnp.where(near, at_left, jnp.where(lane < 48, roll(at_left, 32), others))
    return center, margin, packed


UNROLL = 8
UNROLL_BEGIN = 2
UNROLL_FINISH = 2
PLANES = LEVELS + 2
BESIDE_TILES = (1, 2, 5, 6)


def smooth_kernel(same, place_ref, table_ref, told_ref, block_ref, low_ref, high_ref, left_ref, right_ref, absorption_ref, *refs):
    if same:
        low_c, high_c, left_c, right_c = low_ref, high_ref, left_ref, right_ref
    else:
        low_c, high_c, left_c, right_c = refs[:4]
        refs = refs[4:]
    (
        out_ref, own_m, beside_m, strip_m, own, beside, strip, own_y, beside_y, strip_y,
        wide_r, strip_r, diag, strip_diag,
    ) = refs
    field_start, coef_start, coef_at = 0, LEVELS, 2
    masks(Place(place_ref, told_ref), own_m, beside_m, strip_m)
    base = 4.0 + 2.0 * vertical
    zero = jnp.zeros((8, COLS), jnp.float32)
    lane = iota((8, COLS), 1)
    lanes = [slice(0, COLS), slice(COLS, 2 * COLS)]

    def clear(n, carry):
        at = n * (PLANES - 1)
        for i in range(8):
            s = slice(i * 8, i * 8 + 8)
            for t in range(2):
                for x in (own, own_y, beside, beside_y):
                    x[at, t, s] = zero
            strip[at, 0, s] = zero
            strip_y[at, 0, s] = zero
        return carry

    lax.fori_loop(0, 2, clear, 0)

    def begin(z, carry):
        at = z + 1
        for i in range(8):
            s = slice(i * 8, i * 8 + 8)
            tiles = tiles_of((low_ref, block_ref, high_ref), field_start, (left_ref, right_ref), 0, z, i)
            inner = 1 <= i < 7
            for t in range(2):
                guess = tiles[t] * (1.0 / theta)
                value = guess if t == 0 and 2 <= i < 6 else guess * own_m[t, s]
                own[at, t, s] = value
                own_y[at, t, s] = zero
                if inner:
                    wide_r[z, t, s] = tiles[t]
                beside_y[at, t, s] = zero
                beside[at, t, s] = zero if i in (3, 4) else guess * beside_m[t, s]
            strip[at, 0, s] = tiles[2] * (strip_m[s] * (1.0 / theta))
            strip_y[at, 0, s] = zero
            if inner:
                strip_r[z, 0, s] = tiles[2]
                tiles = tiles_of((low_c, absorption_ref, high_c), coef_start, (left_c, right_c), coef_at, z, i)
                diag[z, 0, s] = tiles[0] + base
                diag[z, 1, s] = tiles[1] + base
                strip_diag[z, 0, s] = tiles[2] + base
        return carry

    lax.fori_loop(0, LEVELS, begin, 0, unroll=UNROLL_BEGIN)
    at_first, at_last = lane == 0, lane == COLS - 1

    def step(here, x, y, r, a, mask, width, i, keep, scale):
        s = slice(i * 8, i * 8 + 8)
        up, down = slice(i * 8 - 1, i * 8 + 7), slice(i * 8 + 1, i * 8 + 9)
        z = here - 1
        now = [x[here, t, s] for t in range(width)]
        back = [roll(v, 1) for v in now]
        fore = [roll(v, -1) for v in now]
        if width == 2:
            back = [jnp.where(at_first, back[1], back[0]), jnp.where(at_first, back[0], back[1])]
            fore = [jnp.where(at_last, fore[1], fore[0]), jnp.where(at_last, fore[0], fore[1])]
        for t in range(width):
            high = x[here - 1, t, s] + x[here + 1, t, s]
            around = (x[here, t, up] + x[here, t, down]) + (back[t] + fore[t])
            around = around + (high + high)
            defect = (r[z, t, s] + around) - a[z, t, s] * now[t]
            move = keep * (now[t] - y[here, t, s]) + scale * defect
            after = now[t] + move
            if mask[t] is not None:
                after = after * mask[t]
            y[here, t, s] = after

    first = ((own, own_y), (beside, beside_y), (strip, strip_y))
    second = tuple((y, x) for x, y in first)

    def sweep(n, arrays):
        keep, scale = table_ref[0, n], table_ref[1, n]
        own, beside, strip = arrays

        def level(z, carry):
            here = z + 1
            for i in range(1, 7):
                s = slice(i * 8, i * 8 + 8)
                free = None if 2 <= i < 6 else own_m[0, s]
                step(here, *own, wide_r, diag, [free, own_m[1, s]], 2, i, keep, scale)
                if i in BESIDE_TILES:
                    step(here, *beside, wide_r, diag, [beside_m[0, s], beside_m[1, s]], 2, i, keep, scale)
                step(here, *strip, strip_r, strip_diag, [strip_m[s]], 1, i, keep, scale)
            return carry

        lax.fori_loop(0, LEVELS, level, 0, unroll=UNROLL)

    def pair(n, carry):
        sweep(2 * n, first)
        sweep(2 * n + 1, second)
        return carry

    lax.fori_loop(0, (KCHEB - 1) // 2, pair, 0)
    near_first, near_last = lane < EDGE, lane >= COLS - EDGE

    def finish(z, carry):
        at = z + 1
        for i in range(1, 7):
            s = slice(i * 8, i * 8 + 8)
            out = slice(i * 8 - 8, i * 8)
            value = strip[at, 0, s]
            at_left = value + roll(value, -32)
            at_right = roll(at_left, 64)
            first = jnp.where(near_first, at_left, jnp.where(near_last, at_right, 0.0))
            second = jnp.where(near_last, at_left, jnp.where(near_first, at_right, 0.0))
            first = first + own[at, 0, s]
            second = second + own[at, 1, s]
            if i in BESIDE_TILES:
                first = first + beside[at, 0, s]
                second = second + beside[at, 1, s]
            out_ref[z, out, lanes[0]] = first
            out_ref[z, out, lanes[1]] = second
        return carry

    lax.fori_loop(0, LEVELS, finish, 0, unroll=UNROLL_FINISH)


def smooth(place, table, told, block, low, high, strips, absorption, coefficient=None):
    wide = (2, TALL, COLS)
    thin = (1, TALL, COLS)

    def scratch(*shape):
        return pltpu.VMEM(shape, jnp.float32)

    more = () if coefficient is None else coefficient
    specs = [SMEM_SPEC] * 2 + [VMEM_SPEC] * 2 + [VMEM_SPEC if more else FIELDS_SPEC] * 2 + [VMEM_SPEC] * 3
    if more:
        specs += [FIELDS_SPEC] * 2 + [VMEM_SPEC] * 2
    return pl.pallas_call(
        functools.partial(smooth_kernel, not more),
        grid=(1,),
        in_specs=specs,
        out_shape=jax.ShapeDtypeStruct((LEVELS, INNER, 2 * COLS), jnp.float32),
        scratch_shapes=[
            scratch(*wide), scratch(*wide), scratch(TALL, COLS),
            scratch(PLANES, *wide), scratch(PLANES, *wide), scratch(PLANES, *thin),
            scratch(PLANES, *wide), scratch(PLANES, *wide), scratch(PLANES, *thin),
            scratch(LEVELS, *wide), scratch(LEVELS, *thin),
            scratch(LEVELS, *wide), scratch(LEVELS, *thin),
        ],
        compiler_params=pltpu.CompilerParams(vmem_limit_bytes=VMEM_LIMIT),
        cost_estimate=pl.CostEstimate(flops=2000000, bytes_accessed=54000000, transcendentals=0),
        name="smoother",
    )(place, table, told, block, low, high, *strips, absorption, *more)


INNER = ROWS + 16


def slots_of(place, told_ref, moves):
    lane = iota((1, COLS), 1)
    slots = jnp.zeros((1, COLS), jnp.float32)
    for n, (down, right) in enumerate(moves):
        row = roll(told_ref[pl.ds(place.index(down, right), 1), :], VECTORS * (n - 1))
        slots = jnp.where((lane >> 5) == n, row, slots)
    return slots.astype(jnp.int32)


def coarse_at(coarse_turned, slots):
    pick = jnp.where(iota((COLS, COLS), 0) == (slots >> 5), 1.0, 0.0)
    found = jnp.dot(coarse_turned, pick, precision=HIGHEST, preferred_element_type=jnp.float32)
    found = jnp.where(iota((VECTORS, COLS), 0) == (slots & 31), found, 0.0)
    return jnp.sum(found, axis=0, keepdims=True)


def add_coarse(place, told_ref, coarse_ref, basis_ref, low_ref, high_ref, left_ref, right_ref, at, sum_ref, x,
               own_c, edge_c, ring_ref, side_ref):
    turned = coarse_ref[...].T[:VECTORS]
    row = coarse_at(turned, slots_of(place, told_ref, ((0, 0), (-1, 0), (1, 0), (0, -1))))
    other = coarse_at(turned, slots_of(place, told_ref, ((0, 1),)))
    lane = iota((8, COLS), 1)
    lane_row = iota((1, COLS), 1)
    column = jnp.broadcast_to(row, (COLS, COLS)).T
    own_c[...] = column[:VECTORS]
    edge_c[...] = column[VECTORS : 3 * VECTORS]
    for n, edge in ((0, low_ref), (1, high_ref)):

        def vector(k, total):
            return total + edge[2 * LEVELS + k] * edge_c[pl.ds(n * VECTORS + k, 1), :]

        ring_ref[n] = lax.fori_loop(0, VECTORS, vector, jnp.zeros((LEVELS, COLS), jnp.float32))
    which = iota((COLS, COLS), 0) >> 5
    for n, (edge, values) in enumerate(((left_ref, roll(row, VECTORS)), (right_ref, other))):
        values = jnp.where(lane_row < VECTORS, values, 0.0)
        values = values + roll(values, 32) + roll(values, 64) + roll(values, 96)
        weights = jnp.broadcast_to(values, (COLS, COLS)).T
        weights = jnp.where(iota((COLS, COLS), 1) == which, weights, 0.0)
        parts = edge[at : at + 2].reshape(2 * TALL, COLS)
        side_ref[n] = jnp.dot(parts, weights, precision=HIGHEST, preferred_element_type=jnp.float32)

    def level(z, carry):
        total = sum_ref[z, 8 : 8 + ROWS, 0:COLS]
        for k in range(VECTORS):
            total = total + basis_ref[k, z].astype(jnp.float32) * own_c[k : k + 1]
        here = z + 1
        x[here, 8 : 8 + ROWS, 0:COLS] = total
        rows = pl.ds(z, 1)
        x[here, 7:8, 0:COLS] = sum_ref[z, 7:8, 0:COLS] + ring_ref[0, rows, :]
        x[here, 8 + ROWS : 9 + ROWS, 0:COLS] = sum_ref[z, 8 + ROWS : 9 + ROWS, 0:COLS] + ring_ref[1, rows, :]
        q = z & 3
        for i in range(ROWS // 8):
            s = pl.ds(pl.multiple_of((z >> 2) * ROWS + i * 8, 8), 8)
            left = pltpu.roll(side_ref[0, s, :], (COLS - 1) - q, 1)
            right = pltpu.roll(side_ref[1, s, :], (COLS - q) & (COLS - 1), 1)
            t = slice(8 + i * 8, 16 + i * 8)
            value = jnp.where(lane == COLS - 1, left, jnp.where(lane == 0, right, 0.0))
            x[here, t, COLS : 2 * COLS] = sum_ref[z, t, COLS : 2 * COLS] + value
        return carry

    lax.fori_loop(0, LEVELS, level, 0, unroll=2)
    zero = jnp.zeros((ROWS, COLS), jnp.float32)
    x[0, 8 : 8 + ROWS, 0:COLS] = zero
    x[PLANES - 1, 8 : 8 + ROWS, 0:COLS] = zero
    return row


def image_at(x, absorption_ref, z, i):
    lane = iota((8, COLS), 1)
    here = z + 1
    s = slice(8 + i * 8, 16 + i * 8)
    up, down = slice(7 + i * 8, 15 + i * 8), slice(9 + i * 8, 17 + i * 8)
    now = x[here, s, 0:COLS]
    margin = x[here, s, COLS : 2 * COLS]
    back = jnp.where(lane == 0, roll(margin, 1), roll(now, 1))
    fore = jnp.where(lane == COLS - 1, roll(margin, -1), roll(now, -1))
    high = x[here - 1, s, 0:COLS] + x[here + 1, s, 0:COLS]
    around = (x[here, up, 0:COLS] + x[here, down, 0:COLS]) + (back + fore)
    diagonal = absorption_ref[z, i * 8 : i * 8 + 8, :] + (4.0 + 2.0 * vertical)
    return now, diagonal * now - around - vertical * high


def total_of(value):
    return jnp.sum(jnp.sum(value, axis=0, keepdims=True), axis=1, keepdims=True)


def scalars(told_ref):
    totals = jnp.sum(told_ref[...], axis=0, keepdims=True)
    return totals[:, 64:65], totals[:, 65:66]


def first_coarse_kernel(
    place_ref, told_ref, coarse_ref, basis_ref, low_ref, high_ref, left_ref, right_ref, sum_ref, source_ref, absorption_ref,
    direction_ref, image_ref, ahead_ref, behind_ref, out_ref, x, own_c, edge_c, ring_ref, side_ref, sums_ref,
):
    place = Place(place_ref, told_ref)
    row = add_coarse(place, told_ref, coarse_ref, basis_ref, low_ref, high_ref, left_ref, right_ref, 4, sum_ref, x,
                     own_c, edge_c, ring_ref, side_ref)
    zero = jnp.zeros((8, COLS), jnp.float32)

    def images(z, carry):
        weight, curve = carry
        for i in range(ROWS // 8):
            s = slice(i * 8, i * 8 + 8)
            now, image = image_at(x, absorption_ref, z, i)
            direction_ref[z, s] = now
            image_ref[z, s] = image
            if i >= 2:
                ahead_ref[z, (i - 2) * 8 : (i - 1) * 8] = image
            else:
                behind_ref[z, s] = image
            weight = weight + source_ref[z, s] * sum_ref[z, 8 + i * 8 : 16 + i * 8, 0:COLS]
            curve = curve + now * image
        return weight, curve

    weight, curve = lax.fori_loop(0, LEVELS, images, (zero, zero), unroll=2)
    half = VECTORS // 2
    for part in range(2):

        def level(z, sums):
            image = image_ref[z]
            return tuple(
                sums[k] + fold_rows(basis_ref[part * half + k, z].astype(jnp.float32) * image) for k in range(half)
            )

        sums = lax.fori_loop(0, LEVELS, level, (zero,) * half)
        for k in range(half):
            sums_ref[part * half + k : part * half + k + 1] = jnp.sum(sums[k], axis=0, keepdims=True)
    lane = iota((1, COLS), 1)
    row = jnp.where(lane < VECTORS, row, 0.0)
    mine = told_ref[pl.ds(place.index(0, 0), 1), :]
    told = roll(row, VECTORS)
    told = told + jnp.where(lane == 64, total_of(weight) + total_of(row * mine), 0.0)
    told = told + jnp.where(lane == 65, total_of(curve), 0.0)
    out_ref[...] = row_of_sums(sums_ref[...]) + told


def second_coarse_kernel(
    place_ref, told_ref, coarse_ref, basis_ref, low_ref, high_ref, left_ref, right_ref, sum_ref, source_ref, absorption_ref,
    again_ref, first_sum_ref, direction_ref, first_ref,
    residual_ref, precond_ref, image_ref, out_ref, x, own_c, edge_c, ring_ref, side_ref,
):
    place = Place(place_ref, told_ref)
    row = add_coarse(place, told_ref, coarse_ref, basis_ref, low_ref, high_ref, left_ref, right_ref, 4, sum_ref, x,
                     own_c, edge_c, ring_ref, side_ref)
    weight0, curve0 = scalars(again_ref)
    step = weight0 / curve0
    zero = jnp.zeros((8, COLS), jnp.float32)

    def images(z, sums):
        weight, own, cross = sums
        for i in range(ROWS // 8):
            s = slice(i * 8, i * 8 + 8)
            t = slice(8 + i * 8, 16 + i * 8)
            now, image = image_at(x, absorption_ref, z, i)
            direction, first = direction_ref[z, s], first_ref[z, s]
            residual = source_ref[z, s] - step * first
            precond = direction - step * now
            image = first - step * image
            residual_ref[z, s] = residual
            precond_ref[z, s] = precond
            image_ref[z, s] = image
            weight = weight + residual * (first_sum_ref[z, t, 0:COLS] - step * sum_ref[z, t, 0:COLS])
            own = own + precond * image
            cross = cross + (precond * first + direction * image)
        return weight, own, cross

    weight, own, cross = lax.fori_loop(0, LEVELS, images, (zero, zero, zero), unroll=2)
    mine = pl.ds(place.index(0, 0), 1)
    lane = iota((1, COLS), 1)
    again = again_ref[mine, :]
    projected = told_ref[mine, :] - step * again
    coarse = roll(again, -VECTORS) - step * row
    both = jnp.where(lane < VECTORS, projected * coarse, 0.0)
    told = jnp.where(lane == 0, total_of(weight) + total_of(both), 0.0)
    told = told + jnp.where(lane == 1, total_of(own), 0.0) + jnp.where(lane == 2, total_of(cross), 0.0)
    out_ref[...] = jnp.broadcast_to(told, (COLS, COLS))


def last_kernel(again_ref, last_ref, direction_ref, first_ref, residual_ref, precond_ref, image_ref, x_ref, r_ref):
    weight0, curve0 = scalars(again_ref)
    step0 = weight0 / curve0
    totals = jnp.sum(last_ref[...], axis=0, keepdims=True)
    weight1, own, cross = totals[:, 0:1], totals[:, 1:2], totals[:, 2:3]
    ratio = weight1 / weight0
    step1 = weight1 / (own + ratio * (cross + ratio * curve0))

    def level(z, carry):
        direction = direction_ref[z]
        x_ref[z] = step0 * direction + step1 * (precond_ref[z] + ratio * direction)
        r_ref[z] = residual_ref[z] - step1 * (image_ref[z] + ratio * first_ref[z])
        return carry

    lax.fori_loop(0, LEVELS, level, 0, unroll=4)


def shards(source, absorption, basis, coarse_inverse, margin_width, coarse_slot):
    block = jax.ShapeDtypeStruct((LEVELS, ROWS, COLS), jnp.float32)
    slab = jax.ShapeDtypeStruct((LEVELS, EDGE, COLS), jnp.float32)
    message = jax.ShapeDtypeStruct((COLS, COLS), jnp.float32)
    params = pltpu.CompilerParams(vmem_limit_bytes=VMEM_LIMIT)

    def scratch(*shape):
        return pltpu.VMEM(shape, jnp.float32)

    coarse_scratch = [
        scratch(PLANES, INNER, 2 * COLS), scratch(VECTORS, COLS), scratch(2 * VECTORS, COLS),
        scratch(2, LEVELS, COLS), scratch(2, 2 * TALL, COLS),
    ]
    place = jnp.stack(
        [lax.axis_index("gx"), lax.axis_index("gy"), lax.axis_size("gx"), lax.axis_size("gy")]
    ).astype(jnp.int32)
    table = jnp.array(list(zip(*chebyshev_table())), jnp.float32)
    rows, ahead, behind, sides = first_projection(
        source, absorption, basis, coarse_slot, margin_width
    )
    low, high = exchange(ahead, behind, "gx")
    told = everyone(rows)
    fields = [pl.BlockSpec(memory_space=pltpu.HBM)] + [VMEM_SPEC] * 2 + [FIELDS_SPEC] * 2 + [VMEM_SPEC]
    strips = exchange(
        *pack(first_pack_kernel, fields, 6, told, source, absorption, low, high, sides), "gy"
    )
    coarse = everyone(solve_rows(told, told, coarse_inverse))
    first_sum = smooth(place, table, told, source, low, high, strips, absorption)
    edges = (low, high, *strips)
    direction, image, ahead, behind, rows = pl.pallas_call(
        first_coarse_kernel,
        in_specs=[SMEM_SPEC] + [VMEM_SPEC] * 10,
        out_shape=[block, block, slab, slab, message],
        scratch_shapes=coarse_scratch + [scratch(VECTORS, COLS)],
        compiler_params=params,
        name="direction_and_image",
    )(place, told, coarse, basis, *edges, first_sum, source, absorption)
    low_w, high_w = exchange(ahead, behind, "gx")
    again = everyone(rows)
    strips_w = exchange(*pack(pack_kernel, [VMEM_SPEC] * 3, 2, image, low_w, high_w), "gy")
    coarse = everyone(solve_rows(again, told, coarse_inverse))
    second_sum = smooth(place, table, told, image, low_w, high_w, strips_w, absorption, edges)
    residual, precond, precond_image, rows = pl.pallas_call(
        second_coarse_kernel,
        in_specs=[SMEM_SPEC] + [VMEM_SPEC] * 14,
        out_shape=[block, block, block, message],
        scratch_shapes=coarse_scratch,
        compiler_params=params,
        name="second_images",
    )(place, told, coarse, basis, *edges, second_sum, source, absorption, again, first_sum, direction, image)
    last = everyone(rows)
    concentration, residual = pl.pallas_call(
        last_kernel, out_shape=[block, block], compiler_params=params, name="update"
    )(again, last, direction, image, residual, precond, precond_image)
    return (concentration, residual)


def solution(mesh):
    return jax.shard_map(
        shards,
        mesh=mesh,
        in_specs=(
            P(None, "gx", "gy"),
            P(None, "gx", "gy"),
            P(None, None, "gx", "gy"),
            P(("gx", "gy"), None),
            P("gx", "gy"),
            P("gx", "gy", None),
        ),
        out_specs=(P(None, "gx", "gy"), P(None, "gx", "gy")),
        check_vma=False,
    )
```

```python
import functools

import jax
import jax.numpy as jnp
from jax import lax
from jax.experimental import pallas as pl
from jax.experimental.pallas import tpu as pltpu
from jax.sharding import PartitionSpec as P

KCHEB = 9
AXES = ("gx", "gy")
LEVELS = 16
ROWS = 32
COLS = 128
VECTORS = 32
EDGE = 16
TALL = ROWS + 2 * EDGE
HIGHEST = lax.Precision.HIGHEST

lowest_rate = 0.05
highest_rate = 18.5
vertical = 2.0
theta = 0.5 * (highest_rate + lowest_rate)
delta = 0.5 * (highest_rate - lowest_rate)
VMEM_LIMIT = 24 * 1024 * 1024
FIRST_LIMIT = 58 * 1024 * 1024


def chebyshev_table():
    ratio = theta / delta
    rho_old = 1.0 / ratio
    table = []
    for _ in range(KCHEB - 1):
        rho_new = 1.0 / (2.0 * ratio - rho_old)
        table.append((rho_new * rho_old, 2.0 * rho_new / delta))
        rho_old = rho_new
    return table


def iota(shape, dim):
    return lax.broadcasted_iota(jnp.int32, shape, dim)


def roll(value, shift):
    return pltpu.roll(value, shift % COLS, 1)


def exchange(forward_value, backward_value, axis):
    count = lax.axis_size(axis)
    forward = [(i, i + 1) for i in range(count - 1)]
    backward = [(target, source) for source, target in forward]
    return lax.ppermute(forward_value, axis, forward), lax.ppermute(backward_value, axis, backward)


def everyone(rows):
    return lax.all_to_all(rows, AXES, 0, 0, tiled=True)


def row_of_sums(sums):
    padded = jnp.concatenate([sums, jnp.zeros((COLS - VECTORS, COLS), jnp.float32)], 0)
    ones = jnp.ones((COLS, COLS), jnp.float32)
    return lax.dot_general(
        ones, padded, (((1,), (1,)), ((), ())), precision=HIGHEST, preferred_element_type=jnp.float32
    )


def fold_rows(product):
    return (product[0:8] + product[8:16]) + (product[16:24] + product[24:32])


def first_kernel(
    field_ref, coefficient_ref, basis_ref, slots_ref, margin_ref,
    out_ref, ahead_ref, behind_ref, sides_ref, sums_ref, edges_ref,
):
    step = pl.program_id(0)
    group = basis_ref.shape[0]

    @pl.when(step == 0)
    def _():
        edges_ref[...] = jnp.zeros_like(edges_ref)

        def level(z, carry):
            ahead_ref[z] = field_ref[z, ROWS - EDGE :, :]
            behind_ref[z] = field_ref[z, :EDGE, :]
            ahead_ref[LEVELS + z] = coefficient_ref[z, ROWS - EDGE :, :]
            behind_ref[LEVELS + z] = coefficient_ref[z, :EDGE, :]
            return carry

        lax.fori_loop(0, LEVELS, level, 0)

    def level(z, sums):
        field = field_ref[z]
        new = []
        for j in range(group):
            values = basis_ref[j, z].astype(jnp.float32)
            new.append(sums[j] + fold_rows(values * field))
            at = 2 * LEVELS + step * group + j
            behind_ref[at, pl.ds(z, 1), :] = values[0:1]
            ahead_ref[at, pl.ds(z, 1), :] = values[ROWS - 1 : ROWS]
        return tuple(new)

    zero = jnp.zeros((8, COLS), jnp.float32)
    sums = lax.fori_loop(0, LEVELS, level, (zero,) * group, unroll=2)
    for j in range(group):
        sums_ref[pl.ds(step * group + j, 1), :] = jnp.sum(sums[j], axis=0, keepdims=True)
    from_lane, to_lane = iota((COLS, COLS), 0), iota((COLS, COLS), 1)
    picks = []
    for j in range(group):
        k = step * group + j
        pick = ((from_lane == 0) & (to_lane == k)) | ((from_lane == COLS - 1) & (to_lane == VECTORS + k))
        picks.append(jnp.where(pick, 1.0, 0.0).astype(jnp.bfloat16))
    values = jnp.concatenate([basis_ref[j].reshape(LEVELS * ROWS, COLS) for j in range(group)], axis=1)
    edges_ref[...] += jnp.dot(values, jnp.concatenate(picks, 0), preferred_element_type=jnp.float32)

    @pl.when(step == pl.num_programs(0) - 1)
    def _():
        told = jnp.concatenate(
            [
                jnp.zeros((1, VECTORS), jnp.float32),
                slots_ref[0].astype(jnp.float32),
                margin_ref[...].astype(jnp.float32),
                jnp.zeros((1, COLS - 65), jnp.float32),
            ],
            axis=1,
        )
        out_ref[...] = row_of_sums(sums_ref[...]) + told
        place = iota((ROWS, COLS), 1) >> 5
        for n in range(LEVELS // 4):
            left = jnp.zeros((ROWS, COLS), jnp.float32)
            right = left
            for q in range(4):
                z = 4 * n + q
                value = edges_ref[z * ROWS : (z + 1) * ROWS]
                left = jnp.where(place == q, roll(value, VECTORS * q), left)
                right = jnp.where(place == q, roll(value, VECTORS * (q - 1)), right)
            sides_ref[n] = left
            sides_ref[LEVELS // 4 + n] = right


def first_projection(field, coefficient, basis, slots, margin):
    group = 8
    rows = 2 * LEVELS + VECTORS
    edge_rows = jax.ShapeDtypeStruct((rows, LEVELS, COLS), jnp.float32)
    edge_cols = jax.ShapeDtypeStruct((LEVELS // 2, ROWS, COLS), jnp.float32)
    block_spec = pl.BlockSpec((LEVELS, ROWS, COLS), lambda i: (0, 0, 0))
    rows_spec = pl.BlockSpec(edge_rows.shape, lambda i: (0, 0, 0))
    cols_spec = pl.BlockSpec(edge_cols.shape, lambda i: (0, 0, 0))
    return pl.pallas_call(
        first_kernel,
        grid=(VECTORS // group,),
        in_specs=[
            block_spec,
            block_spec,
            pl.BlockSpec((group, LEVELS, ROWS, COLS), lambda i: (i, 0, 0, 0)),
            pl.BlockSpec(slots.shape, lambda i: (0, 0, 0)),
            pl.BlockSpec(margin.shape, lambda i: (0, 0)),
        ],
        out_specs=[pl.BlockSpec((COLS, COLS), lambda i: (0, 0)), rows_spec, rows_spec, cols_spec],
        out_shape=[jax.ShapeDtypeStruct((COLS, COLS), jnp.float32), edge_rows, edge_rows, edge_cols],
        scratch_shapes=[
            pltpu.VMEM((VECTORS, COLS), jnp.float32), pltpu.VMEM((LEVELS * ROWS, COLS), jnp.float32)
        ],
        compiler_params=pltpu.CompilerParams(vmem_limit_bytes=FIRST_LIMIT),
        name="first_projection",
    )(field, coefficient, basis, slots, margin)


def coarse_rows(told_ref, slots_ref, inverse_ref, out_ref):
    told = told_ref[...]
    slots = slots_ref[...]
    turned = told.T
    slots_turned = slots.T
    lane = iota((COLS, COLS), 1)
    sub = iota((VECTORS, COLS), 0)
    placed = jnp.zeros((3 * VECTORS, COLS), jnp.float32)
    for k in range(VECTORS):
        slot_column = slots[:, VECTORS + k : VECTORS + k + 1].astype(jnp.int32)
        ones = jnp.where((slot_column & 127) == lane, 1.0, 0.0).astype(jnp.bfloat16)
        slot_row = slots_turned[VECTORS + k : VECTORS + k + 1, :].astype(jnp.int32)
        values = turned[k : k + 1, :]
        spread = jnp.where((slot_row >> 7) == sub, values, 0.0)
        first = spread.astype(jnp.bfloat16)
        rest = spread - first.astype(jnp.float32)
        second = rest.astype(jnp.bfloat16)
        third = (rest - second.astype(jnp.float32)).astype(jnp.bfloat16)
        parts = jnp.concatenate([first, second, third], 0)
        placed = placed + jnp.dot(parts, ones, preferred_element_type=jnp.float32)
    placed = placed[:VECTORS] + placed[VECTORS : 2 * VECTORS] + placed[2 * VECTORS :]
    total = jnp.zeros((VECTORS, COLS), jnp.float32)
    for high in range(VECTORS):
        total = total + inverse_ref[:, high * COLS : (high + 1) * COLS] * placed[high : high + 1]
    out_ref[...] = row_of_sums(total)


def pack_strips(parts, forward_ref, backward_ref, at):
    def levels(group, carry):
        row = 0
        for part, start in parts:
            height = EDGE if part.shape[1] == EDGE else ROWS
            lane = iota((height, COLS), 1)
            ahead = jnp.zeros((height, COLS), jnp.float32)
            behind = ahead
            for j in range(8):
                value = part[start + group * 8 + j]
                mine = (lane >= EDGE * j) & (lane < EDGE * (j + 1))
                ahead = jnp.where(mine, roll(value, EDGE * j - (COLS - EDGE)), ahead)
                behind = jnp.where(mine, roll(value, EDGE * j), behind)
            forward_ref[at + group, row : row + height, :] = ahead
            backward_ref[at + group, row : row + height, :] = behind
            row += height
        return carry

    lax.fori_loop(0, LEVELS // 8, levels, 0)


def first_pack_kernel(
    told_ref, source_ref, absorption_ref, low_ref, high_ref, sides_ref, forward_ref, backward_ref
):
    for f, block in enumerate((source_ref, absorption_ref)):
        pack_strips(((low_ref, LEVELS * f), (block, 0), (high_ref, LEVELS * f)), forward_ref, backward_ref, 2 * f)
    for n in range(LEVELS // 8):
        for half in range(2):
            rows = slice(half * ROWS, (half + 1) * ROWS)
            forward_ref[4 + n, rows, :] = sides_ref[LEVELS // 4 + 2 * n + half]
            backward_ref[4 + n, rows, :] = sides_ref[2 * n + half]


def pack_kernel(block_ref, low_ref, high_ref, forward_ref, backward_ref):
    pack_strips(((low_ref, 0), (block_ref, 0), (high_ref, 0)), forward_ref, backward_ref, 0)


FIELDS_SPEC = pl.BlockSpec((2 * LEVELS, EDGE, COLS), lambda i: (0, 0, 0))
VMEM_SPEC = pl.BlockSpec(memory_space=pltpu.VMEM)
SMEM_SPEC = pl.BlockSpec(memory_space=pltpu.SMEM)


def pack(kernel, specs, strips, *operands):
    strips = jax.ShapeDtypeStruct((strips, TALL, COLS), jnp.float32)
    return pl.pallas_call(
        kernel,
        grid=(1,),
        in_specs=specs,
        out_shape=[strips, strips],
        compiler_params=pltpu.CompilerParams(vmem_limit_bytes=VMEM_LIMIT),
        cost_estimate=pl.CostEstimate(flops=2000000, bytes_accessed=2000000, transcendentals=0),
        name="strips",
    )(*operands)


def solve_rows(*operands):
    return pl.pallas_call(
        coarse_rows,
        out_shape=pltpu.HBM((COLS, COLS), jnp.float32),
        compiler_params=pltpu.CompilerParams(vmem_limit_bytes=VMEM_LIMIT),
        name="coarse_rows",
    )(*operands)


class Place:
    def __init__(self, place_ref, told_ref):
        self.row = place_ref[0]
        self.col = place_ref[1]
        self.rows = place_ref[2]
        self.cols = place_ref[3]
        self.told_ref = told_ref

    def index(self, down, right):
        row = jnp.clip(self.row + down, 0, self.rows - 1)
        col = jnp.clip(self.col + right, 0, self.cols - 1)
        return row * self.cols + col

    def margin(self, down, right):
        row, col = self.row + down, self.col + right
        real = (row >= 0) & (row < self.rows) & (col >= 0) & (col < self.cols)
        margin = self.told_ref[pl.ds(self.index(down, right), 1), :][:, 64:65]
        return jnp.where(real, margin.astype(jnp.int32), -4096)


def masks(place, own_ref, beside_ref, strip_ref):
    shape = (TALL, COLS)
    row = iota(shape, 0) - EDGE
    lane = iota(shape, 1)
    top, bottom = -ROWS * place.row, ROWS * (place.rows - place.row)
    first, last = -COLS * place.col, COLS * (place.cols - place.col)
    row_real = (row >= top) & (row < bottom)
    m = {(i, j): place.margin(i, j) for i in (-1, 0, 1) for j in (-1, 0, 1)}
    upper, lower = row < 8, row >= ROWS - 8
    for tile in range(2):
        col = lane if tile == 0 else jnp.where(lane < 64, lane + COLS, lane - COLS)
        real = row_real & (col >= first) & (col < last)
        if tile == 1:
            real = real & ((lane < EDGE) | (lane >= COLS - EDGE))

        def across(margin):
            return (col >= -margin) & (col < COLS + margin)

        own = m[0, 0]
        inside = real & (row >= -own) & (row < ROWS + own) & across(own)
        own_ref[tile] = jnp.where(inside, 1.0, 0.0)
        above, below = m[-1, 0], m[1, 0]
        inside = (upper & (row < above) & across(above)) | (lower & (row >= ROWS - below) & across(below))
        beside_ref[tile] = jnp.where(real & inside, 1.0, 0.0)
    group = ((lane + EDGE) & 127) >> 5
    away = ((lane + EDGE) & 31) - EDGE
    inside = row < -4096
    for place_of, side in ((0, -1), (2, 1)):
        col = away if side < 0 else away + COLS
        real = row_real & (col >= first) & (col < last)

        def reached(margin):
            return (away < margin) if side < 0 else (away >= -margin)

        level = m[0, side]
        inside = inside | (
            (group == place_of) & real & (row >= -level) & (row < ROWS + level) & reached(level)
        )
        above, below = m[-1, side], m[1, side]
        corner = (upper & (row < above) & reached(above)) | (
            lower & (row >= ROWS - below) & reached(below)
        )
        inside = inside | ((group == place_of + 1) & real & corner)
    strip_ref[...] = jnp.where(inside, 1.0, 0.0)


def tiles_of(parts, start, strips, at, z, i):
    low, block, high = parts
    from_left, from_right = strips
    lane = iota((8, COLS), 1)
    if i < 2:
        center = low[start + z, i * 8 : i * 8 + 8, :]
    elif i < 6:
        center = block[z, (i - 2) * 8 : (i - 2) * 8 + 8, :]
    else:
        center = high[start + z, (i - 6) * 8 : (i - 6) * 8 + 8, :]
    s = slice(i * 8, i * 8 + 8)
    group, shift = at + (z >> 3), EDGE * (z & 7)
    left = pltpu.roll(from_left[group, s, :], (COLS - EDGE) - shift, 1)
    right = pltpu.roll(from_right[group, s, :], (COLS - shift) & (COLS - 1), 1)
    margin = jnp.where(lane >= COLS - EDGE, left, jnp.where(lane < EDGE, right, 0.0))
    at_left = jnp.where(lane >= 64, margin, center)
    at_right = jnp.where(lane < 64, margin, center)
    near = (lane < EDGE) | (lane >= COLS - EDGE)
    others = jnp.where(lane < 80, roll(at_right, 64), roll(at_right, 96))
    packed = jnp.where(near, at_left, jnp.where(lane < 48, roll(at_left, 32), others))
    return center, margin, packed


UNROLL = 8
UNROLL_BEGIN = 2
UNROLL_FINISH = 2
PLANES = LEVELS + 2
BESIDE_TILES = (1, 2, 5, 6)


def smooth_kernel(same, place_ref, table_ref, told_ref, block_ref, low_ref, high_ref, left_ref, right_ref, absorption_ref, *refs):
    if same:
        low_c, high_c, left_c, right_c = low_ref, high_ref, left_ref, right_ref
    else:
        low_c, high_c, left_c, right_c = refs[:4]
        refs = refs[4:]
    (
        out_ref, own_m, beside_m, strip_m, own, beside, strip, own_y, beside_y, strip_y,
        wide_r, strip_r, diag, strip_diag,
    ) = refs
    field_start, coef_start, coef_at = 0, LEVELS, 2
    masks(Place(place_ref, told_ref), own_m, beside_m, strip_m)
    base = 4.0 + 2.0 * vertical
    zero = jnp.zeros((8, COLS), jnp.float32)
    lane = iota((8, COLS), 1)
    lanes = [slice(0, COLS), slice(COLS, 2 * COLS)]

    def clear(n, carry):
        at = n * (PLANES - 1)
        for i in range(8):
            s = slice(i * 8, i * 8 + 8)
            for t in range(2):
                for x in (own, own_y, beside, beside_y):
                    x[at, t, s] = zero
            strip[at, 0, s] = zero
            strip_y[at, 0, s] = zero
        return carry

    lax.fori_loop(0, 2, clear, 0)

    def begin(z, carry):
        at = z + 1
        for i in range(8):
            s = slice(i * 8, i * 8 + 8)
            tiles = tiles_of((low_ref, block_ref, high_ref), field_start, (left_ref, right_ref), 0, z, i)
            inner = 1 <= i < 7
            for t in range(2):
                guess = tiles[t] * (1.0 / theta)
                value = guess if t == 0 and 2 <= i < 6 else guess * own_m[t, s]
                own[at, t, s] = value
                own_y[at, t, s] = zero
                if inner:
                    wide_r[z, t, s] = tiles[t]
                beside_y[at, t, s] = zero
                beside[at, t, s] = zero if i in (3, 4) else guess * beside_m[t, s]
            strip[at, 0, s] = tiles[2] * (strip_m[s] * (1.0 / theta))
            strip_y[at, 0, s] = zero
            if inner:
                strip_r[z, 0, s] = tiles[2]
                tiles = tiles_of((low_c, absorption_ref, high_c), coef_start, (left_c, right_c), coef_at, z, i)
                diag[z, 0, s] = tiles[0] + base
                diag[z, 1, s] = tiles[1] + base
                strip_diag[z, 0, s] = tiles[2] + base
        return carry

    lax.fori_loop(0, LEVELS, begin, 0, unroll=UNROLL_BEGIN)
    at_first, at_last = lane == 0, lane == COLS - 1

    def step(here, x, y, r, a, mask, width, i, keep, scale):
        s = slice(i * 8, i * 8 + 8)
        up, down = slice(i * 8 - 1, i * 8 + 7), slice(i * 8 + 1, i * 8 + 9)
        z = here - 1
        now = [x[here, t, s] for t in range(width)]
        back = [roll(v, 1) for v in now]
        fore = [roll(v, -1) for v in now]
        if width == 2:
            back = [jnp.where(at_first, back[1], back[0]), jnp.where(at_first, back[0], back[1])]
            fore = [jnp.where(at_last, fore[1], fore[0]), jnp.where(at_last, fore[0], fore[1])]
        for t in range(width):
            high = x[here - 1, t, s] + x[here + 1, t, s]
            around = (x[here, t, up] + x[here, t, down]) + (back[t] + fore[t])
            around = around + (high + high)
            defect = (r[z, t, s] + around) - a[z, t, s] * now[t]
            move = keep * (now[t] - y[here, t, s]) + scale * defect
            after = now[t] + move
            if mask[t] is not None:
                after = after * mask[t]
            y[here, t, s] = after

    first = ((own, own_y), (beside, beside_y), (strip, strip_y))
    second = tuple((y, x) for x, y in first)

    def sweep(n, arrays):
        keep, scale = table_ref[0, n], table_ref[1, n]
        own, beside, strip = arrays

        def level(z, carry):
            here = z + 1
            for i in range(1, 7):
                s = slice(i * 8, i * 8 + 8)
                free = None if 2 <= i < 6 else own_m[0, s]
                step(here, *own, wide_r, diag, [free, own_m[1, s]], 2, i, keep, scale)
                if i in BESIDE_TILES:
                    step(here, *beside, wide_r, diag, [beside_m[0, s], beside_m[1, s]], 2, i, keep, scale)
                step(here, *strip, strip_r, strip_diag, [strip_m[s]], 1, i, keep, scale)
            return carry

        lax.fori_loop(0, LEVELS, level, 0, unroll=UNROLL)

    def pair(n, carry):
        sweep(2 * n, first)
        sweep(2 * n + 1, second)
        return carry

    lax.fori_loop(0, (KCHEB - 1) // 2, pair, 0)
    near_first, near_last = lane < EDGE, lane >= COLS - EDGE

    def finish(z, carry):
        at = z + 1
        for i in range(1, 7):
            s = slice(i * 8, i * 8 + 8)
            out = slice(i * 8 - 8, i * 8)
            value = strip[at, 0, s]
            at_left = value + roll(value, -32)
            at_right = roll(at_left, 64)
            first = jnp.where(near_first, at_left, jnp.where(near_last, at_right, 0.0))
            second = jnp.where(near_last, at_left, jnp.where(near_first, at_right, 0.0))
            first = first + own[at, 0, s]
            second = second + own[at, 1, s]
            if i in BESIDE_TILES:
                first = first + beside[at, 0, s]
                second = second + beside[at, 1, s]
            out_ref[z, out, lanes[0]] = first
            out_ref[z, out, lanes[1]] = second
        return carry

    lax.fori_loop(0, LEVELS, finish, 0, unroll=UNROLL_FINISH)


def smooth(place, table, told, block, low, high, strips, absorption, coefficient=None):
    wide = (2, TALL, COLS)
    thin = (1, TALL, COLS)

    def scratch(*shape):
        return pltpu.VMEM(shape, jnp.float32)

    more = () if coefficient is None else coefficient
    specs = [SMEM_SPEC] * 2 + [VMEM_SPEC] * 2 + [VMEM_SPEC if more else FIELDS_SPEC] * 2 + [VMEM_SPEC] * 3
    if more:
        specs += [FIELDS_SPEC] * 2 + [VMEM_SPEC] * 2
    return pl.pallas_call(
        functools.partial(smooth_kernel, not more),
        grid=(1,),
        in_specs=specs,
        out_shape=(pltpu.HBM if more else jax.ShapeDtypeStruct)((LEVELS, INNER, 2 * COLS), jnp.float32),
        scratch_shapes=[
            scratch(*wide), scratch(*wide), scratch(TALL, COLS),
            scratch(PLANES, *wide), scratch(PLANES, *wide), scratch(PLANES, *thin),
            scratch(PLANES, *wide), scratch(PLANES, *wide), scratch(PLANES, *thin),
            scratch(LEVELS, *wide), scratch(LEVELS, *thin),
            scratch(LEVELS, *wide), scratch(LEVELS, *thin),
        ],
        compiler_params=pltpu.CompilerParams(vmem_limit_bytes=VMEM_LIMIT),
        cost_estimate=pl.CostEstimate(flops=2000000, bytes_accessed=54000000, transcendentals=0),
        name="smoother",
    )(place, table, told, block, low, high, *strips, absorption, *more)


INNER = ROWS + 16


def slots_of(place, told_ref, moves):
    lane = iota((1, COLS), 1)
    slots = jnp.zeros((1, COLS), jnp.float32)
    for n, (down, right) in enumerate(moves):
        row = roll(told_ref[pl.ds(place.index(down, right), 1), :], VECTORS * (n - 1))
        slots = jnp.where((lane >> 5) == n, row, slots)
    return slots.astype(jnp.int32)


def coarse_at(coarse_turned, slots):
    pick = jnp.where(iota((COLS, COLS), 0) == (slots >> 5), 1.0, 0.0)
    found = jnp.dot(coarse_turned, pick, precision=HIGHEST, preferred_element_type=jnp.float32)
    found = jnp.where(iota((VECTORS, COLS), 0) == (slots & 31), found, 0.0)
    return jnp.sum(found, axis=0, keepdims=True)


def add_coarse(place, told_ref, coarse_ref, basis_hbm, basis_ref, sems, low_ref, high_ref, left_ref, right_ref, at, sum_ref, x,
               own_c, edge_c, ring_ref, side_ref):
    def part(q):
        levels = pl.ds(q * 4, 4)
        return pltpu.make_async_copy(basis_hbm.at[:, levels], basis_ref.at[:, levels], sems.at[q])

    for q in range(LEVELS // 4):
        part(q).start()
    turned = coarse_ref[...].T[:VECTORS]
    row = coarse_at(turned, slots_of(place, told_ref, ((0, 0), (-1, 0), (1, 0), (0, -1))))
    other = coarse_at(turned, slots_of(place, told_ref, ((0, 1),)))
    lane = iota((8, COLS), 1)
    lane_row = iota((1, COLS), 1)
    column = jnp.broadcast_to(row, (COLS, COLS)).T
    own_c[...] = column[:VECTORS]
    edge_c[...] = column[VECTORS : 3 * VECTORS]
    for n, edge in ((0, low_ref), (1, high_ref)):

        def vector(k, total):
            return total + edge[2 * LEVELS + k] * edge_c[pl.ds(n * VECTORS + k, 1), :]

        ring_ref[n] = lax.fori_loop(0, VECTORS, vector, jnp.zeros((LEVELS, COLS), jnp.float32))
    which = iota((COLS, COLS), 0) >> 5
    for n, (edge, values) in enumerate(((left_ref, roll(row, VECTORS)), (right_ref, other))):
        values = jnp.where(lane_row < VECTORS, values, 0.0)
        values = values + roll(values, 32) + roll(values, 64) + roll(values, 96)
        weights = jnp.broadcast_to(values, (COLS, COLS)).T
        weights = jnp.where(iota((COLS, COLS), 1) == which, weights, 0.0)
        parts = edge[at : at + 2].reshape(2 * TALL, COLS)
        side_ref[n] = jnp.dot(parts, weights, precision=HIGHEST, preferred_element_type=jnp.float32)

    def level(z, carry):
        total = sum_ref[z, 8 : 8 + ROWS, 0:COLS]
        for k in range(VECTORS):
            total = total + basis_ref[k, z].astype(jnp.float32) * own_c[k : k + 1]
        here = z + 1
        x[here, 8 : 8 + ROWS, 0:COLS] = total
        rows = pl.ds(z, 1)
        x[here, 7:8, 0:COLS] = sum_ref[z, 7:8, 0:COLS] + ring_ref[0, rows, :]
        x[here, 8 + ROWS : 9 + ROWS, 0:COLS] = sum_ref[z, 8 + ROWS : 9 + ROWS, 0:COLS] + ring_ref[1, rows, :]
        q = z & 3
        for i in range(ROWS // 8):
            s = pl.ds(pl.multiple_of((z >> 2) * ROWS + i * 8, 8), 8)
            left = pltpu.roll(side_ref[0, s, :], (COLS - 1) - q, 1)
            right = pltpu.roll(side_ref[1, s, :], (COLS - q) & (COLS - 1), 1)
            t = slice(8 + i * 8, 16 + i * 8)
            value = jnp.where(lane == COLS - 1, left, jnp.where(lane == 0, right, 0.0))
            x[here, t, COLS : 2 * COLS] = sum_ref[z, t, COLS : 2 * COLS] + value
        return carry

    def levels(q, carry):
        part(q).wait()
        return lax.fori_loop(0, 2, lambda n, c: level(4 * q + 2 * n + 1, level(4 * q + 2 * n, c)), carry)

    lax.fori_loop(0, LEVELS // 4, levels, 0)
    zero = jnp.zeros((ROWS, COLS), jnp.float32)
    x[0, 8 : 8 + ROWS, 0:COLS] = zero
    x[PLANES - 1, 8 : 8 + ROWS, 0:COLS] = zero
    return row


def image_at(x, absorption_ref, z, i):
    lane = iota((8, COLS), 1)
    here = z + 1
    s = slice(8 + i * 8, 16 + i * 8)
    up, down = slice(7 + i * 8, 15 + i * 8), slice(9 + i * 8, 17 + i * 8)
    now = x[here, s, 0:COLS]
    margin = x[here, s, COLS : 2 * COLS]
    back = jnp.where(lane == 0, roll(margin, 1), roll(now, 1))
    fore = jnp.where(lane == COLS - 1, roll(margin, -1), roll(now, -1))
    high = x[here - 1, s, 0:COLS] + x[here + 1, s, 0:COLS]
    around = (x[here, up, 0:COLS] + x[here, down, 0:COLS]) + (back + fore)
    diagonal = absorption_ref[z, i * 8 : i * 8 + 8, :] + (4.0 + 2.0 * vertical)
    return now, diagonal * now - around - vertical * high


def total_of(value):
    return jnp.sum(jnp.sum(value, axis=0, keepdims=True), axis=1, keepdims=True)


def scalars(told_ref):
    totals = jnp.sum(told_ref[...], axis=0, keepdims=True)
    return totals[:, 64:65], totals[:, 65:66]


def first_coarse_kernel(
    place_ref, told_ref, coarse_ref, basis_hbm, low_ref, high_ref, left_ref, right_ref, sum_ref, source_ref, absorption_ref,
    direction_ref, image_ref, ahead_ref, behind_ref, out_ref, x, own_c, edge_c, ring_ref, side_ref, basis_ref, sems, sums_ref,
):
    place = Place(place_ref, told_ref)
    row = add_coarse(place, told_ref, coarse_ref, basis_hbm, basis_ref, sems, low_ref, high_ref, left_ref, right_ref, 4, sum_ref, x,
                     own_c, edge_c, ring_ref, side_ref)
    zero = jnp.zeros((8, COLS), jnp.float32)

    def images(z, carry):
        weight, curve = carry
        for i in range(ROWS // 8):
            s = slice(i * 8, i * 8 + 8)
            now, image = image_at(x, absorption_ref, z, i)
            direction_ref[z, s] = now
            image_ref[z, s] = image
            if i >= 2:
                ahead_ref[z, (i - 2) * 8 : (i - 1) * 8] = image
            else:
                behind_ref[z, s] = image
            weight = weight + source_ref[z, s] * sum_ref[z, 8 + i * 8 : 16 + i * 8, 0:COLS]
            curve = curve + now * image
        return weight, curve

    weight, curve = lax.fori_loop(0, LEVELS, images, (zero, zero), unroll=2)
    half = VECTORS // 2
    for part in range(2):

        def level(z, sums):
            image = image_ref[z]
            return tuple(
                sums[k] + fold_rows(basis_ref[part * half + k, z].astype(jnp.float32) * image) for k in range(half)
            )

        sums = lax.fori_loop(0, LEVELS, level, (zero,) * half)
        for k in range(half):
            sums_ref[part * half + k : part * half + k + 1] = jnp.sum(sums[k], axis=0, keepdims=True)
    lane = iota((1, COLS), 1)
    row = jnp.where(lane < VECTORS, row, 0.0)
    mine = told_ref[pl.ds(place.index(0, 0), 1), :]
    told = roll(row, VECTORS)
    told = told + jnp.where(lane == 64, total_of(weight) + total_of(row * mine), 0.0)
    told = told + jnp.where(lane == 65, total_of(curve), 0.0)
    out_ref[...] = row_of_sums(sums_ref[...]) + told


def second_coarse_kernel(
    place_ref, told_ref, coarse_ref, basis_hbm, low_ref, high_ref, left_ref, right_ref, sum_ref, source_ref, absorption_ref,
    again_ref, first_sum_ref, direction_ref, first_ref,
    residual_ref, precond_ref, image_ref, out_ref, x, own_c, edge_c, ring_ref, side_ref, basis_ref, sems,
):
    place = Place(place_ref, told_ref)
    row = add_coarse(place, told_ref, coarse_ref, basis_hbm, basis_ref, sems, low_ref, high_ref, left_ref, right_ref, 4, sum_ref, x,
                     own_c, edge_c, ring_ref, side_ref)
    weight0, curve0 = scalars(again_ref)
    step = weight0 / curve0
    zero = jnp.zeros((8, COLS), jnp.float32)

    def images(z, sums):
        weight, own, cross = sums
        for i in range(ROWS // 8):
            s = slice(i * 8, i * 8 + 8)
            t = slice(8 + i * 8, 16 + i * 8)
            now, image = image_at(x, absorption_ref, z, i)
            direction, first = direction_ref[z, s], first_ref[z, s]
            residual = source_ref[z, s] - step * first
            precond = direction - step * now
            image = first - step * image
            residual_ref[z, s] = residual
            precond_ref[z, s] = precond
            image_ref[z, s] = image
            weight = weight + residual * (first_sum_ref[z, t, 0:COLS] - step * sum_ref[z, t, 0:COLS])
            own = own + precond * image
            cross = cross + (precond * first + direction * image)
        return weight, own, cross

    weight, own, cross = lax.fori_loop(0, LEVELS, images, (zero, zero, zero), unroll=2)
    mine = pl.ds(place.index(0, 0), 1)
    lane = iota((1, COLS), 1)
    again = again_ref[mine, :]
    projected = told_ref[mine, :] - step * again
    coarse = roll(again, -VECTORS) - step * row
    both = jnp.where(lane < VECTORS, projected * coarse, 0.0)
    told = jnp.where(lane == 0, total_of(weight) + total_of(both), 0.0)
    told = told + jnp.where(lane == 1, total_of(own), 0.0) + jnp.where(lane == 2, total_of(cross), 0.0)
    out_ref[...] = jnp.broadcast_to(told, (COLS, COLS))


def last_kernel(again_ref, last_ref, direction_ref, first_ref, residual_ref, precond_ref, image_ref, x_ref, r_ref):
    weight0, curve0 = scalars(again_ref)
    step0 = weight0 / curve0
    totals = jnp.sum(last_ref[...], axis=0, keepdims=True)
    weight1, own, cross = totals[:, 0:1], totals[:, 1:2], totals[:, 2:3]
    ratio = weight1 / weight0
    step1 = weight1 / (own + ratio * (cross + ratio * curve0))

    def level(z, carry):
        direction = direction_ref[z]
        x_ref[z] = step0 * direction + step1 * (precond_ref[z] + ratio * direction)
        r_ref[z] = residual_ref[z] - step1 * (image_ref[z] + ratio * first_ref[z])
        return carry

    lax.fori_loop(0, LEVELS, level, 0, unroll=4)


def shards(source, absorption, basis, coarse_inverse, margin_width, coarse_slot):
    block = jax.ShapeDtypeStruct((LEVELS, ROWS, COLS), jnp.float32)
    slab = jax.ShapeDtypeStruct((LEVELS, EDGE, COLS), jnp.float32)
    message = pltpu.HBM((COLS, COLS), jnp.float32)
    params = pltpu.CompilerParams(vmem_limit_bytes=VMEM_LIMIT)

    def scratch(*shape):
        return pltpu.VMEM(shape, jnp.float32)

    coarse_scratch = [
        scratch(PLANES, INNER, 2 * COLS), scratch(VECTORS, COLS), scratch(2 * VECTORS, COLS),
        scratch(2, LEVELS, COLS), scratch(2, 2 * TALL, COLS),
        pltpu.VMEM(basis.shape, basis.dtype), pltpu.SemaphoreType.DMA((LEVELS // 4,)),
    ]
    hbm = pl.BlockSpec(memory_space=pltpu.HBM)
    def in_hbm(value):
        return pltpu.with_memory_space_constraint(value, pltpu.HBM)

    place = jnp.stack(
        [lax.axis_index("gx"), lax.axis_index("gy"), lax.axis_size("gx"), lax.axis_size("gy")]
    ).astype(jnp.int32)
    table = jnp.array(list(zip(*chebyshev_table())), jnp.float32)
    rows, ahead, behind, sides = first_projection(
        source, absorption, basis, coarse_slot, margin_width
    )
    low, high = exchange(ahead, behind, "gx")
    told = everyone(rows)
    fields = [pl.BlockSpec(memory_space=pltpu.HBM)] + [VMEM_SPEC] * 2 + [FIELDS_SPEC] * 2 + [VMEM_SPEC]
    strips = exchange(
        *pack(first_pack_kernel, fields, 6, told, source, absorption, low, high, in_hbm(sides)), "gy"
    )
    coarse = everyone(solve_rows(told, told, coarse_inverse))
    first_sum = smooth(place, table, told, source, low, high, strips, absorption)
    edges = (low, high, *strips)
    direction, image, ahead, behind, rows = pl.pallas_call(
        first_coarse_kernel,
        in_specs=[SMEM_SPEC] + [VMEM_SPEC] * 2 + [hbm] + [VMEM_SPEC] * 7,
        out_shape=[block, block, slab, slab, message],
        scratch_shapes=coarse_scratch + [scratch(VECTORS, COLS)],
        compiler_params=params,
        name="direction_and_image",
    )(place, told, coarse, in_hbm(basis), *edges, first_sum, source, absorption)
    low_w, high_w = exchange(ahead, behind, "gx")
    again = everyone(rows)
    strips_w = exchange(*pack(pack_kernel, [VMEM_SPEC] * 3, 2, image, low_w, high_w), "gy")
    coarse = everyone(solve_rows(again, told, in_hbm(coarse_inverse)))
    second_sum = smooth(place, table, told, image, low_w, high_w, strips_w, absorption, edges)
    residual, precond, precond_image, rows = pl.pallas_call(
        second_coarse_kernel,
        in_specs=[SMEM_SPEC] + [VMEM_SPEC] * 2 + [hbm] + [VMEM_SPEC] * 11,
        out_shape=[block, block, block, message],
        scratch_shapes=coarse_scratch,
        compiler_params=params,
        name="second_images",
    )(place, told, coarse, in_hbm(basis), *edges, in_hbm(second_sum), source, absorption, again, first_sum, direction, image)
    last = everyone(rows)
    concentration, residual = pl.pallas_call(
        last_kernel, out_shape=[block, block], compiler_params=params, name="update"
    )(again, last, direction, image, residual, precond, precond_image)
    return (concentration, residual)


def solution(mesh):
    return jax.shard_map(
        shards,
        mesh=mesh,
        in_specs=(
            P(None, "gx", "gy"),
            P(None, "gx", "gy"),
            P(None, None, "gx", "gy"),
            P(("gx", "gy"), None),
            P("gx", "gy"),
            P("gx", "gy", None),
        ),
        out_specs=(P(None, "gx", "gy"), P(None, "gx", "gy")),
        check_vma=False,
    )
```

```python
import functools

import jax
import jax.numpy as jnp
from jax import lax
from jax.experimental import pallas as pl
from jax.experimental.pallas import tpu as pltpu
from jax.sharding import PartitionSpec as P

KCHEB = 9
AXES = ("gx", "gy")
LEVELS = 16
ROWS = 32
COLS = 128
VECTORS = 32
EDGE = 16
TALL = ROWS + 2 * EDGE
HIGHEST = lax.Precision.HIGHEST

lowest_rate = 0.05
highest_rate = 18.5
vertical = 2.0
theta = 0.5 * (highest_rate + lowest_rate)
delta = 0.5 * (highest_rate - lowest_rate)
VMEM_LIMIT = 24 * 1024 * 1024
FIRST_LIMIT = 58 * 1024 * 1024


def chebyshev_values():
    ratio = theta / delta
    values = [1.0, ratio]
    while len(values) <= KCHEB:
        values.append(2.0 * ratio * values[-1] - values[-2])
    return values


def chebyshev_table():
    return chebyshev_values()[1:KCHEB]


def iota(shape, dim):
    return lax.broadcasted_iota(jnp.int32, shape, dim)


def roll(value, shift):
    return pltpu.roll(value, shift % COLS, 1)


def exchange(forward_value, backward_value, axis):
    count = lax.axis_size(axis)
    forward = [(i, i + 1) for i in range(count - 1)]
    backward = [(target, source) for source, target in forward]
    return lax.ppermute(forward_value, axis, forward), lax.ppermute(backward_value, axis, backward)


def everyone(rows):
    return lax.all_to_all(rows, AXES, 0, 0, tiled=True)


def row_of_sums(sums):
    padded = jnp.concatenate([sums, jnp.zeros((COLS - VECTORS, COLS), jnp.float32)], 0)
    ones = jnp.ones((COLS, COLS), jnp.float32)
    return lax.dot_general(
        ones, padded, (((1,), (1,)), ((), ())), precision=HIGHEST, preferred_element_type=jnp.float32
    )


def fold_rows(product):
    return (product[0:8] + product[8:16]) + (product[16:24] + product[24:32])


def first_kernel(
    field_ref, coefficient_ref, basis_ref, slots_ref, margin_ref,
    out_ref, ahead_ref, behind_ref, sides_ref, sums_ref, edges_ref,
):
    step = pl.program_id(0)
    group = basis_ref.shape[0]

    @pl.when(step == 0)
    def _():
        edges_ref[...] = jnp.zeros_like(edges_ref)

        def level(z, carry):
            ahead_ref[z] = field_ref[z, ROWS - EDGE :, :]
            behind_ref[z] = field_ref[z, :EDGE, :]
            ahead_ref[LEVELS + z] = coefficient_ref[z, ROWS - EDGE :, :]
            behind_ref[LEVELS + z] = coefficient_ref[z, :EDGE, :]
            return carry

        lax.fori_loop(0, LEVELS, level, 0)

    def level(z, sums):
        field = field_ref[z]
        new = []
        for j in range(group):
            values = basis_ref[j, z].astype(jnp.float32)
            new.append(sums[j] + fold_rows(values * field))
            at = 2 * LEVELS + step * group + j
            behind_ref[at, pl.ds(z, 1), :] = values[0:1]
            ahead_ref[at, pl.ds(z, 1), :] = values[ROWS - 1 : ROWS]
        return tuple(new)

    zero = jnp.zeros((8, COLS), jnp.float32)
    sums = lax.fori_loop(0, LEVELS, level, (zero,) * group, unroll=2)
    for j in range(group):
        sums_ref[pl.ds(step * group + j, 1), :] = jnp.sum(sums[j], axis=0, keepdims=True)
    from_lane, to_lane = iota((COLS, COLS), 0), iota((COLS, COLS), 1)
    picks = []
    for j in range(group):
        k = step * group + j
        pick = ((from_lane == 0) & (to_lane == k)) | ((from_lane == COLS - 1) & (to_lane == VECTORS + k))
        picks.append(jnp.where(pick, 1.0, 0.0).astype(jnp.bfloat16))
    values = jnp.concatenate([basis_ref[j].reshape(LEVELS * ROWS, COLS) for j in range(group)], axis=1)
    edges_ref[...] += jnp.dot(values, jnp.concatenate(picks, 0), preferred_element_type=jnp.float32)

    @pl.when(step == pl.num_programs(0) - 1)
    def _():
        told = jnp.concatenate(
            [
                jnp.zeros((1, VECTORS), jnp.float32),
                slots_ref[0].astype(jnp.float32),
                margin_ref[...].astype(jnp.float32),
                jnp.zeros((1, COLS - 65), jnp.float32),
            ],
            axis=1,
        )
        out_ref[...] = row_of_sums(sums_ref[...]) + told
        place = iota((ROWS, COLS), 1) >> 5
        for n in range(LEVELS // 4):
            left = jnp.zeros((ROWS, COLS), jnp.float32)
            right = left
            for q in range(4):
                z = 4 * n + q
                value = edges_ref[z * ROWS : (z + 1) * ROWS]
                left = jnp.where(place == q, roll(value, VECTORS * q), left)
                right = jnp.where(place == q, roll(value, VECTORS * (q - 1)), right)
            sides_ref[n] = left
            sides_ref[LEVELS // 4 + n] = right


def first_projection(field, coefficient, basis, slots, margin):
    group = 8
    rows = 2 * LEVELS + VECTORS
    edge_rows = jax.ShapeDtypeStruct((rows, LEVELS, COLS), jnp.float32)
    edge_cols = jax.ShapeDtypeStruct((LEVELS // 2, ROWS, COLS), jnp.float32)
    block_spec = pl.BlockSpec((LEVELS, ROWS, COLS), lambda i: (0, 0, 0))
    rows_spec = pl.BlockSpec(edge_rows.shape, lambda i: (0, 0, 0))
    cols_spec = pl.BlockSpec(edge_cols.shape, lambda i: (0, 0, 0))
    return pl.pallas_call(
        first_kernel,
        grid=(VECTORS // group,),
        in_specs=[
            block_spec,
            block_spec,
            pl.BlockSpec((group, LEVELS, ROWS, COLS), lambda i: (i, 0, 0, 0)),
            pl.BlockSpec(slots.shape, lambda i: (0, 0, 0)),
            pl.BlockSpec(margin.shape, lambda i: (0, 0)),
        ],
        out_specs=[pl.BlockSpec((COLS, COLS), lambda i: (0, 0)), rows_spec, rows_spec, cols_spec],
        out_shape=[jax.ShapeDtypeStruct((COLS, COLS), jnp.float32), edge_rows, edge_rows, edge_cols],
        scratch_shapes=[
            pltpu.VMEM((VECTORS, COLS), jnp.float32), pltpu.VMEM((LEVELS * ROWS, COLS), jnp.float32)
        ],
        compiler_params=pltpu.CompilerParams(vmem_limit_bytes=FIRST_LIMIT),
        name="first_projection",
    )(field, coefficient, basis, slots, margin)


def coarse_rows(told_ref, slots_ref, inverse_hbm, out_ref, inverse_ref, sem):
    copy = pltpu.make_async_copy(inverse_hbm, inverse_ref, sem)
    copy.start()
    told = told_ref[...]
    slots = slots_ref[...]
    turned = told.T
    slots_turned = slots.T
    lane = iota((COLS, COLS), 1)
    sub = iota((VECTORS, COLS), 0)
    placed = jnp.zeros((3 * VECTORS, COLS), jnp.float32)
    for k in range(VECTORS):
        slot_column = slots[:, VECTORS + k : VECTORS + k + 1].astype(jnp.int32)
        ones = jnp.where((slot_column & 127) == lane, 1.0, 0.0).astype(jnp.bfloat16)
        slot_row = slots_turned[VECTORS + k : VECTORS + k + 1, :].astype(jnp.int32)
        values = turned[k : k + 1, :]
        spread = jnp.where((slot_row >> 7) == sub, values, 0.0)
        first = spread.astype(jnp.bfloat16)
        rest = spread - first.astype(jnp.float32)
        second = rest.astype(jnp.bfloat16)
        third = (rest - second.astype(jnp.float32)).astype(jnp.bfloat16)
        parts = jnp.concatenate([first, second, third], 0)
        placed = placed + jnp.dot(parts, ones, preferred_element_type=jnp.float32)
    placed = placed[:VECTORS] + placed[VECTORS : 2 * VECTORS] + placed[2 * VECTORS :]
    total = jnp.zeros((VECTORS, COLS), jnp.float32)
    copy.wait()
    for high in range(VECTORS):
        total = total + inverse_ref[:, high * COLS : (high + 1) * COLS] * placed[high : high + 1]
    out_ref[...] = row_of_sums(total)


def pack_strips(parts, forward_ref, backward_ref, at):
    def levels(group, carry):
        row = 0
        for part, start in parts:
            height = EDGE if part.shape[1] == EDGE else ROWS
            lane = iota((height, COLS), 1)
            ahead = jnp.zeros((height, COLS), jnp.float32)
            behind = ahead
            for j in range(8):
                value = part[start + group * 8 + j]
                mine = (lane >= EDGE * j) & (lane < EDGE * (j + 1))
                ahead = jnp.where(mine, roll(value, EDGE * j - (COLS - EDGE)), ahead)
                behind = jnp.where(mine, roll(value, EDGE * j), behind)
            forward_ref[at + group, row : row + height, :] = ahead
            backward_ref[at + group, row : row + height, :] = behind
            row += height
        return carry

    lax.fori_loop(0, LEVELS // 8, levels, 0)


def first_pack_kernel(
    told_ref, source_ref, absorption_ref, low_ref, high_ref, sides_hbm, forward_ref, backward_ref, sides_ref, sem
):
    copy = pltpu.make_async_copy(sides_hbm, sides_ref, sem)
    copy.start()
    for f, block in enumerate((source_ref, absorption_ref)):
        pack_strips(((low_ref, LEVELS * f), (block, 0), (high_ref, LEVELS * f)), forward_ref, backward_ref, 2 * f)
    copy.wait()
    for n in range(LEVELS // 8):
        for half in range(2):
            rows = slice(half * ROWS, (half + 1) * ROWS)
            forward_ref[4 + n, rows, :] = sides_ref[LEVELS // 4 + 2 * n + half]
            backward_ref[4 + n, rows, :] = sides_ref[2 * n + half]


def pack_kernel(block_ref, low_ref, high_ref, forward_ref, backward_ref):
    pack_strips(((low_ref, 0), (block_ref, 0), (high_ref, 0)), forward_ref, backward_ref, 0)


FIELDS_SPEC = pl.BlockSpec((2 * LEVELS, EDGE, COLS), lambda i: (0, 0, 0))
VMEM_SPEC = pl.BlockSpec(memory_space=pltpu.VMEM)
HBM_SPEC = pl.BlockSpec(memory_space=pltpu.HBM)
SMEM_SPEC = pl.BlockSpec(memory_space=pltpu.SMEM)


def pack(kernel, specs, strips, scratch, *operands):
    strips = jax.ShapeDtypeStruct((strips, TALL, COLS), jnp.float32)
    return pl.pallas_call(
        kernel,
        grid=(1,),
        in_specs=specs,
        out_shape=[strips, strips],
        scratch_shapes=scratch,
        compiler_params=pltpu.CompilerParams(vmem_limit_bytes=VMEM_LIMIT),
        cost_estimate=pl.CostEstimate(flops=2000000, bytes_accessed=2000000, transcendentals=0),
        name="strips",
    )(*operands)


def solve_rows(*operands):
    return pl.pallas_call(
        coarse_rows,
        in_specs=[VMEM_SPEC] * 2 + [HBM_SPEC],
        out_shape=pltpu.HBM((COLS, COLS), jnp.float32),
        scratch_shapes=[pltpu.VMEM((VECTORS, COLS * VECTORS), jnp.float32), pltpu.SemaphoreType.DMA],
        compiler_params=pltpu.CompilerParams(vmem_limit_bytes=VMEM_LIMIT),
        name="coarse_rows",
    )(*operands)


class Place:
    def __init__(self, place_ref, told_ref):
        self.row = place_ref[0]
        self.col = place_ref[1]
        self.rows = place_ref[2]
        self.cols = place_ref[3]
        self.told_ref = told_ref

    def index(self, down, right):
        row = jnp.clip(self.row + down, 0, self.rows - 1)
        col = jnp.clip(self.col + right, 0, self.cols - 1)
        return row * self.cols + col

    def margin(self, down, right):
        row, col = self.row + down, self.col + right
        real = (row >= 0) & (row < self.rows) & (col >= 0) & (col < self.cols)
        margin = self.told_ref[pl.ds(self.index(down, right), 1), :][:, 64:65]
        return jnp.where(real, margin.astype(jnp.int32), -4096)


def masks(place, own_ref, beside_ref, strip_ref):
    shape = (TALL, COLS)
    row = iota(shape, 0) - EDGE
    lane = iota(shape, 1)
    top, bottom = -ROWS * place.row, ROWS * (place.rows - place.row)
    first, last = -COLS * place.col, COLS * (place.cols - place.col)
    row_real = (row >= top) & (row < bottom)
    m = {(i, j): place.margin(i, j) for i in (-1, 0, 1) for j in (-1, 0, 1)}
    upper, lower = row < 8, row >= ROWS - 8
    for tile in range(2):
        col = lane if tile == 0 else jnp.where(lane < 64, lane + COLS, lane - COLS)
        real = row_real & (col >= first) & (col < last)
        if tile == 1:
            real = real & ((lane < EDGE) | (lane >= COLS - EDGE))

        def across(margin):
            return (col >= -margin) & (col < COLS + margin)

        own = m[0, 0]
        inside = real & (row >= -own) & (row < ROWS + own) & across(own)
        own_ref[tile] = jnp.where(inside, 1.0, 0.0)
        above, below = m[-1, 0], m[1, 0]
        inside = (upper & (row < above) & across(above)) | (lower & (row >= ROWS - below) & across(below))
        beside_ref[tile] = jnp.where(real & inside, 1.0, 0.0)
    group = ((lane + EDGE) & 127) >> 5
    away = ((lane + EDGE) & 31) - EDGE
    inside = row < -4096
    for place_of, side in ((0, -1), (2, 1)):
        col = away if side < 0 else away + COLS
        real = row_real & (col >= first) & (col < last)

        def reached(margin):
            return (away < margin) if side < 0 else (away >= -margin)

        level = m[0, side]
        inside = inside | (
            (group == place_of) & real & (row >= -level) & (row < ROWS + level) & reached(level)
        )
        above, below = m[-1, side], m[1, side]
        corner = (upper & (row < above) & reached(above)) | (
            lower & (row >= ROWS - below) & reached(below)
        )
        inside = inside | ((group == place_of + 1) & real & corner)
    strip_ref[...] = jnp.where(inside, 1.0, 0.0)


def tiles_of(parts, start, strips, at, z, i):
    low, block, high = parts
    from_left, from_right = strips
    lane = iota((8, COLS), 1)
    if i < 2:
        center = low[start + z, i * 8 : i * 8 + 8, :]
    elif i < 6:
        center = block[z, (i - 2) * 8 : (i - 2) * 8 + 8, :]
    else:
        center = high[start + z, (i - 6) * 8 : (i - 6) * 8 + 8, :]
    s = slice(i * 8, i * 8 + 8)
    group, shift = at + (z >> 3), EDGE * (z & 7)
    left = pltpu.roll(from_left[group, s, :], (COLS - EDGE) - shift, 1)
    right = pltpu.roll(from_right[group, s, :], (COLS - shift) & (COLS - 1), 1)
    margin = jnp.where(lane >= COLS - EDGE, left, jnp.where(lane < EDGE, right, 0.0))
    at_left = jnp.where(lane >= 64, margin, center)
    at_right = jnp.where(lane < 64, margin, center)
    near = (lane < EDGE) | (lane >= COLS - EDGE)
    others = jnp.where(lane < 80, roll(at_right, 64), roll(at_right, 96))
    packed = jnp.where(near, at_left, jnp.where(lane < 48, roll(at_left, 32), others))
    return center, margin, packed


UNROLL = 8
UNROLL_BEGIN = 2
UNROLL_FINISH = 2
PLANES = LEVELS + 2
BESIDE_TILES = (1, 2, 5, 6)


def smooth_kernel(same, place_ref, table_ref, told_ref, block_ref, low_ref, high_ref, left_ref, right_ref, absorption_ref, *refs):
    if same:
        low_c, high_c, left_c, right_c = low_ref, high_ref, left_ref, right_ref
    else:
        low_c, high_c, left_c, right_c = refs[:4]
        refs = refs[4:]
    (
        out_ref, own_m, beside_m, strip_m, own, beside, strip, own_y, beside_y, strip_y,
        wide_r, strip_r, diag, strip_diag,
    ) = refs
    field_start, coef_start, coef_at = 0, LEVELS, 2
    masks(Place(place_ref, told_ref), own_m, beside_m, strip_m)
    base = 2.0 * (theta - (4.0 + 2.0 * vertical)) / delta
    last = 1.0 / chebyshev_values()[KCHEB]
    zero = jnp.zeros((8, COLS), jnp.float32)
    lane = iota((8, COLS), 1)
    lanes = [slice(0, COLS), slice(COLS, 2 * COLS)]

    def clear(n, carry):
        at = n * (PLANES - 1)
        for i in range(8):
            s = slice(i * 8, i * 8 + 8)
            for t in range(2):
                for x in (own, own_y, beside, beside_y):
                    x[at, t, s] = zero
            strip[at, 0, s] = zero
            strip_y[at, 0, s] = zero
        return carry

    lax.fori_loop(0, 2, clear, 0)

    def begin(z, carry):
        at = z + 1
        for i in range(8):
            s = slice(i * 8, i * 8 + 8)
            tiles = tiles_of((low_ref, block_ref, high_ref), field_start, (left_ref, right_ref), 0, z, i)
            inner = 1 <= i < 7
            for t in range(2):
                guess = tiles[t] * (1.0 / delta)
                value = guess if t == 0 and 2 <= i < 6 else guess * own_m[t, s]
                own[at, t, s] = value
                own_y[at, t, s] = zero
                if inner:
                    wide_r[z, t, s] = guess + guess
                beside_y[at, t, s] = zero
                beside[at, t, s] = zero if i in (3, 4) else guess * beside_m[t, s]
            guess = tiles[2] * (1.0 / delta)
            strip[at, 0, s] = guess * strip_m[s]
            strip_y[at, 0, s] = zero
            if inner:
                strip_r[z, 0, s] = guess + guess
                tiles = tiles_of((low_c, absorption_ref, high_c), coef_start, (left_c, right_c), coef_at, z, i)
                diag[z, 0, s] = base - (2.0 / delta) * tiles[0]
                diag[z, 1, s] = base - (2.0 / delta) * tiles[1]
                strip_diag[z, 0, s] = base - (2.0 / delta) * tiles[2]
        return carry

    lax.fori_loop(0, LEVELS, begin, 0, unroll=UNROLL_BEGIN)
    at_first, at_last = lane == 0, lane == COLS - 1

    def step(here, x, y, r, a, mask, width, i, amount):
        s = slice(i * 8, i * 8 + 8)
        up, down = slice(i * 8 - 1, i * 8 + 7), slice(i * 8 + 1, i * 8 + 9)
        z = here - 1
        now = [x[here, t, s] for t in range(width)]
        back = [roll(v, 1) for v in now]
        fore = [roll(v, -1) for v in now]
        if width == 2:
            back = [jnp.where(at_first, back[1], back[0]), jnp.where(at_first, back[0], back[1])]
            fore = [jnp.where(at_last, fore[1], fore[0]), jnp.where(at_last, fore[0], fore[1])]
        for t in range(width):
            high = x[here - 1, t, s] + x[here + 1, t, s]
            around = (x[here, t, up] + x[here, t, down]) + (back[t] + fore[t])
            around = around + (high + high)
            after = (a[z, t, s] * now[t] + amount * r[z, t, s]) + ((2.0 / delta) * around - y[here, t, s])
            if mask[t] is not None:
                after = after * mask[t]
            y[here, t, s] = after

    first = ((own, own_y), (beside, beside_y), (strip, strip_y))
    second = tuple((y, x) for x, y in first)

    def sweep(n, arrays):
        amount = table_ref[n]
        own, beside, strip = arrays

        def level(z, carry):
            here = z + 1
            for i in range(1, 7):
                s = slice(i * 8, i * 8 + 8)
                free = None if 2 <= i < 6 else own_m[0, s]
                step(here, *own, wide_r, diag, [free, own_m[1, s]], 2, i, amount)
                if i in BESIDE_TILES:
                    step(here, *beside, wide_r, diag, [beside_m[0, s], beside_m[1, s]], 2, i, amount)
                step(here, *strip, strip_r, strip_diag, [strip_m[s]], 1, i, amount)
            return carry

        lax.fori_loop(0, LEVELS, level, 0, unroll=UNROLL)

    def pair(n, carry):
        sweep(2 * n, first)
        sweep(2 * n + 1, second)
        return carry

    lax.fori_loop(0, (KCHEB - 1) // 2, pair, 0)
    near_first, near_last = lane < EDGE, lane >= COLS - EDGE

    def finish(z, carry):
        at = z + 1
        for i in range(1, 7):
            s = slice(i * 8, i * 8 + 8)
            out = slice(i * 8 - 8, i * 8)
            value = strip[at, 0, s]
            at_left = value + roll(value, -32)
            at_right = roll(at_left, 64)
            first = jnp.where(near_first, at_left, jnp.where(near_last, at_right, 0.0))
            second = jnp.where(near_last, at_left, jnp.where(near_first, at_right, 0.0))
            first = first + own[at, 0, s]
            second = second + own[at, 1, s]
            if i in BESIDE_TILES:
                first = first + beside[at, 0, s]
                second = second + beside[at, 1, s]
            out_ref[z, out, lanes[0]] = first * last
            out_ref[z, out, lanes[1]] = second * last
        return carry

    lax.fori_loop(0, LEVELS, finish, 0, unroll=UNROLL_FINISH)


def smooth(place, table, told, block, low, high, strips, absorption, coefficient=None):
    wide = (2, TALL, COLS)
    thin = (1, TALL, COLS)

    def scratch(*shape):
        return pltpu.VMEM(shape, jnp.float32)

    more = () if coefficient is None else coefficient
    specs = [SMEM_SPEC] * 2 + [VMEM_SPEC] * 2 + [VMEM_SPEC if more else FIELDS_SPEC] * 2 + [VMEM_SPEC] * 3
    if more:
        specs += [FIELDS_SPEC] * 2 + [VMEM_SPEC] * 2
    return pl.pallas_call(
        functools.partial(smooth_kernel, not more),
        grid=(1,),
        in_specs=specs,
        out_shape=(pltpu.HBM if more else jax.ShapeDtypeStruct)((LEVELS, INNER, 2 * COLS), jnp.float32),
        scratch_shapes=[
            scratch(*wide), scratch(*wide), scratch(TALL, COLS),
            scratch(PLANES, *wide), scratch(PLANES, *wide), scratch(PLANES, *thin),
            scratch(PLANES, *wide), scratch(PLANES, *wide), scratch(PLANES, *thin),
            scratch(LEVELS, *wide), scratch(LEVELS, *thin),
            scratch(LEVELS, *wide), scratch(LEVELS, *thin),
        ],
        compiler_params=pltpu.CompilerParams(vmem_limit_bytes=VMEM_LIMIT),
        cost_estimate=pl.CostEstimate(flops=2000000, bytes_accessed=54000000, transcendentals=0),
        name="smoother",
    )(place, table, told, block, low, high, *strips, absorption, *more)


INNER = ROWS + 16


def slots_of(place, told_ref, moves):
    lane = iota((1, COLS), 1)
    slots = jnp.zeros((1, COLS), jnp.float32)
    for n, (down, right) in enumerate(moves):
        row = roll(told_ref[pl.ds(place.index(down, right), 1), :], VECTORS * (n - 1))
        slots = jnp.where((lane >> 5) == n, row, slots)
    return slots.astype(jnp.int32)


def coarse_at(coarse_turned, slots):
    pick = jnp.where(iota((COLS, COLS), 0) == (slots >> 5), 1.0, 0.0)
    found = jnp.dot(coarse_turned, pick, precision=HIGHEST, preferred_element_type=jnp.float32)
    found = jnp.where(iota((VECTORS, COLS), 0) == (slots & 31), found, 0.0)
    return jnp.sum(found, axis=0, keepdims=True)


def add_coarse(place, told_ref, coarse_ref, basis_hbm, basis_ref, sems, low_ref, high_ref, left_ref, right_ref, at, sum_ref, x,
               own_c, edge_c, ring_ref, side_ref, ready=None):
    def part(q):
        levels = pl.ds(q * 4, 4)
        return pltpu.make_async_copy(basis_hbm.at[:, levels], basis_ref.at[:, levels], sems.at[q])

    for q in range(LEVELS // 4):
        part(q).start()
    turned = coarse_ref[...].T[:VECTORS]
    row = coarse_at(turned, slots_of(place, told_ref, ((0, 0), (-1, 0), (1, 0), (0, -1))))
    other = coarse_at(turned, slots_of(place, told_ref, ((0, 1),)))
    lane = iota((8, COLS), 1)
    lane_row = iota((1, COLS), 1)
    column = jnp.broadcast_to(row, (COLS, COLS)).T
    own_c[...] = column[:VECTORS]
    edge_c[...] = column[VECTORS : 3 * VECTORS]
    for n, edge in ((0, low_ref), (1, high_ref)):

        def vector(k, total):
            return total + edge[2 * LEVELS + k] * edge_c[pl.ds(n * VECTORS + k, 1), :]

        ring_ref[n] = lax.fori_loop(0, VECTORS, vector, jnp.zeros((LEVELS, COLS), jnp.float32))
    which = iota((COLS, COLS), 0) >> 5
    for n, (edge, values) in enumerate(((left_ref, roll(row, VECTORS)), (right_ref, other))):
        values = jnp.where(lane_row < VECTORS, values, 0.0)
        values = values + roll(values, 32) + roll(values, 64) + roll(values, 96)
        weights = jnp.broadcast_to(values, (COLS, COLS)).T
        weights = jnp.where(iota((COLS, COLS), 1) == which, weights, 0.0)
        parts = edge[at : at + 2].reshape(2 * TALL, COLS)
        side_ref[n] = jnp.dot(parts, weights, precision=HIGHEST, preferred_element_type=jnp.float32)

    def level(z, carry):
        total = sum_ref[z, 8 : 8 + ROWS, 0:COLS]
        for k in range(VECTORS):
            total = total + basis_ref[k, z].astype(jnp.float32) * own_c[k : k + 1]
        here = z + 1
        x[here, 8 : 8 + ROWS, 0:COLS] = total
        rows = pl.ds(z, 1)
        x[here, 7:8, 0:COLS] = sum_ref[z, 7:8, 0:COLS] + ring_ref[0, rows, :]
        x[here, 8 + ROWS : 9 + ROWS, 0:COLS] = sum_ref[z, 8 + ROWS : 9 + ROWS, 0:COLS] + ring_ref[1, rows, :]
        q = z & 3
        for i in range(ROWS // 8):
            s = pl.ds(pl.multiple_of((z >> 2) * ROWS + i * 8, 8), 8)
            left = pltpu.roll(side_ref[0, s, :], (COLS - 1) - q, 1)
            right = pltpu.roll(side_ref[1, s, :], (COLS - q) & (COLS - 1), 1)
            t = slice(8 + i * 8, 16 + i * 8)
            value = jnp.where(lane == COLS - 1, left, jnp.where(lane == 0, right, 0.0))
            x[here, t, COLS : 2 * COLS] = sum_ref[z, t, COLS : 2 * COLS] + value
        return carry

    if ready is not None:
        ready.wait()

    def levels(q, carry):
        part(q).wait()
        return lax.fori_loop(0, 2, lambda n, c: level(4 * q + 2 * n + 1, level(4 * q + 2 * n, c)), carry)

    lax.fori_loop(0, LEVELS // 4, levels, 0)
    zero = jnp.zeros((ROWS, COLS), jnp.float32)
    x[0, 8 : 8 + ROWS, 0:COLS] = zero
    x[PLANES - 1, 8 : 8 + ROWS, 0:COLS] = zero
    return row


def image_at(x, absorption_ref, z, i):
    lane = iota((8, COLS), 1)
    here = z + 1
    s = slice(8 + i * 8, 16 + i * 8)
    up, down = slice(7 + i * 8, 15 + i * 8), slice(9 + i * 8, 17 + i * 8)
    now = x[here, s, 0:COLS]
    margin = x[here, s, COLS : 2 * COLS]
    back = jnp.where(lane == 0, roll(margin, 1), roll(now, 1))
    fore = jnp.where(lane == COLS - 1, roll(margin, -1), roll(now, -1))
    high = x[here - 1, s, 0:COLS] + x[here + 1, s, 0:COLS]
    around = (x[here, up, 0:COLS] + x[here, down, 0:COLS]) + (back + fore)
    diagonal = absorption_ref[z, i * 8 : i * 8 + 8, :] + (4.0 + 2.0 * vertical)
    return now, diagonal * now - around - vertical * high


def total_of(value):
    return jnp.sum(jnp.sum(value, axis=0, keepdims=True), axis=1, keepdims=True)


def scalars(told_ref):
    totals = jnp.sum(told_ref[...], axis=0, keepdims=True)
    return totals[:, 64:65], totals[:, 65:66]


def first_coarse_kernel(
    place_ref, told_ref, coarse_ref, basis_hbm, low_ref, high_ref, left_ref, right_ref, sum_ref, source_ref, absorption_ref,
    direction_ref, image_ref, ahead_ref, behind_ref, out_ref, x, own_c, edge_c, ring_ref, side_ref, basis_ref, sems, sums_ref,
):
    place = Place(place_ref, told_ref)
    row = add_coarse(place, told_ref, coarse_ref, basis_hbm, basis_ref, sems, low_ref, high_ref, left_ref, right_ref, 4, sum_ref, x,
                     own_c, edge_c, ring_ref, side_ref)
    zero = jnp.zeros((8, COLS), jnp.float32)

    def images(z, carry):
        weight, curve = carry
        for i in range(ROWS // 8):
            s = slice(i * 8, i * 8 + 8)
            now, image = image_at(x, absorption_ref, z, i)
            direction_ref[z, s] = now
            image_ref[z, s] = image
            if i >= 2:
                ahead_ref[z, (i - 2) * 8 : (i - 1) * 8] = image
            else:
                behind_ref[z, s] = image
            weight = weight + source_ref[z, s] * sum_ref[z, 8 + i * 8 : 16 + i * 8, 0:COLS]
            curve = curve + now * image
        return weight, curve

    weight, curve = lax.fori_loop(0, LEVELS, images, (zero, zero), unroll=2)
    half = VECTORS // 2
    for part in range(2):

        def level(z, sums):
            image = image_ref[z]
            return tuple(
                sums[k] + fold_rows(basis_ref[part * half + k, z].astype(jnp.float32) * image) for k in range(half)
            )

        sums = lax.fori_loop(0, LEVELS, level, (zero,) * half)
        for k in range(half):
            sums_ref[part * half + k : part * half + k + 1] = jnp.sum(sums[k], axis=0, keepdims=True)
    lane = iota((1, COLS), 1)
    row = jnp.where(lane < VECTORS, row, 0.0)
    mine = told_ref[pl.ds(place.index(0, 0), 1), :]
    told = roll(row, VECTORS)
    told = told + jnp.where(lane == 64, total_of(weight) + total_of(row * mine), 0.0)
    told = told + jnp.where(lane == 65, total_of(curve), 0.0)
    out_ref[...] = row_of_sums(sums_ref[...]) + told


def second_coarse_kernel(
    place_ref, told_ref, coarse_ref, basis_hbm, low_ref, high_ref, left_ref, right_ref, sum_hbm, source_ref, absorption_ref,
    again_ref, first_sum_ref, direction_ref, first_ref,
    residual_ref, precond_ref, image_ref, out_ref, x, own_c, edge_c, ring_ref, side_ref, basis_ref, sems,
    sum_ref, sum_sem,
):
    copy = pltpu.make_async_copy(sum_hbm, sum_ref, sum_sem)
    copy.start()
    place = Place(place_ref, told_ref)
    row = add_coarse(place, told_ref, coarse_ref, basis_hbm, basis_ref, sems, low_ref, high_ref, left_ref, right_ref, 4, sum_ref, x,
                     own_c, edge_c, ring_ref, side_ref, copy)
    weight0, curve0 = scalars(again_ref)
    step = weight0 / curve0
    zero = jnp.zeros((8, COLS), jnp.float32)

    def images(z, sums):
        weight, own, cross = sums
        for i in range(ROWS // 8):
            s = slice(i * 8, i * 8 + 8)
            t = slice(8 + i * 8, 16 + i * 8)
            now, image = image_at(x, absorption_ref, z, i)
            direction, first = direction_ref[z, s], first_ref[z, s]
            residual = source_ref[z, s] - step * first
            precond = direction - step * now
            image = first - step * image
            residual_ref[z, s] = residual
            precond_ref[z, s] = precond
            image_ref[z, s] = image
            weight = weight + residual * (first_sum_ref[z, t, 0:COLS] - step * sum_ref[z, t, 0:COLS])
            own = own + precond * image
            cross = cross + (precond * first + direction * image)
        return weight, own, cross

    weight, own, cross = lax.fori_loop(0, LEVELS, images, (zero, zero, zero), unroll=2)
    mine = pl.ds(place.index(0, 0), 1)
    lane = iota((1, COLS), 1)
    again = again_ref[mine, :]
    projected = told_ref[mine, :] - step * again
    coarse = roll(again, -VECTORS) - step * row
    both = jnp.where(lane < VECTORS, projected * coarse, 0.0)
    told = jnp.where(lane == 0, total_of(weight) + total_of(both), 0.0)
    told = told + jnp.where(lane == 1, total_of(own), 0.0) + jnp.where(lane == 2, total_of(cross), 0.0)
    out_ref[...] = jnp.broadcast_to(told, (COLS, COLS))


def last_kernel(again_ref, last_ref, direction_ref, first_ref, residual_ref, precond_ref, image_ref, x_ref, r_ref):
    weight0, curve0 = scalars(again_ref)
    step0 = weight0 / curve0
    totals = jnp.sum(last_ref[...], axis=0, keepdims=True)
    weight1, own, cross = totals[:, 0:1], totals[:, 1:2], totals[:, 2:3]
    ratio = weight1 / weight0
    step1 = weight1 / (own + ratio * (cross + ratio * curve0))

    def level(z, carry):
        direction = direction_ref[z]
        x_ref[z] = step0 * direction + step1 * (precond_ref[z] + ratio * direction)
        r_ref[z] = residual_ref[z] - step1 * (image_ref[z] + ratio * first_ref[z])
        return carry

    lax.fori_loop(0, LEVELS, level, 0, unroll=4)


def shards(source, absorption, basis, coarse_inverse, margin_width, coarse_slot):
    block = jax.ShapeDtypeStruct((LEVELS, ROWS, COLS), jnp.float32)
    slab = jax.ShapeDtypeStruct((LEVELS, EDGE, COLS), jnp.float32)
    message = pltpu.HBM((COLS, COLS), jnp.float32)
    params = pltpu.CompilerParams(vmem_limit_bytes=VMEM_LIMIT)

    def scratch(*shape):
        return pltpu.VMEM(shape, jnp.float32)

    coarse_scratch = [
        scratch(PLANES, INNER, 2 * COLS), scratch(VECTORS, COLS), scratch(2 * VECTORS, COLS),
        scratch(2, LEVELS, COLS), scratch(2, 2 * TALL, COLS),
        pltpu.VMEM(basis.shape, basis.dtype), pltpu.SemaphoreType.DMA((LEVELS // 4,)),
    ]
    hbm = pl.BlockSpec(memory_space=pltpu.HBM)
    def in_hbm(value):
        return pltpu.with_memory_space_constraint(value, pltpu.HBM)

    place = jnp.stack(
        [lax.axis_index("gx"), lax.axis_index("gy"), lax.axis_size("gx"), lax.axis_size("gy")]
    ).astype(jnp.int32)
    table = jnp.array(chebyshev_table(), jnp.float32)
    rows, ahead, behind, sides = first_projection(
        source, absorption, basis, coarse_slot, margin_width
    )
    low, high = exchange(ahead, behind, "gx")
    told = everyone(rows)
    fields = [pl.BlockSpec(memory_space=pltpu.HBM)] + [VMEM_SPEC] * 2 + [FIELDS_SPEC] * 2 + [HBM_SPEC]
    strips = exchange(
        *pack(first_pack_kernel, fields, 6, [scratch(LEVELS // 2, ROWS, COLS), pltpu.SemaphoreType.DMA], told, source, absorption, low, high, in_hbm(sides)), "gy"
    )
    coarse = everyone(solve_rows(told, told, in_hbm(coarse_inverse)))
    first_sum = smooth(place, table, told, source, low, high, strips, absorption)
    edges = (low, high, *strips)
    direction, image, ahead, behind, rows = pl.pallas_call(
        first_coarse_kernel,
        in_specs=[SMEM_SPEC] + [VMEM_SPEC] * 2 + [hbm] + [VMEM_SPEC] * 7,
        out_shape=[block, block, slab, slab, message],
        scratch_shapes=coarse_scratch + [scratch(VECTORS, COLS)],
        compiler_params=params,
        name="direction_and_image",
    )(place, told, coarse, in_hbm(basis), *edges, first_sum, source, absorption)
    low_w, high_w = exchange(ahead, behind, "gx")
    again = everyone(rows)
    strips_w = exchange(*pack(pack_kernel, [VMEM_SPEC] * 3, 2, [], image, low_w, high_w), "gy")
    coarse = everyone(solve_rows(again, told, in_hbm(coarse_inverse)))
    second_sum = smooth(place, table, told, image, low_w, high_w, strips_w, absorption, edges)
    residual, precond, precond_image, rows = pl.pallas_call(
        second_coarse_kernel,
        in_specs=[SMEM_SPEC] + [VMEM_SPEC] * 2 + [hbm] + [VMEM_SPEC] * 4 + [hbm] + [VMEM_SPEC] * 6,
        out_shape=[block, block, block, message],
        scratch_shapes=coarse_scratch + [scratch(LEVELS, INNER, 2 * COLS), pltpu.SemaphoreType.DMA],
        compiler_params=params,
        name="second_images",
    )(place, told, coarse, in_hbm(basis), *edges, in_hbm(second_sum), source, absorption, again, first_sum, direction, image)
    last = everyone(rows)
    concentration, residual = pl.pallas_call(
        last_kernel, out_shape=[block, block], compiler_params=params, name="update"
    )(again, last, direction, image, residual, precond, precond_image)
    return (concentration, residual)


def solution(mesh):
    return jax.shard_map(
        shards,
        mesh=mesh,
        in_specs=(
            P(None, "gx", "gy"),
            P(None, "gx", "gy"),
            P(None, None, "gx", "gy"),
            P(("gx", "gy"), None),
            P("gx", "gy"),
            P("gx", "gy", None),
        ),
        out_specs=(P(None, "gx", "gy"), P(None, "gx", "gy")),
        check_vma=False,
    )
```

```python
import functools

import jax
import jax.numpy as jnp
from jax import lax
from jax.experimental import pallas as pl
from jax.experimental.pallas import tpu as pltpu
from jax.sharding import PartitionSpec as P

KCHEB = 9
AXES = ("gx", "gy")
LEVELS = 16
ROWS = 32
COLS = 128
VECTORS = 32
EDGE = 16
TALL = ROWS + 2 * EDGE
HIGHEST = lax.Precision.HIGHEST

lowest_rate = 0.05
highest_rate = 18.5
vertical = 2.0
theta = 0.5 * (highest_rate + lowest_rate)
delta = 0.5 * (highest_rate - lowest_rate)
VMEM_LIMIT = 24 * 1024 * 1024
FIRST_LIMIT = 58 * 1024 * 1024


def chebyshev_values():
    ratio = theta / delta
    values = [1.0, ratio]
    while len(values) <= KCHEB:
        values.append(2.0 * ratio * values[-1] - values[-2])
    return values


def chebyshev_table():
    return chebyshev_values()[1:KCHEB]


def iota(shape, dim):
    return lax.broadcasted_iota(jnp.int32, shape, dim)


def roll(value, shift):
    return pltpu.roll(value, shift % COLS, 1)


def exchange(forward_value, backward_value, axis):
    count = lax.axis_size(axis)
    forward = [(i, i + 1) for i in range(count - 1)]
    backward = [(target, source) for source, target in forward]
    return lax.ppermute(forward_value, axis, forward), lax.ppermute(backward_value, axis, backward)


def everyone(rows):
    return lax.all_to_all(rows, AXES, 0, 0, tiled=True)


def row_of_sums(sums):
    padded = jnp.concatenate([sums, jnp.zeros((COLS - VECTORS, COLS), jnp.float32)], 0)
    ones = jnp.ones((COLS, COLS), jnp.float32)
    return lax.dot_general(
        ones, padded, (((1,), (1,)), ((), ())), precision=HIGHEST, preferred_element_type=jnp.float32
    )


def fold_rows(product):
    return (product[0:8] + product[8:16]) + (product[16:24] + product[24:32])


def first_kernel(
    field_ref, coefficient_ref, basis_ref, slots_ref, margin_ref,
    out_ref, ahead_ref, behind_ref, sides_ref, sums_ref, edges_ref,
):
    step = pl.program_id(0)
    group = basis_ref.shape[0]

    @pl.when(step == 0)
    def _():
        edges_ref[...] = jnp.zeros_like(edges_ref)

        def level(z, carry):
            ahead_ref[z] = field_ref[z, ROWS - EDGE :, :]
            behind_ref[z] = field_ref[z, :EDGE, :]
            ahead_ref[LEVELS + z] = coefficient_ref[z, ROWS - EDGE :, :]
            behind_ref[LEVELS + z] = coefficient_ref[z, :EDGE, :]
            return carry

        lax.fori_loop(0, LEVELS, level, 0)

    def level(z, sums):
        field = field_ref[z]
        new = []
        for j in range(group):
            values = basis_ref[j, z].astype(jnp.float32)
            new.append(sums[j] + fold_rows(values * field))
            at = 2 * LEVELS + step * group + j
            behind_ref[at, pl.ds(z, 1), :] = values[0:1]
            ahead_ref[at, pl.ds(z, 1), :] = values[ROWS - 1 : ROWS]
        return tuple(new)

    zero = jnp.zeros((8, COLS), jnp.float32)
    sums = lax.fori_loop(0, LEVELS, level, (zero,) * group, unroll=2)
    for j in range(group):
        sums_ref[pl.ds(step * group + j, 1), :] = jnp.sum(sums[j], axis=0, keepdims=True)
    from_lane, to_lane = iota((COLS, COLS), 0), iota((COLS, COLS), 1)
    picks = []
    for j in range(group):
        k = step * group + j
        pick = ((from_lane == 0) & (to_lane == k)) | ((from_lane == COLS - 1) & (to_lane == VECTORS + k))
        picks.append(jnp.where(pick, 1.0, 0.0).astype(jnp.bfloat16))
    values = jnp.concatenate([basis_ref[j].reshape(LEVELS * ROWS, COLS) for j in range(group)], axis=1)
    edges_ref[...] += jnp.dot(values, jnp.concatenate(picks, 0), preferred_element_type=jnp.float32)

    @pl.when(step == pl.num_programs(0) - 1)
    def _():
        told = jnp.concatenate(
            [
                jnp.zeros((1, VECTORS), jnp.float32),
                slots_ref[0].astype(jnp.float32),
                margin_ref[...].astype(jnp.float32),
                jnp.zeros((1, COLS - 65), jnp.float32),
            ],
            axis=1,
        )
        out_ref[...] = row_of_sums(sums_ref[...]) + told
        place = iota((ROWS, COLS), 1) >> 5
        for n in range(LEVELS // 4):
            left = jnp.zeros((ROWS, COLS), jnp.float32)
            right = left
            for q in range(4):
                z = 4 * n + q
                value = edges_ref[z * ROWS : (z + 1) * ROWS]
                left = jnp.where(place == q, roll(value, VECTORS * q), left)
                right = jnp.where(place == q, roll(value, VECTORS * (q - 1)), right)
            sides_ref[n] = left
            sides_ref[LEVELS // 4 + n] = right


def first_projection(field, coefficient, basis, slots, margin):
    group = 16
    rows = 2 * LEVELS + VECTORS
    edge_rows = jax.ShapeDtypeStruct((rows, LEVELS, COLS), jnp.float32)
    edge_cols = jax.ShapeDtypeStruct((LEVELS // 2, ROWS, COLS), jnp.float32)
    block_spec = pl.BlockSpec((LEVELS, ROWS, COLS), lambda i: (0, 0, 0))
    rows_spec = pl.BlockSpec(edge_rows.shape, lambda i: (0, 0, 0))
    cols_spec = pl.BlockSpec(edge_cols.shape, lambda i: (0, 0, 0))
    return pl.pallas_call(
        first_kernel,
        grid=(VECTORS // group,),
        in_specs=[
            block_spec,
            block_spec,
            pl.BlockSpec((group, LEVELS, ROWS, COLS), lambda i: (i, 0, 0, 0)),
            pl.BlockSpec(slots.shape, lambda i: (0, 0, 0)),
            pl.BlockSpec(margin.shape, lambda i: (0, 0)),
        ],
        out_specs=[pl.BlockSpec((COLS, COLS), lambda i: (0, 0)), rows_spec, rows_spec, cols_spec],
        out_shape=[jax.ShapeDtypeStruct((COLS, COLS), jnp.float32), edge_rows, edge_rows, edge_cols],
        scratch_shapes=[
            pltpu.VMEM((VECTORS, COLS), jnp.float32), pltpu.VMEM((LEVELS * ROWS, COLS), jnp.float32)
        ],
        compiler_params=pltpu.CompilerParams(vmem_limit_bytes=FIRST_LIMIT),
        name="first_projection",
    )(field, coefficient, basis, slots, margin)


def coarse_rows(told_ref, slots_ref, inverse_hbm, out_ref, inverse_ref, sem):
    copy = pltpu.make_async_copy(inverse_hbm, inverse_ref, sem)
    copy.start()
    told = told_ref[...]
    slots = slots_ref[...]
    turned = told.T
    slots_turned = slots.T
    lane = iota((COLS, COLS), 1)
    sub = iota((VECTORS, COLS), 0)
    placed = jnp.zeros((3 * VECTORS, COLS), jnp.float32)
    for k in range(VECTORS):
        slot_column = slots[:, VECTORS + k : VECTORS + k + 1].astype(jnp.int32)
        ones = jnp.where((slot_column & 127) == lane, 1.0, 0.0).astype(jnp.bfloat16)
        slot_row = slots_turned[VECTORS + k : VECTORS + k + 1, :].astype(jnp.int32)
        values = turned[k : k + 1, :]
        spread = jnp.where((slot_row >> 7) == sub, values, 0.0)
        first = spread.astype(jnp.bfloat16)
        rest = spread - first.astype(jnp.float32)
        second = rest.astype(jnp.bfloat16)
        third = (rest - second.astype(jnp.float32)).astype(jnp.bfloat16)
        parts = jnp.concatenate([first, second, third], 0)
        placed = placed + jnp.dot(parts, ones, preferred_element_type=jnp.float32)
    placed = placed[:VECTORS] + placed[VECTORS : 2 * VECTORS] + placed[2 * VECTORS :]
    total = jnp.zeros((VECTORS, COLS), jnp.float32)
    copy.wait()
    for high in range(VECTORS):
        total = total + inverse_ref[:, high * COLS : (high + 1) * COLS] * placed[high : high + 1]
    out_ref[...] = row_of_sums(total)


def pack_strips(parts, forward_ref, backward_ref, at):
    def levels(group, carry):
        row = 0
        for part, start in parts:
            height = EDGE if part.shape[1] == EDGE else ROWS
            lane = iota((height, COLS), 1)
            ahead = jnp.zeros((height, COLS), jnp.float32)
            behind = ahead
            for j in range(8):
                value = part[start + group * 8 + j]
                mine = (lane >= EDGE * j) & (lane < EDGE * (j + 1))
                ahead = jnp.where(mine, roll(value, EDGE * j - (COLS - EDGE)), ahead)
                behind = jnp.where(mine, roll(value, EDGE * j), behind)
            forward_ref[at + group, row : row + height, :] = ahead
            backward_ref[at + group, row : row + height, :] = behind
            row += height
        return carry

    lax.fori_loop(0, LEVELS // 8, levels, 0)


def first_pack_kernel(
    source_ref, absorption_ref, low_ref, high_ref, sides_hbm, forward_ref, backward_ref, sides_ref, sem
):
    copy = pltpu.make_async_copy(sides_hbm, sides_ref, sem)
    copy.start()
    for f, block in enumerate((source_ref, absorption_ref)):
        pack_strips(((low_ref, LEVELS * f), (block, 0), (high_ref, LEVELS * f)), forward_ref, backward_ref, 2 * f)
    copy.wait()
    for n in range(LEVELS // 8):
        for half in range(2):
            rows = slice(half * ROWS, (half + 1) * ROWS)
            forward_ref[4 + n, rows, :] = sides_ref[LEVELS // 4 + 2 * n + half]
            backward_ref[4 + n, rows, :] = sides_ref[2 * n + half]


def pack_kernel(block_ref, low_ref, high_ref, forward_ref, backward_ref):
    pack_strips(((low_ref, 0), (block_ref, 0), (high_ref, 0)), forward_ref, backward_ref, 0)


FIELDS_SPEC = pl.BlockSpec((2 * LEVELS, EDGE, COLS), lambda i: (0, 0, 0))
VMEM_SPEC = pl.BlockSpec(memory_space=pltpu.VMEM)
HBM_SPEC = pl.BlockSpec(memory_space=pltpu.HBM)
SMEM_SPEC = pl.BlockSpec(memory_space=pltpu.SMEM)


def pack(kernel, specs, strips, scratch, *operands):
    strips = jax.ShapeDtypeStruct((strips, TALL, COLS), jnp.float32)
    return pl.pallas_call(
        kernel,
        grid=(1,),
        in_specs=specs,
        out_shape=[strips, strips],
        scratch_shapes=scratch,
        compiler_params=pltpu.CompilerParams(vmem_limit_bytes=VMEM_LIMIT),
        cost_estimate=pl.CostEstimate(flops=3000000000, bytes_accessed=1000000, transcendentals=0),
        name="strips",
    )(*operands)


def solve_rows(*operands):
    return pl.pallas_call(
        coarse_rows,
        in_specs=[VMEM_SPEC] * 2 + [HBM_SPEC],
        out_shape=pltpu.HBM((COLS, COLS), jnp.float32),
        scratch_shapes=[pltpu.VMEM((VECTORS, COLS * VECTORS), jnp.float32), pltpu.SemaphoreType.DMA],
        compiler_params=pltpu.CompilerParams(vmem_limit_bytes=VMEM_LIMIT),
        cost_estimate=pl.CostEstimate(flops=9200000000, bytes_accessed=1000000, transcendentals=0),
        name="coarse_rows",
    )(*operands)


class Place:
    def __init__(self, place_ref, told_ref):
        self.row = place_ref[0]
        self.col = place_ref[1]
        self.rows = place_ref[2]
        self.cols = place_ref[3]
        self.told_ref = told_ref

    def index(self, down, right):
        row = jnp.clip(self.row + down, 0, self.rows - 1)
        col = jnp.clip(self.col + right, 0, self.cols - 1)
        return row * self.cols + col

    def margin(self, down, right):
        row, col = self.row + down, self.col + right
        real = (row >= 0) & (row < self.rows) & (col >= 0) & (col < self.cols)
        margin = self.told_ref[pl.ds(self.index(down, right), 1), :][:, 64:65]
        return jnp.where(real, margin.astype(jnp.int32), -4096)


def masks(place, own_ref, beside_ref, strip_ref):
    shape = (TALL, COLS)
    row = iota(shape, 0) - EDGE
    lane = iota(shape, 1)
    top, bottom = -ROWS * place.row, ROWS * (place.rows - place.row)
    first, last = -COLS * place.col, COLS * (place.cols - place.col)
    row_real = (row >= top) & (row < bottom)
    m = {(i, j): place.margin(i, j) for i in (-1, 0, 1) for j in (-1, 0, 1)}
    upper, lower = row < 8, row >= ROWS - 8
    for tile in range(2):
        col = lane if tile == 0 else jnp.where(lane < 64, lane + COLS, lane - COLS)
        real = row_real & (col >= first) & (col < last)
        if tile == 1:
            real = real & ((lane < EDGE) | (lane >= COLS - EDGE))

        def across(margin):
            return (col >= -margin) & (col < COLS + margin)

        own = m[0, 0]
        inside = real & (row >= -own) & (row < ROWS + own) & across(own)
        own_ref[tile] = jnp.where(inside, 1.0, 0.0)
        above, below = m[-1, 0], m[1, 0]
        inside = (upper & (row < above) & across(above)) | (lower & (row >= ROWS - below) & across(below))
        beside_ref[tile] = jnp.where(real & inside, 1.0, 0.0)
    group = ((lane + EDGE) & 127) >> 5
    away = ((lane + EDGE) & 31) - EDGE
    inside = row < -4096
    for place_of, side in ((0, -1), (2, 1)):
        col = away if side < 0 else away + COLS
        real = row_real & (col >= first) & (col < last)

        def reached(margin):
            return (away < margin) if side < 0 else (away >= -margin)

        level = m[0, side]
        inside = inside | (
            (group == place_of) & real & (row >= -level) & (row < ROWS + level) & reached(level)
        )
        above, below = m[-1, side], m[1, side]
        corner = (upper & (row < above) & reached(above)) | (
            lower & (row >= ROWS - below) & reached(below)
        )
        inside = inside | ((group == place_of + 1) & real & corner)
    strip_ref[...] = jnp.where(inside, 1.0, 0.0)


def tiles_of(parts, start, strips, at, z, i):
    low, block, high = parts
    from_left, from_right = strips
    lane = iota((8, COLS), 1)
    if i < 2:
        center = low[start + z, i * 8 : i * 8 + 8, :]
    elif i < 6:
        center = block[z, (i - 2) * 8 : (i - 2) * 8 + 8, :]
    else:
        center = high[start + z, (i - 6) * 8 : (i - 6) * 8 + 8, :]
    s = slice(i * 8, i * 8 + 8)
    group, shift = at + (z >> 3), EDGE * (z & 7)
    left = pltpu.roll(from_left[group, s, :], (COLS - EDGE) - shift, 1)
    right = pltpu.roll(from_right[group, s, :], (COLS - shift) & (COLS - 1), 1)
    margin = jnp.where(lane >= COLS - EDGE, left, jnp.where(lane < EDGE, right, 0.0))
    at_left = jnp.where(lane >= 64, margin, center)
    at_right = jnp.where(lane < 64, margin, center)
    near = (lane < EDGE) | (lane >= COLS - EDGE)
    others = jnp.where(lane < 80, roll(at_right, 64), roll(at_right, 96))
    packed = jnp.where(near, at_left, jnp.where(lane < 48, roll(at_left, 32), others))
    return center, margin, packed


UNROLL = 8
UNROLL_BEGIN = 2
UNROLL_FINISH = 2
PLANES = LEVELS + 2
BESIDE_TILES = (1, 2, 5, 6)


def smooth_kernel(same, place_ref, table_ref, told_ref, block_ref, low_ref, high_ref, left_ref, right_ref, absorption_ref, *refs):
    if same:
        low_c, high_c, left_c, right_c = low_ref, high_ref, left_ref, right_ref
    else:
        low_c, high_c, left_c, right_c = refs[:4]
        refs = refs[4:]
    (
        out_ref, own_m, beside_m, strip_m, own, beside, strip, own_y, beside_y, strip_y,
        wide_r, strip_r, diag, strip_diag,
    ) = refs
    field_start, coef_start, coef_at = 0, LEVELS, 2
    masks(Place(place_ref, told_ref), own_m, beside_m, strip_m)
    base = 2.0 * (theta - (4.0 + 2.0 * vertical)) / delta
    last = 1.0 / chebyshev_values()[KCHEB]
    zero = jnp.zeros((8, COLS), jnp.float32)
    lane = iota((8, COLS), 1)
    lanes = [slice(0, COLS), slice(COLS, 2 * COLS)]

    def clear(n, carry):
        at = n * (PLANES - 1)
        for i in range(8):
            s = slice(i * 8, i * 8 + 8)
            for t in range(2):
                for x in (own, own_y, beside, beside_y):
                    x[at, t, s] = zero
            strip[at, 0, s] = zero
            strip_y[at, 0, s] = zero
        return carry

    lax.fori_loop(0, 2, clear, 0)

    def begin(z, carry):
        at = z + 1
        for i in range(8):
            s = slice(i * 8, i * 8 + 8)
            tiles = tiles_of((low_ref, block_ref, high_ref), field_start, (left_ref, right_ref), 0, z, i)
            inner = 1 <= i < 7
            for t in range(2):
                guess = tiles[t] * (1.0 / delta)
                value = guess if t == 0 and 2 <= i < 6 else guess * own_m[t, s]
                own[at, t, s] = value
                own_y[at, t, s] = zero
                if inner:
                    wide_r[z, t, s] = guess + guess
                beside_y[at, t, s] = zero
                beside[at, t, s] = zero if i in (3, 4) else guess * beside_m[t, s]
            guess = tiles[2] * (1.0 / delta)
            strip[at, 0, s] = guess * strip_m[s]
            strip_y[at, 0, s] = zero
            if inner:
                strip_r[z, 0, s] = guess + guess
                tiles = tiles_of((low_c, absorption_ref, high_c), coef_start, (left_c, right_c), coef_at, z, i)
                diag[z, 0, s] = base - (2.0 / delta) * tiles[0]
                diag[z, 1, s] = base - (2.0 / delta) * tiles[1]
                strip_diag[z, 0, s] = base - (2.0 / delta) * tiles[2]
        return carry

    lax.fori_loop(0, LEVELS, begin, 0, unroll=UNROLL_BEGIN)
    at_first, at_last = lane == 0, lane == COLS - 1

    def step(here, x, y, r, a, mask, width, i, amount):
        s = slice(i * 8, i * 8 + 8)
        up, down = slice(i * 8 - 1, i * 8 + 7), slice(i * 8 + 1, i * 8 + 9)
        z = here - 1
        now = [x[here, t, s] for t in range(width)]
        back = [roll(v, 1) for v in now]
        fore = [roll(v, -1) for v in now]
        if width == 2:
            back = [jnp.where(at_first, back[1], back[0]), jnp.where(at_first, back[0], back[1])]
            fore = [jnp.where(at_last, fore[1], fore[0]), jnp.where(at_last, fore[0], fore[1])]
        for t in range(width):
            high = x[here - 1, t, s] + x[here + 1, t, s]
            around = (x[here, t, up] + x[here, t, down]) + (back[t] + fore[t])
            around = around + (high + high)
            after = (a[z, t, s] * now[t] + amount * r[z, t, s]) + ((2.0 / delta) * around - y[here, t, s])
            if mask[t] is not None:
                after = after * mask[t]
            y[here, t, s] = after

    first = ((own, own_y), (beside, beside_y), (strip, strip_y))
    second = tuple((y, x) for x, y in first)

    def sweep(n, arrays):
        amount = table_ref[n]
        own, beside, strip = arrays

        def level(z, carry):
            here = z + 1
            for i in range(1, 7):
                s = slice(i * 8, i * 8 + 8)
                free = None if 2 <= i < 6 else own_m[0, s]
                step(here, *own, wide_r, diag, [free, own_m[1, s]], 2, i, amount)
                if i in BESIDE_TILES:
                    step(here, *beside, wide_r, diag, [beside_m[0, s], beside_m[1, s]], 2, i, amount)
                step(here, *strip, strip_r, strip_diag, [strip_m[s]], 1, i, amount)
            return carry

        lax.fori_loop(0, LEVELS, level, 0, unroll=UNROLL)

    def pair(n, carry):
        sweep(2 * n, first)
        sweep(2 * n + 1, second)
        return carry

    lax.fori_loop(0, (KCHEB - 1) // 2, pair, 0)
    near_first, near_last = lane < EDGE, lane >= COLS - EDGE

    def finish(z, carry):
        at = z + 1
        for i in range(1, 7):
            s = slice(i * 8, i * 8 + 8)
            out = slice(i * 8 - 8, i * 8)
            value = strip[at, 0, s]
            at_left = value + roll(value, -32)
            at_right = roll(at_left, 64)
            first = jnp.where(near_first, at_left, jnp.where(near_last, at_right, 0.0))
            second = jnp.where(near_last, at_left, jnp.where(near_first, at_right, 0.0))
            first = first + own[at, 0, s]
            second = second + own[at, 1, s]
            if i in BESIDE_TILES:
                first = first + beside[at, 0, s]
                second = second + beside[at, 1, s]
            out_ref[z, out, lanes[0]] = first * last
            out_ref[z, out, lanes[1]] = second * last
        return carry

    lax.fori_loop(0, LEVELS, finish, 0, unroll=UNROLL_FINISH)


def smooth(place, table, told, block, low, high, strips, absorption, coefficient=None):
    wide = (2, TALL, COLS)
    thin = (1, TALL, COLS)

    def scratch(*shape):
        return pltpu.VMEM(shape, jnp.float32)

    more = () if coefficient is None else coefficient
    specs = [SMEM_SPEC] * 2 + [VMEM_SPEC] * 2 + [VMEM_SPEC if more else FIELDS_SPEC] * 2 + [VMEM_SPEC] * 3
    if more:
        specs += [FIELDS_SPEC] * 2 + [VMEM_SPEC] * 2
    return pl.pallas_call(
        functools.partial(smooth_kernel, not more),
        grid=(1,),
        in_specs=specs,
        out_shape=(pltpu.HBM if more else jax.ShapeDtypeStruct)((LEVELS, INNER, 2 * COLS), jnp.float32),
        scratch_shapes=[
            scratch(*wide), scratch(*wide), scratch(TALL, COLS),
            scratch(PLANES, *wide), scratch(PLANES, *wide), scratch(PLANES, *thin),
            scratch(PLANES, *wide), scratch(PLANES, *wide), scratch(PLANES, *thin),
            scratch(LEVELS, *wide), scratch(LEVELS, *thin),
            scratch(LEVELS, *wide), scratch(LEVELS, *thin),
        ],
        compiler_params=pltpu.CompilerParams(vmem_limit_bytes=VMEM_LIMIT),
        cost_estimate=pl.CostEstimate(flops=2000000, bytes_accessed=54000000, transcendentals=0),
        name="smoother",
    )(place, table, told, block, low, high, *strips, absorption, *more)


INNER = ROWS + 16


def slots_of(place, told_ref, moves):
    lane = iota((1, COLS), 1)
    slots = jnp.zeros((1, COLS), jnp.float32)
    for n, (down, right) in enumerate(moves):
        row = roll(told_ref[pl.ds(place.index(down, right), 1), :], VECTORS * (n - 1))
        slots = jnp.where((lane >> 5) == n, row, slots)
    return slots.astype(jnp.int32)


def coarse_at(coarse_turned, slots):
    pick = jnp.where(iota((COLS, COLS), 0) == (slots >> 5), 1.0, 0.0)
    found = jnp.dot(coarse_turned, pick, precision=HIGHEST, preferred_element_type=jnp.float32)
    found = jnp.where(iota((VECTORS, COLS), 0) == (slots & 31), found, 0.0)
    return jnp.sum(found, axis=0, keepdims=True)


def add_coarse(place, told_ref, coarse_ref, basis_hbm, basis_ref, sems, low_ref, high_ref, left_ref, right_ref, at, sum_ref, x,
               own_c, edge_c, ring_ref, side_ref, ready=None):
    def part(q):
        levels = pl.ds(q * 4, 4)
        return pltpu.make_async_copy(basis_hbm.at[:, levels], basis_ref.at[:, levels], sems.at[q])

    for q in range(LEVELS // 4):
        part(q).start()
    turned = coarse_ref[...].T[:VECTORS]
    row = coarse_at(turned, slots_of(place, told_ref, ((0, 0), (-1, 0), (1, 0), (0, -1))))
    other = coarse_at(turned, slots_of(place, told_ref, ((0, 1),)))
    lane = iota((8, COLS), 1)
    lane_row = iota((1, COLS), 1)
    column = jnp.broadcast_to(row, (COLS, COLS)).T
    own_c[...] = column[:VECTORS]
    edge_c[...] = column[VECTORS : 3 * VECTORS]
    for n, edge in ((0, low_ref), (1, high_ref)):

        def vector(k, total):
            return total + edge[2 * LEVELS + k] * edge_c[pl.ds(n * VECTORS + k, 1), :]

        ring_ref[n] = lax.fori_loop(0, VECTORS, vector, jnp.zeros((LEVELS, COLS), jnp.float32))
    which = iota((COLS, COLS), 0) >> 5
    for n, (edge, values) in enumerate(((left_ref, roll(row, VECTORS)), (right_ref, other))):
        values = jnp.where(lane_row < VECTORS, values, 0.0)
        values = values + roll(values, 32) + roll(values, 64) + roll(values, 96)
        weights = jnp.broadcast_to(values, (COLS, COLS)).T
        weights = jnp.where(iota((COLS, COLS), 1) == which, weights, 0.0)
        parts = edge[at : at + 2].reshape(2 * TALL, COLS)
        side_ref[n] = jnp.dot(parts, weights, precision=HIGHEST, preferred_element_type=jnp.float32)

    def level(z, carry):
        total = sum_ref[z, 8 : 8 + ROWS, 0:COLS]
        for k in range(VECTORS):
            total = total + basis_ref[k, z].astype(jnp.float32) * own_c[k : k + 1]
        here = z + 1
        x[here, 8 : 8 + ROWS, 0:COLS] = total
        rows = pl.ds(z, 1)
        x[here, 7:8, 0:COLS] = sum_ref[z, 7:8, 0:COLS] + ring_ref[0, rows, :]
        x[here, 8 + ROWS : 9 + ROWS, 0:COLS] = sum_ref[z, 8 + ROWS : 9 + ROWS, 0:COLS] + ring_ref[1, rows, :]
        q = z & 3
        for i in range(ROWS // 8):
            s = pl.ds(pl.multiple_of((z >> 2) * ROWS + i * 8, 8), 8)
            left = pltpu.roll(side_ref[0, s, :], (COLS - 1) - q, 1)
            right = pltpu.roll(side_ref[1, s, :], (COLS - q) & (COLS - 1), 1)
            t = slice(8 + i * 8, 16 + i * 8)
            value = jnp.where(lane == COLS - 1, left, jnp.where(lane == 0, right, 0.0))
            x[here, t, COLS : 2 * COLS] = sum_ref[z, t, COLS : 2 * COLS] + value
        return carry

    if ready is not None:
        ready.wait()

    def levels(q, carry):
        part(q).wait()
        return lax.fori_loop(0, 2, lambda n, c: level(4 * q + 2 * n + 1, level(4 * q + 2 * n, c)), carry)

    lax.fori_loop(0, LEVELS // 4, levels, 0)
    zero = jnp.zeros((ROWS, COLS), jnp.float32)
    x[0, 8 : 8 + ROWS, 0:COLS] = zero
    x[PLANES - 1, 8 : 8 + ROWS, 0:COLS] = zero
    return row


def image_at(x, absorption_ref, z, i):
    lane = iota((8, COLS), 1)
    here = z + 1
    s = slice(8 + i * 8, 16 + i * 8)
    up, down = slice(7 + i * 8, 15 + i * 8), slice(9 + i * 8, 17 + i * 8)
    now = x[here, s, 0:COLS]
    margin = x[here, s, COLS : 2 * COLS]
    back = jnp.where(lane == 0, roll(margin, 1), roll(now, 1))
    fore = jnp.where(lane == COLS - 1, roll(margin, -1), roll(now, -1))
    high = x[here - 1, s, 0:COLS] + x[here + 1, s, 0:COLS]
    around = (x[here, up, 0:COLS] + x[here, down, 0:COLS]) + (back + fore)
    diagonal = absorption_ref[z, i * 8 : i * 8 + 8, :] + (4.0 + 2.0 * vertical)
    return now, diagonal * now - around - vertical * high


def total_of(value):
    return jnp.sum(jnp.sum(value, axis=0, keepdims=True), axis=1, keepdims=True)


def scalars(told_ref):
    totals = jnp.sum(told_ref[...], axis=0, keepdims=True)
    return totals[:, 64:65], totals[:, 65:66]


def first_coarse_kernel(
    place_ref, told_ref, coarse_ref, basis_hbm, low_ref, high_ref, left_ref, right_ref, sum_ref, source_ref, absorption_ref,
    direction_ref, image_ref, ahead_ref, behind_ref, out_ref, x, own_c, edge_c, ring_ref, side_ref, basis_ref, sems, sums_ref,
):
    place = Place(place_ref, told_ref)
    row = add_coarse(place, told_ref, coarse_ref, basis_hbm, basis_ref, sems, low_ref, high_ref, left_ref, right_ref, 4, sum_ref, x,
                     own_c, edge_c, ring_ref, side_ref)
    zero = jnp.zeros((8, COLS), jnp.float32)

    def images(z, carry):
        weight, curve = carry
        for i in range(ROWS // 8):
            s = slice(i * 8, i * 8 + 8)
            now, image = image_at(x, absorption_ref, z, i)
            direction_ref[z, s] = now
            image_ref[z, s] = image
            if i >= 2:
                ahead_ref[z, (i - 2) * 8 : (i - 1) * 8] = image
            else:
                behind_ref[z, s] = image
            weight = weight + source_ref[z, s] * sum_ref[z, 8 + i * 8 : 16 + i * 8, 0:COLS]
            curve = curve + now * image
        return weight, curve

    weight, curve = lax.fori_loop(0, LEVELS, images, (zero, zero), unroll=2)
    half = VECTORS // 2
    for part in range(2):

        def level(z, sums):
            image = image_ref[z]
            return tuple(
                sums[k] + fold_rows(basis_ref[part * half + k, z].astype(jnp.float32) * image) for k in range(half)
            )

        sums = lax.fori_loop(0, LEVELS, level, (zero,) * half)
        for k in range(half):
            sums_ref[part * half + k : part * half + k + 1] = jnp.sum(sums[k], axis=0, keepdims=True)
    lane = iota((1, COLS), 1)
    row = jnp.where(lane < VECTORS, row, 0.0)
    mine = told_ref[pl.ds(place.index(0, 0), 1), :]
    told = roll(row, VECTORS)
    told = told + jnp.where(lane == 64, total_of(weight) + total_of(row * mine), 0.0)
    told = told + jnp.where(lane == 65, total_of(curve), 0.0)
    out_ref[...] = row_of_sums(sums_ref[...]) + told


def second_coarse_kernel(
    place_ref, told_ref, coarse_ref, basis_hbm, low_ref, high_ref, left_ref, right_ref, sum_hbm, source_ref, absorption_ref,
    again_ref, first_sum_ref, direction_ref, first_ref,
    residual_ref, precond_ref, image_ref, out_ref, x, own_c, edge_c, ring_ref, side_ref, basis_ref, sems,
    sum_ref, sum_sem,
):
    copy = pltpu.make_async_copy(sum_hbm, sum_ref, sum_sem)
    copy.start()
    place = Place(place_ref, told_ref)
    row = add_coarse(place, told_ref, coarse_ref, basis_hbm, basis_ref, sems, low_ref, high_ref, left_ref, right_ref, 4, sum_ref, x,
                     own_c, edge_c, ring_ref, side_ref, copy)
    weight0, curve0 = scalars(again_ref)
    step = weight0 / curve0
    zero = jnp.zeros((8, COLS), jnp.float32)

    def images(z, sums):
        weight, own, cross = sums
        for i in range(ROWS // 8):
            s = slice(i * 8, i * 8 + 8)
            t = slice(8 + i * 8, 16 + i * 8)
            now, image = image_at(x, absorption_ref, z, i)
            direction, first = direction_ref[z, s], first_ref[z, s]
            residual = source_ref[z, s] - step * first
            precond = direction - step * now
            image = first - step * image
            residual_ref[z, s] = residual
            precond_ref[z, s] = precond
            image_ref[z, s] = image
            weight = weight + residual * (first_sum_ref[z, t, 0:COLS] - step * sum_ref[z, t, 0:COLS])
            own = own + precond * image
            cross = cross + (precond * first + direction * image)
        return weight, own, cross

    weight, own, cross = lax.fori_loop(0, LEVELS, images, (zero, zero, zero), unroll=2)
    mine = pl.ds(place.index(0, 0), 1)
    lane = iota((1, COLS), 1)
    again = again_ref[mine, :]
    projected = told_ref[mine, :] - step * again
    coarse = roll(again, -VECTORS) - step * row
    both = jnp.where(lane < VECTORS, projected * coarse, 0.0)
    told = jnp.where(lane == 0, total_of(weight) + total_of(both), 0.0)
    told = told + jnp.where(lane == 1, total_of(own), 0.0) + jnp.where(lane == 2, total_of(cross), 0.0)
    out_ref[...] = jnp.broadcast_to(told, (COLS, COLS))


def last_kernel(again_ref, last_ref, direction_ref, first_ref, residual_ref, precond_ref, image_ref, x_ref, r_ref):
    weight0, curve0 = scalars(again_ref)
    step0 = weight0 / curve0
    totals = jnp.sum(last_ref[...], axis=0, keepdims=True)
    weight1, own, cross = totals[:, 0:1], totals[:, 1:2], totals[:, 2:3]
    ratio = weight1 / weight0
    step1 = weight1 / (own + ratio * (cross + ratio * curve0))

    def level(z, carry):
        direction = direction_ref[z]
        x_ref[z] = step0 * direction + step1 * (precond_ref[z] + ratio * direction)
        r_ref[z] = residual_ref[z] - step1 * (image_ref[z] + ratio * first_ref[z])
        return carry

    lax.fori_loop(0, LEVELS, level, 0, unroll=4)


def shards(source, absorption, basis, coarse_inverse, margin_width, coarse_slot):
    block = jax.ShapeDtypeStruct((LEVELS, ROWS, COLS), jnp.float32)
    slab = jax.ShapeDtypeStruct((LEVELS, EDGE, COLS), jnp.float32)
    message = pltpu.HBM((COLS, COLS), jnp.float32)
    params = pltpu.CompilerParams(vmem_limit_bytes=VMEM_LIMIT)

    def scratch(*shape):
        return pltpu.VMEM(shape, jnp.float32)

    coarse_scratch = [
        scratch(PLANES, INNER, 2 * COLS), scratch(VECTORS, COLS), scratch(2 * VECTORS, COLS),
        scratch(2, LEVELS, COLS), scratch(2, 2 * TALL, COLS),
        pltpu.VMEM(basis.shape, basis.dtype), pltpu.SemaphoreType.DMA((LEVELS // 4,)),
    ]
    hbm = pl.BlockSpec(memory_space=pltpu.HBM)
    def in_hbm(value):
        return pltpu.with_memory_space_constraint(value, pltpu.HBM)

    place = jnp.stack(
        [lax.axis_index("gx"), lax.axis_index("gy"), lax.axis_size("gx"), lax.axis_size("gy")]
    ).astype(jnp.int32)
    table = jnp.array(chebyshev_table(), jnp.float32)
    rows, ahead, behind, sides = first_projection(
        source, absorption, basis, coarse_slot, margin_width
    )
    low, high = exchange(ahead, behind, "gx")
    told = everyone(rows)
    fields = [VMEM_SPEC] * 2 + [FIELDS_SPEC] * 2 + [HBM_SPEC]
    strips = exchange(
        *pack(first_pack_kernel, fields, 6, [scratch(LEVELS // 2, ROWS, COLS), pltpu.SemaphoreType.DMA], source, absorption, low, high, in_hbm(sides)), "gy"
    )
    coarse = everyone(solve_rows(told, told, in_hbm(coarse_inverse)))
    first_sum = smooth(place, table, told, source, low, high, strips, absorption)
    edges = (low, high, *strips)
    direction, image, ahead, behind, rows = pl.pallas_call(
        first_coarse_kernel,
        in_specs=[SMEM_SPEC] + [VMEM_SPEC] * 2 + [hbm] + [VMEM_SPEC] * 7,
        out_shape=[block, block, slab, slab, message],
        scratch_shapes=coarse_scratch + [scratch(VECTORS, COLS)],
        compiler_params=params,
        name="direction_and_image",
    )(place, told, coarse, in_hbm(basis), *edges, first_sum, source, absorption)
    low_w, high_w = exchange(ahead, behind, "gx")
    again = everyone(rows)
    strips_w = exchange(*pack(pack_kernel, [VMEM_SPEC] * 3, 2, [], image, low_w, high_w), "gy")
    coarse = everyone(solve_rows(again, told, in_hbm(coarse_inverse)))
    second_sum = smooth(place, table, told, image, low_w, high_w, strips_w, absorption, edges)
    residual, precond, precond_image, rows = pl.pallas_call(
        second_coarse_kernel,
        in_specs=[SMEM_SPEC] + [VMEM_SPEC] * 2 + [hbm] + [VMEM_SPEC] * 4 + [hbm] + [VMEM_SPEC] * 6,
        out_shape=[block, block, block, message],
        scratch_shapes=coarse_scratch + [scratch(LEVELS, INNER, 2 * COLS), pltpu.SemaphoreType.DMA],
        compiler_params=params,
        name="second_images",
    )(place, told, coarse, in_hbm(basis), *edges, in_hbm(second_sum), source, absorption, again, first_sum, direction, image)
    last = everyone(rows)
    concentration, residual = pl.pallas_call(
        last_kernel, out_shape=[block, block], compiler_params=params, name="update"
    )(again, last, direction, image, residual, precond, precond_image)
    return (concentration, residual)


def solution(mesh):
    return jax.shard_map(
        shards,
        mesh=mesh,
        in_specs=(
            P(None, "gx", "gy"),
            P(None, "gx", "gy"),
            P(None, None, "gx", "gy"),
            P(("gx", "gy"), None),
            P("gx", "gy"),
            P("gx", "gy", None),
        ),
        out_specs=(P(None, "gx", "gy"), P(None, "gx", "gy")),
        check_vma=False,
    )
```

```python
import functools

import jax
import jax.numpy as jnp
from jax import lax
from jax.experimental import pallas as pl
from jax.experimental.pallas import tpu as pltpu
from jax.sharding import PartitionSpec as P

KCHEB = 9
AXES = ("gx", "gy")
LEVELS = 16
ROWS = 32
COLS = 128
VECTORS = 32
EDGE = 16
TALL = ROWS + 2 * EDGE
HIGHEST = lax.Precision.HIGHEST

lowest_rate = 0.05
highest_rate = 18.5
vertical = 2.0
theta = 0.5 * (highest_rate + lowest_rate)
delta = 0.5 * (highest_rate - lowest_rate)
VMEM_LIMIT = 24 * 1024 * 1024
FIRST_LIMIT = 58 * 1024 * 1024


def chebyshev_values():
    ratio = theta / delta
    values = [1.0, ratio]
    while len(values) <= KCHEB:
        values.append(2.0 * ratio * values[-1] - values[-2])
    return values


def chebyshev_table():
    return chebyshev_values()[1:KCHEB]


def iota(shape, dim):
    return lax.broadcasted_iota(jnp.int32, shape, dim)


def roll(value, shift):
    return pltpu.roll(value, shift % COLS, 1)


def exchange(forward_value, backward_value, axis):
    count = lax.axis_size(axis)
    forward = [(i, i + 1) for i in range(count - 1)]
    backward = [(target, source) for source, target in forward]
    return lax.ppermute(forward_value, axis, forward), lax.ppermute(backward_value, axis, backward)


def everyone(rows):
    return lax.all_to_all(rows, AXES, 0, 0, tiled=True)


def row_of_sums(sums):
    padded = jnp.concatenate([sums, jnp.zeros((COLS - VECTORS, COLS), jnp.float32)], 0)
    ones = jnp.ones((COLS, COLS), jnp.float32)
    return lax.dot_general(
        ones, padded, (((1,), (1,)), ((), ())), precision=HIGHEST, preferred_element_type=jnp.float32
    )


def fold_rows(product):
    return (product[0:8] + product[8:16]) + (product[16:24] + product[24:32])


def first_kernel(
    field_ref, coefficient_ref, basis_ref, slots_ref, margin_ref,
    out_ref, ahead_ref, behind_ref, sides_ref, sums_ref, edges_ref,
):
    step = pl.program_id(0)
    group = basis_ref.shape[0]

    @pl.when(step == 0)
    def _():
        edges_ref[...] = jnp.zeros_like(edges_ref)

        def level(z, carry):
            ahead_ref[z] = field_ref[z, ROWS - EDGE :, :]
            behind_ref[z] = field_ref[z, :EDGE, :]
            ahead_ref[LEVELS + z] = coefficient_ref[z, ROWS - EDGE :, :]
            behind_ref[LEVELS + z] = coefficient_ref[z, :EDGE, :]
            return carry

        lax.fori_loop(0, LEVELS, level, 0)

    def level(z, sums):
        field = field_ref[z]
        new = []
        for j in range(group):
            values = basis_ref[j, z].astype(jnp.float32)
            new.append(sums[j] + fold_rows(values * field))
            at = 2 * LEVELS + step * group + j
            behind_ref[at, pl.ds(z, 1), :] = values[0:1]
            ahead_ref[at, pl.ds(z, 1), :] = values[ROWS - 1 : ROWS]
        return tuple(new)

    zero = jnp.zeros((8, COLS), jnp.float32)
    sums = lax.fori_loop(0, LEVELS, level, (zero,) * group, unroll=2)
    for j in range(group):
        sums_ref[pl.ds(step * group + j, 1), :] = jnp.sum(sums[j], axis=0, keepdims=True)
    from_lane, to_lane = iota((COLS, COLS), 0), iota((COLS, COLS), 1)
    picks = []
    for j in range(group):
        k = step * group + j
        pick = ((from_lane == 0) & (to_lane == k)) | ((from_lane == COLS - 1) & (to_lane == VECTORS + k))
        picks.append(jnp.where(pick, 1.0, 0.0).astype(jnp.bfloat16))
    values = jnp.concatenate([basis_ref[j].reshape(LEVELS * ROWS, COLS) for j in range(group)], axis=1)
    edges_ref[...] += jnp.dot(values, jnp.concatenate(picks, 0), preferred_element_type=jnp.float32)

    @pl.when(step == pl.num_programs(0) - 1)
    def _():
        told = jnp.concatenate(
            [
                jnp.zeros((1, VECTORS), jnp.float32),
                slots_ref[0].astype(jnp.float32),
                margin_ref[...].astype(jnp.float32),
                jnp.zeros((1, COLS - 65), jnp.float32),
            ],
            axis=1,
        )
        out_ref[...] = row_of_sums(sums_ref[...]) + told
        place = iota((ROWS, COLS), 1) >> 5
        for n in range(LEVELS // 4):
            left = jnp.zeros((ROWS, COLS), jnp.float32)
            right = left
            for q in range(4):
                z = 4 * n + q
                value = edges_ref[z * ROWS : (z + 1) * ROWS]
                left = jnp.where(place == q, roll(value, VECTORS * q), left)
                right = jnp.where(place == q, roll(value, VECTORS * (q - 1)), right)
            sides_ref[n] = left
            sides_ref[LEVELS // 4 + n] = right


def first_projection(field, coefficient, basis, slots, margin):
    group = 16
    rows = 2 * LEVELS + VECTORS
    edge_rows = jax.ShapeDtypeStruct((rows, LEVELS, COLS), jnp.float32)
    edge_cols = jax.ShapeDtypeStruct((LEVELS // 2, ROWS, COLS), jnp.float32)
    block_spec = pl.BlockSpec((LEVELS, ROWS, COLS), lambda i: (0, 0, 0))
    rows_spec = pl.BlockSpec(edge_rows.shape, lambda i: (0, 0, 0))
    cols_spec = pl.BlockSpec(edge_cols.shape, lambda i: (0, 0, 0))
    return pl.pallas_call(
        first_kernel,
        grid=(VECTORS // group,),
        in_specs=[
            block_spec,
            block_spec,
            pl.BlockSpec((group, LEVELS, ROWS, COLS), lambda i: (i, 0, 0, 0)),
            pl.BlockSpec(slots.shape, lambda i: (0, 0, 0)),
            pl.BlockSpec(margin.shape, lambda i: (0, 0)),
        ],
        out_specs=[pl.BlockSpec((COLS, COLS), lambda i: (0, 0)), rows_spec, rows_spec, cols_spec],
        out_shape=[jax.ShapeDtypeStruct((COLS, COLS), jnp.float32), edge_rows, edge_rows, edge_cols],
        scratch_shapes=[
            pltpu.VMEM((VECTORS, COLS), jnp.float32), pltpu.VMEM((LEVELS * ROWS, COLS), jnp.float32)
        ],
        compiler_params=pltpu.CompilerParams(vmem_limit_bytes=FIRST_LIMIT),
        name="first_projection",
    )(field, coefficient, basis, slots, margin)


def coarse_rows(told_ref, slots_ref, inverse_hbm, out_ref, inverse_ref, sem):
    copy = pltpu.make_async_copy(inverse_hbm, inverse_ref, sem)
    copy.start()
    told = told_ref[...]
    slots = slots_ref[...]
    turned = told.T
    slots_turned = slots.T
    lane = iota((COLS, COLS), 1)
    sub = iota((VECTORS, COLS), 0)
    placed = jnp.zeros((3 * VECTORS, COLS), jnp.float32)
    for k in range(VECTORS):
        slot_column = slots[:, VECTORS + k : VECTORS + k + 1].astype(jnp.int32)
        ones = jnp.where((slot_column & 127) == lane, 1.0, 0.0).astype(jnp.bfloat16)
        slot_row = slots_turned[VECTORS + k : VECTORS + k + 1, :].astype(jnp.int32)
        values = turned[k : k + 1, :]
        spread = jnp.where((slot_row >> 7) == sub, values, 0.0)
        first = spread.astype(jnp.bfloat16)
        rest = spread - first.astype(jnp.float32)
        second = rest.astype(jnp.bfloat16)
        third = (rest - second.astype(jnp.float32)).astype(jnp.bfloat16)
        parts = jnp.concatenate([first, second, third], 0)
        placed = placed + jnp.dot(parts, ones, preferred_element_type=jnp.float32)
    placed = placed[:VECTORS] + placed[VECTORS : 2 * VECTORS] + placed[2 * VECTORS :]
    total = jnp.zeros((VECTORS, COLS), jnp.float32)
    copy.wait()
    for high in range(VECTORS):
        total = total + inverse_ref[:, high * COLS : (high + 1) * COLS] * placed[high : high + 1]
    out_ref[...] = row_of_sums(total)


def pack_strips(parts, forward_ref, backward_ref, at):
    def levels(group, carry):
        row = 0
        for part, start in parts:
            height = EDGE if part.shape[1] == EDGE else ROWS
            lane = iota((height, COLS), 1)
            ahead = jnp.zeros((height, COLS), jnp.float32)
            behind = ahead
            for j in range(8):
                value = part[start + group * 8 + j]
                mine = (lane >= EDGE * j) & (lane < EDGE * (j + 1))
                ahead = jnp.where(mine, roll(value, EDGE * j - (COLS - EDGE)), ahead)
                behind = jnp.where(mine, roll(value, EDGE * j), behind)
            forward_ref[at + group, row : row + height, :] = ahead
            backward_ref[at + group, row : row + height, :] = behind
            row += height
        return carry

    lax.fori_loop(0, LEVELS // 8, levels, 0)


def first_pack_kernel(
    source_ref, absorption_ref, low_ref, high_ref, sides_hbm, forward_ref, backward_ref, sides_ref, sem
):
    copy = pltpu.make_async_copy(sides_hbm, sides_ref, sem)
    copy.start()
    for f, block in enumerate((source_ref, absorption_ref)):
        pack_strips(((low_ref, LEVELS * f), (block, 0), (high_ref, LEVELS * f)), forward_ref, backward_ref, 2 * f)
    copy.wait()
    for n in range(LEVELS // 8):
        for half in range(2):
            rows = slice(half * ROWS, (half + 1) * ROWS)
            forward_ref[4 + n, rows, :] = sides_ref[LEVELS // 4 + 2 * n + half]
            backward_ref[4 + n, rows, :] = sides_ref[2 * n + half]


def pack_kernel(block_ref, low_ref, high_ref, forward_ref, backward_ref):
    pack_strips(((low_ref, 0), (block_ref, 0), (high_ref, 0)), forward_ref, backward_ref, 0)


FIELDS_SPEC = pl.BlockSpec((2 * LEVELS, EDGE, COLS), lambda i: (0, 0, 0))
VMEM_SPEC = pl.BlockSpec(memory_space=pltpu.VMEM)
HBM_SPEC = pl.BlockSpec(memory_space=pltpu.HBM)
SMEM_SPEC = pl.BlockSpec(memory_space=pltpu.SMEM)


def pack(kernel, specs, strips, scratch, *operands):
    strips = jax.ShapeDtypeStruct((strips, TALL, COLS), jnp.float32)
    return pl.pallas_call(
        kernel,
        grid=(1,),
        in_specs=specs,
        out_shape=[strips, strips],
        scratch_shapes=scratch,
        compiler_params=pltpu.CompilerParams(vmem_limit_bytes=VMEM_LIMIT),
        cost_estimate=pl.CostEstimate(flops=3000000000, bytes_accessed=1000000, transcendentals=0),
        name="strips",
    )(*operands)


def solve_rows(*operands):
    return pl.pallas_call(
        coarse_rows,
        in_specs=[VMEM_SPEC] * 2 + [HBM_SPEC],
        out_shape=pltpu.HBM((COLS, COLS), jnp.float32),
        scratch_shapes=[pltpu.VMEM((VECTORS, COLS * VECTORS), jnp.float32), pltpu.SemaphoreType.DMA],
        compiler_params=pltpu.CompilerParams(vmem_limit_bytes=VMEM_LIMIT),
        cost_estimate=pl.CostEstimate(flops=9200000000, bytes_accessed=1000000, transcendentals=0),
        name="coarse_rows",
    )(*operands)


class Place:
    def __init__(self, place_ref, told_ref):
        self.row = place_ref[0]
        self.col = place_ref[1]
        self.rows = place_ref[2]
        self.cols = place_ref[3]
        self.told_ref = told_ref

    def index(self, down, right):
        row = jnp.clip(self.row + down, 0, self.rows - 1)
        col = jnp.clip(self.col + right, 0, self.cols - 1)
        return row * self.cols + col

    def margin(self, down, right):
        row, col = self.row + down, self.col + right
        real = (row >= 0) & (row < self.rows) & (col >= 0) & (col < self.cols)
        margin = self.told_ref[pl.ds(self.index(down, right), 1), :][:, 64:65]
        return jnp.where(real, margin.astype(jnp.int32), -4096)


def masks(place, own_ref, beside_ref, strip_ref):
    shape = (TALL, COLS)
    row = iota(shape, 0) - EDGE
    lane = iota(shape, 1)
    top, bottom = -ROWS * place.row, ROWS * (place.rows - place.row)
    first, last = -COLS * place.col, COLS * (place.cols - place.col)
    row_real = (row >= top) & (row < bottom)
    m = {(i, j): place.margin(i, j) for i in (-1, 0, 1) for j in (-1, 0, 1)}
    upper, lower = row < 8, row >= ROWS - 8
    for tile in range(2):
        col = lane if tile == 0 else jnp.where(lane < 64, lane + COLS, lane - COLS)
        real = row_real & (col >= first) & (col < last)
        if tile == 1:
            real = real & ((lane < EDGE) | (lane >= COLS - EDGE))

        def across(margin):
            return (col >= -margin) & (col < COLS + margin)

        own = m[0, 0]
        inside = real & (row >= -own) & (row < ROWS + own) & across(own)
        own_ref[tile] = jnp.where(inside, 1.0, 0.0)
        above, below = m[-1, 0], m[1, 0]
        inside = (upper & (row < above) & across(above)) | (lower & (row >= ROWS - below) & across(below))
        beside_ref[tile] = jnp.where(real & inside, 1.0, 0.0)
    group = ((lane + EDGE) & 127) >> 5
    away = ((lane + EDGE) & 31) - EDGE
    inside = row < -4096
    for place_of, side in ((0, -1), (2, 1)):
        col = away if side < 0 else away + COLS
        real = row_real & (col >= first) & (col < last)

        def reached(margin):
            return (away < margin) if side < 0 else (away >= -margin)

        level = m[0, side]
        inside = inside | (
            (group == place_of) & real & (row >= -level) & (row < ROWS + level) & reached(level)
        )
        above, below = m[-1, side], m[1, side]
        corner = (upper & (row < above) & reached(above)) | (
            lower & (row >= ROWS - below) & reached(below)
        )
        inside = inside | ((group == place_of + 1) & real & corner)
    strip_ref[...] = jnp.where(inside, 1.0, 0.0)


def tiles_of(parts, start, strips, at, z, i):
    low, block, high = parts
    from_left, from_right = strips
    lane = iota((8, COLS), 1)
    if i < 2:
        center = low[start + z, i * 8 : i * 8 + 8, :]
    elif i < 6:
        center = block[z, (i - 2) * 8 : (i - 2) * 8 + 8, :]
    else:
        center = high[start + z, (i - 6) * 8 : (i - 6) * 8 + 8, :]
    s = slice(i * 8, i * 8 + 8)
    group, shift = at + (z >> 3), EDGE * (z & 7)
    left = pltpu.roll(from_left[group, s, :], (COLS - EDGE) - shift, 1)
    right = pltpu.roll(from_right[group, s, :], (COLS - shift) & (COLS - 1), 1)
    margin = jnp.where(lane >= COLS - EDGE, left, jnp.where(lane < EDGE, right, 0.0))
    at_left = jnp.where(lane >= 64, margin, center)
    at_right = jnp.where(lane < 64, margin, center)
    near = (lane < EDGE) | (lane >= COLS - EDGE)
    others = jnp.where(lane < 80, roll(at_right, 64), roll(at_right, 96))
    packed = jnp.where(near, at_left, jnp.where(lane < 48, roll(at_left, 32), others))
    return center, margin, packed


UNROLL = 16
UNROLL_BEGIN = 2
UNROLL_FINISH = 4
PLANES = LEVELS + 2
BESIDE_TILES = (1, 2, 5, 6)


def smooth_kernel(same, place_ref, table_ref, told_ref, block_ref, low_ref, high_ref, left_ref, right_ref, absorption_ref, *refs):
    if same:
        low_c, high_c, left_c, right_c = low_ref, high_ref, left_ref, right_ref
    else:
        low_c, high_c, left_c, right_c = refs[:4]
        refs = refs[4:]
    (
        out_ref, own_m, beside_m, strip_m, own, beside, strip, own_y, beside_y, strip_y,
        wide_r, strip_r, diag, strip_diag,
    ) = refs
    field_start, coef_start, coef_at = 0, LEVELS, 2
    masks(Place(place_ref, told_ref), own_m, beside_m, strip_m)
    base = 2.0 * (theta - (4.0 + 2.0 * vertical)) / delta
    last = 1.0 / chebyshev_values()[KCHEB]
    zero = jnp.zeros((8, COLS), jnp.float32)
    lane = iota((8, COLS), 1)
    lanes = [slice(0, COLS), slice(COLS, 2 * COLS)]

    def clear(n, carry):
        at = n * (PLANES - 1)
        for i in range(8):
            s = slice(i * 8, i * 8 + 8)
            for t in range(2):
                for x in (own, own_y, beside, beside_y):
                    x[at, t, s] = zero
            strip[at, 0, s] = zero
            strip_y[at, 0, s] = zero
        return carry

    lax.fori_loop(0, 2, clear, 0)

    def begin(z, carry):
        at = z + 1
        for i in range(8):
            s = slice(i * 8, i * 8 + 8)
            tiles = tiles_of((low_ref, block_ref, high_ref), field_start, (left_ref, right_ref), 0, z, i)
            inner = 1 <= i < 7
            for t in range(2):
                guess = tiles[t] * (1.0 / delta)
                value = guess if t == 0 and 2 <= i < 6 else guess * own_m[t, s]
                own[at, t, s] = value
                own_y[at, t, s] = zero
                if inner:
                    wide_r[z, t, s] = guess + guess
                beside_y[at, t, s] = zero
                beside[at, t, s] = zero if i in (3, 4) else guess * beside_m[t, s]
            guess = tiles[2] * (1.0 / delta)
            strip[at, 0, s] = guess * strip_m[s]
            strip_y[at, 0, s] = zero
            if inner:
                strip_r[z, 0, s] = guess + guess
                tiles = tiles_of((low_c, absorption_ref, high_c), coef_start, (left_c, right_c), coef_at, z, i)
                diag[z, 0, s] = base - (2.0 / delta) * tiles[0]
                diag[z, 1, s] = base - (2.0 / delta) * tiles[1]
                strip_diag[z, 0, s] = base - (2.0 / delta) * tiles[2]
        return carry

    lax.fori_loop(0, LEVELS, begin, 0, unroll=UNROLL_BEGIN)
    at_first, at_last = lane == 0, lane == COLS - 1

    def step(here, x, y, r, a, mask, width, i, amount):
        s = slice(i * 8, i * 8 + 8)
        up, down = slice(i * 8 - 1, i * 8 + 7), slice(i * 8 + 1, i * 8 + 9)
        z = here - 1
        now = [x[here, t, s] for t in range(width)]
        back = [roll(v, 1) for v in now]
        fore = [roll(v, -1) for v in now]
        if width == 2:
            back = [jnp.where(at_first, back[1], back[0]), jnp.where(at_first, back[0], back[1])]
            fore = [jnp.where(at_last, fore[1], fore[0]), jnp.where(at_last, fore[0], fore[1])]
        for t in range(width):
            high = x[here - 1, t, s] + x[here + 1, t, s]
            around = (x[here, t, up] + x[here, t, down]) + (back[t] + fore[t])
            around = around + (high + high)
            after = (a[z, t, s] * now[t] + amount * r[z, t, s]) + ((2.0 / delta) * around - y[here, t, s])
            if mask[t] is not None:
                after = after * mask[t]
            y[here, t, s] = after

    first = ((own, own_y), (beside, beside_y), (strip, strip_y))
    second = tuple((y, x) for x, y in first)

    def sweep(n, arrays):
        amount = table_ref[n]
        own, beside, strip = arrays

        def level(z, carry):
            here = z + 1
            for i in range(1, 7):
                s = slice(i * 8, i * 8 + 8)
                free = None if 2 <= i < 6 else own_m[0, s]
                step(here, *own, wide_r, diag, [free, own_m[1, s]], 2, i, amount)
                if i in BESIDE_TILES:
                    step(here, *beside, wide_r, diag, [beside_m[0, s], beside_m[1, s]], 2, i, amount)
                step(here, *strip, strip_r, strip_diag, [strip_m[s]], 1, i, amount)
            return carry

        lax.fori_loop(0, LEVELS, level, 0, unroll=UNROLL)

    def pair(n, carry):
        sweep(2 * n, first)
        sweep(2 * n + 1, second)
        return carry

    lax.fori_loop(0, (KCHEB - 1) // 2, pair, 0)
    near_first, near_last = lane < EDGE, lane >= COLS - EDGE

    def finish(z, carry):
        at = z + 1
        for i in range(1, 7):
            s = slice(i * 8, i * 8 + 8)
            out = slice(i * 8 - 8, i * 8)
            value = strip[at, 0, s]
            at_left = value + roll(value, -32)
            at_right = roll(at_left, 64)
            first = jnp.where(near_first, at_left, jnp.where(near_last, at_right, 0.0))
            second = jnp.where(near_last, at_left, jnp.where(near_first, at_right, 0.0))
            first = first + own[at, 0, s]
            second = second + own[at, 1, s]
            if i in BESIDE_TILES:
                first = first + beside[at, 0, s]
                second = second + beside[at, 1, s]
            out_ref[z, out, lanes[0]] = first * last
            out_ref[z, out, lanes[1]] = second * last
        return carry

    lax.fori_loop(0, LEVELS, finish, 0, unroll=UNROLL_FINISH)


def smooth(place, table, told, block, low, high, strips, absorption, coefficient=None):
    wide = (2, TALL, COLS)
    thin = (1, TALL, COLS)

    def scratch(*shape):
        return pltpu.VMEM(shape, jnp.float32)

    more = () if coefficient is None else coefficient
    specs = [SMEM_SPEC] * 2 + [VMEM_SPEC] * 2 + [VMEM_SPEC if more else FIELDS_SPEC] * 2 + [VMEM_SPEC] * 3
    if more:
        specs += [FIELDS_SPEC] * 2 + [VMEM_SPEC] * 2
    return pl.pallas_call(
        functools.partial(smooth_kernel, not more),
        grid=(1,),
        in_specs=specs,
        out_shape=(pltpu.HBM if more else jax.ShapeDtypeStruct)((LEVELS, INNER, 2 * COLS), jnp.float32),
        scratch_shapes=[
            scratch(*wide), scratch(*wide), scratch(TALL, COLS),
            scratch(PLANES, *wide), scratch(PLANES, *wide), scratch(PLANES, *thin),
            scratch(PLANES, *wide), scratch(PLANES, *wide), scratch(PLANES, *thin),
            scratch(LEVELS, *wide), scratch(LEVELS, *thin),
            scratch(LEVELS, *wide), scratch(LEVELS, *thin),
        ],
        compiler_params=pltpu.CompilerParams(vmem_limit_bytes=VMEM_LIMIT),
        cost_estimate=pl.CostEstimate(flops=2000000, bytes_accessed=54000000, transcendentals=0),
        name="smoother",
    )(place, table, told, block, low, high, *strips, absorption, *more)


INNER = ROWS + 16


def slots_of(place, told_ref, moves):
    lane = iota((1, COLS), 1)
    slots = jnp.zeros((1, COLS), jnp.float32)
    for n, (down, right) in enumerate(moves):
        row = roll(told_ref[pl.ds(place.index(down, right), 1), :], VECTORS * (n - 1))
        slots = jnp.where((lane >> 5) == n, row, slots)
    return slots.astype(jnp.int32)


def coarse_at(coarse_turned, slots):
    pick = jnp.where(iota((COLS, COLS), 0) == (slots >> 5), 1.0, 0.0)
    found = jnp.dot(coarse_turned, pick, precision=HIGHEST, preferred_element_type=jnp.float32)
    found = jnp.where(iota((VECTORS, COLS), 0) == (slots & 31), found, 0.0)
    return jnp.sum(found, axis=0, keepdims=True)


def add_coarse(place, told_ref, coarse_ref, basis_hbm, basis_ref, sems, low_ref, high_ref, left_ref, right_ref, at, sum_ref, x,
               own_c, edge_c, ring_ref, side_ref, ready=None):
    def part(q):
        levels = pl.ds(q * 4, 4)
        return pltpu.make_async_copy(basis_hbm.at[:, levels], basis_ref.at[:, levels], sems.at[q])

    for q in range(LEVELS // 4):
        part(q).start()
    turned = coarse_ref[...].T[:VECTORS]
    row = coarse_at(turned, slots_of(place, told_ref, ((0, 0), (-1, 0), (1, 0), (0, -1))))
    other = coarse_at(turned, slots_of(place, told_ref, ((0, 1),)))
    lane = iota((8, COLS), 1)
    lane_row = iota((1, COLS), 1)
    column = jnp.broadcast_to(row, (COLS, COLS)).T
    own_c[...] = column[:VECTORS]
    edge_c[...] = column[VECTORS : 3 * VECTORS]
    for n, edge in ((0, low_ref), (1, high_ref)):

        def vector(k, total):
            return total + edge[2 * LEVELS + k] * edge_c[pl.ds(n * VECTORS + k, 1), :]

        ring_ref[n] = lax.fori_loop(0, VECTORS, vector, jnp.zeros((LEVELS, COLS), jnp.float32))
    which = iota((COLS, COLS), 0) >> 5
    for n, (edge, values) in enumerate(((left_ref, roll(row, VECTORS)), (right_ref, other))):
        values = jnp.where(lane_row < VECTORS, values, 0.0)
        values = values + roll(values, 32) + roll(values, 64) + roll(values, 96)
        weights = jnp.broadcast_to(values, (COLS, COLS)).T
        weights = jnp.where(iota((COLS, COLS), 1) == which, weights, 0.0)
        parts = edge[at : at + 2].reshape(2 * TALL, COLS)
        side_ref[n] = jnp.dot(parts, weights, precision=HIGHEST, preferred_element_type=jnp.float32)

    def level(z, carry):
        total = sum_ref[z, 8 : 8 + ROWS, 0:COLS]
        for k in range(VECTORS):
            total = total + basis_ref[k, z].astype(jnp.float32) * own_c[k : k + 1]
        here = z + 1
        x[here, 8 : 8 + ROWS, 0:COLS] = total
        rows = pl.ds(z, 1)
        x[here, 7:8, 0:COLS] = sum_ref[z, 7:8, 0:COLS] + ring_ref[0, rows, :]
        x[here, 8 + ROWS : 9 + ROWS, 0:COLS] = sum_ref[z, 8 + ROWS : 9 + ROWS, 0:COLS] + ring_ref[1, rows, :]
        q = z & 3
        for i in range(ROWS // 8):
            s = pl.ds(pl.multiple_of((z >> 2) * ROWS + i * 8, 8), 8)
            left = pltpu.roll(side_ref[0, s, :], (COLS - 1) - q, 1)
            right = pltpu.roll(side_ref[1, s, :], (COLS - q) & (COLS - 1), 1)
            t = slice(8 + i * 8, 16 + i * 8)
            value = jnp.where(lane == COLS - 1, left, jnp.where(lane == 0, right, 0.0))
            x[here, t, COLS : 2 * COLS] = sum_ref[z, t, COLS : 2 * COLS] + value
        return carry

    if ready is not None:
        ready.wait()

    def levels(q, carry):
        part(q).wait()
        return lax.fori_loop(0, 2, lambda n, c: level(4 * q + 2 * n + 1, level(4 * q + 2 * n, c)), carry)

    lax.fori_loop(0, LEVELS // 4, levels, 0)
    zero = jnp.zeros((ROWS, COLS), jnp.float32)
    x[0, 8 : 8 + ROWS, 0:COLS] = zero
    x[PLANES - 1, 8 : 8 + ROWS, 0:COLS] = zero
    return row


def image_at(x, absorption_ref, z, i):
    lane = iota((8, COLS), 1)
    here = z + 1
    s = slice(8 + i * 8, 16 + i * 8)
    up, down = slice(7 + i * 8, 15 + i * 8), slice(9 + i * 8, 17 + i * 8)
    now = x[here, s, 0:COLS]
    margin = x[here, s, COLS : 2 * COLS]
    back = jnp.where(lane == 0, roll(margin, 1), roll(now, 1))
    fore = jnp.where(lane == COLS - 1, roll(margin, -1), roll(now, -1))
    high = x[here - 1, s, 0:COLS] + x[here + 1, s, 0:COLS]
    around = (x[here, up, 0:COLS] + x[here, down, 0:COLS]) + (back + fore)
    diagonal = absorption_ref[z, i * 8 : i * 8 + 8, :] + (4.0 + 2.0 * vertical)
    return now, diagonal * now - around - vertical * high


def total_of(value):
    return jnp.sum(jnp.sum(value, axis=0, keepdims=True), axis=1, keepdims=True)


def scalars(told_ref):
    totals = jnp.sum(told_ref[...], axis=0, keepdims=True)
    return totals[:, 64:65], totals[:, 65:66]


def first_coarse_kernel(
    place_ref, told_ref, coarse_ref, basis_hbm, low_ref, high_ref, left_ref, right_ref, sum_ref, source_ref, absorption_ref,
    direction_ref, image_ref, ahead_ref, behind_ref, out_ref, x, own_c, edge_c, ring_ref, side_ref, basis_ref, sems, sums_ref,
):
    place = Place(place_ref, told_ref)
    row = add_coarse(place, told_ref, coarse_ref, basis_hbm, basis_ref, sems, low_ref, high_ref, left_ref, right_ref, 4, sum_ref, x,
                     own_c, edge_c, ring_ref, side_ref)
    zero = jnp.zeros((8, COLS), jnp.float32)

    def images(z, carry):
        weight, curve = carry
        for i in range(ROWS // 8):
            s = slice(i * 8, i * 8 + 8)
            now, image = image_at(x, absorption_ref, z, i)
            direction_ref[z, s] = now
            image_ref[z, s] = image
            if i >= 2:
                ahead_ref[z, (i - 2) * 8 : (i - 1) * 8] = image
            else:
                behind_ref[z, s] = image
            weight = weight + source_ref[z, s] * sum_ref[z, 8 + i * 8 : 16 + i * 8, 0:COLS]
            curve = curve + now * image
        return weight, curve

    weight, curve = lax.fori_loop(0, LEVELS, images, (zero, zero), unroll=2)
    half = VECTORS // 2
    for part in range(2):

        def level(z, sums):
            image = image_ref[z]
            return tuple(
                sums[k] + fold_rows(basis_ref[part * half + k, z].astype(jnp.float32) * image) for k in range(half)
            )

        sums = lax.fori_loop(0, LEVELS, level, (zero,) * half)
        for k in range(half):
            sums_ref[part * half + k : part * half + k + 1] = jnp.sum(sums[k], axis=0, keepdims=True)
    lane = iota((1, COLS), 1)
    row = jnp.where(lane < VECTORS, row, 0.0)
    mine = told_ref[pl.ds(place.index(0, 0), 1), :]
    told = roll(row, VECTORS)
    told = told + jnp.where(lane == 64, total_of(weight) + total_of(row * mine), 0.0)
    told = told + jnp.where(lane == 65, total_of(curve), 0.0)
    out_ref[...] = row_of_sums(sums_ref[...]) + told


def second_coarse_kernel(
    place_ref, told_ref, coarse_ref, basis_hbm, low_ref, high_ref, left_ref, right_ref, sum_hbm, source_ref, absorption_ref,
    again_ref, first_sum_ref, direction_ref, first_ref,
    residual_ref, precond_ref, image_ref, out_ref, x, own_c, edge_c, ring_ref, side_ref, basis_ref, sems,
    sum_ref, sum_sem,
):
    copy = pltpu.make_async_copy(sum_hbm, sum_ref, sum_sem)
    copy.start()
    place = Place(place_ref, told_ref)
    row = add_coarse(place, told_ref, coarse_ref, basis_hbm, basis_ref, sems, low_ref, high_ref, left_ref, right_ref, 4, sum_ref, x,
                     own_c, edge_c, ring_ref, side_ref, copy)
    weight0, curve0 = scalars(again_ref)
    step = weight0 / curve0
    zero = jnp.zeros((8, COLS), jnp.float32)

    def images(z, sums):
        weight, own, cross = sums
        for i in range(ROWS // 8):
            s = slice(i * 8, i * 8 + 8)
            t = slice(8 + i * 8, 16 + i * 8)
            now, image = image_at(x, absorption_ref, z, i)
            direction, first = direction_ref[z, s], first_ref[z, s]
            residual = source_ref[z, s] - step * first
            precond = direction - step * now
            image = first - step * image
            residual_ref[z, s] = residual
            precond_ref[z, s] = precond
            image_ref[z, s] = image
            weight = weight + residual * (first_sum_ref[z, t, 0:COLS] - step * sum_ref[z, t, 0:COLS])
            own = own + precond * image
            cross = cross + (precond * first + direction * image)
        return weight, own, cross

    weight, own, cross = lax.fori_loop(0, LEVELS, images, (zero, zero, zero), unroll=2)
    mine = pl.ds(place.index(0, 0), 1)
    lane = iota((1, COLS), 1)
    again = again_ref[mine, :]
    projected = told_ref[mine, :] - step * again
    coarse = roll(again, -VECTORS) - step * row
    both = jnp.where(lane < VECTORS, projected * coarse, 0.0)
    told = jnp.where(lane == 0, total_of(weight) + total_of(both), 0.0)
    told = told + jnp.where(lane == 1, total_of(own), 0.0) + jnp.where(lane == 2, total_of(cross), 0.0)
    out_ref[...] = jnp.broadcast_to(told, (COLS, COLS))


def last_kernel(again_ref, last_ref, direction_ref, first_ref, residual_ref, precond_ref, image_ref, x_ref, r_ref):
    weight0, curve0 = scalars(again_ref)
    step0 = weight0 / curve0
    totals = jnp.sum(last_ref[...], axis=0, keepdims=True)
    weight1, own, cross = totals[:, 0:1], totals[:, 1:2], totals[:, 2:3]
    ratio = weight1 / weight0
    step1 = weight1 / (own + ratio * (cross + ratio * curve0))

    def level(z, carry):
        direction = direction_ref[z]
        x_ref[z] = step0 * direction + step1 * (precond_ref[z] + ratio * direction)
        r_ref[z] = residual_ref[z] - step1 * (image_ref[z] + ratio * first_ref[z])
        return carry

    lax.fori_loop(0, LEVELS, level, 0, unroll=4)


def shards(source, absorption, basis, coarse_inverse, margin_width, coarse_slot):
    block = jax.ShapeDtypeStruct((LEVELS, ROWS, COLS), jnp.float32)
    slab = jax.ShapeDtypeStruct((LEVELS, EDGE, COLS), jnp.float32)
    message = pltpu.HBM((COLS, COLS), jnp.float32)
    params = pltpu.CompilerParams(vmem_limit_bytes=VMEM_LIMIT)

    def scratch(*shape):
        return pltpu.VMEM(shape, jnp.float32)

    coarse_scratch = [
        scratch(PLANES, INNER, 2 * COLS), scratch(VECTORS, COLS), scratch(2 * VECTORS, COLS),
        scratch(2, LEVELS, COLS), scratch(2, 2 * TALL, COLS),
        pltpu.VMEM(basis.shape, basis.dtype), pltpu.SemaphoreType.DMA((LEVELS // 4,)),
    ]
    hbm = pl.BlockSpec(memory_space=pltpu.HBM)
    def in_hbm(value):
        return pltpu.with_memory_space_constraint(value, pltpu.HBM)

    place = jnp.stack(
        [lax.axis_index("gx"), lax.axis_index("gy"), lax.axis_size("gx"), lax.axis_size("gy")]
    ).astype(jnp.int32)
    table = jnp.array(chebyshev_table(), jnp.float32)
    rows, ahead, behind, sides = first_projection(
        source, absorption, basis, coarse_slot, margin_width
    )
    low, high = exchange(ahead, behind, "gx")
    told = everyone(rows)
    fields = [VMEM_SPEC] * 2 + [FIELDS_SPEC] * 2 + [HBM_SPEC]
    strips = exchange(
        *pack(first_pack_kernel, fields, 6, [scratch(LEVELS // 2, ROWS, COLS), pltpu.SemaphoreType.DMA], source, absorption, low, high, in_hbm(sides)), "gy"
    )
    coarse = everyone(solve_rows(told, told, in_hbm(coarse_inverse)))
    first_sum = smooth(place, table, told, source, low, high, strips, absorption)
    edges = (low, high, *strips)
    direction, image, ahead, behind, rows = pl.pallas_call(
        first_coarse_kernel,
        in_specs=[SMEM_SPEC] + [VMEM_SPEC] * 2 + [hbm] + [VMEM_SPEC] * 7,
        out_shape=[block, block, slab, slab, message],
        scratch_shapes=coarse_scratch + [scratch(VECTORS, COLS)],
        compiler_params=params,
        name="direction_and_image",
    )(place, told, coarse, in_hbm(basis), *edges, first_sum, source, absorption)
    low_w, high_w = exchange(ahead, behind, "gx")
    again = everyone(rows)
    strips_w = exchange(*pack(pack_kernel, [VMEM_SPEC] * 3, 2, [], image, low_w, high_w), "gy")
    coarse = everyone(solve_rows(again, told, in_hbm(coarse_inverse)))
    second_sum = smooth(place, table, told, image, low_w, high_w, strips_w, absorption, edges)
    residual, precond, precond_image, rows = pl.pallas_call(
        second_coarse_kernel,
        in_specs=[SMEM_SPEC] + [VMEM_SPEC] * 2 + [hbm] + [VMEM_SPEC] * 4 + [hbm] + [VMEM_SPEC] * 6,
        out_shape=[block, block, block, message],
        scratch_shapes=coarse_scratch + [scratch(LEVELS, INNER, 2 * COLS), pltpu.SemaphoreType.DMA],
        compiler_params=params,
        name="second_images",
    )(place, told, coarse, in_hbm(basis), *edges, in_hbm(second_sum), source, absorption, again, first_sum, direction, image)
    last = everyone(rows)
    concentration, residual = pl.pallas_call(
        last_kernel, out_shape=[block, block], compiler_params=params, name="update"
    )(again, last, direction, image, residual, precond, precond_image)
    return (concentration, residual)


def solution(mesh):
    return jax.shard_map(
        shards,
        mesh=mesh,
        in_specs=(
            P(None, "gx", "gy"),
            P(None, "gx", "gy"),
            P(None, None, "gx", "gy"),
            P(("gx", "gy"), None),
            P("gx", "gy"),
            P("gx", "gy", None),
        ),
        out_specs=(P(None, "gx", "gy"), P(None, "gx", "gy")),
        check_vma=False,
    )
```

```python
import functools

import jax
import jax.numpy as jnp
from jax import lax
from jax.experimental import pallas as pl
from jax.experimental.pallas import tpu as pltpu
from jax.sharding import PartitionSpec as P

KCHEB = 9
AXES = ("gx", "gy")
LEVELS = 16
ROWS = 32
COLS = 128
VECTORS = 32
EDGE = 16
TALL = ROWS + 2 * EDGE
HIGHEST = lax.Precision.HIGHEST

lowest_rate = 0.05
highest_rate = 18.5
vertical = 2.0
theta = 0.5 * (highest_rate + lowest_rate)
delta = 0.5 * (highest_rate - lowest_rate)
VMEM_LIMIT = 24 * 1024 * 1024
FIRST_LIMIT = 58 * 1024 * 1024


def chebyshev_values():
    ratio = theta / delta
    values = [1.0, ratio]
    while len(values) <= KCHEB:
        values.append(2.0 * ratio * values[-1] - values[-2])
    return values


def chebyshev_table():
    return chebyshev_values()[1:KCHEB]


def iota(shape, dim):
    return lax.broadcasted_iota(jnp.int32, shape, dim)


def roll(value, shift):
    return pltpu.roll(value, shift % COLS, 1)


def exchange(forward_value, backward_value, axis):
    count = lax.axis_size(axis)
    forward = [(i, i + 1) for i in range(count - 1)]
    backward = [(target, source) for source, target in forward]
    return lax.ppermute(forward_value, axis, forward), lax.ppermute(backward_value, axis, backward)


def everyone(rows):
    return lax.all_to_all(rows, AXES, 0, 0, tiled=True)


def row_of_sums(sums):
    padded = jnp.concatenate([sums, jnp.zeros((COLS - VECTORS, COLS), jnp.float32)], 0)
    ones = jnp.ones((COLS, COLS), jnp.float32)
    return lax.dot_general(
        ones, padded, (((1,), (1,)), ((), ())), precision=HIGHEST, preferred_element_type=jnp.float32
    )


def fold_rows(product):
    return (product[0:8] + product[8:16]) + (product[16:24] + product[24:32])


def first_kernel(
    field_ref, coefficient_ref, basis_ref, slots_ref, margin_ref,
    out_ref, ahead_ref, behind_ref, sides_ref, sums_ref, edges_ref,
):
    step = pl.program_id(0)
    group = basis_ref.shape[0]

    @pl.when(step == 0)
    def _():
        edges_ref[...] = jnp.zeros_like(edges_ref)

        def level(z, carry):
            ahead_ref[z] = field_ref[z, ROWS - EDGE :, :]
            behind_ref[z] = field_ref[z, :EDGE, :]
            ahead_ref[LEVELS + z] = coefficient_ref[z, ROWS - EDGE :, :]
            behind_ref[LEVELS + z] = coefficient_ref[z, :EDGE, :]
            return carry

        lax.fori_loop(0, LEVELS, level, 0)

    def level(z, sums):
        field = field_ref[z]
        new = []
        for j in range(group):
            values = basis_ref[j, z].astype(jnp.float32)
            new.append(sums[j] + fold_rows(values * field))
            at = 2 * LEVELS + step * group + j
            behind_ref[at, pl.ds(z, 1), :] = values[0:1]
            ahead_ref[at, pl.ds(z, 1), :] = values[ROWS - 1 : ROWS]
        return tuple(new)

    zero = jnp.zeros((8, COLS), jnp.float32)
    sums = lax.fori_loop(0, LEVELS, level, (zero,) * group, unroll=2)
    for j in range(group):
        sums_ref[pl.ds(step * group + j, 1), :] = jnp.sum(sums[j], axis=0, keepdims=True)
    from_lane, to_lane = iota((COLS, COLS), 0), iota((COLS, COLS), 1)
    picks = []
    for j in range(group):
        k = step * group + j
        pick = ((from_lane == 0) & (to_lane == k)) | ((from_lane == COLS - 1) & (to_lane == VECTORS + k))
        picks.append(jnp.where(pick, 1.0, 0.0).astype(jnp.bfloat16))
    values = jnp.concatenate([basis_ref[j].reshape(LEVELS * ROWS, COLS) for j in range(group)], axis=1)
    edges_ref[...] += jnp.dot(values, jnp.concatenate(picks, 0), preferred_element_type=jnp.float32)

    @pl.when(step == pl.num_programs(0) - 1)
    def _():
        told = jnp.concatenate(
            [
                jnp.zeros((1, VECTORS), jnp.float32),
                slots_ref[0].astype(jnp.float32),
                margin_ref[...].astype(jnp.float32),
                jnp.zeros((1, COLS - 65), jnp.float32),
            ],
            axis=1,
        )
        out_ref[...] = row_of_sums(sums_ref[...]) + told
        place = iota((ROWS, COLS), 1) >> 5
        for n in range(LEVELS // 4):
            left = jnp.zeros((ROWS, COLS), jnp.float32)
            right = left
            for q in range(4):
                z = 4 * n + q
                value = edges_ref[z * ROWS : (z + 1) * ROWS]
                left = jnp.where(place == q, roll(value, VECTORS * q), left)
                right = jnp.where(place == q, roll(value, VECTORS * (q - 1)), right)
            sides_ref[n] = left
            sides_ref[LEVELS // 4 + n] = right


def first_projection(field, coefficient, basis, slots, margin):
    group = 16
    rows = 2 * LEVELS + VECTORS
    edge_rows = jax.ShapeDtypeStruct((rows, LEVELS, COLS), jnp.float32)
    edge_cols = jax.ShapeDtypeStruct((LEVELS // 2, ROWS, COLS), jnp.float32)
    block_spec = pl.BlockSpec((LEVELS, ROWS, COLS), lambda i: (0, 0, 0))
    rows_spec = pl.BlockSpec(edge_rows.shape, lambda i: (0, 0, 0))
    cols_spec = pl.BlockSpec(edge_cols.shape, lambda i: (0, 0, 0))
    return pl.pallas_call(
        first_kernel,
        grid=(VECTORS // group,),
        in_specs=[
            block_spec,
            block_spec,
            pl.BlockSpec((group, LEVELS, ROWS, COLS), lambda i: (i, 0, 0, 0)),
            pl.BlockSpec(slots.shape, lambda i: (0, 0, 0)),
            pl.BlockSpec(margin.shape, lambda i: (0, 0)),
        ],
        out_specs=[pl.BlockSpec((COLS, COLS), lambda i: (0, 0)), rows_spec, rows_spec, cols_spec],
        out_shape=[jax.ShapeDtypeStruct((COLS, COLS), jnp.float32), edge_rows, edge_rows, edge_cols],
        scratch_shapes=[
            pltpu.VMEM((VECTORS, COLS), jnp.float32), pltpu.VMEM((LEVELS * ROWS, COLS), jnp.float32)
        ],
        compiler_params=pltpu.CompilerParams(vmem_limit_bytes=FIRST_LIMIT),
        name="first_projection",
    )(field, coefficient, basis, slots, margin)


def coarse_rows(told_ref, slots_ref, inverse_hbm, out_ref, inverse_ref, sem):
    copy = pltpu.make_async_copy(inverse_hbm, inverse_ref, sem)
    copy.start()
    told = told_ref[...]
    slots = slots_ref[...]
    turned = told.T
    slots_turned = slots.T
    lane = iota((COLS, COLS), 1)
    sub = iota((VECTORS, COLS), 0)
    placed = jnp.zeros((3 * VECTORS, COLS), jnp.float32)
    for k in range(VECTORS):
        slot_column = slots[:, VECTORS + k : VECTORS + k + 1].astype(jnp.int32)
        ones = jnp.where((slot_column & 127) == lane, 1.0, 0.0).astype(jnp.bfloat16)
        slot_row = slots_turned[VECTORS + k : VECTORS + k + 1, :].astype(jnp.int32)
        values = turned[k : k + 1, :]
        spread = jnp.where((slot_row >> 7) == sub, values, 0.0)
        first = spread.astype(jnp.bfloat16)
        rest = spread - first.astype(jnp.float32)
        second = rest.astype(jnp.bfloat16)
        third = (rest - second.astype(jnp.float32)).astype(jnp.bfloat16)
        parts = jnp.concatenate([first, second, third], 0)
        placed = placed + jnp.dot(parts, ones, preferred_element_type=jnp.float32)
    placed = placed[:VECTORS] + placed[VECTORS : 2 * VECTORS] + placed[2 * VECTORS :]
    total = jnp.zeros((VECTORS, COLS), jnp.float32)
    copy.wait()
    for high in range(VECTORS):
        total = total + inverse_ref[:, high * COLS : (high + 1) * COLS] * placed[high : high + 1]
    out_ref[...] = row_of_sums(total)


def pack_strips(parts, forward_ref, backward_ref, at):
    def levels(group, carry):
        row = 0
        for part, start in parts:
            height = EDGE if part.shape[1] == EDGE else ROWS
            lane = iota((height, COLS), 1)
            ahead = jnp.zeros((height, COLS), jnp.float32)
            behind = ahead
            for j in range(8):
                value = part[start + group * 8 + j]
                mine = (lane >= EDGE * j) & (lane < EDGE * (j + 1))
                ahead = jnp.where(mine, roll(value, EDGE * j - (COLS - EDGE)), ahead)
                behind = jnp.where(mine, roll(value, EDGE * j), behind)
            forward_ref[at + group, row : row + height, :] = ahead
            backward_ref[at + group, row : row + height, :] = behind
            row += height
        return carry

    lax.fori_loop(0, LEVELS // 8, levels, 0)


def first_pack_kernel(
    source_ref, absorption_ref, low_ref, high_ref, sides_hbm, forward_ref, backward_ref, sides_ref, sem
):
    copy = pltpu.make_async_copy(sides_hbm, sides_ref, sem)
    copy.start()
    for f, block in enumerate((source_ref, absorption_ref)):
        pack_strips(((low_ref, LEVELS * f), (block, 0), (high_ref, LEVELS * f)), forward_ref, backward_ref, 2 * f)
    copy.wait()
    for n in range(LEVELS // 8):
        for half in range(2):
            rows = slice(half * ROWS, (half + 1) * ROWS)
            forward_ref[4 + n, rows, :] = sides_ref[LEVELS // 4 + 2 * n + half]
            backward_ref[4 + n, rows, :] = sides_ref[2 * n + half]


def pack_kernel(block_ref, low_ref, high_ref, forward_ref, backward_ref):
    pack_strips(((low_ref, 0), (block_ref, 0), (high_ref, 0)), forward_ref, backward_ref, 0)


FIELDS_SPEC = pl.BlockSpec((2 * LEVELS, EDGE, COLS), lambda i: (0, 0, 0))
VMEM_SPEC = pl.BlockSpec(memory_space=pltpu.VMEM)
HBM_SPEC = pl.BlockSpec(memory_space=pltpu.HBM)
SMEM_SPEC = pl.BlockSpec(memory_space=pltpu.SMEM)


def pack(kernel, specs, strips, scratch, *operands):
    strips = jax.ShapeDtypeStruct((strips, TALL, COLS), jnp.float32)
    return pl.pallas_call(
        kernel,
        grid=(1,),
        in_specs=specs,
        out_shape=[strips, strips],
        scratch_shapes=scratch,
        compiler_params=pltpu.CompilerParams(vmem_limit_bytes=VMEM_LIMIT),
        cost_estimate=pl.CostEstimate(flops=3000000000, bytes_accessed=1000000, transcendentals=0),
        name="strips",
    )(*operands)


def solve_rows(*operands):
    return pl.pallas_call(
        coarse_rows,
        in_specs=[VMEM_SPEC] * 2 + [HBM_SPEC],
        out_shape=pltpu.HBM((COLS, COLS), jnp.float32),
        scratch_shapes=[pltpu.VMEM((VECTORS, COLS * VECTORS), jnp.float32), pltpu.SemaphoreType.DMA],
        compiler_params=pltpu.CompilerParams(vmem_limit_bytes=VMEM_LIMIT),
        cost_estimate=pl.CostEstimate(flops=9200000000, bytes_accessed=1000000, transcendentals=0),
        name="coarse_rows",
    )(*operands)


class Place:
    def __init__(self, place_ref, told_ref):
        self.row = place_ref[0]
        self.col = place_ref[1]
        self.rows = place_ref[2]
        self.cols = place_ref[3]
        self.told_ref = told_ref

    def index(self, down, right):
        row = jnp.clip(self.row + down, 0, self.rows - 1)
        col = jnp.clip(self.col + right, 0, self.cols - 1)
        return row * self.cols + col

    def margin(self, down, right):
        row, col = self.row + down, self.col + right
        real = (row >= 0) & (row < self.rows) & (col >= 0) & (col < self.cols)
        margin = self.told_ref[pl.ds(self.index(down, right), 1), :][:, 64:65]
        return jnp.where(real, margin.astype(jnp.int32), -4096)


def masks(place, own_ref, beside_ref, strip_ref):
    shape = (TALL, COLS)
    row = iota(shape, 0) - EDGE
    lane = iota(shape, 1)
    top, bottom = -ROWS * place.row, ROWS * (place.rows - place.row)
    first, last = -COLS * place.col, COLS * (place.cols - place.col)
    row_real = (row >= top) & (row < bottom)
    m = {(i, j): place.margin(i, j) for i in (-1, 0, 1) for j in (-1, 0, 1)}
    upper, lower = row < 8, row >= ROWS - 8
    for tile in range(2):
        col = lane if tile == 0 else jnp.where(lane < 64, lane + COLS, lane - COLS)
        real = row_real & (col >= first) & (col < last)
        if tile == 1:
            real = real & ((lane < EDGE) | (lane >= COLS - EDGE))

        def across(margin):
            return (col >= -margin) & (col < COLS + margin)

        own = m[0, 0]
        inside = real & (row >= -own) & (row < ROWS + own) & across(own)
        own_ref[tile] = jnp.where(inside, 1.0, 0.0)
        above, below = m[-1, 0], m[1, 0]
        inside = (upper & (row < above) & across(above)) | (lower & (row >= ROWS - below) & across(below))
        beside_ref[tile] = jnp.where(real & inside, 1.0, 0.0)
    group = ((lane + EDGE) & 127) >> 5
    away = ((lane + EDGE) & 31) - EDGE
    inside = row < -4096
    for place_of, side in ((0, -1), (2, 1)):
        col = away if side < 0 else away + COLS
        real = row_real & (col >= first) & (col < last)

        def reached(margin):
            return (away < margin) if side < 0 else (away >= -margin)

        level = m[0, side]
        inside = inside | (
            (group == place_of) & real & (row >= -level) & (row < ROWS + level) & reached(level)
        )
        above, below = m[-1, side], m[1, side]
        corner = (upper & (row < above) & reached(above)) | (
            lower & (row >= ROWS - below) & reached(below)
        )
        inside = inside | ((group == place_of + 1) & real & corner)
    strip_ref[...] = jnp.where(inside, 1.0, 0.0)


def tiles_of(parts, start, strips, at, z, i):
    low, block, high = parts
    from_left, from_right = strips
    lane = iota((8, COLS), 1)
    if i < 2:
        center = low[start + z, i * 8 : i * 8 + 8, :]
    elif i < 6:
        center = block[z, (i - 2) * 8 : (i - 2) * 8 + 8, :]
    else:
        center = high[start + z, (i - 6) * 8 : (i - 6) * 8 + 8, :]
    s = slice(i * 8, i * 8 + 8)
    group, shift = at + (z >> 3), EDGE * (z & 7)
    left = pltpu.roll(from_left[group, s, :], (COLS - EDGE) - shift, 1)
    right = pltpu.roll(from_right[group, s, :], (COLS - shift) & (COLS - 1), 1)
    margin = jnp.where(lane >= COLS - EDGE, left, jnp.where(lane < EDGE, right, 0.0))
    at_left = jnp.where(lane >= 64, margin, center)
    at_right = jnp.where(lane < 64, margin, center)
    near = (lane < EDGE) | (lane >= COLS - EDGE)
    others = jnp.where(lane < 80, roll(at_right, 64), roll(at_right, 96))
    packed = jnp.where(near, at_left, jnp.where(lane < 48, roll(at_left, 32), others))
    return center, margin, packed


UNROLL = 16
UNROLL_BEGIN = 2
UNROLL_FINISH = 4
PLANES = LEVELS + 2
BESIDE_TILES = (1, 2, 5, 6)


def smooth_kernel(same, place_ref, table_ref, told_ref, block_ref, low_ref, high_ref, left_ref, right_ref, absorption_ref, *refs):
    if same:
        low_c, high_c, left_c, right_c = low_ref, high_ref, left_ref, right_ref
    else:
        low_c, high_c, left_c, right_c = refs[:4]
        refs = refs[4:]
    (
        out_ref, own_m, beside_m, strip_m, own, beside, strip, own_y, beside_y, strip_y,
        wide_r, strip_r, diag, strip_diag,
    ) = refs
    field_start, coef_start, coef_at = 0, LEVELS, 2
    masks(Place(place_ref, told_ref), own_m, beside_m, strip_m)
    base = 2.0 * (theta - (4.0 + 2.0 * vertical)) / delta
    last = 1.0 / chebyshev_values()[KCHEB]
    zero = jnp.zeros((8, COLS), jnp.float32)
    lane = iota((8, COLS), 1)
    lanes = [slice(0, COLS), slice(COLS, 2 * COLS)]

    def clear(n, carry):
        at = n * (PLANES - 1)
        for i in range(8):
            s = slice(i * 8, i * 8 + 8)
            for t in range(2):
                for x in (own, own_y, beside, beside_y):
                    x[at, t, s] = zero
            strip[at, 0, s] = zero
            strip_y[at, 0, s] = zero
        return carry

    lax.fori_loop(0, 2, clear, 0)

    def begin(z, carry):
        at = z + 1
        for i in range(8):
            s = slice(i * 8, i * 8 + 8)
            tiles = tiles_of((low_ref, block_ref, high_ref), field_start, (left_ref, right_ref), 0, z, i)
            inner = 1 <= i < 7
            for t in range(2):
                guess = tiles[t] * (1.0 / delta)
                value = guess if t == 0 and 2 <= i < 6 else guess * own_m[t, s]
                own[at, t, s] = value
                own_y[at, t, s] = zero
                if inner:
                    wide_r[z, t, s] = guess + guess
                beside_y[at, t, s] = zero
                beside[at, t, s] = zero if i in (3, 4) else guess * beside_m[t, s]
            guess = tiles[2] * (1.0 / delta)
            strip[at, 0, s] = guess * strip_m[s]
            strip_y[at, 0, s] = zero
            if inner:
                strip_r[z, 0, s] = guess + guess
                tiles = tiles_of((low_c, absorption_ref, high_c), coef_start, (left_c, right_c), coef_at, z, i)
                diag[z, 0, s] = base - (2.0 / delta) * tiles[0]
                diag[z, 1, s] = base - (2.0 / delta) * tiles[1]
                strip_diag[z, 0, s] = base - (2.0 / delta) * tiles[2]
        return carry

    lax.fori_loop(0, LEVELS, begin, 0, unroll=UNROLL_BEGIN)
    at_first, at_last = lane == 0, lane == COLS - 1

    def step(here, x, y, r, a, mask, width, i, amount):
        s = slice(i * 8, i * 8 + 8)
        up, down = slice(i * 8 - 1, i * 8 + 7), slice(i * 8 + 1, i * 8 + 9)
        z = here - 1
        now = [x[here, t, s] for t in range(width)]
        back = [roll(v, 1) for v in now]
        fore = [roll(v, -1) for v in now]
        if width == 2:
            back = [jnp.where(at_first, back[1], back[0]), jnp.where(at_first, back[0], back[1])]
            fore = [jnp.where(at_last, fore[1], fore[0]), jnp.where(at_last, fore[0], fore[1])]
        for t in range(width):
            high = x[here - 1, t, s] + x[here + 1, t, s]
            around = (x[here, t, up] + x[here, t, down]) + (back[t] + fore[t])
            around = around + (high + high)
            after = (a[z, t, s] * now[t] + amount * r[z, t, s]) + ((2.0 / delta) * around - y[here, t, s])
            if mask[t] is not None:
                after = after * mask[t]
            y[here, t, s] = after

    first = ((own, own_y), (beside, beside_y), (strip, strip_y))
    second = tuple((y, x) for x, y in first)

    def sweep(n, arrays):
        amount = table_ref[n]
        own, beside, strip = arrays

        def level(z, carry):
            here = z + 1
            for i in range(1, 7):
                s = slice(i * 8, i * 8 + 8)
                free = None if 2 <= i < 6 else own_m[0, s]
                step(here, *own, wide_r, diag, [free, own_m[1, s]], 2, i, amount)
                if i in BESIDE_TILES:
                    step(here, *beside, wide_r, diag, [beside_m[0, s], beside_m[1, s]], 2, i, amount)
                step(here, *strip, strip_r, strip_diag, [strip_m[s]], 1, i, amount)
            return carry

        lax.fori_loop(0, LEVELS, level, 0, unroll=UNROLL)

    def pair(n, carry):
        sweep(2 * n, first)
        sweep(2 * n + 1, second)
        return carry

    lax.fori_loop(0, (KCHEB - 1) // 2, pair, 0)
    near_first, near_last = lane < EDGE, lane >= COLS - EDGE

    def finish(z, carry):
        at = z + 1
        for i in range(1, 7):
            s = slice(i * 8, i * 8 + 8)
            out = slice(i * 8 - 8, i * 8)
            value = strip[at, 0, s]
            at_left = value + roll(value, -32)
            at_right = roll(at_left, 64)
            first = jnp.where(near_first, at_left, jnp.where(near_last, at_right, 0.0))
            second = jnp.where(near_last, at_left, jnp.where(near_first, at_right, 0.0))
            first = first + own[at, 0, s]
            second = second + own[at, 1, s]
            if i in BESIDE_TILES:
                first = first + beside[at, 0, s]
                second = second + beside[at, 1, s]
            out_ref[z, out, lanes[0]] = first * last
            out_ref[z, out, lanes[1]] = second * last
        return carry

    lax.fori_loop(0, LEVELS, finish, 0, unroll=UNROLL_FINISH)


def smooth(place, table, told, block, low, high, strips, absorption, coefficient=None):
    wide = (2, TALL, COLS)
    thin = (1, TALL, COLS)

    def scratch(*shape):
        return pltpu.VMEM(shape, jnp.float32)

    more = () if coefficient is None else coefficient
    specs = [SMEM_SPEC] * 2 + [VMEM_SPEC] * 2 + [VMEM_SPEC if more else FIELDS_SPEC] * 2 + [VMEM_SPEC] * 3
    if more:
        specs += [FIELDS_SPEC] * 2 + [VMEM_SPEC] * 2
    return pl.pallas_call(
        functools.partial(smooth_kernel, not more),
        grid=(1,),
        in_specs=specs,
        out_shape=(pltpu.HBM if more else jax.ShapeDtypeStruct)((LEVELS, INNER, 2 * COLS), jnp.float32),
        scratch_shapes=[
            scratch(*wide), scratch(*wide), scratch(TALL, COLS),
            scratch(PLANES, *wide), scratch(PLANES, *wide), scratch(PLANES, *thin),
            scratch(PLANES, *wide), scratch(PLANES, *wide), scratch(PLANES, *thin),
            scratch(LEVELS, *wide), scratch(LEVELS, *thin),
            scratch(LEVELS, *wide), scratch(LEVELS, *thin),
        ],
        compiler_params=pltpu.CompilerParams(vmem_limit_bytes=VMEM_LIMIT),
        cost_estimate=pl.CostEstimate(flops=2000000, bytes_accessed=54000000, transcendentals=0),
        name="smoother",
    )(place, table, told, block, low, high, *strips, absorption, *more)


INNER = ROWS + 16


def slots_of(place, told_ref, moves):
    lane = iota((1, COLS), 1)
    slots = jnp.zeros((1, COLS), jnp.float32)
    for n, (down, right) in enumerate(moves):
        row = roll(told_ref[pl.ds(place.index(down, right), 1), :], VECTORS * (n - 1))
        slots = jnp.where((lane >> 5) == n, row, slots)
    return slots.astype(jnp.int32)


def coarse_at(coarse_turned, slots):
    pick = jnp.where(iota((COLS, COLS), 0) == (slots >> 5), 1.0, 0.0)
    found = jnp.dot(coarse_turned, pick, precision=HIGHEST, preferred_element_type=jnp.float32)
    found = jnp.where(iota((VECTORS, COLS), 0) == (slots & 31), found, 0.0)
    return jnp.sum(found, axis=0, keepdims=True)


def add_coarse(place, told_ref, coarse_ref, basis_hbm, basis_ref, sems, low_ref, high_ref, left_ref, right_ref, at, sum_ref, x,
               own_c, edge_c, ring_ref, side_ref, ready=None):
    def part(q):
        levels = pl.ds(q * 4, 4)
        return pltpu.make_async_copy(basis_hbm.at[:, levels], basis_ref.at[:, levels], sems.at[q])

    for q in range(LEVELS // 4):
        part(q).start()
    turned = coarse_ref[...].T[:VECTORS]
    row = coarse_at(turned, slots_of(place, told_ref, ((0, 0), (-1, 0), (1, 0), (0, -1))))
    other = coarse_at(turned, slots_of(place, told_ref, ((0, 1),)))
    lane = iota((8, COLS), 1)
    lane_row = iota((1, COLS), 1)
    column = jnp.broadcast_to(row, (COLS, COLS)).T
    own_c[...] = column[:VECTORS]
    edge_c[...] = column[VECTORS : 3 * VECTORS]
    for n, edge in ((0, low_ref), (1, high_ref)):

        def vector(k, total):
            return total + edge[2 * LEVELS + k] * edge_c[pl.ds(n * VECTORS + k, 1), :]

        ring_ref[n] = lax.fori_loop(0, VECTORS, vector, jnp.zeros((LEVELS, COLS), jnp.float32))
    which = iota((COLS, COLS), 0) >> 5
    for n, (edge, values) in enumerate(((left_ref, roll(row, VECTORS)), (right_ref, other))):
        values = jnp.where(lane_row < VECTORS, values, 0.0)
        values = values + roll(values, 32) + roll(values, 64) + roll(values, 96)
        weights = jnp.broadcast_to(values, (COLS, COLS)).T
        weights = jnp.where(iota((COLS, COLS), 1) == which, weights, 0.0)
        parts = edge[at : at + 2].reshape(2 * TALL, COLS)
        side_ref[n] = jnp.dot(parts, weights, precision=HIGHEST, preferred_element_type=jnp.float32)

    def level(z, carry):
        total = sum_ref[z, 8 : 8 + ROWS, 0:COLS]
        for k in range(VECTORS):
            total = total + basis_ref[k, z].astype(jnp.float32) * own_c[k : k + 1]
        here = z + 1
        x[here, 8 : 8 + ROWS, 0:COLS] = total
        rows = pl.ds(z, 1)
        x[here, 7:8, 0:COLS] = sum_ref[z, 7:8, 0:COLS] + ring_ref[0, rows, :]
        x[here, 8 + ROWS : 9 + ROWS, 0:COLS] = sum_ref[z, 8 + ROWS : 9 + ROWS, 0:COLS] + ring_ref[1, rows, :]
        q = z & 3
        for i in range(ROWS // 8):
            s = pl.ds(pl.multiple_of((z >> 2) * ROWS + i * 8, 8), 8)
            left = pltpu.roll(side_ref[0, s, :], (COLS - 1) - q, 1)
            right = pltpu.roll(side_ref[1, s, :], (COLS - q) & (COLS - 1), 1)
            t = slice(8 + i * 8, 16 + i * 8)
            value = jnp.where(lane == COLS - 1, left, jnp.where(lane == 0, right, 0.0))
            x[here, t, COLS : 2 * COLS] = sum_ref[z, t, COLS : 2 * COLS] + value
        return carry

    if ready is not None:
        ready.wait()

    def levels(q, carry):
        part(q).wait()
        return lax.fori_loop(0, 2, lambda n, c: level(4 * q + 2 * n + 1, level(4 * q + 2 * n, c)), carry)

    lax.fori_loop(0, LEVELS // 4, levels, 0)
    zero = jnp.zeros((ROWS, COLS), jnp.float32)
    x[0, 8 : 8 + ROWS, 0:COLS] = zero
    x[PLANES - 1, 8 : 8 + ROWS, 0:COLS] = zero
    return row


def image_at(x, absorption_ref, z, i):
    lane = iota((8, COLS), 1)
    here = z + 1
    s = slice(8 + i * 8, 16 + i * 8)
    up, down = slice(7 + i * 8, 15 + i * 8), slice(9 + i * 8, 17 + i * 8)
    now = x[here, s, 0:COLS]
    margin = x[here, s, COLS : 2 * COLS]
    back = jnp.where(lane == 0, roll(margin, 1), roll(now, 1))
    fore = jnp.where(lane == COLS - 1, roll(margin, -1), roll(now, -1))
    high = x[here - 1, s, 0:COLS] + x[here + 1, s, 0:COLS]
    around = (x[here, up, 0:COLS] + x[here, down, 0:COLS]) + (back + fore)
    diagonal = absorption_ref[z, i * 8 : i * 8 + 8, :] + (4.0 + 2.0 * vertical)
    return now, diagonal * now - around - vertical * high


def total_of(value):
    return jnp.sum(jnp.sum(value, axis=0, keepdims=True), axis=1, keepdims=True)


def scalars(told_ref):
    totals = jnp.sum(told_ref[...], axis=0, keepdims=True)
    return totals[:, 64:65], totals[:, 65:66]


def first_coarse_kernel(
    place_ref, told_ref, coarse_ref, basis_hbm, low_ref, high_ref, left_ref, right_ref, sum_ref, source_ref, absorption_ref,
    direction_ref, image_ref, ahead_ref, behind_ref, out_ref, x, own_c, edge_c, ring_ref, side_ref, basis_ref, sems, sums_ref,
):
    place = Place(place_ref, told_ref)
    row = add_coarse(place, told_ref, coarse_ref, basis_hbm, basis_ref, sems, low_ref, high_ref, left_ref, right_ref, 4, sum_ref, x,
                     own_c, edge_c, ring_ref, side_ref)
    zero = jnp.zeros((8, COLS), jnp.float32)

    def images(z, carry):
        weight, curve = carry
        for i in range(ROWS // 8):
            s = slice(i * 8, i * 8 + 8)
            now, image = image_at(x, absorption_ref, z, i)
            direction_ref[z, s] = now
            image_ref[z, s] = image
            if i >= 2:
                ahead_ref[z, (i - 2) * 8 : (i - 1) * 8] = image
            else:
                behind_ref[z, s] = image
            weight = weight + source_ref[z, s] * sum_ref[z, 8 + i * 8 : 16 + i * 8, 0:COLS]
            curve = curve + now * image
        return weight, curve

    weight, curve = lax.fori_loop(0, LEVELS, images, (zero, zero), unroll=4)
    half = VECTORS // 2
    for part in range(2):

        def level(z, sums):
            image = image_ref[z]
            return tuple(
                sums[k] + fold_rows(basis_ref[part * half + k, z].astype(jnp.float32) * image) for k in range(half)
            )

        sums = lax.fori_loop(0, LEVELS, level, (zero,) * half, unroll=2)
        for k in range(half):
            sums_ref[part * half + k : part * half + k + 1] = jnp.sum(sums[k], axis=0, keepdims=True)
    lane = iota((1, COLS), 1)
    row = jnp.where(lane < VECTORS, row, 0.0)
    mine = told_ref[pl.ds(place.index(0, 0), 1), :]
    told = roll(row, VECTORS)
    told = told + jnp.where(lane == 64, total_of(weight) + total_of(row * mine), 0.0)
    told = told + jnp.where(lane == 65, total_of(curve), 0.0)
    out_ref[...] = row_of_sums(sums_ref[...]) + told


def second_coarse_kernel(
    place_ref, told_ref, coarse_ref, basis_hbm, low_ref, high_ref, left_ref, right_ref, sum_hbm, source_ref, absorption_ref,
    again_ref, first_sum_ref, direction_ref, first_ref,
    residual_ref, precond_ref, image_ref, out_ref, x, own_c, edge_c, ring_ref, side_ref, basis_ref, sems,
    sum_ref, sum_sem,
):
    copy = pltpu.make_async_copy(sum_hbm, sum_ref, sum_sem)
    copy.start()
    place = Place(place_ref, told_ref)
    row = add_coarse(place, told_ref, coarse_ref, basis_hbm, basis_ref, sems, low_ref, high_ref, left_ref, right_ref, 4, sum_ref, x,
                     own_c, edge_c, ring_ref, side_ref, copy)
    weight0, curve0 = scalars(again_ref)
    step = weight0 / curve0
    zero = jnp.zeros((8, COLS), jnp.float32)

    def images(z, sums):
        weight, own, cross = sums
        for i in range(ROWS // 8):
            s = slice(i * 8, i * 8 + 8)
            t = slice(8 + i * 8, 16 + i * 8)
            now, image = image_at(x, absorption_ref, z, i)
            direction, first = direction_ref[z, s], first_ref[z, s]
            residual = source_ref[z, s] - step * first
            precond = direction - step * now
            image = first - step * image
            residual_ref[z, s] = residual
            precond_ref[z, s] = precond
            image_ref[z, s] = image
            weight = weight + residual * (first_sum_ref[z, t, 0:COLS] - step * sum_ref[z, t, 0:COLS])
            own = own + precond * image
            cross = cross + (precond * first + direction * image)
        return weight, own, cross

    weight, own, cross = lax.fori_loop(0, LEVELS, images, (zero, zero, zero), unroll=4)
    mine = pl.ds(place.index(0, 0), 1)
    lane = iota((1, COLS), 1)
    again = again_ref[mine, :]
    projected = told_ref[mine, :] - step * again
    coarse = roll(again, -VECTORS) - step * row
    both = jnp.where(lane < VECTORS, projected * coarse, 0.0)
    told = jnp.where(lane == 0, total_of(weight) + total_of(both), 0.0)
    told = told + jnp.where(lane == 1, total_of(own), 0.0) + jnp.where(lane == 2, total_of(cross), 0.0)
    out_ref[...] = jnp.broadcast_to(told, (COLS, COLS))


def last_kernel(again_ref, last_ref, direction_ref, first_ref, residual_ref, precond_ref, image_ref, x_ref, r_ref):
    weight0, curve0 = scalars(again_ref)
    step0 = weight0 / curve0
    totals = jnp.sum(last_ref[...], axis=0, keepdims=True)
    weight1, own, cross = totals[:, 0:1], totals[:, 1:2], totals[:, 2:3]
    ratio = weight1 / weight0
    step1 = weight1 / (own + ratio * (cross + ratio * curve0))

    def level(z, carry):
        direction = direction_ref[z]
        x_ref[z] = step0 * direction + step1 * (precond_ref[z] + ratio * direction)
        r_ref[z] = residual_ref[z] - step1 * (image_ref[z] + ratio * first_ref[z])
        return carry

    lax.fori_loop(0, LEVELS, level, 0, unroll=4)


def shards(source, absorption, basis, coarse_inverse, margin_width, coarse_slot):
    block = jax.ShapeDtypeStruct((LEVELS, ROWS, COLS), jnp.float32)
    slab = jax.ShapeDtypeStruct((LEVELS, EDGE, COLS), jnp.float32)
    message = pltpu.HBM((COLS, COLS), jnp.float32)
    params = pltpu.CompilerParams(vmem_limit_bytes=VMEM_LIMIT)

    def scratch(*shape):
        return pltpu.VMEM(shape, jnp.float32)

    coarse_scratch = [
        scratch(PLANES, INNER, 2 * COLS), scratch(VECTORS, COLS), scratch(2 * VECTORS, COLS),
        scratch(2, LEVELS, COLS), scratch(2, 2 * TALL, COLS),
        pltpu.VMEM(basis.shape, basis.dtype), pltpu.SemaphoreType.DMA((LEVELS // 4,)),
    ]
    hbm = pl.BlockSpec(memory_space=pltpu.HBM)
    def in_hbm(value):
        return pltpu.with_memory_space_constraint(value, pltpu.HBM)

    place = jnp.stack(
        [lax.axis_index("gx"), lax.axis_index("gy"), lax.axis_size("gx"), lax.axis_size("gy")]
    ).astype(jnp.int32)
    table = jnp.array(chebyshev_table(), jnp.float32)
    rows, ahead, behind, sides = first_projection(
        source, absorption, basis, coarse_slot, margin_width
    )
    low, high = exchange(ahead, behind, "gx")
    told = everyone(rows)
    fields = [VMEM_SPEC] * 2 + [FIELDS_SPEC] * 2 + [HBM_SPEC]
    strips = exchange(
        *pack(first_pack_kernel, fields, 6, [scratch(LEVELS // 2, ROWS, COLS), pltpu.SemaphoreType.DMA], source, absorption, low, high, in_hbm(sides)), "gy"
    )
    coarse = everyone(solve_rows(told, told, in_hbm(coarse_inverse)))
    first_sum = smooth(place, table, told, source, low, high, strips, absorption)
    edges = (low, high, *strips)
    direction, image, ahead, behind, rows = pl.pallas_call(
        first_coarse_kernel,
        in_specs=[SMEM_SPEC] + [VMEM_SPEC] * 2 + [hbm] + [VMEM_SPEC] * 7,
        out_shape=[block, block, slab, slab, message],
        scratch_shapes=coarse_scratch + [scratch(VECTORS, COLS)],
        compiler_params=params,
        name="direction_and_image",
    )(place, told, coarse, in_hbm(basis), *edges, first_sum, source, absorption)
    low_w, high_w = exchange(ahead, behind, "gx")
    again = everyone(rows)
    strips_w = exchange(*pack(pack_kernel, [VMEM_SPEC] * 3, 2, [], image, low_w, high_w), "gy")
    coarse = everyone(solve_rows(again, told, in_hbm(coarse_inverse)))
    second_sum = smooth(place, table, told, image, low_w, high_w, strips_w, absorption, edges)
    residual, precond, precond_image, rows = pl.pallas_call(
        second_coarse_kernel,
        in_specs=[SMEM_SPEC] + [VMEM_SPEC] * 2 + [hbm] + [VMEM_SPEC] * 4 + [hbm] + [VMEM_SPEC] * 6,
        out_shape=[block, block, block, message],
        scratch_shapes=coarse_scratch + [scratch(LEVELS, INNER, 2 * COLS), pltpu.SemaphoreType.DMA],
        compiler_params=params,
        name="second_images",
    )(place, told, coarse, in_hbm(basis), *edges, in_hbm(second_sum), source, absorption, again, first_sum, direction, image)
    last = everyone(rows)
    concentration, residual = pl.pallas_call(
        last_kernel, out_shape=[block, block], compiler_params=params, name="update"
    )(again, last, direction, image, residual, precond, precond_image)
    return (concentration, residual)


def solution(mesh):
    return jax.shard_map(
        shards,
        mesh=mesh,
        in_specs=(
            P(None, "gx", "gy"),
            P(None, "gx", "gy"),
            P(None, None, "gx", "gy"),
            P(("gx", "gy"), None),
            P("gx", "gy"),
            P("gx", "gy", None),
        ),
        out_specs=(P(None, "gx", "gy"), P(None, "gx", "gy")),
        check_vma=False,
    )
```

```python
import functools

import jax
import jax.numpy as jnp
from jax import lax
from jax.experimental import pallas as pl
from jax.experimental.pallas import tpu as pltpu
from jax.sharding import PartitionSpec as P

KCHEB = 9
AXES = ("gx", "gy")
LEVELS = 16
ROWS = 32
COLS = 128
VECTORS = 32
EDGE = 16
TALL = ROWS + 2 * EDGE
HIGHEST = lax.Precision.HIGHEST

lowest_rate = 0.05
highest_rate = 18.5
vertical = 2.0
theta = 0.5 * (highest_rate + lowest_rate)
delta = 0.5 * (highest_rate - lowest_rate)
VMEM_LIMIT = 24 * 1024 * 1024
FIRST_LIMIT = 58 * 1024 * 1024


def chebyshev_values():
    ratio = theta / delta
    values = [1.0, ratio]
    while len(values) <= KCHEB:
        values.append(2.0 * ratio * values[-1] - values[-2])
    return values


def chebyshev_table():
    return chebyshev_values()[1:KCHEB]


def iota(shape, dim):
    return lax.broadcasted_iota(jnp.int32, shape, dim)


def roll(value, shift):
    return pltpu.roll(value, shift % COLS, 1)


def exchange(forward_value, backward_value, axis):
    count = lax.axis_size(axis)
    forward = [(i, i + 1) for i in range(count - 1)]
    backward = [(target, source) for source, target in forward]
    return lax.ppermute(forward_value, axis, forward), lax.ppermute(backward_value, axis, backward)


def everyone(rows):
    return lax.all_to_all(rows, AXES, 0, 0, tiled=True)


def row_of_sums(sums):
    padded = jnp.concatenate([sums, jnp.zeros((COLS - VECTORS, COLS), jnp.float32)], 0)
    ones = jnp.ones((COLS, COLS), jnp.float32)
    return lax.dot_general(
        ones, padded, (((1,), (1,)), ((), ())), precision=HIGHEST, preferred_element_type=jnp.float32
    )


def fold_rows(product):
    return (product[0:8] + product[8:16]) + (product[16:24] + product[24:32])


def first_kernel(
    field_ref, coefficient_ref, basis_ref, slots_ref, margin_ref,
    out_ref, ahead_ref, behind_ref, sides_ref, sums_ref, edges_ref,
):
    step = pl.program_id(0)
    group = basis_ref.shape[0]

    @pl.when(step == 0)
    def _():
        edges_ref[...] = jnp.zeros_like(edges_ref)

        def level(z, carry):
            ahead_ref[z] = field_ref[z, ROWS - EDGE :, :]
            behind_ref[z] = field_ref[z, :EDGE, :]
            ahead_ref[LEVELS + z] = coefficient_ref[z, ROWS - EDGE :, :]
            behind_ref[LEVELS + z] = coefficient_ref[z, :EDGE, :]
            return carry

        lax.fori_loop(0, LEVELS, level, 0)

    def level(z, sums):
        field = field_ref[z]
        new = []
        for j in range(group):
            values = basis_ref[j, z].astype(jnp.float32)
            new.append(sums[j] + fold_rows(values * field))
            at = 2 * LEVELS + step * group + j
            behind_ref[at, pl.ds(z, 1), :] = values[0:1]
            ahead_ref[at, pl.ds(z, 1), :] = values[ROWS - 1 : ROWS]
        return tuple(new)

    zero = jnp.zeros((8, COLS), jnp.float32)
    sums = lax.fori_loop(0, LEVELS, level, (zero,) * group, unroll=2)
    for j in range(group):
        sums_ref[pl.ds(step * group + j, 1), :] = jnp.sum(sums[j], axis=0, keepdims=True)
    from_lane, to_lane = iota((COLS, COLS), 0), iota((COLS, COLS), 1)
    picks = []
    for j in range(group):
        k = step * group + j
        pick = ((from_lane == 0) & (to_lane == k)) | ((from_lane == COLS - 1) & (to_lane == VECTORS + k))
        picks.append(jnp.where(pick, 1.0, 0.0).astype(jnp.bfloat16))
    values = jnp.concatenate([basis_ref[j].reshape(LEVELS * ROWS, COLS) for j in range(group)], axis=1)
    edges_ref[...] += jnp.dot(values, jnp.concatenate(picks, 0), preferred_element_type=jnp.float32)

    @pl.when(step == pl.num_programs(0) - 1)
    def _():
        told = jnp.concatenate(
            [
                jnp.zeros((1, VECTORS), jnp.float32),
                slots_ref[0].astype(jnp.float32),
                margin_ref[...].astype(jnp.float32),
                jnp.zeros((1, COLS - 65), jnp.float32),
            ],
            axis=1,
        )
        out_ref[...] = row_of_sums(sums_ref[...]) + told
        place = iota((ROWS, COLS), 1) >> 5
        for n in range(LEVELS // 4):
            left = jnp.zeros((ROWS, COLS), jnp.float32)
            right = left
            for q in range(4):
                z = 4 * n + q
                value = edges_ref[z * ROWS : (z + 1) * ROWS]
                left = jnp.where(place == q, roll(value, VECTORS * q), left)
                right = jnp.where(place == q, roll(value, VECTORS * (q - 1)), right)
            sides_ref[n] = left
            sides_ref[LEVELS // 4 + n] = right


def first_projection(field, coefficient, basis, slots, margin):
    group = 16
    rows = 2 * LEVELS + VECTORS
    edge_rows = jax.ShapeDtypeStruct((rows, LEVELS, COLS), jnp.float32)
    edge_cols = jax.ShapeDtypeStruct((LEVELS // 2, ROWS, COLS), jnp.float32)
    block_spec = pl.BlockSpec((LEVELS, ROWS, COLS), lambda i: (0, 0, 0))
    rows_spec = pl.BlockSpec(edge_rows.shape, lambda i: (0, 0, 0))
    cols_spec = pl.BlockSpec(edge_cols.shape, lambda i: (0, 0, 0))
    return pl.pallas_call(
        first_kernel,
        grid=(VECTORS // group,),
        in_specs=[
            block_spec,
            block_spec,
            pl.BlockSpec((group, LEVELS, ROWS, COLS), lambda i: (i, 0, 0, 0)),
            pl.BlockSpec(slots.shape, lambda i: (0, 0, 0)),
            pl.BlockSpec(margin.shape, lambda i: (0, 0)),
        ],
        out_specs=[pl.BlockSpec((COLS, COLS), lambda i: (0, 0)), rows_spec, rows_spec, cols_spec],
        out_shape=[jax.ShapeDtypeStruct((COLS, COLS), jnp.float32), edge_rows, edge_rows, edge_cols],
        scratch_shapes=[
            pltpu.VMEM((VECTORS, COLS), jnp.float32), pltpu.VMEM((LEVELS * ROWS, COLS), jnp.float32)
        ],
        compiler_params=pltpu.CompilerParams(vmem_limit_bytes=FIRST_LIMIT),
        name="first_projection",
    )(field, coefficient, basis, slots, margin)


def coarse_rows(told_ref, slots_ref, inverse_hbm, out_ref, inverse_ref, sem):
    copy = pltpu.make_async_copy(inverse_hbm, inverse_ref, sem)
    copy.start()
    told = told_ref[...]
    slots = slots_ref[...]
    turned = told.T
    slots_turned = slots.T
    lane = iota((COLS, COLS), 1)
    sub = iota((VECTORS, COLS), 0)
    placed = jnp.zeros((3 * VECTORS, COLS), jnp.float32)
    for k in range(VECTORS):
        slot_column = slots[:, VECTORS + k : VECTORS + k + 1].astype(jnp.int32)
        ones = jnp.where((slot_column & 127) == lane, 1.0, 0.0).astype(jnp.bfloat16)
        slot_row = slots_turned[VECTORS + k : VECTORS + k + 1, :].astype(jnp.int32)
        values = turned[k : k + 1, :]
        spread = jnp.where((slot_row >> 7) == sub, values, 0.0)
        first = spread.astype(jnp.bfloat16)
        rest = spread - first.astype(jnp.float32)
        second = rest.astype(jnp.bfloat16)
        third = (rest - second.astype(jnp.float32)).astype(jnp.bfloat16)
        parts = jnp.concatenate([first, second, third], 0)
        placed = placed + jnp.dot(parts, ones, preferred_element_type=jnp.float32)
    placed = placed[:VECTORS] + placed[VECTORS : 2 * VECTORS] + placed[2 * VECTORS :]
    total = jnp.zeros((VECTORS, COLS), jnp.float32)
    copy.wait()
    for high in range(VECTORS):
        total = total + inverse_ref[:, high * COLS : (high + 1) * COLS] * placed[high : high + 1]
    out_ref[...] = row_of_sums(total)


def pack_strips(parts, forward_ref, backward_ref, at):
    def levels(group, carry):
        row = 0
        for part, start in parts:
            height = EDGE if part.shape[1] == EDGE else ROWS
            lane = iota((height, COLS), 1)
            ahead = jnp.zeros((height, COLS), jnp.float32)
            behind = ahead
            for j in range(8):
                value = part[start + group * 8 + j]
                mine = (lane >= EDGE * j) & (lane < EDGE * (j + 1))
                ahead = jnp.where(mine, roll(value, EDGE * j - (COLS - EDGE)), ahead)
                behind = jnp.where(mine, roll(value, EDGE * j), behind)
            forward_ref[at + group, row : row + height, :] = ahead
            backward_ref[at + group, row : row + height, :] = behind
            row += height
        return carry

    lax.fori_loop(0, LEVELS // 8, levels, 0)


def first_pack_kernel(
    source_ref, absorption_ref, low_ref, high_ref, sides_hbm, forward_ref, backward_ref, sides_ref, sem
):
    copy = pltpu.make_async_copy(sides_hbm, sides_ref, sem)
    copy.start()
    for f, block in enumerate((source_ref, absorption_ref)):
        pack_strips(((low_ref, LEVELS * f), (block, 0), (high_ref, LEVELS * f)), forward_ref, backward_ref, 2 * f)
    copy.wait()
    for n in range(LEVELS // 8):
        for half in range(2):
            rows = slice(half * ROWS, (half + 1) * ROWS)
            forward_ref[4 + n, rows, :] = sides_ref[LEVELS // 4 + 2 * n + half]
            backward_ref[4 + n, rows, :] = sides_ref[2 * n + half]


def pack_kernel(block_ref, low_ref, high_ref, forward_ref, backward_ref):
    pack_strips(((low_ref, 0), (block_ref, 0), (high_ref, 0)), forward_ref, backward_ref, 0)


FIELDS_SPEC = pl.BlockSpec((2 * LEVELS, EDGE, COLS), lambda i: (0, 0, 0))
VMEM_SPEC = pl.BlockSpec(memory_space=pltpu.VMEM)
HBM_SPEC = pl.BlockSpec(memory_space=pltpu.HBM)
SMEM_SPEC = pl.BlockSpec(memory_space=pltpu.SMEM)


def pack(kernel, specs, strips, scratch, *operands):
    strips = jax.ShapeDtypeStruct((strips, TALL, COLS), jnp.float32)
    return pl.pallas_call(
        kernel,
        grid=(1,),
        in_specs=specs,
        out_shape=[strips, strips],
        scratch_shapes=scratch,
        compiler_params=pltpu.CompilerParams(vmem_limit_bytes=VMEM_LIMIT),
        cost_estimate=pl.CostEstimate(flops=3000000000, bytes_accessed=1000000, transcendentals=0),
        name="strips",
    )(*operands)


def solve_rows(*operands):
    return pl.pallas_call(
        coarse_rows,
        in_specs=[VMEM_SPEC] * 2 + [HBM_SPEC],
        out_shape=pltpu.HBM((COLS, COLS), jnp.float32),
        scratch_shapes=[pltpu.VMEM((VECTORS, COLS * VECTORS), jnp.float32), pltpu.SemaphoreType.DMA],
        compiler_params=pltpu.CompilerParams(vmem_limit_bytes=VMEM_LIMIT),
        cost_estimate=pl.CostEstimate(flops=9200000000, bytes_accessed=1000000, transcendentals=0),
        name="coarse_rows",
    )(*operands)


class Place:
    def __init__(self, place_ref, told_ref):
        self.row = place_ref[0]
        self.col = place_ref[1]
        self.rows = place_ref[2]
        self.cols = place_ref[3]
        self.told_ref = told_ref

    def index(self, down, right):
        row = jnp.clip(self.row + down, 0, self.rows - 1)
        col = jnp.clip(self.col + right, 0, self.cols - 1)
        return row * self.cols + col

    def margin(self, down, right):
        row, col = self.row + down, self.col + right
        real = (row >= 0) & (row < self.rows) & (col >= 0) & (col < self.cols)
        margin = self.told_ref[pl.ds(self.index(down, right), 1), :][:, 64:65]
        return jnp.where(real, margin.astype(jnp.int32), -4096)


def masks(place, own_ref, beside_ref, strip_ref):
    shape = (TALL, COLS)
    row = iota(shape, 0) - EDGE
    lane = iota(shape, 1)
    top, bottom = -ROWS * place.row, ROWS * (place.rows - place.row)
    first, last = -COLS * place.col, COLS * (place.cols - place.col)
    row_real = (row >= top) & (row < bottom)
    m = {(i, j): place.margin(i, j) for i in (-1, 0, 1) for j in (-1, 0, 1)}
    upper, lower = row < 8, row >= ROWS - 8
    for tile in range(2):
        col = lane if tile == 0 else jnp.where(lane < 64, lane + COLS, lane - COLS)
        real = row_real & (col >= first) & (col < last)
        if tile == 1:
            real = real & ((lane < EDGE) | (lane >= COLS - EDGE))

        def across(margin):
            return (col >= -margin) & (col < COLS + margin)

        own = m[0, 0]
        inside = real & (row >= -own) & (row < ROWS + own) & across(own)
        own_ref[tile] = jnp.where(inside, 1.0, 0.0)
        above, below = m[-1, 0], m[1, 0]
        inside = (upper & (row < above) & across(above)) | (lower & (row >= ROWS - below) & across(below))
        beside_ref[tile] = jnp.where(real & inside, 1.0, 0.0)
    group = ((lane + EDGE) & 127) >> 5
    away = ((lane + EDGE) & 31) - EDGE
    inside = row < -4096
    for place_of, side in ((0, -1), (2, 1)):
        col = away if side < 0 else away + COLS
        real = row_real & (col >= first) & (col < last)

        def reached(margin):
            return (away < margin) if side < 0 else (away >= -margin)

        level = m[0, side]
        inside = inside | (
            (group == place_of) & real & (row >= -level) & (row < ROWS + level) & reached(level)
        )
        above, below = m[-1, side], m[1, side]
        corner = (upper & (row < above) & reached(above)) | (
            lower & (row >= ROWS - below) & reached(below)
        )
        inside = inside | ((group == place_of + 1) & real & corner)
    strip_ref[...] = jnp.where(inside, 1.0, 0.0)


def tiles_of(parts, start, strips, at, z, i):
    low, block, high = parts
    from_left, from_right = strips
    lane = iota((8, COLS), 1)
    if i < 2:
        center = low[start + z, i * 8 : i * 8 + 8, :]
    elif i < 6:
        center = block[z, (i - 2) * 8 : (i - 2) * 8 + 8, :]
    else:
        center = high[start + z, (i - 6) * 8 : (i - 6) * 8 + 8, :]
    s = slice(i * 8, i * 8 + 8)
    group, shift = at + (z >> 3), EDGE * (z & 7)
    left = pltpu.roll(from_left[group, s, :], (COLS - EDGE) - shift, 1)
    right = pltpu.roll(from_right[group, s, :], (COLS - shift) & (COLS - 1), 1)
    margin = jnp.where(lane >= COLS - EDGE, left, jnp.where(lane < EDGE, right, 0.0))
    at_left = jnp.where(lane >= 64, margin, center)
    at_right = jnp.where(lane < 64, margin, center)
    near = (lane < EDGE) | (lane >= COLS - EDGE)
    others = jnp.where(lane < 80, roll(at_right, 64), roll(at_right, 96))
    packed = jnp.where(near, at_left, jnp.where(lane < 48, roll(at_left, 32), others))
    return center, margin, packed


UNROLL = 16
UNROLL_BEGIN = 2
UNROLL_FINISH = 4
PLANES = LEVELS + 2
BESIDE_TILES = (1, 2, 5, 6)


def smooth_kernel(same, place_ref, table_ref, told_ref, block_ref, low_ref, high_ref, left_ref, right_ref, absorption_ref, *refs):
    if same:
        low_c, high_c, left_c, right_c = low_ref, high_ref, left_ref, right_ref
    else:
        low_c, high_c, left_c, right_c = refs[:4]
        refs = refs[4:]
    (
        out_ref, own_m, beside_m, strip_m, own, beside, strip, own_y, beside_y, strip_y,
        wide_r, strip_r, diag, strip_diag,
    ) = refs
    field_start, coef_start, coef_at = 0, LEVELS, 2
    masks(Place(place_ref, told_ref), own_m, beside_m, strip_m)
    base = 2.0 * (theta - (4.0 + 2.0 * vertical)) / delta
    last = 1.0 / chebyshev_values()[KCHEB]
    zero = jnp.zeros((8, COLS), jnp.float32)
    lane = iota((8, COLS), 1)
    lanes = [slice(0, COLS), slice(COLS, 2 * COLS)]

    def clear(n, carry):
        at = n * (PLANES - 1)
        for i in range(8):
            s = slice(i * 8, i * 8 + 8)
            for t in range(2):
                for x in (own, own_y, beside, beside_y):
                    x[at, t, s] = zero
            strip[at, 0, s] = zero
            strip_y[at, 0, s] = zero
        return carry

    lax.fori_loop(0, 2, clear, 0)

    def begin(z, carry):
        at = z + 1
        for i in range(8):
            s = slice(i * 8, i * 8 + 8)
            tiles = tiles_of((low_ref, block_ref, high_ref), field_start, (left_ref, right_ref), 0, z, i)
            inner = 1 <= i < 7
            for t in range(2):
                guess = tiles[t] * (1.0 / delta)
                value = guess if t == 0 and 2 <= i < 6 else guess * own_m[t, s]
                own[at, t, s] = value
                own_y[at, t, s] = zero
                if inner:
                    wide_r[z, t, s] = guess + guess
                beside_y[at, t, s] = zero
                beside[at, t, s] = zero if i in (3, 4) else guess * beside_m[t, s]
            guess = tiles[2] * (1.0 / delta)
            strip[at, 0, s] = guess * strip_m[s]
            strip_y[at, 0, s] = zero
            if inner:
                strip_r[z, 0, s] = guess + guess
                tiles = tiles_of((low_c, absorption_ref, high_c), coef_start, (left_c, right_c), coef_at, z, i)
                diag[z, 0, s] = base - (2.0 / delta) * tiles[0]
                diag[z, 1, s] = base - (2.0 / delta) * tiles[1]
                strip_diag[z, 0, s] = base - (2.0 / delta) * tiles[2]
        return carry

    lax.fori_loop(0, LEVELS, begin, 0, unroll=UNROLL_BEGIN)
    at_first, at_last = lane == 0, lane == COLS - 1

    def step(here, x, y, r, a, mask, width, i, amount):
        s = slice(i * 8, i * 8 + 8)
        up, down = slice(i * 8 - 1, i * 8 + 7), slice(i * 8 + 1, i * 8 + 9)
        z = here - 1
        now = [x[here, t, s] for t in range(width)]
        back = [roll(v, 1) for v in now]
        fore = [roll(v, -1) for v in now]
        if width == 2:
            back = [jnp.where(at_first, back[1], back[0]), jnp.where(at_first, back[0], back[1])]
            fore = [jnp.where(at_last, fore[1], fore[0]), jnp.where(at_last, fore[0], fore[1])]
        for t in range(width):
            high = x[here - 1, t, s] + x[here + 1, t, s]
            around = (x[here, t, up] + x[here, t, down]) + (back[t] + fore[t])
            around = around + (high + high)
            after = (a[z, t, s] * now[t] + amount * r[z, t, s]) + ((2.0 / delta) * around - y[here, t, s])
            if mask[t] is not None:
                after = after * mask[t]
            y[here, t, s] = after

    first = ((own, own_y), (beside, beside_y), (strip, strip_y))
    second = tuple((y, x) for x, y in first)

    def sweep(n, arrays):
        amount = table_ref[n]
        own, beside, strip = arrays

        def level(z, carry):
            here = z + 1
            for i in range(1, 7):
                s = slice(i * 8, i * 8 + 8)
                free = None if 2 <= i < 6 else own_m[0, s]
                step(here, *own, wide_r, diag, [free, own_m[1, s]], 2, i, amount)
                if i in BESIDE_TILES:
                    step(here, *beside, wide_r, diag, [beside_m[0, s], beside_m[1, s]], 2, i, amount)
                step(here, *strip, strip_r, strip_diag, [strip_m[s]], 1, i, amount)
            return carry

        lax.fori_loop(0, LEVELS, level, 0, unroll=UNROLL)

    def pair(n, carry):
        sweep(2 * n, first)
        sweep(2 * n + 1, second)
        return carry

    lax.fori_loop(0, (KCHEB - 1) // 2, pair, 0)
    near_first, near_last = lane < EDGE, lane >= COLS - EDGE

    def finish(z, carry):
        at = z + 1
        for i in range(1, 7):
            s = slice(i * 8, i * 8 + 8)
            out = slice(i * 8 - 8, i * 8)
            value = strip[at, 0, s]
            at_left = value + roll(value, -32)
            at_right = roll(at_left, 64)
            first = jnp.where(near_first, at_left, jnp.where(near_last, at_right, 0.0))
            second = jnp.where(near_last, at_left, jnp.where(near_first, at_right, 0.0))
            first = first + own[at, 0, s]
            second = second + own[at, 1, s]
            if i in BESIDE_TILES:
                first = first + beside[at, 0, s]
                second = second + beside[at, 1, s]
            out_ref[z, out, lanes[0]] = first * last
            out_ref[z, out, lanes[1]] = second * last
        return carry

    lax.fori_loop(0, LEVELS, finish, 0, unroll=UNROLL_FINISH)


def smooth(place, table, told, block, low, high, strips, absorption, coefficient=None):
    wide = (2, TALL, COLS)
    thin = (1, TALL, COLS)

    def scratch(*shape):
        return pltpu.VMEM(shape, jnp.float32)

    more = () if coefficient is None else coefficient
    specs = [SMEM_SPEC] * 2 + [VMEM_SPEC] * 2 + [VMEM_SPEC if more else FIELDS_SPEC] * 2 + [VMEM_SPEC] * 3
    if more:
        specs += [FIELDS_SPEC] * 2 + [VMEM_SPEC] * 2
    return pl.pallas_call(
        functools.partial(smooth_kernel, not more),
        grid=(1,),
        in_specs=specs,
        out_shape=(pltpu.HBM if more else jax.ShapeDtypeStruct)((LEVELS, INNER, 2 * COLS), jnp.float32),
        scratch_shapes=[
            scratch(*wide), scratch(*wide), scratch(TALL, COLS),
            scratch(PLANES, *wide), scratch(PLANES, *wide), scratch(PLANES, *thin),
            scratch(PLANES, *wide), scratch(PLANES, *wide), scratch(PLANES, *thin),
            scratch(LEVELS, *wide), scratch(LEVELS, *thin),
            scratch(LEVELS, *wide), scratch(LEVELS, *thin),
        ],
        compiler_params=pltpu.CompilerParams(vmem_limit_bytes=VMEM_LIMIT),
        cost_estimate=pl.CostEstimate(flops=2000000, bytes_accessed=54000000, transcendentals=0),
        name="smoother",
    )(place, table, told, block, low, high, *strips, absorption, *more)


INNER = ROWS + 16


def slots_of(place, told_ref, moves):
    lane = iota((1, COLS), 1)
    slots = jnp.zeros((1, COLS), jnp.float32)
    for n, (down, right) in enumerate(moves):
        row = roll(told_ref[pl.ds(place.index(down, right), 1), :], VECTORS * (n - 1))
        slots = jnp.where((lane >> 5) == n, row, slots)
    return slots.astype(jnp.int32)


def coarse_at(coarse_turned, slots):
    pick = jnp.where(iota((COLS, COLS), 0) == (slots >> 5), 1.0, 0.0)
    found = jnp.dot(coarse_turned, pick, precision=HIGHEST, preferred_element_type=jnp.float32)
    found = jnp.where(iota((VECTORS, COLS), 0) == (slots & 31), found, 0.0)
    return jnp.sum(found, axis=0, keepdims=True)


def add_coarse(place, told_ref, coarse_ref, basis_hbm, basis_ref, sems, low_ref, high_ref, left_ref, right_ref, at, sum_ref, x,
               own_c, edge_c, ring_ref, side_ref, ready=None):
    def part(q):
        levels = pl.ds(q * 4, 4)
        return pltpu.make_async_copy(basis_hbm.at[:, levels], basis_ref.at[:, levels], sems.at[q])

    for q in range(LEVELS // 4):
        part(q).start()
    turned = coarse_ref[...].T[:VECTORS]
    row = coarse_at(turned, slots_of(place, told_ref, ((0, 0), (-1, 0), (1, 0), (0, -1))))
    other = coarse_at(turned, slots_of(place, told_ref, ((0, 1),)))
    lane = iota((8, COLS), 1)
    lane_row = iota((1, COLS), 1)
    column = jnp.broadcast_to(row, (COLS, COLS)).T
    own_c[...] = column[:VECTORS]
    edge_c[...] = column[VECTORS : 3 * VECTORS]
    for n, edge in ((0, low_ref), (1, high_ref)):

        def vector(k, total):
            return total + edge[2 * LEVELS + k] * edge_c[pl.ds(n * VECTORS + k, 1), :]

        ring_ref[n] = lax.fori_loop(0, VECTORS, vector, jnp.zeros((LEVELS, COLS), jnp.float32), unroll=8)
    which = iota((COLS, COLS), 0) >> 5
    for n, (edge, values) in enumerate(((left_ref, roll(row, VECTORS)), (right_ref, other))):
        values = jnp.where(lane_row < VECTORS, values, 0.0)
        values = values + roll(values, 32) + roll(values, 64) + roll(values, 96)
        weights = jnp.broadcast_to(values, (COLS, COLS)).T
        weights = jnp.where(iota((COLS, COLS), 1) == which, weights, 0.0)
        parts = edge[at : at + 2].reshape(2 * TALL, COLS)
        side_ref[n] = jnp.dot(parts, weights, precision=HIGHEST, preferred_element_type=jnp.float32)

    def level(z, carry):
        total = sum_ref[z, 8 : 8 + ROWS, 0:COLS]
        for k in range(VECTORS):
            total = total + basis_ref[k, z].astype(jnp.float32) * own_c[k : k + 1]
        here = z + 1
        x[here, 8 : 8 + ROWS, 0:COLS] = total
        rows = pl.ds(z, 1)
        x[here, 7:8, 0:COLS] = sum_ref[z, 7:8, 0:COLS] + ring_ref[0, rows, :]
        x[here, 8 + ROWS : 9 + ROWS, 0:COLS] = sum_ref[z, 8 + ROWS : 9 + ROWS, 0:COLS] + ring_ref[1, rows, :]
        q = z & 3
        for i in range(ROWS // 8):
            s = pl.ds(pl.multiple_of((z >> 2) * ROWS + i * 8, 8), 8)
            left = pltpu.roll(side_ref[0, s, :], (COLS - 1) - q, 1)
            right = pltpu.roll(side_ref[1, s, :], (COLS - q) & (COLS - 1), 1)
            t = slice(8 + i * 8, 16 + i * 8)
            value = jnp.where(lane == COLS - 1, left, jnp.where(lane == 0, right, 0.0))
            x[here, t, COLS : 2 * COLS] = sum_ref[z, t, COLS : 2 * COLS] + value
        return carry

    if ready is not None:
        ready.wait()

    def levels(q, carry):
        part(q).wait()
        return lax.fori_loop(0, 2, lambda n, c: level(4 * q + 2 * n + 1, level(4 * q + 2 * n, c)), carry)

    lax.fori_loop(0, LEVELS // 4, levels, 0)
    zero = jnp.zeros((ROWS, COLS), jnp.float32)
    x[0, 8 : 8 + ROWS, 0:COLS] = zero
    x[PLANES - 1, 8 : 8 + ROWS, 0:COLS] = zero
    return row


def image_at(x, absorption_ref, z, i):
    lane = iota((8, COLS), 1)
    here = z + 1
    s = slice(8 + i * 8, 16 + i * 8)
    up, down = slice(7 + i * 8, 15 + i * 8), slice(9 + i * 8, 17 + i * 8)
    now = x[here, s, 0:COLS]
    margin = x[here, s, COLS : 2 * COLS]
    back = jnp.where(lane == 0, roll(margin, 1), roll(now, 1))
    fore = jnp.where(lane == COLS - 1, roll(margin, -1), roll(now, -1))
    high = x[here - 1, s, 0:COLS] + x[here + 1, s, 0:COLS]
    around = (x[here, up, 0:COLS] + x[here, down, 0:COLS]) + (back + fore)
    diagonal = absorption_ref[z, i * 8 : i * 8 + 8, :] + (4.0 + 2.0 * vertical)
    return now, diagonal * now - around - vertical * high


def total_of(value):
    return jnp.sum(jnp.sum(value, axis=0, keepdims=True), axis=1, keepdims=True)


def scalars(told_ref):
    totals = jnp.sum(told_ref[...], axis=0, keepdims=True)
    return totals[:, 64:65], totals[:, 65:66]


def first_coarse_kernel(
    place_ref, told_ref, coarse_ref, basis_hbm, low_ref, high_ref, left_ref, right_ref, sum_ref, source_ref, absorption_ref,
    direction_ref, image_ref, ahead_ref, behind_ref, out_ref, x, own_c, edge_c, ring_ref, side_ref, basis_ref, sems, sums_ref,
):
    place = Place(place_ref, told_ref)
    row = add_coarse(place, told_ref, coarse_ref, basis_hbm, basis_ref, sems, low_ref, high_ref, left_ref, right_ref, 4, sum_ref, x,
                     own_c, edge_c, ring_ref, side_ref)
    zero = jnp.zeros((8, COLS), jnp.float32)

    def images(z, carry):
        weight, curve = carry
        for i in range(ROWS // 8):
            s = slice(i * 8, i * 8 + 8)
            now, image = image_at(x, absorption_ref, z, i)
            direction_ref[z, s] = now
            image_ref[z, s] = image
            if i >= 2:
                ahead_ref[z, (i - 2) * 8 : (i - 1) * 8] = image
            else:
                behind_ref[z, s] = image
            weight = weight + source_ref[z, s] * sum_ref[z, 8 + i * 8 : 16 + i * 8, 0:COLS]
            curve = curve + now * image
        return weight, curve

    weight, curve = lax.fori_loop(0, LEVELS, images, (zero, zero), unroll=4)
    half = VECTORS // 2
    for part in range(2):

        def level(z, sums):
            image = image_ref[z]
            return tuple(
                sums[k] + fold_rows(basis_ref[part * half + k, z].astype(jnp.float32) * image) for k in range(half)
            )

        sums = lax.fori_loop(0, LEVELS, level, (zero,) * half, unroll=2)
        for k in range(half):
            sums_ref[part * half + k : part * half + k + 1] = jnp.sum(sums[k], axis=0, keepdims=True)
    lane = iota((1, COLS), 1)
    row = jnp.where(lane < VECTORS, row, 0.0)
    mine = told_ref[pl.ds(place.index(0, 0), 1), :]
    told = roll(row, VECTORS)
    told = told + jnp.where(lane == 64, total_of(weight) + total_of(row * mine), 0.0)
    told = told + jnp.where(lane == 65, total_of(curve), 0.0)
    out_ref[...] = row_of_sums(sums_ref[...]) + told


def second_coarse_kernel(
    place_ref, told_ref, coarse_ref, basis_hbm, low_ref, high_ref, left_ref, right_ref, sum_hbm, source_ref, absorption_ref,
    again_ref, first_sum_ref, direction_ref, first_ref,
    residual_ref, precond_ref, image_ref, out_ref, x, own_c, edge_c, ring_ref, side_ref, basis_ref, sems,
    sum_ref, sum_sem,
):
    copy = pltpu.make_async_copy(sum_hbm, sum_ref, sum_sem)
    copy.start()
    place = Place(place_ref, told_ref)
    row = add_coarse(place, told_ref, coarse_ref, basis_hbm, basis_ref, sems, low_ref, high_ref, left_ref, right_ref, 4, sum_ref, x,
                     own_c, edge_c, ring_ref, side_ref, copy)
    weight0, curve0 = scalars(again_ref)
    step = weight0 / curve0
    zero = jnp.zeros((8, COLS), jnp.float32)

    def images(z, sums):
        weight, own, cross = sums
        for i in range(ROWS // 8):
            s = slice(i * 8, i * 8 + 8)
            t = slice(8 + i * 8, 16 + i * 8)
            now, image = image_at(x, absorption_ref, z, i)
            direction, first = direction_ref[z, s], first_ref[z, s]
            residual = source_ref[z, s] - step * first
            precond = direction - step * now
            image = first - step * image
            residual_ref[z, s] = residual
            precond_ref[z, s] = precond
            image_ref[z, s] = image
            weight = weight + residual * (first_sum_ref[z, t, 0:COLS] - step * sum_ref[z, t, 0:COLS])
            own = own + precond * image
            cross = cross + (precond * first + direction * image)
        return weight, own, cross

    weight, own, cross = lax.fori_loop(0, LEVELS, images, (zero, zero, zero), unroll=4)
    mine = pl.ds(place.index(0, 0), 1)
    lane = iota((1, COLS), 1)
    again = again_ref[mine, :]
    projected = told_ref[mine, :] - step * again
    coarse = roll(again, -VECTORS) - step * row
    both = jnp.where(lane < VECTORS, projected * coarse, 0.0)
    told = jnp.where(lane == 0, total_of(weight) + total_of(both), 0.0)
    told = told + jnp.where(lane == 1, total_of(own), 0.0) + jnp.where(lane == 2, total_of(cross), 0.0)
    out_ref[...] = jnp.broadcast_to(told, (COLS, COLS))


def last_kernel(again_ref, last_ref, direction_ref, first_ref, residual_ref, precond_ref, image_ref, x_ref, r_ref):
    weight0, curve0 = scalars(again_ref)
    step0 = weight0 / curve0
    totals = jnp.sum(last_ref[...], axis=0, keepdims=True)
    weight1, own, cross = totals[:, 0:1], totals[:, 1:2], totals[:, 2:3]
    ratio = weight1 / weight0
    step1 = weight1 / (own + ratio * (cross + ratio * curve0))

    def level(z, carry):
        direction = direction_ref[z]
        x_ref[z] = step0 * direction + step1 * (precond_ref[z] + ratio * direction)
        r_ref[z] = residual_ref[z] - step1 * (image_ref[z] + ratio * first_ref[z])
        return carry

    lax.fori_loop(0, LEVELS, level, 0, unroll=4)


def shards(source, absorption, basis, coarse_inverse, margin_width, coarse_slot):
    block = jax.ShapeDtypeStruct((LEVELS, ROWS, COLS), jnp.float32)
    slab = jax.ShapeDtypeStruct((LEVELS, EDGE, COLS), jnp.float32)
    message = pltpu.HBM((COLS, COLS), jnp.float32)
    params = pltpu.CompilerParams(vmem_limit_bytes=VMEM_LIMIT)

    def scratch(*shape):
        return pltpu.VMEM(shape, jnp.float32)

    coarse_scratch = [
        scratch(PLANES, INNER, 2 * COLS), scratch(VECTORS, COLS), scratch(2 * VECTORS, COLS),
        scratch(2, LEVELS, COLS), scratch(2, 2 * TALL, COLS),
        pltpu.VMEM(basis.shape, basis.dtype), pltpu.SemaphoreType.DMA((LEVELS // 4,)),
    ]
    hbm = pl.BlockSpec(memory_space=pltpu.HBM)
    def in_hbm(value):
        return pltpu.with_memory_space_constraint(value, pltpu.HBM)

    place = jnp.stack(
        [lax.axis_index("gx"), lax.axis_index("gy"), lax.axis_size("gx"), lax.axis_size("gy")]
    ).astype(jnp.int32)
    table = jnp.array(chebyshev_table(), jnp.float32)
    rows, ahead, behind, sides = first_projection(
        source, absorption, basis, coarse_slot, margin_width
    )
    low, high = exchange(ahead, behind, "gx")
    told = everyone(rows)
    fields = [VMEM_SPEC] * 2 + [FIELDS_SPEC] * 2 + [HBM_SPEC]
    strips = exchange(
        *pack(first_pack_kernel, fields, 6, [scratch(LEVELS // 2, ROWS, COLS), pltpu.SemaphoreType.DMA], source, absorption, low, high, in_hbm(sides)), "gy"
    )
    coarse = everyone(solve_rows(told, told, in_hbm(coarse_inverse)))
    first_sum = smooth(place, table, told, source, low, high, strips, absorption)
    edges = (low, high, *strips)
    direction, image, ahead, behind, rows = pl.pallas_call(
        first_coarse_kernel,
        in_specs=[SMEM_SPEC] + [VMEM_SPEC] * 2 + [hbm] + [VMEM_SPEC] * 7,
        out_shape=[block, block, slab, slab, message],
        scratch_shapes=coarse_scratch + [scratch(VECTORS, COLS)],
        compiler_params=params,
        name="direction_and_image",
    )(place, told, coarse, in_hbm(basis), *edges, first_sum, source, absorption)
    low_w, high_w = exchange(ahead, behind, "gx")
    again = everyone(rows)
    strips_w = exchange(*pack(pack_kernel, [VMEM_SPEC] * 3, 2, [], image, low_w, high_w), "gy")
    coarse = everyone(solve_rows(again, told, in_hbm(coarse_inverse)))
    second_sum = smooth(place, table, told, image, low_w, high_w, strips_w, absorption, edges)
    residual, precond, precond_image, rows = pl.pallas_call(
        second_coarse_kernel,
        in_specs=[SMEM_SPEC] + [VMEM_SPEC] * 2 + [hbm] + [VMEM_SPEC] * 4 + [hbm] + [VMEM_SPEC] * 6,
        out_shape=[block, block, block, message],
        scratch_shapes=coarse_scratch + [scratch(LEVELS, INNER, 2 * COLS), pltpu.SemaphoreType.DMA],
        compiler_params=params,
        name="second_images",
    )(place, told, coarse, in_hbm(basis), *edges, in_hbm(second_sum), source, absorption, again, first_sum, direction, image)
    last = everyone(rows)
    concentration, residual = pl.pallas_call(
        last_kernel, out_shape=[block, block], compiler_params=params, name="update"
    )(again, last, direction, image, residual, precond, precond_image)
    return (concentration, residual)


def solution(mesh):
    return jax.shard_map(
        shards,
        mesh=mesh,
        in_specs=(
            P(None, "gx", "gy"),
            P(None, "gx", "gy"),
            P(None, None, "gx", "gy"),
            P(("gx", "gy"), None),
            P("gx", "gy"),
            P("gx", "gy", None),
        ),
        out_specs=(P(None, "gx", "gy"), P(None, "gx", "gy")),
        check_vma=False,
    )
```
